32 devices in a mesh: gx: 2 (over y), gy: 4 (over x, core), gz: 4 (over z).
Axes of the slice: x: 2, y: 2, z: 4, core: 2. Of those that a mesh axis runs over, the one named last changes fastest.
Arguments:
- fields: float32 [4, 128, 64, 512], P(None, 'gz', 'gx', 'gy'), may hold values from -6 to 6
- material: int32 [128, 64, 512], P('gz', 'gx', 'gy'), may hold values from 0 to 15
- depth_order: int32 [4], replicated, may hold values from 0 to 3, each once
- table: float32 [4, 16], replicated, may hold values from 0.2 to 2
Outputs:
- image: float32 [4, 64, 512], P(None, ('gx', 'gz'), 'gy')
The draws below stay inside these ranges and needn't reach their ends.
Inputs may be any that keep to these rules, and one draw needn't show every extreme that they name: `depth_order`: a permutation: each brick layer along gz gets a distinct rank, 0 nearest the viewer.
All inputs are finite; a program needn't handle non-finite values.
Results may differ from the reference program's by a relative error of at most 0.0003.
Values sent between devices are 32-bit elements; how exact they have to be, the bound alone decides.
No kernel may reach another device: no remote copies, remote signals or barrier semaphores. Data moves between devices by JAX's collectives and lax.ppermute only.
A program may use at most 64 MiB of HBM per device.

```python
import jax
import jax.numpy as jnp
from jax import lax

BX = 32
BY = 128
BZ = 32
MATS = 16
NX = 64
NY = 512
NZ = 128
N_GX = 2
N_GY = 4
N_GZ = 4


def with_ends(values, key, least, top_value):
    longest = values.shape.index(max(values.shape))
    spots = []
    for shift in (0, 1):
        where = [jax.random.randint(jax.random.fold_in(key, axis), (), 0, length) for axis, length in enumerate(values.shape)]
        where[longest] = (where[longest] + shift) % values.shape[longest]
        spots.append(tuple(where))
    return values.at[spots[0]].set(least).at[spots[1]].set(top_value)


def levels(own_key, dims, pieces, low, largest):
    factor_of = 1.0
    for position, shards_of in pieces:
        draws = jax.random.uniform(jax.random.fold_in(jax.random.fold_in(own_key, 6), position), (shards_of,), jnp.float32, low / len(pieces), largest / len(pieces))
        factor_of = factor_of * jnp.repeat(jnp.exp(draws), dims[position] // shards_of).reshape((-1,) + (1,) * (len(dims) - 1 - position))
    return factor_of


def noise(rng, extent, deviation, limit, split=(), kind=jnp.bfloat16):
    gain = levels(rng, extent, split, -0.22, 0.18) if split else 1.0
    drawn = jax.random.normal(rng, extent, jnp.float32) * deviation * gain
    return jnp.minimum(jnp.maximum(drawn, -limit), limit).astype(kind)


def setup_inputs(seed: int = 0) -> dict:
    key_of = jax.random.split(jax.random.key(seed), 5)
    fields = noise(key_of[0], (4, NZ, NX, NY), 1.0, 6.0, ((1, 4), (2, 2), (3, 4)), jnp.float32)
    material = with_ends(jax.random.randint(key_of[1], (NZ, NX, NY), 0, MATS), jax.random.fold_in(key_of[1], 1), 0, MATS - 1).astype(jnp.int32)
    depth_order = jax.random.permutation(key_of[2], N_GZ).astype(jnp.int32)
    table = jnp.clip(jax.random.uniform(key_of[3], (4, MATS), jnp.float32, 0.2, 2.0), 0.2, 2.0)
    return {"fields": fields, "material": material, "depth_order": depth_order, "table": table}


ambient = 0.3
diffuse = 1.2
grad_floor = 0.0025
light_z = 2.0 / 3.0
light_x = 1.0 / 3.0
light_y = 2.0 / 3.0

def blur_axis(values, which):
    length = values.shape[which]
    lower = lax.slice_in_dim(values, 0, length - 2, axis=which)
    middle = lax.slice_in_dim(values, 1, length - 1, axis=which)
    upper = lax.slice_in_dim(values, 2, length, axis=which)
    return (lower + 2.0 * middle + upper) * 0.25

def slope_axis(values, which):
    length = values.shape[which]
    lower = lax.slice_in_dim(values, 0, length - 2, axis=which)
    upper = lax.slice_in_dim(values, 2, length, axis=which)
    return (upper - lower) * 0.5

def smooth_all(values):
    for which in (1, 2, 3):
        values = blur_axis(values, which)
    return values

def shade_brick(smoothed, density, material, table, depth_total):
    grad_z = blur_axis(blur_axis(slope_axis(density, 0), 1), 2)
    grad_x = blur_axis(blur_axis(slope_axis(density, 1), 0), 2)
    grad_y = blur_axis(blur_axis(slope_axis(density, 2), 0), 1)
    facing = jnp.abs(light_z * grad_z + light_x * grad_x + light_y * grad_y)
    length = jnp.sqrt(grad_z * grad_z + grad_x * grad_x + grad_y * grad_y + grad_floor)
    shading = ambient + diffuse * facing / length
    entries = table.shape[1]
    onehot = (material[None] == jnp.arange(entries, dtype=jnp.int32)[:, None, None, None]).astype(jnp.float32)
    looked = jnp.einsum('cm,mzxy->czxy', table, onehot, precision=lax.Precision.HIGHEST)
    extinct = looked[3] * jax.nn.softplus(3.0 * smoothed[0]) * (2.0 / depth_total)
    colour = looked[:3] * shading[None] * (0.5 + jax.nn.sigmoid(2.0 * smoothed[1:]))
    ahead = jnp.cumsum(extinct, axis=0) - extinct
    weight = jnp.exp(-ahead) * -jnp.expm1(-extinct)
    return (lax.optimization_barrier(jnp.sum(weight[None] * colour, axis=1)), lax.optimization_barrier(jnp.sum(extinct, axis=0)))

def reference(fields, material, depth_order, table):
    depth_total = BZ * N_GZ
    width_total = BX * N_GX
    height_total = BY * N_GY
    padded = jnp.pad(fields, ((0, 0), (2, 2), (2, 2), (2, 2)))

    def one_brick(brick):
        start = brick * BZ
        slab_part = lax.dynamic_slice_in_dim(padded, start, BZ + 4, axis=1)
        smoothed = smooth_all(slab_part)
        zpos = start - 1 + jnp.arange(BZ + 2, dtype=jnp.int32)
        xpos = jnp.arange(width_total + 2, dtype=jnp.int32) - 1
        ypos = jnp.arange(height_total + 2, dtype=jnp.int32) - 1
        inside = ((zpos >= 0) & (zpos < depth_total))[:, None, None] & ((xpos >= 0) & (xpos < width_total))[None, :, None] & ((ypos >= 0) & (ypos < height_total))[None, None, :]
        density = jnp.where(inside, smoothed[0], jnp.zeros_like(smoothed[0]))
        local_ids = lax.dynamic_slice_in_dim(material, start, BZ, axis=0)
        return shade_brick(smoothed[:, 1:-1, 1:-1, 1:-1], density, local_ids, table, depth_total)
    colours, depths = lax.map(one_brick, jnp.arange(N_GZ, dtype=jnp.int32))
    before = (depth_order[None, :] < depth_order[:, None]).astype(jnp.float32)
    prior = jnp.einsum('gh,hxy->gxy', before, depths, precision=lax.Precision.HIGHEST)
    colour = lax.optimization_barrier(jnp.sum(jnp.exp(-prior)[:, None] * colours, axis=0))
    total = lax.optimization_barrier(jnp.sum(depths, axis=0))
    return jnp.concatenate([colour, (-jnp.expm1(-total))[None]], axis=0)
```

```python
import functools

import jax
import jax.numpy as jnp
import ml_dtypes
import numpy as np
from jax import lax
from jax.experimental import pallas as pl
from jax.experimental.pallas import tpu as pltpu
from jax.sharding import PartitionSpec as P

VMEM_LIMIT = 40 * 1024 * 1024
GROUP = 12
SLOT = 10
TILE = 8

LOG1P = (
    0.9999999210036055, -0.49999256382627166, 0.3331601629975906, -0.24825678829156395, 0.19056042448764499,
    -0.13584082453646767, 0.07754165725755505, -0.029210865679975186, 0.005186113813986752,
)
EXPM1 = (
    1.0, -0.4999995231628418, 0.1666584461927414, -0.04160914570093155, 0.00814302358776331, -0.0010865303920581937,
)


def horner(coefficients, value):
    total = jnp.full_like(value, coefficients[-1])
    for c in coefficients[-2::-1]:
        total = total * value + c
    return total


def band_matrix(ysize):
    blur = {-1: 1.0, 0: 2.0, 1: 1.0}
    blur2 = {-2: 1.0, -1: 4.0, 0: 6.0, 1: 4.0, 2: 1.0}
    slope = {-2: -2.0, -1: -4.0, 1: 4.0, 2: 2.0}
    m = np.zeros((2 * 128, 6 * ysize), np.float32)
    for block, (taps, scale, field) in enumerate(
        ((blur, 1 / 64, 0), (blur2, 1 / 4096, 0), (slope, 1 / 4096, 0), (blur, 1 / 64, 1), (blur, 1 / 64, 2), (blur, 1 / 64, 3))
    ):
        if field == 0:
            lane_of = {-2: 0, -1: 1, ysize: 2, ysize + 1: 3}
        else:
            lane_of = {-1: 2 + 2 * field, ysize: 3 + 2 * field}
        for out in range(ysize):
            for off, w in taps.items():
                src = out + off
                row = src if 0 <= src < ysize else 128 + lane_of[src]
                m[row, block * ysize + out] += w * scale
    return m.astype(ml_dtypes.bfloat16)


def pack_x_kernel(zs, flag_ref, tile_ref, zlo_ref, zhi_ref, out_ref):
    xs = zlo_ref.shape[0] // 5
    first, last = flag_ref[0], flag_ref[1]
    base = flag_ref[2]
    toff = flag_ref[3]
    out_ref[...] = jnp.zeros_like(out_ref)
    for group in range(5):
        field = max(group - 1, 0)
        if group < 2:
            step = group
            row = base + step
            trow = toff + step
        else:
            row = jnp.where(base == 0, 0, xs - 1)
            trow = jnp.where(base == 0, 0, TILE - 1)
        own = tile_ref[field, pl.ds(trow, zs, stride=TILE), :]
        out_ref[group, 2 : 2 + zs, :] = own
        if group < 2:
            lo2 = zlo_ref[pl.ds(row, 1), :]
            lo1 = zlo_ref[pl.ds(xs + row, 1), :]
            hi0 = zhi_ref[pl.ds(row, 1), :]
            hi1 = zhi_ref[pl.ds(xs + row, 1), :]
            out_ref[group, 0:1, :] = jnp.where(first == 1, -own[0:1], lo2)
            out_ref[group, 1:2, :] = lo1
            out_ref[group, 2 + zs : 3 + zs, :] = hi0
            out_ref[group, 3 + zs : 4 + zs, :] = jnp.where(last == 1, -own[zs - 1 : zs], hi1)
        else:
            out_ref[group, 1:2, :] = zlo_ref[pl.ds((1 + field) * xs + row, 1), :]
            out_ref[group, 2 + zs : 3 + zs, :] = zhi_ref[pl.ds((1 + field) * xs + row, 1), :]


def extend_kernel(zs, xs, flag_ref, fields_ref, zlo_ref, zhi_ref, xlo_ref, xhi_ref, ext_ref, pack_ref):
    zfirst, zlast, xfirst, xlast = flag_ref[0], flag_ref[1], flag_ref[2], flag_ref[3]
    block = xs + TILE
    layers = zs + 4
    ext_ref[...] = jnp.zeros_like(ext_ref)
    for field in range(4):
        for z in range(zs):
            ext_ref[field, pl.ds((z + 2) * block + TILE, xs), :] = fields_ref[field, z]
    ext_ref[0, pl.ds(TILE, xs), :] = jnp.where(zfirst == 1, -fields_ref[0, 0], zlo_ref[0])
    ext_ref[0, pl.ds((zs + 3) * block + TILE, xs), :] = jnp.where(zlast == 1, -fields_ref[0, zs - 1], zhi_ref[1])
    ext_ref[0, pl.ds(block + TILE, xs), :] = zlo_ref[1]
    ext_ref[0, pl.ds((zs + 2) * block + TILE, xs), :] = zhi_ref[0]
    for field in range(1, 4):
        ext_ref[field, pl.ds(block + TILE, xs), :] = zlo_ref[1 + field]
        ext_ref[field, pl.ds((zs + 2) * block + TILE, xs), :] = zhi_ref[1 + field]
    low = ext_ref[0, pl.ds(TILE, layers, stride=block), :]
    high = ext_ref[0, pl.ds(TILE + xs - 1, layers, stride=block), :]
    ext_ref[0, pl.ds(TILE - 2, layers, stride=block), :] = jnp.where(xfirst == 1, -low, xlo_ref[0, :layers])
    ext_ref[0, pl.ds(TILE + xs + 1, layers, stride=block), :] = jnp.where(xlast == 1, -high, xhi_ref[1, :layers])
    for field in range(4):
        lo = xlo_ref[1 + field, :layers]
        hi = xhi_ref[0 if field == 0 else 1 + field, :layers]
        ext_ref[field, pl.ds(TILE - 1, layers, stride=block), :] = jnp.where(xfirst == 1, 0.0, lo)
        ext_ref[field, pl.ds(TILE + xs, layers, stride=block), :] = jnp.where(xlast == 1, 0.0, hi)
    lane = lax.broadcasted_iota(jnp.int32, (1, 128), 1)
    for group in range(pack_ref.shape[0]):
        packed = jnp.zeros((block, 128), jnp.float32)
        for k in range(GROUP + 1):
            zi = group * GROUP + k
            at = SLOT * k
            if k == GROUP and zi != layers or zi > layers:
                continue
            rows = block if zi < layers else TILE
            for field in range(4 if zi < layers else 1):
                start = at + (0 if field == 0 else 2 + 2 * field)
                count = 4 if field == 0 else 2
                values = ext_ref[field, pl.ds(zi * block, rows), :]
                values = pltpu.roll(values, (start + count // 2) % 128, 1)
                if rows < block:
                    values = jnp.concatenate([values, jnp.zeros((block - rows, 128), jnp.float32)], axis=0)
                packed = jnp.where((lane >= start) & (lane < start + count), values, packed)
        pack_ref[group] = packed


def split(values):
    high = values.astype(jnp.bfloat16)
    return high, (values - high.astype(jnp.float32)).astype(jnp.bfloat16)


def render_kernel(zs, xs, scale, flag_ref, table_ref, ext_ref, own_ref, left_ref, right_ref, band_ref, material_ref, out_ref, rows_ref, merged_ref, cross_ref):
    block = xs + TILE
    layers = zs + 4
    yfirst, ylast = flag_ref[4], flag_ref[5]
    lane = lax.broadcasted_iota(jnp.int32, (1, 128), 1)
    place = lax.rem(lane, SLOT)
    from_left = (place < 2) | ((place >= 4) & (lax.rem(place, 2) == 0))
    for group in range(own_ref.shape[0]):
        own = own_ref[group]
        fill_left = jnp.where(place == 0, -pltpu.roll(own, 126, 1), 0.0)
        fill_right = jnp.where(place == 3, -pltpu.roll(own, 2, 1), 0.0)
        left = jnp.where(yfirst == 1, fill_left, left_ref[group])
        right = jnp.where(ylast == 1, fill_right, right_ref[group])
        merged_ref[group] = jnp.where(from_left, left, right)

    def along_y(base, halo):
        halo_hi, halo_lo = split(halo)
        for field in range(4):
            hi, lo = split(ext_ref[field, pl.ds(base, halo.shape[0]), :])
            columns = slice(0, 384) if field == 0 else slice(256 + 128 * field, 384 + 128 * field)
            weights = band_ref[:, columns]
            result = jnp.dot(
                jnp.concatenate([hi, halo_hi], axis=1), weights, preferred_element_type=jnp.float32
            ) + jnp.dot(jnp.concatenate([lo, halo_lo], axis=1), weights, preferred_element_type=jnp.float32)
            if field == 0:
                for part in range(3):
                    rows_ref[part, pl.ds(base, halo.shape[0]), :] = result[:, 128 * part : 128 * part + 128]
            else:
                rows_ref[2 + field, pl.ds(base, halo.shape[0]), :] = result

    for group in range(own_ref.shape[0]):

        def pair_step(pair, carry):
            first = pair * (2 * SLOT)
            halo = jnp.concatenate(
                [
                    pltpu.roll(merged_ref[group], lax.rem(128 - first, 128), 1),
                    pltpu.roll(merged_ref[group], lax.rem(256 - SLOT - first, 128), 1),
                ],
                axis=0,
            )
            base = pl.multiple_of((group * GROUP + 2 * pair) * block, 16)
            along_y(base, halo)
            return carry

        pairs = min(GROUP, layers - group * GROUP) // 2
        lax.fori_loop(0, pairs, pair_step, 0)
    end = pltpu.roll(merged_ref[own_ref.shape[0] - 1, 0:TILE, :], (128 - SLOT * GROUP) % 128, 1)
    along_y(layers * block, jnp.concatenate([end, jnp.zeros((TILE, 128), jnp.float32)], axis=0))

    def cross_step(zi, carry):
        base = zi * block + TILE

        def at(part, off):
            return rows_ref[part, pl.ds(base + off, xs), :]

        for part in (0, 3, 4, 5):
            cross_ref[part, pl.ds(zi * xs, xs), :] = at(part, -1) + at(part, 1) + 2.0 * at(part, 0)
        a, b, c, d, e = (at(1, off) for off in (-2, -1, 0, 1, 2))
        cross_ref[1, pl.ds(zi * xs, xs), :] = (a + e) + 4.0 * (b + d) + 6.0 * c
        cross_ref[2, pl.ds(zi * xs, xs), :] = 2.0 * (e - a) + 4.0 * (d - b)
        a, b, c, d, e = (at(2, off) for off in (-2, -1, 0, 1, 2))
        cross_ref[6, pl.ds(zi * xs, xs), :] = (a + e) + 4.0 * (b + d) + 6.0 * c
        return carry

    lax.fori_loop(0, layers, cross_step, 0)

    looked_rows = [jnp.broadcast_to(table_ref[c : c + 1, :], (xs, 128)) for c in range(4)]

    def depth_step(z, carry):
        passed, red, green, blue, depth = carry

        def at(part, off):
            return cross_ref[part, pl.ds((z + 2 + off) * xs, xs), :]

        def blur(part):
            return at(part, -1) + at(part, 1) + 2.0 * at(part, 0)

        def blur2(part):
            return (at(part, -2) + at(part, 2)) + 4.0 * (at(part, -1) + at(part, 1)) + 6.0 * at(part, 0)

        grad_z = 2.0 * (at(1, 2) - at(1, -2)) + 4.0 * (at(1, 1) - at(1, -1))
        grad_x = blur2(2)
        grad_y = blur2(6)
        facing = jnp.abs(0.8 * (grad_z + grad_y) + 0.4 * grad_x)
        shading = 0.3 + facing * lax.rsqrt(grad_z * grad_z + grad_x * grad_x + grad_y * grad_y + 0.0025)
        density = 3.0 * blur(0)
        t = jnp.exp(-jnp.abs(density))
        soft = jnp.maximum(density, 0.0) + t * horner(LOG1P, t)
        ids = material_ref[z]
        looked = [jnp.take_along_axis(looked_rows[c], ids, axis=1, mode="promise_in_bounds") for c in range(4)]
        extinct = looked[3] * (soft * scale)
        fade = extinct * horner(EXPM1, extinct)
        weight = passed * fade
        lit = weight * shading
        parts = []
        for c, total in enumerate((red, green, blue)):
            parts.append(total + (looked[c] * lit) * (1.0 + 0.5 * jnp.tanh(blur(3 + c))))
        return (passed - weight, parts[0], parts[1], parts[2], depth + extinct)

    zero = jnp.zeros((xs, 128), jnp.float32)
    _, red, green, blue, depth = lax.fori_loop(0, zs, depth_step, (zero + 1.0, zero, zero, zero, zero))
    out_ref[0] = red
    out_ref[1] = green
    out_ref[2] = blue
    out_ref[3] = depth


def call(kernel, out_shape, specs, scratch=(), flops=0, nbytes=0, name=None):
    where = {"s": pltpu.SMEM, "v": pltpu.VMEM}
    return pl.pallas_call(
        kernel,
        out_shape=out_shape,
        in_specs=[pl.BlockSpec(memory_space=where[s]) for s in specs],
        out_specs=jax.tree.map(lambda _: pl.BlockSpec(memory_space=pltpu.VMEM), out_shape),
        scratch_shapes=list(scratch),
        compiler_params=pltpu.CompilerParams(vmem_limit_bytes=VMEM_LIMIT),
        cost_estimate=pl.CostEstimate(flops=flops, bytes_accessed=nbytes, transcendentals=0),
        name=name,
    )


def shift(values, axis, step):
    count = lax.axis_size(axis)
    pairs = [(i, i + step) for i in range(count) if 0 <= i + step < count]
    return lax.ppermute(values, axis, pairs)


def on_device(fields, material, depth_order, table):
    _, zs, xs, ys = fields.shape
    nx, ny, nz = (lax.axis_size(a) for a in ("gx", "gy", "gz"))
    ix, iy, iz = (lax.axis_index(a) for a in ("gx", "gy", "gz"))
    depth_total = zs * nz
    block = xs + TILE
    layers = zs + 4
    flags = jnp.stack([iz == 0, iz == nz - 1, ix == 0, ix == nx - 1, iy == 0, iy == ny - 1]).astype(jnp.int32)

    z_lo = shift(jnp.concatenate([fields[0, zs - 2 :], fields[1:, zs - 1]], axis=0), "gz", 1)
    z_hi = shift(jnp.concatenate([fields[0, :2], fields[1:, 0]], axis=0), "gz", -1)

    wide = -(-layers // 8) * 8
    pack_x = call(
        functools.partial(pack_x_kernel, zs), jax.ShapeDtypeStruct((5, wide, ys), jnp.float32), "svvv", name="pack_x"
    )

    def side(high):
        start = jnp.where(high, xs - TILE, 0)
        tile = lax.dynamic_slice_in_dim(fields, start, TILE, axis=2).reshape(4, zs * TILE, ys)
        own = jnp.stack([flags[0], flags[1], jnp.where(high, xs - 2, 0), jnp.where(high, TILE - 2, 0)])
        return pack_x(own.astype(jnp.int32), tile, z_lo.reshape(5 * xs, ys), z_hi.reshape(5 * xs, ys))

    if nx == 2:
        x_lo = x_hi = lax.ppermute(side(ix == 0), "gx", [(0, 1), (1, 0)])
    else:
        x_lo = shift(side(jnp.bool_(True)), "gx", 1)
        x_hi = shift(side(jnp.bool_(False)), "gx", -1)

    groups = -(-layers // GROUP)
    rows = (layers + 1) * block
    ext, own = call(
        functools.partial(extend_kernel, zs, xs),
        (
            jax.ShapeDtypeStruct((4, rows, ys), jnp.float32),
            jax.ShapeDtypeStruct((groups, block, 128), jnp.float32),
        ),
        "svvvvv",
        name="extend",
    )(flags, fields, z_lo, z_hi, x_lo, x_hi)
    left = shift(own, "gy", 1)
    right = shift(own, "gy", -1)

    band = jnp.asarray(band_matrix(ys))
    wide_table = jnp.pad(table, ((0, 4), (0, 128 - table.shape[1])))
    image = call(
        functools.partial(render_kernel, zs, xs, 2.0 / depth_total),
        jax.ShapeDtypeStruct((4, xs, ys), jnp.float32),
        "svvvvvvv",
        [
            pltpu.VMEM((6, rows, ys), jnp.float32),
            pltpu.VMEM((groups, block, 128), jnp.float32),
            pltpu.VMEM((7, layers * xs, ys), jnp.float32),
        ],
        name="render",
    )(flags, wide_table, ext, own, left, right, band, material)

    part = xs // nz
    mine = lax.all_to_all(image.reshape(4, nz, part, ys), "gz", split_axis=1, concat_axis=1)
    depths = mine[3]
    nearer = depth_order[None, :] < depth_order[:, None]
    prior = jnp.sum(jnp.where(nearer[:, :, None, None], depths[None], 0.0), axis=1)
    colour = jnp.sum(jnp.exp(-prior)[None] * mine[:3], axis=1)
    opacity = -jnp.expm1(-jnp.sum(depths, axis=0))
    return jnp.concatenate([colour, opacity[None]], axis=0)


def solution(mesh):
    return jax.shard_map(
        on_device,
        mesh=mesh,
        in_specs=(P(None, "gz", "gx", "gy"), P("gz", "gx", "gy"), P(), P()),
        out_specs=P(None, ("gx", "gz"), "gy"),
        check_vma=False,
    )
```

```python
import functools

import jax
import jax.numpy as jnp
import ml_dtypes
import numpy as np
from jax import lax
from jax.experimental import pallas as pl
from jax.experimental.pallas import tpu as pltpu
from jax.sharding import PartitionSpec as P

VMEM_LIMIT = 40 * 1024 * 1024
GROUP = 12
SLOT = 10
TILE = 8

LOG1P = (
    0.9999999210036055, -0.49999256382627166, 0.3331601629975906, -0.24825678829156395, 0.19056042448764499,
    -0.13584082453646767, 0.07754165725755505, -0.029210865679975186, 0.005186113813986752,
)
EXPM1 = (
    1.0, -0.4999995231628418, 0.1666584461927414, -0.04160914570093155, 0.00814302358776331, -0.0010865303920581937,
)


def horner(coefficients, value):
    total = jnp.full_like(value, coefficients[-1])
    for c in coefficients[-2::-1]:
        total = total * value + c
    return total


def band_matrix(ysize):
    blur = {-1: 1.0, 0: 2.0, 1: 1.0}
    blur2 = {-2: 1.0, -1: 4.0, 0: 6.0, 1: 4.0, 2: 1.0}
    slope = {-2: -2.0, -1: -4.0, 1: 4.0, 2: 2.0}
    m = np.zeros((2 * 128, 6 * ysize), np.float32)
    for block, (taps, scale, field) in enumerate(
        ((blur, 1 / 64, 0), (blur2, 1 / 4096, 0), (slope, 1 / 4096, 0), (blur, 1 / 64, 1), (blur, 1 / 64, 2), (blur, 1 / 64, 3))
    ):
        if field == 0:
            lane_of = {-2: 0, -1: 1, ysize: 2, ysize + 1: 3}
        else:
            lane_of = {-1: 2 + 2 * field, ysize: 3 + 2 * field}
        for out in range(ysize):
            for off, w in taps.items():
                src = out + off
                row = src if 0 <= src < ysize else 128 + lane_of[src]
                m[row, block * ysize + out] += w * scale
    return m.astype(ml_dtypes.bfloat16)


def pack_x_kernel(zs, flag_ref, side_ref, tile_ref, za_ref, zb_ref, out_ref):
    xs = za_ref.shape[0] // 5
    first, last, odd = flag_ref[0], flag_ref[1], flag_ref[6]
    base = side_ref[0]
    toff = side_ref[1]

    def low(at):
        return jnp.where(first == 1, 0.0, jnp.where(odd == 1, za_ref[pl.ds(at, 1), :], zb_ref[pl.ds(at, 1), :]))

    def high(at):
        return jnp.where(last == 1, 0.0, jnp.where(odd == 1, zb_ref[pl.ds(at, 1), :], za_ref[pl.ds(at, 1), :]))

    out_ref[...] = jnp.zeros_like(out_ref)
    for group in range(5):
        field = max(group - 1, 0)
        if group < 2:
            step = group
            row = base + step
            trow = toff + step
        else:
            row = jnp.where(base == 0, 0, xs - 1)
            trow = jnp.where(base == 0, 0, TILE - 1)
        own = tile_ref[field, pl.ds(trow, zs, stride=TILE), :]
        out_ref[group, 2 : 2 + zs, :] = own
        if group < 2:
            out_ref[group, 0:1, :] = jnp.where(first == 1, -own[0:1], low(row))
            out_ref[group, 1:2, :] = low(xs + row)
            out_ref[group, 2 + zs : 3 + zs, :] = high(row)
            out_ref[group, 3 + zs : 4 + zs, :] = jnp.where(last == 1, -own[zs - 1 : zs], high(xs + row))
        else:
            out_ref[group, 1:2, :] = low((1 + field) * xs + row)
            out_ref[group, 2 + zs : 3 + zs, :] = high((1 + field) * xs + row)


def extend_kernel(zs, xs, flag_ref, fields_ref, za_ref, zb_ref, xlo_ref, xhi_ref, ext_ref, pack_ref):
    zfirst, zlast, xfirst, xlast, zodd = (flag_ref[k] for k in (0, 1, 2, 3, 6))

    def below(at):
        return jnp.where(zfirst == 1, 0.0, jnp.where(zodd == 1, za_ref[at], zb_ref[at]))

    def above(at):
        return jnp.where(zlast == 1, 0.0, jnp.where(zodd == 1, zb_ref[at], za_ref[at]))

    block = xs + TILE
    layers = zs + 4
    ext_ref[...] = jnp.zeros_like(ext_ref)
    for field in range(4):
        for z in range(zs):
            ext_ref[field, pl.ds((z + 2) * block + TILE, xs), :] = fields_ref[field, z]
    ext_ref[0, pl.ds(TILE, xs), :] = jnp.where(zfirst == 1, -fields_ref[0, 0], below(0))
    ext_ref[0, pl.ds((zs + 3) * block + TILE, xs), :] = jnp.where(zlast == 1, -fields_ref[0, zs - 1], above(1))
    ext_ref[0, pl.ds(block + TILE, xs), :] = below(1)
    ext_ref[0, pl.ds((zs + 2) * block + TILE, xs), :] = above(0)
    for field in range(1, 4):
        ext_ref[field, pl.ds(block + TILE, xs), :] = below(1 + field)
        ext_ref[field, pl.ds((zs + 2) * block + TILE, xs), :] = above(1 + field)
    low = ext_ref[0, pl.ds(TILE, layers, stride=block), :]
    high = ext_ref[0, pl.ds(TILE + xs - 1, layers, stride=block), :]
    ext_ref[0, pl.ds(TILE - 2, layers, stride=block), :] = jnp.where(xfirst == 1, -low, xlo_ref[0, :layers])
    ext_ref[0, pl.ds(TILE + xs + 1, layers, stride=block), :] = jnp.where(xlast == 1, -high, xhi_ref[1, :layers])
    for field in range(4):
        lo = xlo_ref[1 + field, :layers]
        hi = xhi_ref[0 if field == 0 else 1 + field, :layers]
        ext_ref[field, pl.ds(TILE - 1, layers, stride=block), :] = jnp.where(xfirst == 1, 0.0, lo)
        ext_ref[field, pl.ds(TILE + xs, layers, stride=block), :] = jnp.where(xlast == 1, 0.0, hi)
    lane = lax.broadcasted_iota(jnp.int32, (1, 128), 1)
    for group in range(pack_ref.shape[0]):
        packed = jnp.zeros((block, 128), jnp.float32)
        for k in range(GROUP + 1):
            zi = group * GROUP + k
            at = SLOT * k
            if k == GROUP and zi != layers or zi > layers:
                continue
            rows = block if zi < layers else TILE
            for field in range(4 if zi < layers else 1):
                start = at + (0 if field == 0 else 2 + 2 * field)
                count = 4 if field == 0 else 2
                values = ext_ref[field, pl.ds(zi * block, rows), :]
                values = pltpu.roll(values, (start + count // 2) % 128, 1)
                if rows < block:
                    values = jnp.concatenate([values, jnp.zeros((block - rows, 128), jnp.float32)], axis=0)
                packed = jnp.where((lane >= start) & (lane < start + count), values, packed)
        pack_ref[group] = packed


def split(values):
    high = values.astype(jnp.bfloat16)
    return high, (values - high.astype(jnp.float32)).astype(jnp.bfloat16)


def render_kernel(zs, xs, scale, flag_ref, table_ref, ext_ref, own_ref, ya_ref, yb_ref, band_ref, material_ref, *rest):
    out_refs, (rows_ref, merged_ref, cross_ref, image_ref) = rest[:-4], rest[-4:]
    block = xs + TILE
    layers = zs + 4
    yfirst, ylast, yodd = flag_ref[4], flag_ref[5], flag_ref[7]
    lane = lax.broadcasted_iota(jnp.int32, (1, 128), 1)
    place = lax.rem(lane, SLOT)
    from_left = (place < 2) | ((place >= 4) & (lax.rem(place, 2) == 0))
    for group in range(own_ref.shape[0]):
        own = own_ref[group]
        fill_left = jnp.where(place == 0, -pltpu.roll(own, 126, 1), 0.0)
        fill_right = jnp.where(place == 3, -pltpu.roll(own, 2, 1), 0.0)
        first, second = ya_ref[group], yb_ref[group]
        left = jnp.where(yfirst == 1, fill_left, jnp.where(yodd == 1, first, second))
        right = jnp.where(ylast == 1, fill_right, jnp.where(yodd == 1, second, first))
        merged_ref[group] = jnp.where(from_left, left, right)

    def along_y(base, halo):
        halo_hi, halo_lo = split(halo)
        for field in range(4):
            hi, lo = split(ext_ref[field, pl.ds(base, halo.shape[0]), :])
            columns = slice(0, 384) if field == 0 else slice(256 + 128 * field, 384 + 128 * field)
            weights = band_ref[:, columns]
            result = jnp.dot(
                jnp.concatenate([hi, halo_hi], axis=1), weights, preferred_element_type=jnp.float32
            ) + jnp.dot(jnp.concatenate([lo, halo_lo], axis=1), weights, preferred_element_type=jnp.float32)
            if field == 0:
                for part in range(3):
                    rows_ref[part, pl.ds(base, halo.shape[0]), :] = result[:, 128 * part : 128 * part + 128]
            else:
                rows_ref[2 + field, pl.ds(base, halo.shape[0]), :] = result

    for group in range(own_ref.shape[0]):

        def pair_step(pair, carry):
            first = pair * (2 * SLOT)
            halo = jnp.concatenate(
                [
                    pltpu.roll(merged_ref[group], lax.rem(128 - first, 128), 1),
                    pltpu.roll(merged_ref[group], lax.rem(256 - SLOT - first, 128), 1),
                ],
                axis=0,
            )
            base = pl.multiple_of((group * GROUP + 2 * pair) * block, 16)
            along_y(base, halo)
            return carry

        pairs = min(GROUP, layers - group * GROUP) // 2
        lax.fori_loop(0, pairs, pair_step, 0)
    end = pltpu.roll(merged_ref[own_ref.shape[0] - 1, 0:TILE, :], (128 - SLOT * GROUP) % 128, 1)
    along_y(layers * block, jnp.concatenate([end, jnp.zeros((TILE, 128), jnp.float32)], axis=0))

    def cross_step(zi, carry):
        base = zi * block + TILE

        def at(part, off):
            return rows_ref[part, pl.ds(base + off, xs), :]

        for part in (0, 3, 4, 5):
            cross_ref[part, pl.ds(zi * xs, xs), :] = at(part, -1) + at(part, 1) + 2.0 * at(part, 0)
        a, b, c, d, e = (at(1, off) for off in (-2, -1, 0, 1, 2))
        cross_ref[1, pl.ds(zi * xs, xs), :] = (a + e) + 4.0 * (b + d) + 6.0 * c
        cross_ref[2, pl.ds(zi * xs, xs), :] = 2.0 * (e - a) + 4.0 * (d - b)
        a, b, c, d, e = (at(2, off) for off in (-2, -1, 0, 1, 2))
        cross_ref[6, pl.ds(zi * xs, xs), :] = (a + e) + 4.0 * (b + d) + 6.0 * c
        return carry

    lax.fori_loop(0, layers, cross_step, 0)

    looked_rows = [jnp.broadcast_to(table_ref[c : c + 1, :], (xs, 128)) for c in range(4)]

    def depth_step(z, carry):
        passed, red, green, blue, depth = carry

        def at(part, off):
            return cross_ref[part, pl.ds((z + 2 + off) * xs, xs), :]

        def blur(part):
            return at(part, -1) + at(part, 1) + 2.0 * at(part, 0)

        def blur2(part):
            return (at(part, -2) + at(part, 2)) + 4.0 * (at(part, -1) + at(part, 1)) + 6.0 * at(part, 0)

        grad_z = 2.0 * (at(1, 2) - at(1, -2)) + 4.0 * (at(1, 1) - at(1, -1))
        grad_x = blur2(2)
        grad_y = blur2(6)
        facing = jnp.abs(0.8 * (grad_z + grad_y) + 0.4 * grad_x)
        shading = 0.3 + facing * lax.rsqrt(grad_z * grad_z + grad_x * grad_x + grad_y * grad_y + 0.0025)
        density = 3.0 * blur(0)
        t = jnp.exp(-jnp.abs(density))
        soft = jnp.maximum(density, 0.0) + t * horner(LOG1P, t)
        ids = material_ref[z]
        looked = [jnp.take_along_axis(looked_rows[c], ids, axis=1, mode="promise_in_bounds") for c in range(4)]
        extinct = looked[3] * (soft * scale)
        fade = extinct * horner(EXPM1, extinct)
        weight = passed * fade
        lit = weight * shading
        parts = []
        for c, total in enumerate((red, green, blue)):
            parts.append(total + (looked[c] * lit) * (1.0 + 0.5 * jnp.tanh(blur(3 + c))))
        return (passed - weight, parts[0], parts[1], parts[2], depth + extinct)

    zero = jnp.zeros((xs, 128), jnp.float32)
    _, red, green, blue, depth = lax.fori_loop(0, zs, depth_step, (zero + 1.0, zero, zero, zero, zero))
    if len(out_refs) == 1:
        for c, total in enumerate((red, green, blue, depth)):
            out_refs[0][c] = total
    else:
        for c, total in enumerate((red, green, blue, depth)):
            image_ref[c] = total
        part = xs // len(out_refs)
        for k, ref in enumerate(out_refs):
            ref[...] = image_ref[:, pl.ds(pl.multiple_of(flag_ref[8 + k], part), part), :]


def call(kernel, out_shape, specs, scratch=(), flops=0, nbytes=0, name=None):
    where = {"s": pltpu.SMEM, "v": pltpu.VMEM}
    return pl.pallas_call(
        kernel,
        out_shape=out_shape,
        in_specs=[pl.BlockSpec(memory_space=where[s]) for s in specs],
        out_specs=jax.tree.map(lambda _: pl.BlockSpec(memory_space=pltpu.VMEM), out_shape),
        scratch_shapes=list(scratch),
        compiler_params=pltpu.CompilerParams(vmem_limit_bytes=VMEM_LIMIT),
        cost_estimate=pl.CostEstimate(flops=flops, bytes_accessed=nbytes, transcendentals=0),
        name=name,
    )


def swap_pairs(first, second, axis):
    count = lax.axis_size(axis)
    one = lax.ppermute(first, axis, [(i, i ^ 1) for i in range(count)])
    if count == 2:
        return one, one
    ends = [(0, 0), (count - 1, count - 1)]
    return one, lax.ppermute(second, axis, ends + [(i, i + 1 if i % 2 else i - 1) for i in range(1, count - 1)])


def on_device(fields, material, depth_order, table):
    _, zs, xs, ys = fields.shape
    nx, ny, nz = (lax.axis_size(a) for a in ("gx", "gy", "gz"))
    ix, iy, iz = (lax.axis_index(a) for a in ("gx", "gy", "gz"))
    depth_total = zs * nz
    block = xs + TILE
    layers = zs + 4
    part = xs // nz
    swaps = nz in (2, 4)
    entries = [iz == 0, iz == nz - 1, ix == 0, ix == nx - 1, iy == 0, iy == ny - 1, iz % 2, iy % 2]
    if swaps:
        entries += [(iz ^ k) * part for k in range(nz)]
    flags = jnp.stack([jnp.asarray(e, jnp.int32) for e in entries])

    def z_side(high):
        two = lax.dynamic_slice_in_dim(fields[0], jnp.where(high, zs - 2, 0), 2, axis=0)
        one = lax.dynamic_slice_in_dim(fields[1:], jnp.where(high, zs - 1, 0), 1, axis=1)
        return jnp.concatenate([two, one[:, 0]], axis=0)

    z_a, z_b = swap_pairs(z_side(iz % 2 == 0), z_side(iz % 2 == 1), "gz")

    wide = -(-layers // 8) * 8
    pack_x = call(
        functools.partial(pack_x_kernel, zs), jax.ShapeDtypeStruct((5, wide, ys), jnp.float32), "ssvvv", name="pack_x"
    )

    def x_side(high):
        start = jnp.where(high, xs - TILE, 0)
        tile = lax.dynamic_slice_in_dim(fields, start, TILE, axis=2).reshape(4, zs * TILE, ys)
        own = jnp.stack([jnp.where(high, xs - 2, 0), jnp.where(high, TILE - 2, 0)]).astype(jnp.int32)
        return pack_x(flags, own, tile, z_a.reshape(5 * xs, ys), z_b.reshape(5 * xs, ys))

    x_a, x_b = swap_pairs(x_side(ix % 2 == 0), x_side(ix % 2 == 1) if nx > 2 else None, "gx")
    if nx == 2:
        x_lo = x_hi = x_a
    else:
        x_lo, x_hi = jnp.where(ix % 2 == 1, x_a, x_b), jnp.where(ix % 2 == 1, x_b, x_a)

    groups = -(-layers // GROUP)
    rows = (layers + 1) * block
    ext, own = call(
        functools.partial(extend_kernel, zs, xs),
        (
            jax.ShapeDtypeStruct((4, rows, ys), jnp.float32),
            jax.ShapeDtypeStruct((groups, block, 128), jnp.float32),
        ),
        "svvvvv",
        name="extend",
    )(flags, fields, z_a, z_b, x_lo, x_hi)
    y_a, y_b = swap_pairs(own, own, "gy")

    band = jnp.asarray(band_matrix(ys))
    wide_table = jnp.pad(table, ((0, 4), (0, 128 - table.shape[1])))
    images = call(
        functools.partial(render_kernel, zs, xs, 2.0 / depth_total),
        [jax.ShapeDtypeStruct((4, part, ys), jnp.float32)] * nz if swaps else [jax.ShapeDtypeStruct((4, xs, ys), jnp.float32)],
        "svvvvvvv",
        [
            pltpu.VMEM((6, rows, ys), jnp.float32),
            pltpu.VMEM((groups, block, 128), jnp.float32),
            pltpu.VMEM((7, layers * xs, ys), jnp.float32),
            pltpu.VMEM((4, xs, ys), jnp.float32),
        ],
        name="render",
    )(flags, wide_table, ext, own, y_a, y_b, band, material)

    if swaps:
        mine = [images[0]]
        for k in range(1, nz):
            mine.append(lax.ppermute(images[k], "gz", [(i, i ^ k) for i in range(nz)]))
        ranks = [depth_order[iz ^ k] for k in range(nz)]
    else:
        stacked = lax.all_to_all(images[0].reshape(4, nz, part, ys), "gz", split_axis=1, concat_axis=1)
        mine = [stacked[:, b] for b in range(nz)]
        ranks = [depth_order[b] for b in range(nz)]
    colour = jnp.zeros_like(mine[0][:3])
    for b in range(nz):
        prior = jnp.zeros_like(mine[0][3])
        for other in range(nz):
            if other != b:
                prior += jnp.where(ranks[other] < ranks[b], mine[other][3], 0.0)
        colour += jnp.exp(-prior)[None] * mine[b][:3]
    total = functools.reduce(jnp.add, [m[3] for m in mine])
    return jnp.concatenate([colour, -jnp.expm1(-total)[None]], axis=0)


def solution(mesh):
    return jax.shard_map(
        on_device,
        mesh=mesh,
        in_specs=(P(None, "gz", "gx", "gy"), P("gz", "gx", "gy"), P(), P()),
        out_specs=P(None, ("gx", "gz"), "gy"),
        check_vma=False,
    )
```

```python
import functools

import jax
import jax.numpy as jnp
from jax import lax
from jax.experimental import pallas as pl
from jax.experimental.pallas import tpu as pltpu
from jax.sharding import PartitionSpec as P

VMEM_LIMIT = 40 * 1024 * 1024
GROUP = 12
SLOT = 10
TILE = 8
FACE = 5

ZFIRST, ZLAST, XFIRST, XLAST, YFIRST, YLAST, ZODD, XODD, YODD, PEERS = range(10)

LOG1P = (
    0.9999999210036055, -0.49999256382627166, 0.3331601629975906, -0.24825678829156395, 0.19056042448764499,
    -0.13584082453646767, 0.07754165725755505, -0.029210865679975186, 0.005186113813986752,
)
EXPM1 = (
    1.0, -0.4999995231628418, 0.1666584461927414, -0.04160914570093155, 0.00814302358776331, -0.0010865303920581937,
)


def horner(coefficients, value):
    total = jnp.full_like(value, coefficients[-1])
    for c in coefficients[-2::-1]:
        total = total * value + c
    return total


def pick(flag, yes, no):
    return jnp.where(flag == 1, yes, no)


def rows_kernel(zs, xs, high_ref, fields_ref, out_ref, tile_ref, sem):
    high = high_ref[0]
    start = pl.multiple_of(high * (xs - TILE), TILE)
    copy = pltpu.make_async_copy(fields_ref.at[:, :, pl.ds(start, TILE), :], tile_ref, sem)
    copy.start()
    copy.wait()
    for group in range(FACE):
        field = max(group - 1, 0)
        for value in (0, 1):
            row = (TILE - 2 if value else 0) + group if group < 2 else (TILE - 1 if value else 0)

            @pl.when(high == value)
            def _():
                out_ref[group] = tile_ref.at[field].reshape(zs * TILE, 128)[pl.ds(row, zs, stride=TILE), :]


def lookup_kernel(zs, xs, table_ref, material_ref, out_ref):
    tables = [jnp.broadcast_to(table_ref[c : c + 1, :], (xs, 128)) for c in range(4)]

    def step(z, carry):
        ids = material_ref[z]
        for c in range(4):
            out_ref[c, z] = jnp.take_along_axis(tables[c], ids, axis=1, mode="promise_in_bounds")
        return carry

    lax.fori_loop(0, zs, step, 0)


def extend_kernel(zs, xs, flag_ref, fields_ref, xa_ref, xb_ref, ext_ref, pack_ref):
    xfirst, xlast, xodd = flag_ref[XFIRST], flag_ref[XLAST], flag_ref[XODD]
    block = xs + TILE
    zeros = jnp.zeros((TILE, 128), jnp.float32)
    for field in range(4):
        for z in range(zs):
            ext_ref[field, pl.ds(z * block, TILE), :] = zeros
            ext_ref[field, pl.ds(z * block + TILE, xs), :] = fields_ref[field, z]
        ext_ref[field, pl.ds(zs * block, TILE), :] = zeros
    low = ext_ref[0, pl.ds(TILE, zs, stride=block), :]
    high = ext_ref[0, pl.ds(TILE + xs - 1, zs, stride=block), :]
    ext_ref[0, pl.ds(TILE - 2, zs, stride=block), :] = pick(xfirst, -low, pick(xodd, xa_ref[0], xb_ref[0]))
    ext_ref[0, pl.ds(TILE + xs + 1, zs, stride=block), :] = pick(xlast, -high, pick(xodd, xb_ref[1], xa_ref[1]))
    for field in range(4):
        at = 0 if field == 0 else 1 + field
        below = pick(xodd, xa_ref[1 + field], xb_ref[1 + field])
        above = pick(xodd, xb_ref[at], xa_ref[at])
        ext_ref[field, pl.ds(TILE - 1, zs, stride=block), :] = pick(xfirst, 0.0, below)
        ext_ref[field, pl.ds(TILE + xs, zs, stride=block), :] = pick(xlast, 0.0, above)
    lane = lax.broadcasted_iota(jnp.int32, (1, 128), 1)
    for group in range(pack_ref.shape[0]):
        packed = jnp.zeros((block, 128), jnp.float32)
        for k in range(GROUP):
            z = group * GROUP + k
            if z > zs:
                continue
            rows = block if z < zs else TILE
            for field in range(4):
                start = SLOT * k + (0 if field == 0 else 2 + 2 * field)
                count = 4 if field == 0 else 2
                values = pltpu.roll(ext_ref[field, pl.ds(z * block, rows), :], (start + count // 2) % 128, 1)
                if rows < block:
                    values = jnp.concatenate([values, jnp.zeros((block - rows, 128), jnp.float32)], axis=0)
                packed = jnp.where((lane >= start) & (lane < start + count), values, packed)
        pack_ref[group] = packed


def face_kernel(zs, xs, flag_ref, ext_ref, own_ref, ya_ref, yb_ref, merged_ref, fa_ref, fb_ref, strip_ref):
    yfirst, ylast, yodd, zodd = flag_ref[YFIRST], flag_ref[YLAST], flag_ref[YODD], flag_ref[ZODD]
    block = xs + TILE
    wide = xs + 4
    lane = lax.broadcasted_iota(jnp.int32, (1, 128), 1)
    place = lax.rem(lane, SLOT)
    from_left = (place < 2) | ((place >= 4) & (lax.rem(place, 2) == 0))
    for group in range(own_ref.shape[0]):
        own = own_ref[group]
        fill_left = jnp.where(place == 0, -pltpu.roll(own, 126, 1), 0.0)
        fill_right = jnp.where(place == 3, -pltpu.roll(own, 2, 1), 0.0)
        first, second = ya_ref[group], yb_ref[group]
        left = pick(yfirst, fill_left, pick(yodd, first, second))
        right = pick(ylast, fill_right, pick(yodd, second, first))
        merged_ref[group] = jnp.where(from_left, left, right)

    def strips(z, lanes_from):
        group, k = divmod(z, GROUP)
        strip_ref[0:block, :] = pltpu.roll(merged_ref[group], (lanes_from - SLOT * k) % 128, 1)
        group, k = divmod(z + 1, GROUP)
        strip_ref[block : block + TILE, :] = pltpu.roll(merged_ref[group, 0:TILE], (lanes_from - SLOT * k) % 128, 1)
        return strip_ref[TILE - 2 : TILE - 2 + wide, :]

    for j in range(FACE):
        field = max(j - 1, 0)
        low_z = j if j < 2 else 0
        high_z = zs - 2 + j if j < 2 else zs - 1
        low = ext_ref[field, pl.ds(low_z * block + TILE - 2, wide), :]
        high = ext_ref[field, pl.ds(high_z * block + TILE - 2, wide), :]
        fa_ref[j * wide : j * wide + wide, :] = pick(zodd, low, high)
        fb_ref[j * wide : j * wide + wide, :] = pick(zodd, high, low)
    low = jnp.where(lane < SLOT, strips(0, 0), strips(1, SLOT))
    high = jnp.where(lane < SLOT, strips(zs - 2, 0), strips(zs - 1, SLOT))
    fa_ref[FACE * wide : FACE * wide + wide, :] = pick(zodd, low, high)
    fb_ref[FACE * wide : FACE * wide + wide, :] = pick(zodd, high, low)


def along_y(values, halo, lane, density):
    def shifted(off):
        mixed = jnp.where(lane >= 128 - off if off > 0 else lane < -off, halo, values)
        return pltpu.roll(mixed, off % 128, 1)

    m1, p1 = shifted(1), shifted(-1)
    near = m1 + p1
    blur = near + 2.0 * values
    if not density:
        return (blur,)
    m2, p2 = shifted(2), shifted(-2)
    return blur, (m2 + p2) + 4.0 * near + 6.0 * values, 2.0 * (p2 - m2) + 4.0 * (p1 - m1)


def along_x(at, density):
    fields = [at(part, -1) + at(part, 1) + 2.0 * at(part, 0) for part in ((0, 3, 4, 5) if not density else ())]
    if not density:
        return fields
    a, b, c, d, e = (at(1, off) for off in (-2, -1, 0, 1, 2))
    blurred, sloped = (a + e) + 4.0 * (b + d) + 6.0 * c, 2.0 * (e - a) + 4.0 * (d - b)
    a, b, c, d, e = (at(2, off) for off in (-2, -1, 0, 1, 2))
    return [blurred, sloped, (a + e) + 4.0 * (b + d) + 6.0 * c]


def shade(at, looked, scale):
    def blur(part):
        return at(part, -1) + at(part, 1) + 2.0 * at(part, 0)

    def blur2(part):
        return (at(part, -2) + at(part, 2)) + 4.0 * (at(part, -1) + at(part, 1)) + 6.0 * at(part, 0)

    unit = 1.0 / 4096.0
    grad_z = 2.0 * (at(4, 2) - at(4, -2)) + 4.0 * (at(4, 1) - at(4, -1))
    grad_x = blur2(5)
    grad_y = blur2(6)
    facing = jnp.abs((0.8 * unit) * (grad_z + grad_y) + (0.4 * unit) * grad_x)
    square = grad_z * grad_z + grad_x * grad_x + grad_y * grad_y
    shading = 0.3 + facing * lax.rsqrt(square * (unit * unit) + 0.0025)
    density = (3.0 / 64.0) * blur(0)
    t = jnp.exp(-jnp.abs(density))
    soft = jnp.maximum(density, 0.0) + t * horner(LOG1P, t)
    extinct = looked[3] * (soft * scale)
    fade = extinct * horner(EXPM1, extinct)
    colours = [(looked[c] * shading) * (1.0 + 0.5 * jnp.tanh((1.0 / 64.0) * blur(1 + c))) for c in range(3)]
    return extinct, fade, colours


def over(state, layer):
    passed, red, green, blue, depth = state
    extinct, fade, colours = layer
    weight = passed * fade
    return (
        passed - weight,
        red + weight * colours[0],
        green + weight * colours[1],
        blue + weight * colours[2],
        depth + extinct,
    )


def inner_kernel(zs, xs, scale, ext_ref, merged_ref, looked_ref, inner_ref, cross_ref, rows_ref):
    block = xs + TILE
    lane = lax.broadcasted_iota(jnp.int32, (1, 128), 1)

    def y_step(base, strips, shift):
        rows = strips.shape[0]
        for field in range(4):
            own = 126 if field == 0 else 127 - (2 + 2 * field)
            halo = pltpu.roll(strips, lax.rem(own + 128 - shift, 128), 1)
            results = along_y(ext_ref[field, pl.ds(base, rows), :], halo, lane, field == 0)
            for part, result in zip((0, 1, 2) if field == 0 else (2 + field,), results):
                rows_ref[part, pl.ds(base, rows), :] = result

    for group in range(merged_ref.shape[0]):

        def group_step(k, carry):
            base = pl.multiple_of((group * GROUP + k) * block, TILE)
            y_step(base, merged_ref[group], k * SLOT)
            return carry

        lax.fori_loop(0, min(GROUP, zs - group * GROUP), group_step, 0)
    group, k = divmod(zs, GROUP)
    y_step(zs * block, merged_ref[group, 0:TILE], k * SLOT)

    def x_step(z, carry):
        base = z * block + TILE

        def at(part, off):
            return rows_ref[part, pl.ds(base + off, xs), :]

        for part, result in enumerate(along_x(at, False) + along_x(at, True)):
            cross_ref[part, z] = result
        return carry

    lax.fori_loop(0, zs, x_step, 0)

    unroll = 4 if (zs - 4) % 4 == 0 else 1

    def z_step(step, state):
        for k in range(unroll):
            z = 2 + step * unroll + k
            looked = [looked_ref[c, z] for c in range(4)]
            state = over(state, shade(lambda part, off: cross_ref[part, z + off], looked, scale))
        return state

    zero = jnp.zeros((xs, 128), jnp.float32)
    state = lax.fori_loop(0, (zs - 4) // unroll, z_step, (zero + 1.0, zero, zero, zero, zero))
    for k, values in enumerate(state):
        inner_ref[k] = values


def edge_kernel(zs, xs, scale, flag_ref, fa_ref, fb_ref, cross_ref, looked_ref, inner_ref, *rest):
    out_refs, (face_ref, near_ref, rows_ref, image_ref) = rest[:-4], rest[-4:]
    zfirst, zlast, zodd = flag_ref[ZFIRST], flag_ref[ZLAST], flag_ref[ZODD]
    wide = xs + 4
    lane = lax.broadcasted_iota(jnp.int32, (1, 128), 1)
    for side in range(2):
        edge = zfirst if side == 0 else zlast
        first, second = (fa_ref, fb_ref) if side == 0 else (fb_ref, fa_ref)
        strips = pick(zodd, first[FACE * wide : FACE * wide + wide, :], second[FACE * wide : FACE * wide + wide, :])
        for j in range(FACE):
            field = max(j - 1, 0)
            values = pick(zodd, first[j * wide : j * wide + wide, :], second[j * wide : j * wide + wide, :])
            layer = j if j < 2 else (1 if side == 0 else 0)
            at_lane = SLOT * layer + (0 if field == 0 else 2 + 2 * field)
            halo = pltpu.roll(strips, ((126 if field == 0 else 127) - at_lane) % 128, 1)
            results = along_y(values, halo, lane, field == 0)
            for part, result in zip((0, 1, 2) if field == 0 else (2 + field,), results):
                rows_ref[side, layer, part, 0:wide, :] = result
        for layer in range(2):

            def at(part, off):
                return rows_ref[side, layer, part, 2 + off : 2 + off + xs, :]

            mirrored = 0 if side == 0 else zs - 1
            outer = layer == (0 if side == 0 else 1)
            for part, result in enumerate(along_x(at, True)):
                fill = -cross_ref[4 + part, mirrored] if outer else 0.0
                near_ref[4 + part, 2 * side + layer] = pick(edge, fill, result)
            if not outer:
                for part, result in enumerate(along_x(at, False)):
                    near_ref[part, 2 * side + layer] = pick(edge, 0.0, result)

    def layer_of(z):
        def at(part, off):
            k = z + off
            if k < 0:
                return near_ref[part, k + 2]
            if k >= zs:
                return near_ref[part, k - zs + 2]
            return cross_ref[part, k]

        return shade(at, [looked_ref[c, z] for c in range(4)], scale)

    zero = jnp.zeros((xs, 128), jnp.float32)
    state = over(over((zero + 1.0, zero, zero, zero, zero), layer_of(0)), layer_of(1))
    passed = state[0]
    state = (
        passed * inner_ref[0],
        state[1] + passed * inner_ref[1],
        state[2] + passed * inner_ref[2],
        state[3] + passed * inner_ref[3],
        state[4] + inner_ref[4],
    )
    state = over(over(state, layer_of(zs - 2)), layer_of(zs - 1))
    if len(out_refs) == 1:
        for c in range(4):
            out_refs[0][c] = state[1 + c]
    else:
        for c in range(4):
            image_ref[c] = state[1 + c]
        part = xs // len(out_refs)
        for k, ref in enumerate(out_refs):
            ref[...] = image_ref[:, pl.ds(pl.multiple_of(flag_ref[PEERS + k], part), part), :]


def blend_kernel(order_ref, peer_ref, *refs):
    images, out_ref = refs[:-1], refs[-1]
    count = len(images)
    ranks = [order_ref[peer_ref[k]] for k in range(count)]
    depths = [image[3] for image in images]
    colours = [jnp.zeros_like(depths[0])] * 3
    for k in range(count):
        prior = jnp.zeros_like(depths[0])
        for other in range(count):
            if other != k:
                prior += jnp.where(ranks[other] < ranks[k], depths[other], 0.0)
        through = jnp.exp(-prior)
        colours = [colours[c] + through * images[k][c] for c in range(3)]
    total = functools.reduce(jnp.add, depths)
    out_ref[0], out_ref[1], out_ref[2] = colours
    small = total * horner(EXPM1, total)
    out_ref[3] = jnp.where(total < 0.5, small, 1.0 - jnp.exp(-total))


def call(kernel, out_shape, specs, scratch=(), cost=1.0, name=None, limit=VMEM_LIMIT):
    where = {"s": pltpu.SMEM, "v": pltpu.VMEM, "a": pl.ANY, "h": pltpu.HBM}
    return pl.pallas_call(
        kernel,
        out_shape=out_shape,
        in_specs=[pl.BlockSpec(memory_space=where[s]) for s in specs],
        out_specs=jax.tree.map(lambda _: pl.BlockSpec(memory_space=pltpu.VMEM), out_shape),
        scratch_shapes=list(scratch),
        compiler_params=pltpu.CompilerParams(vmem_limit_bytes=limit),
        cost_estimate=pl.CostEstimate(flops=0, bytes_accessed=int(cost * 3.0e6), transcendentals=0),
        name=name,
    )


def swap_pairs(first, second, axis):
    count = lax.axis_size(axis)
    one = lax.ppermute(first, axis, [(i, i ^ 1) for i in range(count)])
    if count == 2:
        return one, one
    ends = [(0, 0), (count - 1, count - 1)]
    return one, lax.ppermute(second, axis, ends + [(i, i + 1 if i % 2 else i - 1) for i in range(1, count - 1)])


def on_device(fields, material, depth_order, table):
    _, zs, xs, ys = fields.shape
    nx, ny, nz = (lax.axis_size(a) for a in ("gx", "gy", "gz"))
    ix, iy, iz = (lax.axis_index(a) for a in ("gx", "gy", "gz"))
    block = xs + TILE
    part = xs // nz
    swaps = nz in (2, 4)
    peers = [iz ^ k for k in range(nz)] if swaps else list(range(nz))
    entries = [iz == 0, iz == nz - 1, ix == 0, ix == nx - 1, iy == 0, iy == ny - 1, iz % 2, ix % 2, iy % 2]
    entries += [p * part for p in peers]
    flags = jnp.stack([jnp.asarray(e, jnp.int32) for e in entries])
    f32 = lambda *shape: jax.ShapeDtypeStruct(shape, jnp.float32)

    side = call(
        functools.partial(rows_kernel, zs, xs),
        f32(FACE, zs, ys),
        "sh",
        [pltpu.VMEM((4, zs, TILE, ys), jnp.float32), pltpu.SemaphoreType.DMA(())],
        name="x_rows",
        limit=60 * 1024 * 1024,
    )
    high = (1 - ix % 2).astype(jnp.int32)[None]
    x_a, x_b = swap_pairs(side(high, fields), side(1 - high, fields) if nx > 2 else None, "gx")

    wide_table = jnp.pad(table, ((0, 4), (0, 128 - table.shape[1])))
    looked = call(functools.partial(lookup_kernel, zs, xs), f32(4, zs, xs, ys), "vv", cost=1.5, name="lookup")(
        wide_table, material
    )
    x_a, x_b, looked = lax.optimization_barrier((x_a, x_b, looked))

    groups = -(-(zs + 1) // GROUP)
    rows = zs * block + TILE
    ext, own = call(
        functools.partial(extend_kernel, zs, xs), (f32(4, rows, ys), f32(groups, block, 128)), "svvv", name="extend"
    )(flags, fields, x_a, x_b)
    y_a, y_b = swap_pairs(own, own, "gy")

    faces = f32((FACE + 1) * (xs + 4), ys)
    merged, f_a, f_b = call(
        functools.partial(face_kernel, zs, xs),
        (f32(groups, block, 128), faces, faces),
        "svvvv",
        [pltpu.VMEM((block + TILE, 128), jnp.float32)],
        name="faces",
    )(flags, ext, own, y_a, y_b)
    z_a, z_b = swap_pairs(f_a, f_b, "gz")

    scale = 2.0 / (zs * nz)
    inner, cross = call(
        functools.partial(inner_kernel, zs, xs, scale),
        (f32(5, xs, ys), f32(7, zs, xs, ys)),
        "vvv",
        [pltpu.VMEM((6, rows, ys), jnp.float32)],
        cost=4.0,
        name="inner",
    )(ext, merged, looked)

    images = call(
        functools.partial(edge_kernel, zs, xs, scale),
        [f32(4, part, ys)] * nz if swaps else [f32(4, xs, ys)],
        "svvvvv",
        [
            pltpu.VMEM((FACE, xs + TILE, ys), jnp.float32),
            pltpu.VMEM((7, 4, xs, ys), jnp.float32),
            pltpu.VMEM((2, 2, 6, xs + TILE, ys), jnp.float32),
            pltpu.VMEM((4, xs, ys), jnp.float32),
        ],
        name="edges",
    )(flags, z_a, z_b, cross, looked, inner)

    if swaps:
        mine = [images[0]]
        for k in range(1, nz):
            mine.append(lax.ppermute(images[k], "gz", [(i, i ^ k) for i in range(nz)]))
    else:
        stacked = lax.all_to_all(images[0].reshape(4, nz, part, ys), "gz", split_axis=1, concat_axis=1)
        mine = [stacked[:, b] for b in range(nz)]
    whose = jnp.stack([jnp.asarray(p, jnp.int32) for p in peers])
    return call(blend_kernel, f32(4, part, ys), "ss" + "v" * nz, name="blend")(depth_order, whose, *mine)


def solution(mesh):
    return jax.shard_map(
        on_device,
        mesh=mesh,
        in_specs=(P(None, "gz", "gx", "gy"), P("gz", "gx", "gy"), P(), P()),
        out_specs=P(None, ("gx", "gz"), "gy"),
        check_vma=False,
    )
```

```python
import functools

import jax
import jax.numpy as jnp
from jax import lax
from jax.experimental import pallas as pl
from jax.experimental.pallas import tpu as pltpu
from jax.sharding import PartitionSpec as P

VMEM_LIMIT = 40 * 1024 * 1024
GROUP = 12
SLOT = 10
TILE = 8
FACE = 5

LOG1P = (
    0.9999995186059567, -0.49996356582563917, 0.33265255844036573, -0.24453388969978707, 0.17659864766821842,
    -0.10679931280022417, 0.043659288844443055, -0.008466410404849948,
)
EXPM1 = (
    1.0, -0.4999995231628418, 0.1666584461927414, -0.04160914570093155, 0.00814302358776331, -0.0010865303920581937,
)


def horner(coefficients, value):
    total = jnp.full_like(value, coefficients[-1])
    for c in coefficients[-2::-1]:
        total = total * value + c
    return total


def place_of(axis):
    at = lax.axis_index(axis)
    return at == 0, at == lax.axis_size(axis) - 1, lax.rem(at, 2) == 1


def rows_kernel(zs, xs, even_high, fields_ref, out_ref, tile_ref, sems):
    high = (lax.rem(lax.axis_index("gx"), 2) == 0) == even_high
    start = pl.multiple_of(jnp.where(high, xs - TILE, 0), TILE)
    copies = []
    for field in range(4):
        copy = pltpu.make_async_copy(
            fields_ref.at[field, :, pl.ds(start, TILE), :], tile_ref.at[field], sems.at[field]
        )
        copy.start()
        copies.append(copy)
    for field in range(4):
        copies[field].wait()
        for group in (0, 1) if field == 0 else (1 + field,):
            tiles = tile_ref.at[field].reshape(zs * TILE, 128)
            low_row = group if group < 2 else 0
            high_row = TILE - 2 + group if group < 2 else TILE - 1
            out_ref[group] = jnp.where(
                high, tiles[pl.ds(high_row, zs, stride=TILE), :], tiles[pl.ds(low_row, zs, stride=TILE), :]
            )


def slot_of(field):
    return (0, 4) if field == 0 else (2 + 2 * field, 2)


def pack_strips(load, layers, lane, rows):
    packed = jnp.zeros((rows, 128), jnp.float32)
    for k, z in enumerate(layers):
        for field in range(4):
            first, count = slot_of(field)
            start = SLOT * k + first
            values = pltpu.roll(load(field, z), (start + count // 2) % 128, 1)
            packed = jnp.where((lane >= start) & (lane < start + count), values, packed)
    return packed


def stage_kernel(zs, xs, peers, table_ref, order_ref, fields_ref, material_ref, held_ref, looked_ref, pack_ref, near_ref, tables_ref, sems):
    copies = [pltpu.make_async_copy(fields_ref.at[f], held_ref.at[f], sems.at[f]) for f in range(4)]
    for copy in copies:
        copy.start()
    tables_ref[...] = jnp.zeros_like(tables_ref)
    tables_ref[:, 0 : table_ref.shape[1]] = table_ref[...]
    tables = [jnp.broadcast_to(tables_ref[c : c + 1, :], (xs, 128)) for c in range(4)]
    each = 8

    def step(k, carry):
        for j in range(each):
            ids = material_ref[k * each + j]
            for c in range(4):
                looked_ref[c, k * each + j] = jnp.take_along_axis(tables[c], ids, axis=1, mode="promise_in_bounds")
        return carry

    lax.fori_loop(0, zs // each, step, 0)
    iz, count = lax.axis_index("gz"), lax.axis_size("gz")
    ranks = [order_ref[iz ^ k if peers else k] for k in range(count)]
    for k in range(count):
        for other in range(count):
            nearer = jnp.where(ranks[other] < ranks[k], 1.0, 0.0)
            near_ref[k * count + other] = jnp.full((1, 128), nearer, jnp.float32)
    for copy in copies:
        copy.wait()
    lane = lax.broadcasted_iota(jnp.int32, (1, 128), 1)
    for group in range(pack_ref.shape[0]):
        layers = range(group * GROUP, min(zs, group * GROUP + GROUP))
        pack_ref[group] = pack_strips(lambda f, z: held_ref[f, z], layers, lane, xs)


def x_halo_kernel(zs, xs, held_ref, main_ref, xa_ref, xb_ref, halo_ref, pack_ref):
    first, last, odd = place_of("gx")
    halo_ref[...] = jnp.zeros_like(halo_ref)
    for field in range(4):
        tiles = halo_ref.at[field].reshape((zs + 1) * TILE, 128)
        own = held_ref.at[field].reshape(zs * xs, 128)
        at = 0 if field == 0 else 1 + field
        below = jnp.where(odd, xa_ref[1 + field], xb_ref[1 + field])
        above = jnp.where(odd, xb_ref[at], xa_ref[at])
        tiles[pl.ds(TILE - 1, zs, stride=TILE), :] = jnp.where(first, 0.0, below)
        tiles[pl.ds(TILE, zs, stride=TILE), :] = jnp.where(last, 0.0, above)
        if field == 0:
            low, high = own[pl.ds(0, zs, stride=xs), :], own[pl.ds(xs - 1, zs, stride=xs), :]
            tiles[pl.ds(TILE - 2, zs, stride=TILE), :] = jnp.where(first, -low, jnp.where(odd, xa_ref[0], xb_ref[0]))
            tiles[pl.ds(TILE + 1, zs, stride=TILE), :] = jnp.where(last, -high, jnp.where(odd, xb_ref[1], xa_ref[1]))
    lane = lax.broadcasted_iota(jnp.int32, (1, 128), 1)
    for group in range(pack_ref.shape[0]):
        layers = range(group * GROUP, min(zs + 1, group * GROUP + GROUP))
        pack_ref[group, 0:TILE] = pack_strips(lambda f, z: halo_ref[f, z], layers, lane, TILE)
        pack_ref[group, TILE:] = main_ref[group]


def face_kernel(zs, xs, held_ref, halo_ref, own_ref, ya_ref, yb_ref, merged_ref, fa_ref, fb_ref, strip_ref):
    yfirst, ylast, yodd = place_of("gy")
    zodd = place_of("gz")[2]
    block = xs + TILE
    wide = xs + 4
    lane = lax.broadcasted_iota(jnp.int32, (1, 128), 1)
    place = lax.rem(lane, SLOT)
    from_left = (place < 2) | ((place >= 4) & (lax.rem(place, 2) == 0))
    for group in range(own_ref.shape[0]):
        own = own_ref[group]
        fill_left = jnp.where(place == 0, -pltpu.roll(own, 126, 1), 0.0)
        fill_right = jnp.where(place == 3, -pltpu.roll(own, 2, 1), 0.0)
        first, second = ya_ref[group], yb_ref[group]
        left = jnp.where(yfirst, fill_left, jnp.where(yodd, first, second))
        right = jnp.where(ylast, fill_right, jnp.where(yodd, second, first))
        merged_ref[group] = jnp.where(from_left, left, right)

    def strips(z, lanes_from):
        group, k = divmod(z, GROUP)
        strip_ref[0:block, :] = pltpu.roll(merged_ref[group], (lanes_from - SLOT * k) % 128, 1)
        group, k = divmod(z + 1, GROUP)
        strip_ref[block : block + TILE, :] = pltpu.roll(merged_ref[group, 0:TILE], (lanes_from - SLOT * k) % 128, 1)
        return strip_ref[TILE - 2 : TILE - 2 + wide, :]

    for j in range(FACE):
        field = max(j - 1, 0)
        low_z = j if j < 2 else 0
        high_z = zs - 2 + j if j < 2 else zs - 1
        at = j * wide
        for out_ref, swapped in ((fa_ref, False), (fb_ref, True)):
            low = zodd != swapped

            def put(row, count, load):
                out_ref[at + row : at + row + count, :] = jnp.where(low, load(low_z), load(high_z))

            put(0, 2, lambda z: halo_ref[field, z, TILE - 2 : TILE, :])
            put(2, xs, lambda z: held_ref[field, z])
            put(2 + xs, 2, lambda z: halo_ref[field, z + 1, 0:2, :])
    low = jnp.where(lane < SLOT, strips(0, 0), strips(1, SLOT))
    high = jnp.where(lane < SLOT, strips(zs - 2, 0), strips(zs - 1, SLOT))
    fa_ref[FACE * wide : FACE * wide + wide, :] = jnp.where(zodd, low, high)
    fb_ref[FACE * wide : FACE * wide + wide, :] = jnp.where(zodd, high, low)


def along_y(values, halo, lane, density):
    def shifted(off):
        mixed = jnp.where(lane >= 128 - off if off > 0 else lane < -off, halo, values)
        return pltpu.roll(mixed, off % 128, 1)

    m1, p1 = shifted(1), shifted(-1)
    near = m1 + p1
    blur = near + 2.0 * values
    if not density:
        return (blur,)
    m2, p2 = shifted(2), shifted(-2)
    return blur, (m2 + p2) + 4.0 * near + 6.0 * values, 2.0 * (p2 - m2) + 4.0 * (p1 - m1)


def along_x(at, density):
    fields = [at(part, -1) + at(part, 1) + 2.0 * at(part, 0) for part in ((0, 3, 4, 5) if not density else ())]
    if not density:
        return fields
    a, b, c, d, e = (at(1, off) for off in (-2, -1, 0, 1, 2))
    blurred, sloped = (a + e) + 4.0 * (b + d) + 6.0 * c, 2.0 * (e - a) + 4.0 * (d - b)
    a, b, c, d, e = (at(2, off) for off in (-2, -1, 0, 1, 2))
    return [blurred, sloped, (a + e) + 4.0 * (b + d) + 6.0 * c]


class Sums:
    def __init__(self, load):
        self.load, self.made = load, {}

    def pair(self, part, z, level):
        if level == 0:
            key, make = (part, z, 0), lambda: self.load(part, z)
        else:
            key, make = (part, z, level), lambda: self.pair(part, z, level - 1) + self.pair(part, z + 1, level - 1)
        if key not in self.made:
            self.made[key] = make()
        return self.made[key]

    def blur(self, part, z):
        return self.pair(part, z - 1, 2)

    def blur2(self, part, z):
        return self.pair(part, z - 2, 4)

    def slope(self, part, z):
        return 2.0 * (self.pair(part, z, 2) - self.pair(part, z - 2, 2))


def shade(sums, z, looked, scale):
    unit = 1.0 / 4096.0
    grad_z = sums.slope(4, z)
    grad_x = sums.blur2(5, z)
    grad_y = sums.blur2(6, z)
    facing = jnp.abs((0.8 * unit) * (grad_z + grad_y) + (0.4 * unit) * grad_x)
    square = grad_z * grad_z + grad_x * grad_x + grad_y * grad_y
    shading = 0.3 + facing * lax.rsqrt(square * (unit * unit) + 0.0025)
    density = (3.0 / 64.0) * sums.blur(0, z)
    t = jnp.exp(-jnp.abs(density))
    soft = jnp.maximum(density, 0.0) + t * horner(LOG1P, t)
    extinct = looked[3] * (soft * scale)
    fade = extinct * horner(EXPM1, extinct)
    colours = [(looked[c] * shading) * (1.0 + 0.5 * jnp.tanh((1.0 / 64.0) * sums.blur(1 + c, z))) for c in range(3)]
    return extinct, fade, colours


def over(state, layer):
    passed, red, green, blue, depth = state
    extinct, fade, colours = layer
    weight = passed * fade
    return (
        passed - weight,
        red + weight * colours[0],
        green + weight * colours[1],
        blue + weight * colours[2],
        depth + extinct,
    )


def inner_kernel(zs, xs, scale, held_ref, halo_ref, merged_ref, looked_ref, inner_ref, cross_ref, rows_ref):
    block = xs + TILE
    lane = lax.broadcasted_iota(jnp.int32, (1, 128), 1)

    def y_step(z, strips, shift):
        for field in range(4):
            own = 126 if field == 0 else 127 - (2 + 2 * field)
            near = pltpu.roll(strips, lax.rem(own + 128 - shift, 128), 1)
            pieces = [(halo_ref[field, z], near[0:TILE], 0)]
            if strips.shape[0] > TILE:
                pieces.append((held_ref[field, z], near[TILE:], TILE))
            for values, halo, at in pieces:
                results = along_y(values, halo, lane, field == 0)
                for part, result in zip((0, 1, 2) if field == 0 else (2 + field,), results):
                    rows_ref[part, pl.ds(pl.multiple_of(z * block + at, TILE), values.shape[0]), :] = result

    each = 4
    for group in range(merged_ref.shape[0]):

        def group_step(step, carry):
            for j in range(each):
                k = step * each + j
                y_step(group * GROUP + k, merged_ref[group], k * SLOT)
            return carry

        lax.fori_loop(0, min(GROUP, zs - group * GROUP) // each, group_step, 0)
    group, k = divmod(zs, GROUP)
    y_step(zs, merged_ref[group, 0:TILE], k * SLOT)

    def tile_step(tile, carry):
        at = pl.multiple_of(tile * TILE, TILE)
        crossed = {}

        def load(part, z):
            if z not in crossed:
                rows = lambda part, off: rows_ref[part, pl.ds(at + (z * block + TILE + off), TILE), :]
                crossed[z] = along_x(rows, False) + along_x(rows, True)
                if z < 4 or z >= zs - 4:
                    for k, values in enumerate(crossed[z]):
                        cross_ref[k, z if z < 4 else z - zs + 8, pl.ds(at, TILE), :] = values
            return crossed[z][part]

        load(0, 0)
        load(0, zs - 1)
        sums = Sums(load)
        zero = jnp.zeros((TILE, 128), jnp.float32)
        state = (zero + 1.0, zero, zero, zero, zero)
        for z in range(2, zs - 2):
            looked = [looked_ref[c, z, pl.ds(at, TILE), :] for c in range(4)]
            state = over(state, shade(sums, z, looked, scale))
        for k, values in enumerate(state):
            inner_ref[k, pl.ds(at, TILE), :] = values
        return carry

    lax.fori_loop(0, xs // TILE, tile_step, 0)


def edge_kernel(zs, xs, scale, fa_ref, fb_ref, cross_ref, looked_ref, inner_ref, *rest):
    out_refs, (near_ref, rows_ref, image_ref) = rest[:-3], rest[-3:]
    zfirst, zlast, zodd = place_of("gz")
    wide = xs + 4
    lane = lax.broadcasted_iota(jnp.int32, (1, 128), 1)
    for side in range(2):
        edge = zfirst if side == 0 else zlast
        first, second = (fa_ref, fb_ref) if side == 0 else (fb_ref, fa_ref)
        strips = jnp.where(zodd, first[FACE * wide : FACE * wide + wide, :], second[FACE * wide : FACE * wide + wide, :])
        for j in range(FACE):
            field = max(j - 1, 0)
            values = jnp.where(zodd, first[j * wide : j * wide + wide, :], second[j * wide : j * wide + wide, :])
            layer = j if j < 2 else (1 if side == 0 else 0)
            at_lane = SLOT * layer + slot_of(field)[0]
            halo = pltpu.roll(strips, ((126 if field == 0 else 127) - at_lane) % 128, 1)
            results = along_y(values, halo, lane, field == 0)
            for part, result in zip((0, 1, 2) if field == 0 else (2 + field,), results):
                rows_ref[side, layer, part, 0:wide, :] = result
    for side in range(2):
        edge = zfirst if side == 0 else zlast
        for layer in range(2):

            def at(part, off):
                return rows_ref[side, layer, part, 2 + off : 2 + off + xs, :]

            mirrored = 0 if side == 0 else 7
            outer = layer == side
            for part, result in enumerate(along_x(at, True)):
                fill = -cross_ref[4 + part, mirrored] if outer else 0.0
                near_ref[4 + part, 2 * side + layer] = jnp.where(edge, fill, result)
            if not outer:
                for part, result in enumerate(along_x(at, False)):
                    near_ref[part, 2 * side + layer] = jnp.where(edge, 0.0, result)

    def load(part, z):
        if z < 0:
            return near_ref[part, z + 2]
        if z >= zs:
            return near_ref[part, z - zs + 2]
        return cross_ref[part, z if z < 4 else z - zs + 8]

    def layer_of(z):
        return shade(Sums(load), z, [looked_ref[c, z] for c in range(4)], scale)

    zero = jnp.zeros((xs, 128), jnp.float32)
    state = over(over((zero + 1.0, zero, zero, zero, zero), layer_of(0)), layer_of(1))
    passed = state[0]
    state = (
        passed * inner_ref[0],
        state[1] + passed * inner_ref[1],
        state[2] + passed * inner_ref[2],
        state[3] + passed * inner_ref[3],
        state[4] + inner_ref[4],
    )
    state = over(over(state, layer_of(zs - 2)), layer_of(zs - 1))
    if len(out_refs) == 1:
        for c in range(4):
            out_refs[0][c] = state[1 + c]
    else:
        for c in range(4):
            image_ref[c] = state[1 + c]
        part = xs // len(out_refs)
        for k, ref in enumerate(out_refs):
            ref[...] = image_ref[:, pl.ds(pl.multiple_of((lax.axis_index("gz") ^ k) * part, part), part), :]


def blend_kernel(near_ref, *refs):
    images, out_ref = refs[:-1], refs[-1]
    count = len(images)
    depths = [image[3] for image in images]
    colours = [jnp.zeros_like(depths[0])] * 3
    for k in range(count):
        prior = jnp.zeros_like(depths[0])
        for other in range(count):
            if other != k:
                prior += near_ref[k * count + other] * depths[other]
        through = jnp.exp(-prior)
        colours = [colours[c] + through * images[k][c] for c in range(3)]
    total = functools.reduce(jnp.add, depths)
    out_ref[0], out_ref[1], out_ref[2] = colours
    small = total * horner(EXPM1, total)
    out_ref[3] = jnp.where(total < 0.5, small, 1.0 - jnp.exp(-total))


def call(kernel, out_shape, specs, scratch=(), cost=1.0, name=None, limit=VMEM_LIMIT):
    where = {"s": pltpu.SMEM, "v": pltpu.VMEM, "a": pl.ANY}
    return pl.pallas_call(
        kernel,
        out_shape=out_shape,
        in_specs=[pl.BlockSpec(memory_space=where[s]) for s in specs],
        out_specs=jax.tree.map(lambda _: pl.BlockSpec(memory_space=pltpu.VMEM), out_shape),
        scratch_shapes=list(scratch),
        compiler_params=pltpu.CompilerParams(vmem_limit_bytes=limit),
        cost_estimate=pl.CostEstimate(flops=0, bytes_accessed=int(cost * 3.0e6), transcendentals=0),
        name=name,
    )


def swap_pairs(first, second, axis):
    count = lax.axis_size(axis)
    one = lax.ppermute(first, axis, [(i, i ^ 1) for i in range(count)])
    if count == 2:
        return one, one
    ends = [(0, 0), (count - 1, count - 1)]
    return one, lax.ppermute(second, axis, ends + [(i, i + 1 if i % 2 else i - 1) for i in range(1, count - 1)])


def on_device(fields, material, depth_order, table):
    _, zs, xs, ys = fields.shape
    nx, nz = lax.axis_size("gx"), lax.axis_size("gz")
    block = xs + TILE
    part = xs // nz
    swaps = nz in (2, 4)
    groups = -(-(zs + 1) // GROUP)
    f32 = lambda *shape: jax.ShapeDtypeStruct(shape, jnp.float32)

    def side(even_high):
        return call(
            functools.partial(rows_kernel, zs, xs, even_high),
            f32(FACE, zs, ys),
            "a",
            [pltpu.VMEM((4, zs, TILE, ys), jnp.float32), pltpu.SemaphoreType.DMA((4,))],
            name="x_rows",
            limit=60 * 1024 * 1024,
        )(fields)

    x_a, x_b = swap_pairs(side(True), side(False) if nx > 2 else None, "gx")
    held, looked, main, nearer = call(
        functools.partial(stage_kernel, zs, xs, swaps),
        (f32(4, zs, xs, ys), f32(4, zs, xs, ys), f32(groups, xs, 128), f32(nz * nz, 1, 128)),
        "vsav",
        [pltpu.VMEM((4, 128), jnp.float32), pltpu.SemaphoreType.DMA((4,))],
        cost=2.0,
        name="stage",
    )(table, depth_order, fields, material)
    x_a, x_b, held = lax.optimization_barrier((x_a, x_b, held))

    halo, own = call(
        functools.partial(x_halo_kernel, zs, xs), (f32(4, zs + 1, TILE, ys), f32(groups, block, 128)), "vvvv", name="x_halo"
    )(held, main, x_a, x_b)
    y_a, y_b = swap_pairs(own, own, "gy")

    faces = f32((FACE + 1) * (xs + 4), ys)
    merged, f_a, f_b = call(
        functools.partial(face_kernel, zs, xs),
        (f32(groups, block, 128), faces, faces),
        "vvvvv",
        [pltpu.VMEM((block + TILE, 128), jnp.float32)],
        name="faces",
    )(held, halo, own, y_a, y_b)
    z_a, z_b = swap_pairs(f_a, f_b, "gz")

    scale = 2.0 / (zs * nz)
    inner, cross = call(
        functools.partial(inner_kernel, zs, xs, scale),
        (f32(5, xs, ys), f32(7, 8, xs, ys)),
        "vvvv",
        [pltpu.VMEM((6, zs * block + TILE, ys), jnp.float32)],
        cost=4.0,
        name="inner",
    )(held, halo, merged, looked)

    images = call(
        functools.partial(edge_kernel, zs, xs, scale),
        [f32(4, part, ys)] * nz if swaps else [f32(4, xs, ys)],
        "vvvvv",
        [
            pltpu.VMEM((7, 4, xs, ys), jnp.float32),
            pltpu.VMEM((2, 2, 6, xs + TILE, ys), jnp.float32),
            pltpu.VMEM((4, xs, ys), jnp.float32),
        ],
        name="edges",
    )(z_a, z_b, cross, looked, inner)

    if swaps:
        mine = [images[0]]
        for k in range(1, nz):
            mine.append(lax.ppermute(images[k], "gz", [(i, i ^ k) for i in range(nz)]))
    else:
        stacked = lax.all_to_all(images[0].reshape(4, nz, part, ys), "gz", split_axis=1, concat_axis=1)
        mine = [stacked[:, b] for b in range(nz)]
    return call(blend_kernel, f32(4, part, ys), "v" + "v" * nz, name="blend")(nearer, *mine)


def solution(mesh):
    return jax.shard_map(
        on_device,
        mesh=mesh,
        in_specs=(P(None, "gz", "gx", "gy"), P("gz", "gx", "gy"), P(), P()),
        out_specs=P(None, ("gx", "gz"), "gy"),
        check_vma=False,
    )
```

```python
import functools

import jax
import jax.numpy as jnp
from jax import lax
from jax.experimental import pallas as pl
from jax.experimental.pallas import tpu as pltpu
from jax.sharding import PartitionSpec as P

VMEM_LIMIT = 40 * 1024 * 1024
GROUP = 12
SLOT = 10
TILE = 8
FACE = 5

LOG1P = (
    0.9999995186059567, -0.49996356582563917, 0.33265255844036573, -0.24453388969978707, 0.17659864766821842,
    -0.10679931280022417, 0.043659288844443055, -0.008466410404849948,
)
EXPM1 = (
    1.0, -0.4999995231628418, 0.1666584461927414, -0.04160914570093155, 0.00814302358776331, -0.0010865303920581937,
)


def horner(coefficients, value):
    total = jnp.full_like(value, coefficients[-1])
    for c in coefficients[-2::-1]:
        total = total * value + c
    return total


def place_of(axis):
    at = lax.axis_index(axis)
    return at == 0, at == lax.axis_size(axis) - 1, lax.rem(at, 2) == 1


def rows_kernel(zs, xs, even_high, fields_ref, out_ref):
    high = (lax.rem(lax.axis_index("gx"), 2) == 0) == even_high
    for group in range(FACE):
        field = max(group - 1, 0)
        rows = fields_ref.at[field].reshape(zs * xs, 128)
        low_row = group if group < 2 else 0
        high_row = xs - 2 + group if group < 2 else xs - 1
        out_ref[group] = rows[pl.ds(jnp.where(high, high_row, low_row), zs, stride=xs), :]


def slot_of(field):
    return (0, 4) if field == 0 else (2 + 2 * field, 2)


def pack_strips(load, layers, lane, rows):
    packed = jnp.zeros((rows, 128), jnp.float32)
    for k, z in enumerate(layers):
        for field in range(4):
            first, count = slot_of(field)
            start = SLOT * k + first
            values = pltpu.roll(load(field, z), (start + count // 2) % 128, 1)
            packed = jnp.where((lane >= start) & (lane < start + count), values, packed)
    return packed


def stage_kernel(zs, xs, peers, order_ref, fields_ref, material_ref, held_ref, ids_ref, pack_ref, near_ref, sems):
    copies = [pltpu.make_async_copy(fields_ref.at[f], held_ref.at[f], sems.at[f]) for f in range(4)]
    copies.append(pltpu.make_async_copy(material_ref, ids_ref, sems.at[4]))
    for copy in copies:
        copy.start()
    iz, count = lax.axis_index("gz"), lax.axis_size("gz")
    ranks = [order_ref[iz ^ k if peers else k] for k in range(count)]
    for k in range(count):
        for other in range(count):
            nearer = jnp.where(ranks[other] < ranks[k], 1.0, 0.0)
            near_ref[k * count + other] = jnp.full((1, 128), nearer, jnp.float32)
    for copy in copies:
        copy.wait()
    lane = lax.broadcasted_iota(jnp.int32, (1, 128), 1)
    for group in range(pack_ref.shape[0]):
        layers = range(group * GROUP, min(zs, group * GROUP + GROUP))
        pack_ref[group] = pack_strips(lambda f, z: held_ref[f, z], layers, lane, xs)


def lookup_kernel(zs, xs, table_ref, ids_ref, looked_ref, tables_ref):
    tables_ref[...] = jnp.zeros_like(tables_ref)
    tables_ref[:, 0 : table_ref.shape[1]] = table_ref[...]
    tables = [jnp.broadcast_to(tables_ref[c : c + 1, :], (TILE, 128)) for c in range(4)]
    each = 8
    tiles = xs // TILE

    def step(k, carry):
        for j in range(each):
            z = k * each + j
            for t in range(tiles):
                ids = ids_ref[z, pl.ds(t, TILE, stride=tiles), :]
                for c in range(4):
                    looked_ref[c, z, t * TILE : t * TILE + TILE, :] = jnp.take_along_axis(
                        tables[c], ids, axis=1, mode="promise_in_bounds"
                    )
        return carry

    lax.fori_loop(0, zs // each, step, 0)


def x_halo_kernel(zs, xs, held_ref, main_ref, xa_ref, xb_ref, halo_ref, pack_ref):
    first, last, odd = place_of("gx")
    halo_ref[...] = jnp.zeros_like(halo_ref)
    for field in range(4):
        tiles = halo_ref.at[field].reshape((zs + 1) * TILE, 128)
        own = held_ref.at[field].reshape(zs * xs, 128)
        at = 0 if field == 0 else 1 + field
        below = jnp.where(odd, xa_ref[1 + field], xb_ref[1 + field])
        above = jnp.where(odd, xb_ref[at], xa_ref[at])
        tiles[pl.ds(TILE - 1, zs, stride=TILE), :] = jnp.where(first, 0.0, below)
        tiles[pl.ds(TILE, zs, stride=TILE), :] = jnp.where(last, 0.0, above)
        if field == 0:
            low, high = own[pl.ds(0, zs, stride=xs), :], own[pl.ds(xs - 1, zs, stride=xs), :]
            tiles[pl.ds(TILE - 2, zs, stride=TILE), :] = jnp.where(first, -low, jnp.where(odd, xa_ref[0], xb_ref[0]))
            tiles[pl.ds(TILE + 1, zs, stride=TILE), :] = jnp.where(last, -high, jnp.where(odd, xb_ref[1], xa_ref[1]))
    lane = lax.broadcasted_iota(jnp.int32, (1, 128), 1)
    for group in range(pack_ref.shape[0]):
        layers = range(group * GROUP, min(zs + 1, group * GROUP + GROUP))
        pack_ref[group, 0:TILE] = pack_strips(lambda f, z: halo_ref[f, z], layers, lane, TILE)
        pack_ref[group, TILE:] = main_ref[group]


def face_kernel(zs, xs, held_ref, halo_ref, own_ref, ya_ref, yb_ref, merged_ref, fa_ref, fb_ref):
    yfirst, ylast, yodd = place_of("gy")
    zodd = place_of("gz")[2]
    block = xs + TILE
    lane = lax.broadcasted_iota(jnp.int32, (1, 128), 1)
    place = lax.rem(lane, SLOT)
    from_left = (place < 2) | ((place >= 4) & (lax.rem(place, 2) == 0))
    for group in range(own_ref.shape[0]):
        own = own_ref[group]
        fill_left = jnp.where(place == 0, -pltpu.roll(own, 126, 1), 0.0)
        fill_right = jnp.where(place == 3, -pltpu.roll(own, 2, 1), 0.0)
        first, second = ya_ref[group], yb_ref[group]
        left = jnp.where(yfirst, fill_left, jnp.where(yodd, first, second))
        right = jnp.where(ylast, fill_right, jnp.where(yodd, second, first))
        merged_ref[group] = jnp.where(from_left, left, right)

    upper = lax.broadcasted_iota(jnp.int32, (TILE, 1), 0) < TILE // 2

    def strips(z, lanes_from):
        group, k = divmod(z, GROUP)
        here = pltpu.roll(merged_ref[group], (lanes_from - SLOT * k) % 128, 1)
        group, k = divmod(z + 1, GROUP)
        after = pltpu.roll(merged_ref[group, 0:TILE], (lanes_from - SLOT * k) % 128, 1)
        return here[TILE:], jnp.where(upper, after, here[0:TILE])

    def put(at, low, high):
        for out_ref, swapped in ((fa_ref, False), (fb_ref, True)):
            for (start, count), a, b in zip(((0, xs), (xs, TILE)), low, high):
                out_ref[at * block + start : at * block + start + count, :] = jnp.where(zodd != swapped, a, b)

    def layer(field, z):
        return held_ref[field, z], jnp.where(upper, halo_ref[field, z + 1], halo_ref[field, z])

    for j in range(FACE):
        field = max(j - 1, 0)
        put(j, layer(field, j if j < 2 else 0), layer(field, zs - 2 + j if j < 2 else zs - 1))

    def both(z):
        return [jnp.where(lane < SLOT, a, b) for a, b in zip(strips(z, 0), strips(z + 1, SLOT))]

    put(FACE, both(0), both(zs - 2))


def along_y(values, halo, lane, density):
    def shifted(off):
        mixed = jnp.where(lane >= 128 - off if off > 0 else lane < -off, halo, values)
        return pltpu.roll(mixed, off % 128, 1)

    m1, p1 = shifted(1), shifted(-1)
    near = m1 + p1
    blur = near + 2.0 * values
    if not density:
        return (blur,)
    m2, p2 = shifted(2), shifted(-2)
    return blur, (m2 + p2) + 4.0 * near + 6.0 * values, 2.0 * (p2 - m2) + 4.0 * (p1 - m1)


def along_x(at, density):
    fields = [at(part, -1) + at(part, 1) + 2.0 * at(part, 0) for part in ((0, 3, 4, 5) if not density else ())]
    if not density:
        return fields
    a, b, c, d, e = (at(1, off) for off in (-2, -1, 0, 1, 2))
    blurred, sloped = (a + e) + 4.0 * (b + d) + 6.0 * c, 2.0 * (e - a) + 4.0 * (d - b)
    a, b, c, d, e = (at(2, off) for off in (-2, -1, 0, 1, 2))
    return [blurred, sloped, (a + e) + 4.0 * (b + d) + 6.0 * c]


class Sums:
    def __init__(self, load):
        self.load, self.made = load, {}

    def pair(self, part, z, level):
        if level == 0:
            key, make = (part, z, 0), lambda: self.load(part, z)
        else:
            key, make = (part, z, level), lambda: self.pair(part, z, level - 1) + self.pair(part, z + 1, level - 1)
        if key not in self.made:
            self.made[key] = make()
        return self.made[key]

    def blur(self, part, z):
        return self.pair(part, z - 1, 2)

    def blur2(self, part, z):
        return self.pair(part, z - 2, 4)

    def slope(self, part, z):
        return 2.0 * (self.pair(part, z, 2) - self.pair(part, z - 2, 2))


def shade(sums, z, looked, scale):
    unit = 1.0 / 4096.0
    grad_z = sums.slope(4, z)
    grad_x = sums.blur2(5, z)
    grad_y = sums.blur2(6, z)
    facing = jnp.abs((0.8 * unit) * (grad_z + grad_y) + (0.4 * unit) * grad_x)
    square = grad_z * grad_z + grad_x * grad_x + grad_y * grad_y
    shading = 0.3 + facing * lax.rsqrt(square * (unit * unit) + 0.0025)
    density = (3.0 / 64.0) * sums.blur(0, z)
    t = jnp.exp(-jnp.abs(density))
    soft = jnp.maximum(density, 0.0) + t * horner(LOG1P, t)
    extinct = looked[3] * (soft * scale)
    fade = extinct * horner(EXPM1, extinct)
    colours = [(looked[c] * shading) * (1.0 + 0.5 * jnp.tanh((1.0 / 64.0) * sums.blur(1 + c, z))) for c in range(3)]
    return extinct, fade, colours


def over(state, layer):
    passed, red, green, blue, depth = state
    extinct, fade, colours = layer
    weight = passed * fade
    return (
        passed - weight,
        red + weight * colours[0],
        green + weight * colours[1],
        blue + weight * colours[2],
        depth + extinct,
    )


def inner_kernel(zs, xs, scale, held_ref, halo_ref, merged_ref, looked_ref, inner_ref, cross_ref, rows_ref):
    block = xs + TILE
    lane = lax.broadcasted_iota(jnp.int32, (1, 128), 1)

    def y_step(z, strips, shift):
        for field in range(4):
            own = 126 if field == 0 else 127 - (2 + 2 * field)
            near = pltpu.roll(strips, lax.rem(own + 128 - shift, 128), 1)
            pieces = [(halo_ref[field, z], near[0:TILE], 0)]
            if strips.shape[0] > TILE:
                pieces.append((held_ref[field, z], near[TILE:], TILE))
            for values, halo, at in pieces:
                results = along_y(values, halo, lane, field == 0)
                for part, result in zip((0, 1, 2) if field == 0 else (2 + field,), results):
                    rows_ref[part, pl.ds(pl.multiple_of(z * block + at, TILE), values.shape[0]), :] = result

    each = 4
    for group in range(merged_ref.shape[0]):

        def group_step(step, carry):
            for j in range(each):
                k = step * each + j
                y_step(group * GROUP + k, merged_ref[group], k * SLOT)
            return carry

        lax.fori_loop(0, min(GROUP, zs - group * GROUP) // each, group_step, 0)
    group, k = divmod(zs, GROUP)
    y_step(zs, merged_ref[group, 0:TILE], k * SLOT)

    tiles = xs // TILE

    def tile_step(tile, carry):
        at = pl.multiple_of(tile * TILE, TILE)
        crossed = {}

        def load(part, z):
            if z not in crossed:
                rows = lambda part, off: rows_ref[part, pl.ds(tile + (z * block + TILE + off), TILE, stride=tiles), :]
                crossed[z] = along_x(rows, False) + along_x(rows, True)
                if z < 4 or z >= zs - 4:
                    for k, values in enumerate(crossed[z]):
                        cross_ref[k, z if z < 4 else z - zs + 8, pl.ds(at, TILE), :] = values
            return crossed[z][part]

        load(0, 0)
        load(0, zs - 1)
        sums = Sums(load)
        zero = jnp.zeros((TILE, 128), jnp.float32)
        state = (zero + 1.0, zero, zero, zero, zero)
        for z in range(2, zs - 2):
            looked = [looked_ref[c, z, pl.ds(at, TILE), :] for c in range(4)]
            state = over(state, shade(sums, z, looked, scale))
        for k, values in enumerate(state):
            inner_ref[k, pl.ds(at, TILE), :] = values
        return carry

    lax.fori_loop(0, xs // TILE, tile_step, 0)


def edge_kernel(zs, xs, scale, fa_ref, fb_ref, cross_ref, looked_ref, inner_ref, *rest):
    out_refs, (near_ref, rows_ref, image_ref) = rest[:-3], rest[-3:]
    zfirst, zlast, zodd = place_of("gz")
    block = xs + TILE
    tiles = xs // TILE
    lane = lax.broadcasted_iota(jnp.int32, (1, 128), 1)
    for side in range(2):
        first, second = (fa_ref, fb_ref) if side == 0 else (fb_ref, fa_ref)

        def face(at):
            return jnp.where(zodd, first[at * block : at * block + block, :], second[at * block : at * block + block, :])

        strips = face(FACE)
        for j in range(FACE):
            field = max(j - 1, 0)
            layer = j if j < 2 else (1 if side == 0 else 0)
            at_lane = SLOT * layer + slot_of(field)[0]
            halo = pltpu.roll(strips, ((126 if field == 0 else 127) - at_lane) % 128, 1)
            results = along_y(face(j), halo, lane, field == 0)
            for part, result in zip((0, 1, 2) if field == 0 else (2 + field,), results):
                rows_ref[side, layer, part, 0:TILE, :] = result[xs:]
                rows_ref[side, layer, part, TILE:, :] = result
    for side in range(2):
        edge = zfirst if side == 0 else zlast
        for layer in range(2):
            mirrored = 0 if side == 0 else 7
            outer = layer == side
            for t in range(tiles):

                def at(part, off):
                    return rows_ref[side, layer, part, pl.ds(TILE + t + off, TILE, stride=tiles), :]

                rows = slice(t * TILE, t * TILE + TILE)
                for part, result in enumerate(along_x(at, True)):
                    fill = -cross_ref[4 + part, mirrored, rows] if outer else 0.0
                    near_ref[4 + part, 2 * side + layer, rows] = jnp.where(edge, fill, result)
                if not outer:
                    for part, result in enumerate(along_x(at, False)):
                        near_ref[part, 2 * side + layer, rows] = jnp.where(edge, 0.0, result)

    def load(part, z):
        if z < 0:
            return near_ref[part, z + 2]
        if z >= zs:
            return near_ref[part, z - zs + 2]
        return cross_ref[part, z if z < 4 else z - zs + 8]

    def layer_of(z):
        return shade(Sums(load), z, [looked_ref[c, z] for c in range(4)], scale)

    zero = jnp.zeros((xs, 128), jnp.float32)
    state = over(over((zero + 1.0, zero, zero, zero, zero), layer_of(0)), layer_of(1))
    passed = state[0]
    state = (
        passed * inner_ref[0],
        state[1] + passed * inner_ref[1],
        state[2] + passed * inner_ref[2],
        state[3] + passed * inner_ref[3],
        state[4] + inner_ref[4],
    )
    state = over(over(state, layer_of(zs - 2)), layer_of(zs - 1))
    for c in range(4):
        for t in range(tiles):
            image_ref[c, pl.ds(t, TILE, stride=tiles), :] = state[1 + c][t * TILE : t * TILE + TILE]
    if len(out_refs) == 1:
        out_refs[0][...] = image_ref[...]
    else:
        part = xs // len(out_refs)
        for k, ref in enumerate(out_refs):
            ref[...] = image_ref[:, pl.ds(pl.multiple_of((lax.axis_index("gz") ^ k) * part, part), part), :]


def blend_kernel(near_ref, *refs):
    images, out_ref = refs[:-1], refs[-1]
    count = len(images)
    depths = [image[3] for image in images]
    colours = [jnp.zeros_like(depths[0])] * 3
    for k in range(count):
        prior = jnp.zeros_like(depths[0])
        for other in range(count):
            if other != k:
                prior += near_ref[k * count + other] * depths[other]
        through = jnp.exp(-prior)
        colours = [colours[c] + through * images[k][c] for c in range(3)]
    total = functools.reduce(jnp.add, depths)
    out_ref[0], out_ref[1], out_ref[2] = colours
    small = total * horner(EXPM1, total)
    out_ref[3] = jnp.where(total < 0.5, small, 1.0 - jnp.exp(-total))


def call(kernel, out_shape, specs, scratch=(), cost=1.0, name=None, limit=VMEM_LIMIT):
    where = {"s": pltpu.SMEM, "v": pltpu.VMEM, "a": pl.ANY}
    return pl.pallas_call(
        kernel,
        out_shape=out_shape,
        in_specs=[pl.BlockSpec(memory_space=where[s]) for s in specs],
        out_specs=jax.tree.map(lambda _: pl.BlockSpec(memory_space=pltpu.VMEM), out_shape),
        scratch_shapes=list(scratch),
        compiler_params=pltpu.CompilerParams(vmem_limit_bytes=limit),
        cost_estimate=pl.CostEstimate(flops=0, bytes_accessed=int(cost * 3.0e6), transcendentals=0),
        name=name,
    )


def swap_pairs(first, second, axis):
    count = lax.axis_size(axis)
    one = lax.ppermute(first, axis, [(i, i ^ 1) for i in range(count)])
    if count == 2:
        return one, one
    ends = [(0, 0), (count - 1, count - 1)]
    return one, lax.ppermute(second, axis, ends + [(i, i + 1 if i % 2 else i - 1) for i in range(1, count - 1)])


def on_device(fields, material, depth_order, table):
    _, zs, xs, ys = fields.shape
    nx, nz = lax.axis_size("gx"), lax.axis_size("gz")
    block = xs + TILE
    part = xs // nz
    swaps = nz in (2, 4)
    groups = -(-(zs + 1) // GROUP)
    f32 = lambda *shape: jax.ShapeDtypeStruct(shape, jnp.float32)

    def side(even_high):
        return call(functools.partial(rows_kernel, zs, xs, even_high), f32(FACE, zs, ys), "v", name="x_rows")(fields)

    x_a, x_b = swap_pairs(side(True), side(False) if nx > 2 else None, "gx")
    held, ids, main, nearer = call(
        functools.partial(stage_kernel, zs, xs, swaps),
        (
            f32(4, zs, xs, ys),
            jax.ShapeDtypeStruct((zs, xs, ys), jnp.int32),
            f32(groups, xs, 128),
            f32(nz * nz, 1, 128),
        ),
        "saa",
        [pltpu.SemaphoreType.DMA((5,))],
        cost=2.0,
        name="stage",
    )(depth_order, fields, material)
    x_a, x_b, held = lax.optimization_barrier((x_a, x_b, held))

    halo, own = call(
        functools.partial(x_halo_kernel, zs, xs), (f32(4, zs + 1, TILE, ys), f32(groups, block, 128)), "vvvv", name="x_halo"
    )(held, main, x_a, x_b)
    y_a, y_b = swap_pairs(own, own, "gy")
    looked = call(
        functools.partial(lookup_kernel, zs, xs),
        f32(4, zs, xs, ys),
        "vv",
        [pltpu.VMEM((4, 128), jnp.float32)],
        cost=2.0,
        name="lookup",
    )(table, ids)
    y_a, y_b, looked = lax.optimization_barrier((y_a, y_b, looked))

    faces = f32((FACE + 1) * block, ys)
    merged, f_a, f_b = call(
        functools.partial(face_kernel, zs, xs), (f32(groups, block, 128), faces, faces), "vvvvv", name="faces"
    )(held, halo, own, y_a, y_b)
    z_a, z_b = swap_pairs(f_a, f_b, "gz")

    scale = 2.0 / (zs * nz)
    inner, cross = call(
        functools.partial(inner_kernel, zs, xs, scale),
        (f32(5, xs, ys), f32(7, 8, xs, ys)),
        "vvvv",
        [pltpu.VMEM((6, zs * block + TILE, ys), jnp.float32)],
        cost=4.0,
        name="inner",
    )(held, halo, merged, looked)

    images = call(
        functools.partial(edge_kernel, zs, xs, scale),
        [f32(4, part, ys)] * nz if swaps else [f32(4, xs, ys)],
        "vvvvv",
        [
            pltpu.VMEM((7, 4, xs, ys), jnp.float32),
            pltpu.VMEM((2, 2, 6, block + TILE, ys), jnp.float32),
            pltpu.VMEM((4, xs, ys), jnp.float32),
        ],
        name="edges",
    )(z_a, z_b, cross, looked, inner)

    if swaps:
        mine = [images[0]]
        for k in range(1, nz):
            mine.append(lax.ppermute(images[k], "gz", [(i, i ^ k) for i in range(nz)]))
    else:
        stacked = lax.all_to_all(images[0].reshape(4, nz, part, ys), "gz", split_axis=1, concat_axis=1)
        mine = [stacked[:, b] for b in range(nz)]
    return call(blend_kernel, f32(4, part, ys), "v" + "v" * nz, name="blend")(nearer, *mine)


def solution(mesh):
    return jax.shard_map(
        on_device,
        mesh=mesh,
        in_specs=(P(None, "gz", "gx", "gy"), P("gz", "gx", "gy"), P(), P()),
        out_specs=P(None, ("gx", "gz"), "gy"),
        check_vma=False,
    )
```

```python
import functools

import jax
import jax.numpy as jnp
from jax import lax
from jax.experimental import pallas as pl
from jax.experimental.pallas import tpu as pltpu
from jax.sharding import PartitionSpec as P

VMEM_LIMIT = 40 * 1024 * 1024
GROUP = 12
SLOT = 10
TILE = 8
FACE = 5

LOG1P = (
    0.9999995186059567, -0.49996356582563917, 0.33265255844036573, -0.24453388969978707, 0.17659864766821842,
    -0.10679931280022417, 0.043659288844443055, -0.008466410404849948,
)
EXPM1 = (
    1.0, -0.4999995231628418, 0.1666584461927414, -0.04160914570093155, 0.00814302358776331, -0.0010865303920581937,
)


def horner(coefficients, value):
    total = jnp.full_like(value, coefficients[-1])
    for c in coefficients[-2::-1]:
        total = total * value + c
    return total


def place_of(axis):
    at = lax.axis_index(axis)
    return at == 0, at == lax.axis_size(axis) - 1, lax.rem(at, 2) == 1


def rows_kernel(zs, xs, even_high, fields_ref, out_ref):
    high = (lax.rem(lax.axis_index("gx"), 2) == 0) == even_high
    for group in range(FACE):
        field = max(group - 1, 0)
        rows = fields_ref.at[field].reshape(zs * xs, 128)
        low_row = group if group < 2 else 0
        high_row = xs - 2 + group if group < 2 else xs - 1
        out_ref[group] = rows[pl.ds(jnp.where(high, high_row, low_row), zs, stride=xs), :]


def slot_of(field):
    return (0, 4) if field == 0 else (2 + 2 * field, 2)


def pack_strips(load, layers, lane, rows):
    packed = jnp.zeros((rows, 128), jnp.float32)
    for k, z in enumerate(layers):
        for field in range(4):
            first, count = slot_of(field)
            start = SLOT * k + first
            values = pltpu.roll(load(field, z), (start + count // 2) % 128, 1)
            packed = jnp.where((lane >= start) & (lane < start + count), values, packed)
    return packed


def stage_kernel(zs, xs, peers, order_ref, fields_ref, material_ref, held_ref, ids_ref, pack_ref, near_ref, sems):
    copies = [pltpu.make_async_copy(fields_ref.at[f], held_ref.at[f], sems.at[f]) for f in range(4)]
    copies.append(pltpu.make_async_copy(material_ref, ids_ref, sems.at[4]))
    for copy in copies:
        copy.start()
    iz, count = lax.axis_index("gz"), lax.axis_size("gz")
    ranks = [order_ref[iz ^ k if peers else k] for k in range(count)]
    for k in range(count):
        for other in range(count):
            nearer = jnp.where(ranks[other] < ranks[k], 1.0, 0.0)
            near_ref[k * count + other] = jnp.full((1, 128), nearer, jnp.float32)
    for copy in copies:
        copy.wait()
    lane = lax.broadcasted_iota(jnp.int32, (1, 128), 1)
    for group in range(pack_ref.shape[0]):
        layers = range(group * GROUP, min(zs, group * GROUP + GROUP))
        pack_ref[group] = pack_strips(lambda f, z: held_ref[f, z], layers, lane, xs)


def lookup_kernel(zs, xs, table_ref, ids_ref, looked_ref, tables_ref):
    tables_ref[...] = jnp.zeros_like(tables_ref)
    tables_ref[:, 0 : table_ref.shape[1]] = table_ref[...]
    tables = [jnp.broadcast_to(tables_ref[c : c + 1, :], (TILE, 128)) for c in range(4)]
    each = 8
    tiles = xs // TILE

    def step(k, carry):
        for j in range(each):
            z = k * each + j
            for t in range(tiles):
                ids = ids_ref[z, pl.ds(t, TILE, stride=tiles), :]
                for c in range(4):
                    looked_ref[c, z, t * TILE : t * TILE + TILE, :] = jnp.take_along_axis(
                        tables[c], ids, axis=1, mode="promise_in_bounds"
                    )
        return carry

    lax.fori_loop(0, zs // each, step, 0)


def x_halo_kernel(zs, xs, held_ref, main_ref, xa_ref, xb_ref, halo_ref, pack_ref):
    first, last, odd = place_of("gx")
    halo_ref[...] = jnp.zeros_like(halo_ref)
    for field in range(4):
        tiles = halo_ref.at[field].reshape((zs + 1) * TILE, 128)
        own = held_ref.at[field].reshape(zs * xs, 128)
        at = 0 if field == 0 else 1 + field
        below = jnp.where(odd, xa_ref[1 + field], xb_ref[1 + field])
        above = jnp.where(odd, xb_ref[at], xa_ref[at])
        tiles[pl.ds(TILE - 1, zs, stride=TILE), :] = jnp.where(first, 0.0, below)
        tiles[pl.ds(TILE, zs, stride=TILE), :] = jnp.where(last, 0.0, above)
        if field == 0:
            low, high = own[pl.ds(0, zs, stride=xs), :], own[pl.ds(xs - 1, zs, stride=xs), :]
            tiles[pl.ds(TILE - 2, zs, stride=TILE), :] = jnp.where(first, -low, jnp.where(odd, xa_ref[0], xb_ref[0]))
            tiles[pl.ds(TILE + 1, zs, stride=TILE), :] = jnp.where(last, -high, jnp.where(odd, xb_ref[1], xa_ref[1]))
    lane = lax.broadcasted_iota(jnp.int32, (1, 128), 1)
    for group in range(pack_ref.shape[0]):
        layers = range(group * GROUP, min(zs + 1, group * GROUP + GROUP))
        pack_ref[group, 0:TILE] = pack_strips(lambda f, z: halo_ref[f, z], layers, lane, TILE)
        pack_ref[group, TILE:] = main_ref[group]


def face_kernel(zs, xs, held_ref, halo_ref, own_ref, ya_ref, yb_ref, merged_ref, fa_ref, fb_ref):
    yfirst, ylast, yodd = place_of("gy")
    zodd = place_of("gz")[2]
    block = xs + TILE
    lane = lax.broadcasted_iota(jnp.int32, (1, 128), 1)
    place = lax.rem(lane, SLOT)
    from_left = (place < 2) | ((place >= 4) & (lax.rem(place, 2) == 0))
    for group in range(own_ref.shape[0]):
        own = own_ref[group]
        fill_left = jnp.where(place == 0, -pltpu.roll(own, 126, 1), 0.0)
        fill_right = jnp.where(place == 3, -pltpu.roll(own, 2, 1), 0.0)
        first, second = ya_ref[group], yb_ref[group]
        left = jnp.where(yfirst, fill_left, jnp.where(yodd, first, second))
        right = jnp.where(ylast, fill_right, jnp.where(yodd, second, first))
        merged_ref[group] = jnp.where(from_left, left, right)

    upper = lax.broadcasted_iota(jnp.int32, (TILE, 1), 0) < TILE // 2

    def strips(z, lanes_from):
        group, k = divmod(z, GROUP)
        here = pltpu.roll(merged_ref[group], (lanes_from - SLOT * k) % 128, 1)
        group, k = divmod(z + 1, GROUP)
        after = pltpu.roll(merged_ref[group, 0:TILE], (lanes_from - SLOT * k) % 128, 1)
        return here[TILE:], jnp.where(upper, after, here[0:TILE])

    def put(at, low, high):
        for out_ref, swapped in ((fa_ref, False), (fb_ref, True)):
            for (start, count), a, b in zip(((0, xs), (xs, TILE)), low, high):
                out_ref[at * block + start : at * block + start + count, :] = jnp.where(zodd != swapped, a, b)

    def layer(field, z):
        return held_ref[field, z], jnp.where(upper, halo_ref[field, z + 1], halo_ref[field, z])

    for j in range(FACE):
        field = max(j - 1, 0)
        put(j, layer(field, j if j < 2 else 0), layer(field, zs - 2 + j if j < 2 else zs - 1))

    def both(z):
        return [jnp.where(lane < SLOT, a, b) for a, b in zip(strips(z, 0), strips(z + 1, SLOT))]

    put(FACE, both(0), both(zs - 2))


def along_y(values, halo, lane, density):
    def shifted(off):
        mixed = jnp.where(lane >= 128 - off if off > 0 else lane < -off, halo, values)
        return pltpu.roll(mixed, off % 128, 1)

    m1, p1 = shifted(1), shifted(-1)
    near = m1 + p1
    blur = near + 2.0 * values
    if not density:
        return (blur,)
    m2, p2 = shifted(2), shifted(-2)
    return blur, (m2 + p2) + 4.0 * near + 6.0 * values, 2.0 * (p2 - m2) + 4.0 * (p1 - m1)


def along_x(at, density):
    fields = [at(part, -1) + at(part, 1) + 2.0 * at(part, 0) for part in ((0, 3, 4, 5) if not density else ())]
    if not density:
        return fields
    a, b, c, d, e = (at(1, off) for off in (-2, -1, 0, 1, 2))
    blurred, sloped = (a + e) + 4.0 * (b + d) + 6.0 * c, 2.0 * (e - a) + 4.0 * (d - b)
    a, b, c, d, e = (at(2, off) for off in (-2, -1, 0, 1, 2))
    return [blurred, sloped, (a + e) + 4.0 * (b + d) + 6.0 * c]


class Sums:
    def __init__(self, load):
        self.load, self.made = load, {}

    def pair(self, part, z, level):
        if level == 0:
            key, make = (part, z, 0), lambda: self.load(part, z)
        else:
            key, make = (part, z, level), lambda: self.pair(part, z, level - 1) + self.pair(part, z + 1, level - 1)
        if key not in self.made:
            self.made[key] = make()
        return self.made[key]

    def blur(self, part, z):
        return self.pair(part, z - 1, 2)

    def blur2(self, part, z):
        return self.pair(part, z - 2, 4)

    def slope(self, part, z):
        return 2.0 * (self.pair(part, z, 2) - self.pair(part, z - 2, 2))


def shade(sums, z, looked, scale):
    unit = 1.0 / 4096.0
    grad_z = sums.slope(4, z)
    grad_x = sums.blur2(5, z)
    grad_y = sums.blur2(6, z)
    facing = jnp.abs((0.8 * unit) * (grad_z + grad_y) + (0.4 * unit) * grad_x)
    square = grad_z * grad_z + grad_x * grad_x + grad_y * grad_y
    shading = 0.3 + facing * lax.rsqrt(square * (unit * unit) + 0.0025)
    density = (3.0 / 64.0) * sums.blur(0, z)
    t = jnp.exp(-jnp.abs(density))
    soft = jnp.maximum(density, 0.0) + t * horner(LOG1P, t)
    extinct = looked[3] * (soft * scale)
    fade = extinct * horner(EXPM1, extinct)
    colours = [(looked[c] * shading) * (1.0 + 0.5 * jnp.tanh((1.0 / 64.0) * sums.blur(1 + c, z))) for c in range(3)]
    return extinct, fade, colours


def over(state, layer):
    passed, red, green, blue, depth = state
    extinct, fade, colours = layer
    weight = passed * fade
    return (
        passed - weight,
        red + weight * colours[0],
        green + weight * colours[1],
        blue + weight * colours[2],
        depth + extinct,
    )


def inner_kernel(zs, xs, scale, held_ref, halo_ref, merged_ref, looked_ref, inner_ref, cross_ref, rows_ref):
    block = xs + TILE
    lane = lax.broadcasted_iota(jnp.int32, (1, 128), 1)

    def y_step(z, strips, k):
        for field in range(4):
            own = (126 if field == 0 else 127) - slot_of(field)[0]
            near = pltpu.roll(strips, (own - k * SLOT) % 128, 1)
            pieces = [(halo_ref[field, z], near[0:TILE], 0)]
            if strips.shape[0] > TILE:
                pieces.append((held_ref[field, z], near[TILE:], TILE))
            for values, halo, at in pieces:
                results = along_y(values, halo, lane, field == 0)
                for part, result in zip((0, 1, 2) if field == 0 else (2 + field,), results):
                    rows_ref[part, pl.ds(pl.multiple_of(z * block + at, TILE), values.shape[0]), :] = result

    whole = zs // GROUP

    def group_step(group, carry):
        for k in range(GROUP):
            y_step(group * GROUP + k, merged_ref[group], k)
        return carry

    lax.fori_loop(0, whole, group_step, 0)
    for z in range(whole * GROUP, zs + 1):
        group, k = divmod(z, GROUP)
        y_step(z, merged_ref[group] if z < zs else merged_ref[group, 0:TILE], k)

    tiles = xs // TILE

    def tile_step(tile, carry):
        at = pl.multiple_of(tile * TILE, TILE)
        crossed = {}

        def load(part, z):
            if z not in crossed:
                rows = lambda part, off: rows_ref[part, pl.ds(tile + (z * block + TILE + off), TILE, stride=tiles), :]
                crossed[z] = along_x(rows, False) + along_x(rows, True)
                if z < 4 or z >= zs - 4:
                    for k, values in enumerate(crossed[z]):
                        cross_ref[k, z if z < 4 else z - zs + 8, pl.ds(at, TILE), :] = values
            return crossed[z][part]

        load(0, 0)
        load(0, zs - 1)
        sums = Sums(load)
        zero = jnp.zeros((TILE, 128), jnp.float32)
        state = (zero + 1.0, zero, zero, zero, zero)
        for z in range(2, zs - 2):
            looked = [looked_ref[c, z, pl.ds(at, TILE), :] for c in range(4)]
            state = over(state, shade(sums, z, looked, scale))
        for k, values in enumerate(state):
            inner_ref[k, pl.ds(at, TILE), :] = values
        return carry

    lax.fori_loop(0, xs // TILE, tile_step, 0)


def edge_kernel(zs, xs, scale, fa_ref, fb_ref, cross_ref, looked_ref, inner_ref, *rest):
    out_refs, (near_ref, rows_ref, image_ref) = rest[:-3], rest[-3:]
    zfirst, zlast, zodd = place_of("gz")
    block = xs + TILE
    tiles = xs // TILE
    lane = lax.broadcasted_iota(jnp.int32, (1, 128), 1)
    for side in range(2):
        first, second = (fa_ref, fb_ref) if side == 0 else (fb_ref, fa_ref)

        def face(at):
            return jnp.where(zodd, first[at * block : at * block + block, :], second[at * block : at * block + block, :])

        strips = face(FACE)
        for j in range(FACE):
            field = max(j - 1, 0)
            layer = j if j < 2 else (1 if side == 0 else 0)
            at_lane = SLOT * layer + slot_of(field)[0]
            halo = pltpu.roll(strips, ((126 if field == 0 else 127) - at_lane) % 128, 1)
            results = along_y(face(j), halo, lane, field == 0)
            for part, result in zip((0, 1, 2) if field == 0 else (2 + field,), results):
                rows_ref[side, layer, part, 0:TILE, :] = result[xs:]
                rows_ref[side, layer, part, TILE:, :] = result
    for side in range(2):
        edge = zfirst if side == 0 else zlast
        for layer in range(2):
            mirrored = 0 if side == 0 else 7
            outer = layer == side
            for t in range(tiles):

                def at(part, off):
                    return rows_ref[side, layer, part, pl.ds(TILE + t + off, TILE, stride=tiles), :]

                rows = slice(t * TILE, t * TILE + TILE)
                for part, result in enumerate(along_x(at, True)):
                    fill = -cross_ref[4 + part, mirrored, rows] if outer else 0.0
                    near_ref[4 + part, 2 * side + layer, rows] = jnp.where(edge, fill, result)
                if not outer:
                    for part, result in enumerate(along_x(at, False)):
                        near_ref[part, 2 * side + layer, rows] = jnp.where(edge, 0.0, result)

    def load(part, z):
        if z < 0:
            return near_ref[part, z + 2]
        if z >= zs:
            return near_ref[part, z - zs + 2]
        return cross_ref[part, z if z < 4 else z - zs + 8]

    def layer_of(z):
        return shade(Sums(load), z, [looked_ref[c, z] for c in range(4)], scale)

    zero = jnp.zeros((xs, 128), jnp.float32)
    state = over(over((zero + 1.0, zero, zero, zero, zero), layer_of(0)), layer_of(1))
    passed = state[0]
    state = (
        passed * inner_ref[0],
        state[1] + passed * inner_ref[1],
        state[2] + passed * inner_ref[2],
        state[3] + passed * inner_ref[3],
        state[4] + inner_ref[4],
    )
    state = over(over(state, layer_of(zs - 2)), layer_of(zs - 1))
    for c in range(4):
        for t in range(tiles):
            image_ref[c, pl.ds(t, TILE, stride=tiles), :] = state[1 + c][t * TILE : t * TILE + TILE]
    if len(out_refs) == 1:
        out_refs[0][...] = image_ref[...]
    else:
        part = xs // len(out_refs)
        for k, ref in enumerate(out_refs):
            ref[...] = image_ref[:, pl.ds(pl.multiple_of((lax.axis_index("gz") ^ k) * part, part), part), :]


def blend_kernel(near_ref, *refs):
    images, out_ref = refs[:-1], refs[-1]
    count = len(images)
    depths = [image[3] for image in images]
    colours = [jnp.zeros_like(depths[0])] * 3
    for k in range(count):
        prior = jnp.zeros_like(depths[0])
        for other in range(count):
            if other != k:
                prior += near_ref[k * count + other] * depths[other]
        through = jnp.exp(-prior)
        colours = [colours[c] + through * images[k][c] for c in range(3)]
    total = functools.reduce(jnp.add, depths)
    out_ref[0], out_ref[1], out_ref[2] = colours
    small = total * horner(EXPM1, total)
    out_ref[3] = jnp.where(total < 0.5, small, 1.0 - jnp.exp(-total))


def call(kernel, out_shape, specs, scratch=(), cost=1.0, name=None, limit=VMEM_LIMIT):
    where = {"s": pltpu.SMEM, "v": pltpu.VMEM, "a": pl.ANY}
    return pl.pallas_call(
        kernel,
        out_shape=out_shape,
        in_specs=[pl.BlockSpec(memory_space=where[s]) for s in specs],
        out_specs=jax.tree.map(lambda _: pl.BlockSpec(memory_space=pltpu.VMEM), out_shape),
        scratch_shapes=list(scratch),
        compiler_params=pltpu.CompilerParams(vmem_limit_bytes=limit),
        cost_estimate=pl.CostEstimate(flops=0, bytes_accessed=int(cost * 3.0e6), transcendentals=0),
        name=name,
    )


def swap_pairs(first, second, axis):
    count = lax.axis_size(axis)
    one = lax.ppermute(first, axis, [(i, i ^ 1) for i in range(count)])
    if count == 2:
        return one, one
    ends = [(0, 0), (count - 1, count - 1)]
    return one, lax.ppermute(second, axis, ends + [(i, i + 1 if i % 2 else i - 1) for i in range(1, count - 1)])


def on_device(fields, material, depth_order, table):
    _, zs, xs, ys = fields.shape
    nx, nz = lax.axis_size("gx"), lax.axis_size("gz")
    block = xs + TILE
    part = xs // nz
    swaps = nz in (2, 4)
    groups = -(-(zs + 1) // GROUP)
    f32 = lambda *shape: jax.ShapeDtypeStruct(shape, jnp.float32)

    def side(even_high):
        return call(functools.partial(rows_kernel, zs, xs, even_high), f32(FACE, zs, ys), "v", name="x_rows")(fields)

    x_a, x_b = swap_pairs(side(True), side(False) if nx > 2 else None, "gx")
    held, ids, main, nearer = call(
        functools.partial(stage_kernel, zs, xs, swaps),
        (
            f32(4, zs, xs, ys),
            jax.ShapeDtypeStruct((zs, xs, ys), jnp.int32),
            f32(groups, xs, 128),
            f32(nz * nz, 1, 128),
        ),
        "saa",
        [pltpu.SemaphoreType.DMA((5,))],
        cost=2.0,
        name="stage",
    )(depth_order, fields, material)
    x_a, x_b, held = lax.optimization_barrier((x_a, x_b, held))

    halo, own = call(
        functools.partial(x_halo_kernel, zs, xs), (f32(4, zs + 1, TILE, ys), f32(groups, block, 128)), "vvvv", name="x_halo"
    )(held, main, x_a, x_b)
    y_a, y_b = swap_pairs(own, own, "gy")
    looked = call(
        functools.partial(lookup_kernel, zs, xs),
        f32(4, zs, xs, ys),
        "vv",
        [pltpu.VMEM((4, 128), jnp.float32)],
        cost=2.0,
        name="lookup",
    )(table, ids)
    y_a, y_b, looked = lax.optimization_barrier((y_a, y_b, looked))

    faces = f32((FACE + 1) * block, ys)
    merged, f_a, f_b = call(
        functools.partial(face_kernel, zs, xs), (f32(groups, block, 128), faces, faces), "vvvvv", name="faces"
    )(held, halo, own, y_a, y_b)
    z_a, z_b = swap_pairs(f_a, f_b, "gz")

    scale = 2.0 / (zs * nz)
    inner, cross = call(
        functools.partial(inner_kernel, zs, xs, scale),
        (f32(5, xs, ys), f32(7, 8, xs, ys)),
        "vvvv",
        [pltpu.VMEM((6, zs * block + TILE, ys), jnp.float32)],
        cost=4.0,
        name="inner",
    )(held, halo, merged, looked)

    images = call(
        functools.partial(edge_kernel, zs, xs, scale),
        [f32(4, part, ys)] * nz if swaps else [f32(4, xs, ys)],
        "vvvvv",
        [
            pltpu.VMEM((7, 4, xs, ys), jnp.float32),
            pltpu.VMEM((2, 2, 6, block + TILE, ys), jnp.float32),
            pltpu.VMEM((4, xs, ys), jnp.float32),
        ],
        name="edges",
    )(z_a, z_b, cross, looked, inner)

    if swaps:
        mine = [images[0]]
        for k in range(1, nz):
            mine.append(lax.ppermute(images[k], "gz", [(i, i ^ k) for i in range(nz)]))
    else:
        stacked = lax.all_to_all(images[0].reshape(4, nz, part, ys), "gz", split_axis=1, concat_axis=1)
        mine = [stacked[:, b] for b in range(nz)]
    return call(blend_kernel, f32(4, part, ys), "v" + "v" * nz, name="blend")(nearer, *mine)


def solution(mesh):
    return jax.shard_map(
        on_device,
        mesh=mesh,
        in_specs=(P(None, "gz", "gx", "gy"), P("gz", "gx", "gy"), P(), P()),
        out_specs=P(None, ("gx", "gz"), "gy"),
        check_vma=False,
    )
```

```python
import functools

import jax
import jax.numpy as jnp
import ml_dtypes
import numpy as np
from jax import lax
from jax.experimental import pallas as pl
from jax.experimental.pallas import tpu as pltpu
from jax.sharding import PartitionSpec as P

VMEM_LIMIT = 40 * 1024 * 1024
GROUP = 12
SLOT = 10
TILE = 8
FACE = 5

LOG1P = (
    0.9999995186059567, -0.49996356582563917, 0.33265255844036573, -0.24453388969978707, 0.17659864766821842,
    -0.10679931280022417, 0.043659288844443055, -0.008466410404849948,
)
EXPM1 = (
    1.0, -0.4999995231628418, 0.1666584461927414, -0.04160914570093155, 0.00814302358776331, -0.0010865303920581937,
)


def polynomial(coefficients, value):
    terms = list(coefficients)
    power = value
    while len(terms) > 1:
        paired = [terms[k] + terms[k + 1] * power for k in range(0, len(terms) - 1, 2)]
        terms = paired + ([terms[-1]] if len(terms) % 2 else [])
        power = power * power if len(terms) > 1 else power
    return terms[0]


def band_matrices(ysize):
    stencils = ({-1: 1, 0: 2, 1: 1}, {-2: 1, -1: 4, 0: 6, 1: 4, 2: 1}, {-2: -2, -1: -4, 1: 4, 2: 2})
    cells = np.zeros((ysize, 3 * ysize), np.float32)
    strips = np.zeros((128, 6 * ysize), np.float32)
    for block, (taps, field) in enumerate([(t, 0) for t in stencils] + [(stencils[0], f) for f in (1, 2, 3)]):
        first = slot_of(field)[0]
        outside = {-2: 0, -1: 1, ysize: 2, ysize + 1: 3} if field == 0 else {-1: first, ysize: first + 1}
        for out in range(ysize):
            for off, weight in taps.items():
                at = out + off
                if not 0 <= at < ysize:
                    strips[outside[at], block * ysize + out] = weight
                elif block < 3:
                    cells[at, block * ysize + out] = weight
    return [np.concatenate([m, m], axis=0).astype(ml_dtypes.bfloat16) for m in (cells, strips)]


def halves(values):
    high = values.astype(jnp.bfloat16)
    low = (values - high.astype(jnp.float32)).astype(jnp.bfloat16)
    return jnp.concatenate([high, low], axis=1)


def place_of(axis):
    at = lax.axis_index(axis)
    return at == 0, at == lax.axis_size(axis) - 1, lax.rem(at, 2) == 1


def rows_kernel(zs, xs, even_high, fields_ref, out_ref):
    high = (lax.rem(lax.axis_index("gx"), 2) == 0) == even_high
    for group in range(FACE):
        field = max(group - 1, 0)
        rows = fields_ref.at[field].reshape(zs * xs, 128)
        low_row = group if group < 2 else 0
        high_row = xs - 2 + group if group < 2 else xs - 1
        out_ref[group] = rows[pl.ds(jnp.where(high, high_row, low_row), zs, stride=xs), :]


def slot_of(field):
    return (0, 4) if field == 0 else (2 + 2 * field, 2)


def pack_strips(load, layers, lane, rows):
    packed = jnp.zeros((rows, 128), jnp.float32)
    for k, z in enumerate(layers):
        for field in range(4):
            first, count = slot_of(field)
            start = SLOT * k + first
            values = pltpu.roll(load(field, z), (start + count // 2) % 128, 1)
            packed = jnp.where((lane >= start) & (lane < start + count), values, packed)
    return packed


def stage_kernel(zs, xs, peers, order_ref, fields_ref, material_ref, held_ref, ids_ref, pack_ref, near_ref, sems):
    copies = [pltpu.make_async_copy(fields_ref.at[f], held_ref.at[f], sems.at[f]) for f in range(4)]
    copies.append(pltpu.make_async_copy(material_ref, ids_ref, sems.at[4]))
    for copy in copies:
        copy.start()
    iz, count = lax.axis_index("gz"), lax.axis_size("gz")
    ranks = [order_ref[iz ^ k if peers else k] for k in range(count)]
    for k in range(count):
        for other in range(count):
            nearer = jnp.where(ranks[other] < ranks[k], 1.0, 0.0)
            near_ref[k * count + other] = jnp.full((1, 128), nearer, jnp.float32)
    for copy in copies:
        copy.wait()
    lane = lax.broadcasted_iota(jnp.int32, (1, 128), 1)
    for group in range(pack_ref.shape[0]):
        layers = range(group * GROUP, min(zs, group * GROUP + GROUP))
        pack_ref[group] = pack_strips(lambda f, z: held_ref[f, z], layers, lane, xs)


def lookup_kernel(zs, xs, table_ref, ids_ref, looked_ref, tables_ref):
    tables_ref[...] = jnp.zeros_like(tables_ref)
    tables_ref[:, 0 : table_ref.shape[1]] = table_ref[...]
    tables = [jnp.broadcast_to(tables_ref[c : c + 1, :], (TILE, 128)) for c in range(4)]
    each = 8
    tiles = xs // TILE

    def step(k, carry):
        for j in range(each):
            z = k * each + j
            for t in range(tiles):
                ids = ids_ref[z, pl.ds(t, TILE, stride=tiles), :]
                for c in range(4):
                    looked_ref[c, z, t * TILE : t * TILE + TILE, :] = jnp.take_along_axis(
                        tables[c], ids, axis=1, mode="promise_in_bounds"
                    )
        return carry

    lax.fori_loop(0, zs // each, step, 0)


def x_halo_kernel(zs, xs, held_ref, main_ref, xa_ref, xb_ref, halo_ref, pack_ref):
    first, last, odd = place_of("gx")
    halo_ref[...] = jnp.zeros_like(halo_ref)
    for field in range(4):
        tiles = halo_ref.at[field].reshape((zs + 2) * TILE, 128)
        own = held_ref.at[field].reshape(zs * xs, 128)
        at = 0 if field == 0 else 1 + field
        below = jnp.where(odd, xa_ref[1 + field], xb_ref[1 + field])
        above = jnp.where(odd, xb_ref[at], xa_ref[at])
        tiles[pl.ds(TILE - 1, zs, stride=TILE), :] = jnp.where(first, 0.0, below)
        tiles[pl.ds(TILE, zs, stride=TILE), :] = jnp.where(last, 0.0, above)
        if field == 0:
            low, high = own[pl.ds(0, zs, stride=xs), :], own[pl.ds(xs - 1, zs, stride=xs), :]
            tiles[pl.ds(TILE - 2, zs, stride=TILE), :] = jnp.where(first, -low, jnp.where(odd, xa_ref[0], xb_ref[0]))
            tiles[pl.ds(TILE + 1, zs, stride=TILE), :] = jnp.where(last, -high, jnp.where(odd, xb_ref[1], xa_ref[1]))
    lane = lax.broadcasted_iota(jnp.int32, (1, 128), 1)
    for group in range(pack_ref.shape[0]):
        layers = range(group * GROUP, min(zs + 1, group * GROUP + GROUP))
        pack_ref[group, 0:TILE] = pack_strips(lambda f, z: halo_ref[f, z], layers, lane, TILE)
        pack_ref[group, TILE:] = main_ref[group]


def face_kernel(zs, xs, held_ref, halo_ref, own_ref, ya_ref, yb_ref, merged_ref, fa_ref, fb_ref):
    yfirst, ylast, yodd = place_of("gy")
    zodd = place_of("gz")[2]
    block = xs + TILE
    lane = lax.broadcasted_iota(jnp.int32, (1, 128), 1)
    place = lax.rem(lane, SLOT)
    from_left = (place < 2) | ((place >= 4) & (lax.rem(place, 2) == 0))
    for group in range(own_ref.shape[0]):
        own = own_ref[group]
        fill_left = jnp.where(place == 0, -pltpu.roll(own, 126, 1), 0.0)
        fill_right = jnp.where(place == 3, -pltpu.roll(own, 2, 1), 0.0)
        first, second = ya_ref[group], yb_ref[group]
        left = jnp.where(yfirst, fill_left, jnp.where(yodd, first, second))
        right = jnp.where(ylast, fill_right, jnp.where(yodd, second, first))
        merged_ref[group] = jnp.where(from_left, left, right)

    upper = lax.broadcasted_iota(jnp.int32, (TILE, 1), 0) < TILE // 2

    def strips(z, lanes_from):
        group, k = divmod(z, GROUP)
        here = pltpu.roll(merged_ref[group], (lanes_from - SLOT * k) % 128, 1)
        group, k = divmod(z + 1, GROUP)
        after = pltpu.roll(merged_ref[group, 0:TILE], (lanes_from - SLOT * k) % 128, 1)
        return here[TILE:], jnp.where(upper, after, here[0:TILE])

    def put(at, low, high):
        for out_ref, swapped in ((fa_ref, False), (fb_ref, True)):
            for (start, count), a, b in zip(((0, xs), (xs, TILE)), low, high):
                out_ref[at * block + start : at * block + start + count, :] = jnp.where(zodd != swapped, a, b)

    def layer(field, z):
        return held_ref[field, z], jnp.where(upper, halo_ref[field, z + 1], halo_ref[field, z])

    for j in range(FACE):
        field = max(j - 1, 0)
        put(j, layer(field, j if j < 2 else 0), layer(field, zs - 2 + j if j < 2 else zs - 1))

    def both(z):
        return [jnp.where(lane < SLOT, a, b) for a, b in zip(strips(z, 0), strips(z + 1, SLOT))]

    put(FACE, both(0), both(zs - 2))


def along_y(values, halo, lane, density):
    def shifted(off):
        mixed = jnp.where(lane >= 128 - off if off > 0 else lane < -off, halo, values)
        return pltpu.roll(mixed, off % 128, 1)

    m1, p1 = shifted(1), shifted(-1)
    near = m1 + p1
    blur = near + 2.0 * values
    if not density:
        return (blur,)
    m2, p2 = shifted(2), shifted(-2)
    return blur, (m2 + p2) + 4.0 * near + 6.0 * values, 2.0 * (p2 - m2) + 4.0 * (p1 - m1)


def along_x(at, density):
    fields = [at(part, -1) + at(part, 1) + 2.0 * at(part, 0) for part in ((0, 3, 4, 5) if not density else ())]
    if not density:
        return fields
    a, b, c, d, e = (at(1, off) for off in (-2, -1, 0, 1, 2))
    blurred, sloped = (a + e) + 4.0 * (b + d) + 6.0 * c, 2.0 * (e - a) + 4.0 * (d - b)
    a, b, c, d, e = (at(2, off) for off in (-2, -1, 0, 1, 2))
    return [blurred, sloped, (a + e) + 4.0 * (b + d) + 6.0 * c]


class Sums:
    def __init__(self, load):
        self.load, self.made = load, {}

    def pair(self, part, z, level):
        if level == 0:
            key, make = (part, z, 0), lambda: self.load(part, z)
        else:
            key, make = (part, z, level), lambda: self.pair(part, z, level - 1) + self.pair(part, z + 1, level - 1)
        if key not in self.made:
            self.made[key] = make()
        return self.made[key]

    def blur(self, part, z):
        return self.pair(part, z - 1, 2)

    def blur2(self, part, z):
        return self.pair(part, z - 2, 4)

    def slope(self, part, z):
        return 2.0 * (self.pair(part, z, 2) - self.pair(part, z - 2, 2))


def shade(sums, z, looked, scale):
    unit = 1.0 / 4096.0
    grad_z = sums.slope(4, z)
    grad_x = sums.blur2(5, z)
    grad_y = sums.blur2(6, z)
    facing = jnp.abs((0.8 * unit) * (grad_z + grad_y) + (0.4 * unit) * grad_x)
    square = grad_z * grad_z + grad_x * grad_x + grad_y * grad_y
    shading = 0.3 + facing * lax.rsqrt(square * (unit * unit) + 0.0025)
    density = (3.0 / 64.0) * sums.blur(0, z)
    t = jnp.exp(-jnp.abs(density))
    soft = jnp.maximum(density, 0.0) + t * polynomial(LOG1P, t)
    extinct = looked[3] * (soft * scale)
    fade = extinct * polynomial(EXPM1, extinct)
    colours = [(looked[c] * shading) * (1.0 + 0.5 * jnp.tanh((1.0 / 64.0) * sums.blur(1 + c, z))) for c in range(3)]
    return extinct, fade, colours


def over(state, layer):
    passed, red, green, blue, depth = state
    extinct, fade, colours = layer
    weight = passed * fade
    return (
        passed - weight,
        red + weight * colours[0],
        green + weight * colours[1],
        blue + weight * colours[2],
        depth + extinct,
    )


def inner_kernel(zs, xs, scale, held_ref, halo_ref, merged_ref, looked_ref, cell_ref, strip_ref, inner_ref, cross_ref, rows_ref):
    block = xs + TILE
    tiles = xs // TILE
    each = 8

    def along_y_of(load, strips, put):
        edges = jnp.dot(halves(strips), strip_ref[...], preferred_element_type=jnp.float32)
        cells = jnp.dot(halves(load(0)), cell_ref[...], preferred_element_type=jnp.float32)
        for part in range(3):
            put(part, cells[:, 128 * part : 128 * part + 128] + edges[:, 128 * part : 128 * part + 128])
        for field in (1, 2, 3):
            cells = jnp.dot(halves(load(field)), cell_ref[:, 0:128], preferred_element_type=jnp.float32)
            part = 2 + field
            put(part, cells + edges[:, 128 * part : 128 * part + 128])

    def rolled(group, k, rows):
        return pltpu.roll(merged_ref[group, rows], lax.rem(128 - SLOT * k, 128), 1)

    def y_step(step, carry):
        first = step * each
        strips = []
        for j in range(each):
            group = lax.div(first + j, GROUP)
            strips.append(rolled(group, first + j - group * GROUP, slice(TILE, block)))

        def put(part, values):
            for j in range(each):
                base = pl.multiple_of((first + j) * block + TILE, TILE)
                rows_ref[part, pl.ds(base, xs), :] = values[j * xs : j * xs + xs]

        along_y_of(
            lambda field: held_ref[field, pl.ds(first, each)].reshape(each * xs, 128), jnp.concatenate(strips, axis=0), put
        )
        return carry

    lax.fori_loop(0, zs // each, y_step, 0)
    strips = [rolled(z // GROUP, z % GROUP, slice(0, TILE)) for z in range(zs + 1)]
    strips.append(jnp.zeros((TILE, 128), jnp.float32))

    def put_halo(part, values):
        for z in range(zs + 1):
            rows_ref[part, z * block : z * block + TILE, :] = values[z * TILE : z * TILE + TILE]

    along_y_of(
        lambda field: halo_ref[field].reshape((zs + 2) * TILE, 128), jnp.concatenate(strips, axis=0), put_halo
    )

    def x_step(step, carry):
        for j in range(2):
            z = 2 * step + j
            for t in range(tiles):

                def at(part, off):
                    return rows_ref[part, pl.ds(z * block + (TILE + t + off), TILE, stride=tiles), :]

                for part, values in enumerate(along_x(at, False) + along_x(at, True)):
                    cross_ref[part, z, t * TILE : t * TILE + TILE, :] = values
        return carry

    lax.fori_loop(0, zs // 2, x_step, 0)

    def z_step(step, state):
        sums = Sums(lambda part, z: cross_ref[part, 2 * step + z])
        for j in range(2):
            z = 2 + 2 * step + j
            looked = [looked_ref[c, z] for c in range(4)]
            state = over(state, shade(sums, 2 + j, looked, scale))
        return state

    zero = jnp.zeros((xs, 128), jnp.float32)
    state = lax.fori_loop(0, (zs - 4) // 2, z_step, (zero + 1.0, zero, zero, zero, zero))
    for k, values in enumerate(state):
        inner_ref[k] = values


def edge_kernel(zs, xs, scale, fa_ref, fb_ref, cross_ref, looked_ref, inner_ref, *rest):
    out_refs, (near_ref, rows_ref, image_ref) = rest[:-3], rest[-3:]
    zfirst, zlast, zodd = place_of("gz")
    block = xs + TILE
    tiles = xs // TILE
    lane = lax.broadcasted_iota(jnp.int32, (1, 128), 1)
    for side in range(2):
        first, second = (fa_ref, fb_ref) if side == 0 else (fb_ref, fa_ref)

        def face(at):
            return jnp.where(zodd, first[at * block : at * block + block, :], second[at * block : at * block + block, :])

        strips = face(FACE)
        for j in range(FACE):
            field = max(j - 1, 0)
            layer = j if j < 2 else (1 if side == 0 else 0)
            at_lane = SLOT * layer + slot_of(field)[0]
            halo = pltpu.roll(strips, ((126 if field == 0 else 127) - at_lane) % 128, 1)
            results = along_y(face(j), halo, lane, field == 0)
            for part, result in zip((0, 1, 2) if field == 0 else (2 + field,), results):
                rows_ref[side, layer, part, 0:TILE, :] = result[xs:]
                rows_ref[side, layer, part, TILE:, :] = result
    for side in range(2):
        edge = zfirst if side == 0 else zlast
        for layer in range(2):
            mirrored = 0 if side == 0 else zs - 1
            outer = layer == side
            for t in range(tiles):

                def at(part, off):
                    return rows_ref[side, layer, part, pl.ds(TILE + t + off, TILE, stride=tiles), :]

                rows = slice(t * TILE, t * TILE + TILE)
                for part, result in enumerate(along_x(at, True)):
                    fill = -cross_ref[4 + part, mirrored, rows] if outer else 0.0
                    near_ref[4 + part, 2 * side + layer, rows] = jnp.where(edge, fill, result)
                if not outer:
                    for part, result in enumerate(along_x(at, False)):
                        near_ref[part, 2 * side + layer, rows] = jnp.where(edge, 0.0, result)

    def load(part, z):
        if z < 0:
            return near_ref[part, z + 2]
        if z >= zs:
            return near_ref[part, z - zs + 2]
        return cross_ref[part, z]

    def layer_of(z):
        return shade(Sums(load), z, [looked_ref[c, z] for c in range(4)], scale)

    zero = jnp.zeros((xs, 128), jnp.float32)
    state = over(over((zero + 1.0, zero, zero, zero, zero), layer_of(0)), layer_of(1))
    passed = state[0]
    state = (
        passed * inner_ref[0],
        state[1] + passed * inner_ref[1],
        state[2] + passed * inner_ref[2],
        state[3] + passed * inner_ref[3],
        state[4] + inner_ref[4],
    )
    state = over(over(state, layer_of(zs - 2)), layer_of(zs - 1))
    for c in range(4):
        for t in range(tiles):
            image_ref[c, pl.ds(t, TILE, stride=tiles), :] = state[1 + c][t * TILE : t * TILE + TILE]
    if len(out_refs) == 1:
        out_refs[0][...] = image_ref[...]
    else:
        part = xs // len(out_refs)
        for k, ref in enumerate(out_refs):
            ref[...] = image_ref[:, pl.ds(pl.multiple_of((lax.axis_index("gz") ^ k) * part, part), part), :]


def blend_kernel(near_ref, *refs):
    images, out_ref = refs[:-1], refs[-1]
    count = len(images)
    depths = [image[3] for image in images]
    colours = [jnp.zeros_like(depths[0])] * 3
    for k in range(count):
        prior = jnp.zeros_like(depths[0])
        for other in range(count):
            if other != k:
                prior += near_ref[k * count + other] * depths[other]
        through = jnp.exp(-prior)
        colours = [colours[c] + through * images[k][c] for c in range(3)]
    total = functools.reduce(jnp.add, depths)
    out_ref[0], out_ref[1], out_ref[2] = colours
    small = total * polynomial(EXPM1, total)
    out_ref[3] = jnp.where(total < 0.5, small, 1.0 - jnp.exp(-total))


def call(kernel, out_shape, specs, scratch=(), cost=1.0, name=None, limit=VMEM_LIMIT):
    where = {"s": pltpu.SMEM, "v": pltpu.VMEM, "a": pl.ANY}
    return pl.pallas_call(
        kernel,
        out_shape=out_shape,
        in_specs=[pl.BlockSpec(memory_space=where[s]) for s in specs],
        out_specs=jax.tree.map(lambda _: pl.BlockSpec(memory_space=pltpu.VMEM), out_shape),
        scratch_shapes=list(scratch),
        compiler_params=pltpu.CompilerParams(vmem_limit_bytes=limit),
        cost_estimate=pl.CostEstimate(flops=0, bytes_accessed=int(cost * 3.0e6), transcendentals=0),
        name=name,
    )


def swap_pairs(first, second, axis):
    count = lax.axis_size(axis)
    one = lax.ppermute(first, axis, [(i, i ^ 1) for i in range(count)])
    if count == 2:
        return one, one
    ends = [(0, 0), (count - 1, count - 1)]
    return one, lax.ppermute(second, axis, ends + [(i, i + 1 if i % 2 else i - 1) for i in range(1, count - 1)])


def on_device(fields, material, depth_order, table):
    _, zs, xs, ys = fields.shape
    nx, nz = lax.axis_size("gx"), lax.axis_size("gz")
    block = xs + TILE
    part = xs // nz
    swaps = nz in (2, 4)
    groups = -(-(zs + 1) // GROUP)
    f32 = lambda *shape: jax.ShapeDtypeStruct(shape, jnp.float32)

    def side(even_high):
        return call(functools.partial(rows_kernel, zs, xs, even_high), f32(FACE, zs, ys), "v", name="x_rows")(fields)

    x_a, x_b = swap_pairs(side(True), side(False) if nx > 2 else None, "gx")
    held, ids, main, nearer = call(
        functools.partial(stage_kernel, zs, xs, swaps),
        (
            f32(4, zs, xs, ys),
            jax.ShapeDtypeStruct((zs, xs, ys), jnp.int32),
            f32(groups, xs, 128),
            f32(nz * nz, 1, 128),
        ),
        "saa",
        [pltpu.SemaphoreType.DMA((5,))],
        cost=2.0,
        name="stage",
    )(depth_order, fields, material)
    x_a, x_b, held = lax.optimization_barrier((x_a, x_b, held))

    halo, own = call(
        functools.partial(x_halo_kernel, zs, xs), (f32(4, zs + 2, TILE, ys), f32(groups, block, 128)), "vvvv", name="x_halo"
    )(held, main, x_a, x_b)
    y_a, y_b = swap_pairs(own, own, "gy")
    looked = call(
        functools.partial(lookup_kernel, zs, xs),
        f32(4, zs, xs, ys),
        "vv",
        [pltpu.VMEM((4, 128), jnp.float32)],
        cost=2.0,
        name="lookup",
    )(table, ids)
    y_a, y_b, looked = lax.optimization_barrier((y_a, y_b, looked))

    faces = f32((FACE + 1) * block, ys)
    merged, f_a, f_b = call(
        functools.partial(face_kernel, zs, xs), (f32(groups, block, 128), faces, faces), "vvvvv", name="faces"
    )(held, halo, own, y_a, y_b)
    z_a, z_b = swap_pairs(f_a, f_b, "gz")

    scale = 2.0 / (zs * nz)
    inner, cross = call(
        functools.partial(inner_kernel, zs, xs, scale),
        (f32(5, xs, ys), f32(7, zs, xs, ys)),
        "vvvvvv",
        [pltpu.VMEM((6, zs * block + TILE, ys), jnp.float32)],
        cost=4.0,
        name="inner",
    )(held, halo, merged, looked, *[jnp.asarray(m) for m in band_matrices(ys)])

    images = call(
        functools.partial(edge_kernel, zs, xs, scale),
        [f32(4, part, ys)] * nz if swaps else [f32(4, xs, ys)],
        "vvvvv",
        [
            pltpu.VMEM((7, 4, xs, ys), jnp.float32),
            pltpu.VMEM((2, 2, 6, block + TILE, ys), jnp.float32),
            pltpu.VMEM((4, xs, ys), jnp.float32),
        ],
        name="edges",
    )(z_a, z_b, cross, looked, inner)

    if swaps:
        mine = [images[0]]
        for k in range(1, nz):
            mine.append(lax.ppermute(images[k], "gz", [(i, i ^ k) for i in range(nz)]))
    else:
        stacked = lax.all_to_all(images[0].reshape(4, nz, part, ys), "gz", split_axis=1, concat_axis=1)
        mine = [stacked[:, b] for b in range(nz)]
    return call(blend_kernel, f32(4, part, ys), "v" + "v" * nz, name="blend")(nearer, *mine)


def solution(mesh):
    return jax.shard_map(
        on_device,
        mesh=mesh,
        in_specs=(P(None, "gz", "gx", "gy"), P("gz", "gx", "gy"), P(), P()),
        out_specs=P(None, ("gx", "gz"), "gy"),
        check_vma=False,
    )
```

```python
import functools

import jax
import jax.numpy as jnp
import ml_dtypes
import numpy as np
from jax import lax
from jax.experimental import pallas as pl
from jax.experimental.pallas import tpu as pltpu
from jax.sharding import PartitionSpec as P

VMEM_LIMIT = 40 * 1024 * 1024
GROUP = 12
SLOT = 10
TILE = 8
FACE = 5

LOG1P = (
    0.9999995186059567, -0.49996356582563917, 0.33265255844036573, -0.24453388969978707, 0.17659864766821842,
    -0.10679931280022417, 0.043659288844443055, -0.008466410404849948,
)
EXPM1 = (
    1.0, -0.4999995231628418, 0.1666584461927414, -0.04160914570093155, 0.00814302358776331, -0.0010865303920581937,
)


def polynomial(coefficients, value):
    terms = list(coefficients)
    power = value
    while len(terms) > 1:
        paired = [terms[k] + terms[k + 1] * power for k in range(0, len(terms) - 1, 2)]
        terms = paired + ([terms[-1]] if len(terms) % 2 else [])
        power = power * power if len(terms) > 1 else power
    return terms[0]


BLUR, BLUR2, SLOPE = {-1: 1, 0: 2, 1: 1}, {-2: 1, -1: 4, 0: 6, 1: 4, 2: 1}, {-2: -1, -1: -2, 1: 2, 2: 1}


def band_matrices(ysize):
    cells = np.zeros((ysize, 3 * ysize), np.float32)
    strips = np.zeros((128, 7 * ysize), np.float32)
    for block, taps in enumerate((BLUR, BLUR2, SLOPE)):
        for out in range(ysize):
            for off, weight in taps.items():
                if 0 <= out + off < ysize:
                    cells[out + off, block * ysize + out] = weight
    for block, (taps, field) in enumerate([(BLUR, f) for f in range(4)] + [(BLUR2, 0), (SLOPE, 0), (BLUR2, 0)]):
        first = slot_of(field)[0]
        outside = {-2: 0, -1: 1, ysize: 2, ysize + 1: 3} if field == 0 else {-1: first, ysize: first + 1}
        for out in range(ysize):
            for off, weight in taps.items():
                if not 0 <= out + off < ysize:
                    strips[outside[out + off], block * ysize + out] = weight
    return [np.concatenate([m, m], axis=0).astype(ml_dtypes.bfloat16) for m in (cells, strips)]


def halves(values):
    high = values.astype(jnp.bfloat16)
    low = (values - high.astype(jnp.float32)).astype(jnp.bfloat16)
    return jnp.concatenate([high, low], axis=1)


def place_of(axis):
    at = lax.axis_index(axis)
    return at == 0, at == lax.axis_size(axis) - 1, lax.rem(at, 2) == 1


def rows_kernel(zs, xs, even_high, fields_ref, out_ref):
    high = (lax.rem(lax.axis_index("gx"), 2) == 0) == even_high
    for group in range(FACE):
        field = max(group - 1, 0)
        rows = fields_ref.at[field].reshape(zs * xs, 128)
        low_row = group if group < 2 else 0
        high_row = xs - 2 + group if group < 2 else xs - 1
        out_ref[group] = rows[pl.ds(jnp.where(high, high_row, low_row), zs, stride=xs), :]


def slot_of(field):
    return (0, 4) if field == 0 else (2 + 2 * field, 2)


def pack_strips(load, layers, lane, rows):
    packed = jnp.zeros((rows, 128), jnp.float32)
    for k, z in enumerate(layers):
        for field in range(4):
            first, count = slot_of(field)
            start = SLOT * k + first
            values = pltpu.roll(load(field, z), (start + count // 2) % 128, 1)
            packed = jnp.where((lane >= start) & (lane < start + count), values, packed)
    return packed


def stage_kernel(zs, xs, peers, order_ref, fields_ref, material_ref, held_ref, ids_ref, pack_ref, near_ref, sems):
    copies = [pltpu.make_async_copy(fields_ref.at[f], held_ref.at[f], sems.at[f]) for f in range(4)]
    copies.append(pltpu.make_async_copy(material_ref, ids_ref, sems.at[4]))
    for copy in copies:
        copy.start()
    iz, count = lax.axis_index("gz"), lax.axis_size("gz")
    ranks = [order_ref[iz ^ k if peers else k] for k in range(count)]
    for k in range(count):
        for other in range(count):
            nearer = jnp.where(ranks[other] < ranks[k], 1.0, 0.0)
            near_ref[k * count + other] = jnp.full((1, 128), nearer, jnp.float32)
    for copy in copies:
        copy.wait()
    lane = lax.broadcasted_iota(jnp.int32, (1, 128), 1)
    for group in range(pack_ref.shape[0]):
        layers = range(group * GROUP, min(zs, group * GROUP + GROUP))
        pack_ref[group] = pack_strips(lambda f, z: held_ref[f, z], layers, lane, xs)


def lookup_kernel(zs, xs, table_ref, ids_ref, looked_ref, tables_ref):
    tables_ref[...] = jnp.zeros_like(tables_ref)
    tables_ref[:, 0 : table_ref.shape[1]] = table_ref[...]
    tables = [jnp.broadcast_to(tables_ref[c : c + 1, :], (TILE, 128)) for c in range(4)]
    each = 8
    tiles = xs // TILE

    def step(k, carry):
        for j in range(each):
            z = k * each + j
            for t in range(tiles):
                ids = ids_ref[z, pl.ds(t, TILE, stride=tiles), :]
                for c in range(4):
                    looked_ref[c, z, t * TILE : t * TILE + TILE, :] = jnp.take_along_axis(
                        tables[c], ids, axis=1, mode="promise_in_bounds"
                    )
        return carry

    lax.fori_loop(0, zs // each, step, 0)


def x_halo_kernel(zs, xs, held_ref, main_ref, xa_ref, xb_ref, halo_ref, pack_ref):
    first, last, odd = place_of("gx")
    halo_ref[...] = jnp.zeros_like(halo_ref)
    for field in range(4):
        tiles = halo_ref.at[field].reshape(zs * TILE, 128)
        own = held_ref.at[field].reshape(zs * xs, 128)
        at = 0 if field == 0 else 1 + field
        below = jnp.where(odd, xa_ref[1 + field], xb_ref[1 + field])
        above = jnp.where(odd, xb_ref[at], xa_ref[at])
        tiles[pl.ds(0, zs, stride=TILE), :] = jnp.where(first, 0.0, below)
        tiles[pl.ds(TILE - 1, zs, stride=TILE), :] = jnp.where(last, 0.0, above)
        if field == 0:
            low, high = own[pl.ds(0, zs, stride=xs), :], own[pl.ds(xs - 1, zs, stride=xs), :]
            tiles[pl.ds(1, zs, stride=TILE), :] = jnp.where(first, -low, jnp.where(odd, xa_ref[0], xb_ref[0]))
            tiles[pl.ds(TILE - 2, zs, stride=TILE), :] = jnp.where(last, -high, jnp.where(odd, xb_ref[1], xa_ref[1]))
    lane = lax.broadcasted_iota(jnp.int32, (1, 128), 1)
    for group in range(pack_ref.shape[0]):
        layers = range(group * GROUP, min(zs, group * GROUP + GROUP))
        pack_ref[group, 0:TILE] = pack_strips(lambda f, z: halo_ref[f, z], layers, lane, TILE)
        pack_ref[group, TILE:] = main_ref[group]


def face_kernel(zs, xs, held_ref, halo_ref, own_ref, ya_ref, yb_ref, merged_ref, fa_ref, fb_ref):
    yfirst, ylast, yodd = place_of("gy")
    zodd = place_of("gz")[2]
    block = xs + TILE
    lane = lax.broadcasted_iota(jnp.int32, (1, 128), 1)
    place = lax.rem(lane, SLOT)
    from_left = (place < 2) | ((place >= 4) & (lax.rem(place, 2) == 0))
    for group in range(own_ref.shape[0]):
        own = own_ref[group]
        fill_left = jnp.where(place == 0, -pltpu.roll(own, 126, 1), 0.0)
        fill_right = jnp.where(place == 3, -pltpu.roll(own, 2, 1), 0.0)
        first, second = ya_ref[group], yb_ref[group]
        left = jnp.where(yfirst, fill_left, jnp.where(yodd, first, second))
        right = jnp.where(ylast, fill_right, jnp.where(yodd, second, first))
        merged_ref[group] = jnp.where(from_left, left, right)

    def put(at, low, high):
        for out_ref, swapped in ((fa_ref, False), (fb_ref, True)):
            for (start, count), a, b in zip(((0, TILE), (TILE, xs)), low, high):
                out_ref[at * block + start : at * block + start + count, :] = jnp.where(zodd != swapped, a, b)

    def layer(field, z):
        return halo_ref[field, z], held_ref[field, z]

    def strips(z):
        group, k = divmod(z, GROUP)
        moved = pltpu.roll(merged_ref[group], (-SLOT * k) % 128, 1)
        return moved[0:TILE], moved[TILE:]

    for j in range(FACE):
        field = max(j - 1, 0)
        put(j, layer(field, j if j < 2 else 0), layer(field, zs - 2 + j if j < 2 else zs - 1))
    put(FACE, strips(0), strips(zs - 2))


def along_y(values, halo, lane, density):
    def shifted(off):
        mixed = jnp.where(lane >= 128 - off if off > 0 else lane < -off, halo, values)
        return pltpu.roll(mixed, off % 128, 1)

    m1, p1 = shifted(1), shifted(-1)
    near = m1 + p1
    blur = near + 2.0 * values
    if not density:
        return (blur,)
    m2, p2 = shifted(2), shifted(-2)
    return blur, (m2 + p2) + 4.0 * near + 6.0 * values, (p2 - m2) + 2.0 * (p1 - m1)


class Rows:
    def __init__(self, tiles, halo):
        self.tiles, self.halo = list(tiles), halo
        self.sub = lax.broadcasted_iota(jnp.int32, (TILE, 1), 0)
        self.made = {}

    def row(self, t):
        count = len(self.tiles)
        if 0 <= t < count:
            return self.tiles[t]
        if t not in self.made:
            down = t < 0
            step = -t - 1 if down else t - count
            halo = self.halo if step == 0 else pltpu.roll(self.halo, TILE - 1 if down else 1, 0)
            inner = pltpu.roll(self.tiles[t % count], 1 if down else TILE - 1, 0)
            self.made[t] = jnp.where(self.sub == (0 if down else TILE - 1), halo, inner)
        return self.made[t]

    def pair(self, level, t):
        if level == 0:
            return self.row(t)
        if (level, t) not in self.made:
            self.made[level, t] = self.pair(level - 1, t) + self.pair(level - 1, t + 1)
        return self.made[level, t]

    def blur(self):
        return [self.pair(2, t - 1) for t in range(len(self.tiles))]

    def blur2(self):
        return [self.pair(4, t - 2) for t in range(len(self.tiles))]

    def slope(self):
        return [self.pair(2, t) - self.pair(2, t - 2) for t in range(len(self.tiles))]


def cells_kernel(zs, xs, fields_ref, cell_ref, out_ref):
    each, tiles = 8, xs // TILE

    def step(k, carry):
        first = k * each
        for field in range(4):
            rows = [
                fields_ref[field, first + j, pl.ds(t, TILE, stride=tiles), :] for j in range(each) for t in range(tiles)
            ]
            weights = cell_ref[...] if field == 0 else cell_ref[:, 0:128]
            result = jnp.dot(halves(jnp.concatenate(rows, axis=0)), weights, preferred_element_type=jnp.float32)
            for part in (0, 1, 2) if field == 0 else (2 + field,):
                columns = slice(128 * part, 128 * part + 128) if field == 0 else slice(0, 128)
                out_ref[part, pl.ds(first, each)] = result[:, columns].reshape(each, xs, 128)
        return carry

    lax.fori_loop(0, zs // each, step, 0)


def cross_kernel(zs, xs, rows_ref, halo_ref, cell_ref, out_ref, edge_ref):
    each, tiles = 4, xs // TILE
    for field in range(4):
        weights = cell_ref[...] if field == 0 else cell_ref[:, 0:128]
        result = jnp.dot(
            halves(halo_ref[field].reshape(zs * TILE, 128)), weights, preferred_element_type=jnp.float32
        )
        for part in (0, 1, 2) if field == 0 else (2 + field,):
            columns = slice(128 * part, 128 * part + 128) if field == 0 else slice(0, 128)
            edge_ref[part] = result[:, columns].reshape(zs, TILE, 128)

    def step(k, carry):
        for j in range(each):
            z = k * each + j

            def part_rows(part):
                return Rows([rows_ref[part, z, t * TILE : t * TILE + TILE, :] for t in range(tiles)], edge_ref[part, z])

            twice, sloped = part_rows(1), part_rows(2)
            results = [part_rows(part).blur() for part in (0, 3, 4, 5)]
            results += [twice.blur2(), twice.slope(), sloped.blur2()]
            for part, values in enumerate(results):
                for t in range(tiles):
                    out_ref[part, z, t * TILE : t * TILE + TILE, :] = values[t]
        return carry

    lax.fori_loop(0, zs // each, step, 0)


def before_shade(load, z):
    def blur(part):
        return load(part, z - 1) + load(part, z + 1) + 2.0 * load(part, z)

    def blur2(part):
        return (load(part, z - 2) + load(part, z + 2)) + 4.0 * (load(part, z - 1) + load(part, z + 1)) + 6.0 * load(part, z)

    unit = 1.0 / 2048.0
    near = load(4, z + 1) - load(4, z - 1)
    grad_z = (load(4, z + 2) - load(4, z - 2)) + (near + near)
    grad_x = blur2(5)
    grad_y = blur2(6)
    facing = jnp.abs((0.8 * unit) * (grad_z + grad_y) + (0.4 * unit) * grad_x)
    square = grad_z * grad_z + grad_x * grad_x + grad_y * grad_y
    shading = 0.3 + facing * lax.rsqrt(square * (unit * unit) + 0.0025)
    density = (3.0 / 64.0) * blur(0)
    return [density, jnp.exp(-jnp.abs(density)), shading] + [blur(1 + c) for c in range(3)]


def shade(state, taken, looked, scale):
    density, t, shading = taken[:3]
    soft = jnp.maximum(density, 0.0) + t * polynomial(LOG1P, t)
    extinct = looked[3] * (soft * scale)
    passed, total, depth = state[0], state[1:4], state[4]
    weight = passed * (extinct * polynomial(EXPM1, extinct))
    lit = weight * shading
    colours = [
        total[c] + (looked[c] * lit) * (1.0 + 0.5 * jnp.tanh((1.0 / 64.0) * taken[3 + c])) for c in range(3)
    ]
    return (passed - weight, *colours, depth + extinct)


def inner_kernel(zs, xs, scale, cross_ref, merged_ref, looked_ref, strip_ref, inner_ref, full_ref, filtered_ref, taken_ref):
    tiles, each = xs // TILE, 8
    for group in range(merged_ref.shape[0]):
        rows = Rows([merged_ref[group, pl.ds(TILE + t, TILE, stride=tiles), :] for t in range(tiles)], merged_ref[group, 0:TILE])
        for k, values in enumerate((rows.blur(), rows.blur2(), rows.slope())):
            for t in range(tiles):
                filtered_ref[k, group, t * TILE : t * TILE + TILE, :] = values[t]

    def strip_step(step, carry):
        first = step * each
        for k, parts in enumerate(((0, 1, 2, 3), (4, 6), (5,))):
            strips = []
            for j in range(each):
                group = lax.div(first + j, GROUP)
                slot = first + j - group * GROUP
                strips.append(pltpu.roll(filtered_ref[k, group], lax.rem(128 - SLOT * slot, 128), 1))
            columns = slice((0, 512, 768)[k], (512, 768, 896)[k])
            result = jnp.dot(
                halves(jnp.concatenate(strips, axis=0)), strip_ref[:, columns], preferred_element_type=jnp.float32
            )
            for n, part in enumerate(parts):
                share = result[:, 128 * n : 128 * n + 128].reshape(each, xs, 128)
                full_ref[part, pl.ds(first, each)] = cross_ref[part, pl.ds(first, each)] + share
        return carry

    lax.fori_loop(0, zs // each, strip_step, 0)

    pairs = (zs - 4) // 2

    def take(step):
        for j in range(2):
            z = 2 + 2 * step + j
            for k, values in enumerate(before_shade(lambda part, z: full_ref[part, z], z)):
                taken_ref[k, j] = values

    def advance(step, state):
        for j in range(2):
            looked = [looked_ref[c, 2 + 2 * step + j] for c in range(4)]
            state = shade(state, [taken_ref[k, j] for k in range(6)], looked, scale)
        return state

    def z_step(step, state):
        state = advance(step, state)
        take(step + 1)
        return state

    zero = jnp.zeros((xs, 128), jnp.float32)
    take(0)
    state = lax.fori_loop(0, pairs - 1, z_step, (zero + 1.0, zero, zero, zero, zero))
    for k, values in enumerate(advance(pairs - 1, state)):
        inner_ref[k] = values


def edge_kernel(zs, xs, scale, fa_ref, fb_ref, cross_ref, looked_ref, inner_ref, *rest):
    out_refs, (near_ref, rows_ref, image_ref) = rest[:-3], rest[-3:]
    zfirst, zlast, zodd = place_of("gz")
    block = xs + TILE
    tiles = xs // TILE
    lane = lax.broadcasted_iota(jnp.int32, (1, 128), 1)
    for side in range(2):
        first, second = (fa_ref, fb_ref) if side == 0 else (fb_ref, fa_ref)

        def face(at):
            return jnp.where(zodd, first[at * block : at * block + block, :], second[at * block : at * block + block, :])

        strips = face(FACE)
        for j in range(FACE):
            field = max(j - 1, 0)
            layer = j if j < 2 else (1 if side == 0 else 0)
            at_lane = SLOT * layer + slot_of(field)[0]
            halo = pltpu.roll(strips, ((126 if field == 0 else 127) - at_lane) % 128, 1)
            results = along_y(face(j), halo, lane, field == 0)
            for part, result in zip((0, 1, 2) if field == 0 else (2 + field,), results):
                rows_ref[side, layer, part] = result
    for side in range(2):
        edge = zfirst if side == 0 else zlast
        for layer in range(2):
            mirrored = 0 if side == 0 else zs - 1
            outer = layer == side

            def part_rows(part):
                ref = rows_ref.at[side, layer, part]
                return Rows([ref[pl.ds(TILE + t, TILE, stride=tiles), :] for t in range(tiles)], ref[0:TILE, :])

            twice, sloped = part_rows(1), part_rows(2)
            for part, values in zip((4, 5, 6), (twice.blur2(), twice.slope(), sloped.blur2())):
                for t in range(tiles):
                    rows = slice(t * TILE, t * TILE + TILE)
                    fill = -cross_ref[part, mirrored, rows] if outer else 0.0
                    near_ref[part, 2 * side + layer, rows] = jnp.where(edge, fill, values[t])
            if not outer:
                for part, source in enumerate((0, 3, 4, 5)):
                    for t, values in enumerate(part_rows(source).blur()):
                        near_ref[part, 2 * side + layer, t * TILE : t * TILE + TILE] = jnp.where(edge, 0.0, values)

    def load(part, z):
        if z < 0:
            return near_ref[part, z + 2]
        if z >= zs:
            return near_ref[part, z - zs + 2]
        return cross_ref[part, z]

    def behind(state, z):
        return shade(state, before_shade(load, z), [looked_ref[c, z] for c in range(4)], scale)

    zero = jnp.zeros((xs, 128), jnp.float32)
    state = behind(behind((zero + 1.0, zero, zero, zero, zero), 0), 1)
    passed = state[0]
    state = (
        passed * inner_ref[0],
        state[1] + passed * inner_ref[1],
        state[2] + passed * inner_ref[2],
        state[3] + passed * inner_ref[3],
        state[4] + inner_ref[4],
    )
    state = behind(behind(state, zs - 2), zs - 1)
    for c in range(4):
        for t in range(tiles):
            image_ref[c, pl.ds(t, TILE, stride=tiles), :] = state[1 + c][t * TILE : t * TILE + TILE]
    if len(out_refs) == 1:
        out_refs[0][...] = image_ref[...]
    else:
        part = xs // len(out_refs)
        for k, ref in enumerate(out_refs):
            ref[...] = image_ref[:, pl.ds(pl.multiple_of((lax.axis_index("gz") ^ k) * part, part), part), :]


def blend_kernel(near_ref, *refs):
    images, out_ref = refs[:-1], refs[-1]
    count = len(images)
    depths = [image[3] for image in images]
    colours = [jnp.zeros_like(depths[0])] * 3
    for k in range(count):
        prior = jnp.zeros_like(depths[0])
        for other in range(count):
            if other != k:
                prior += near_ref[k * count + other] * depths[other]
        through = jnp.exp(-prior)
        colours = [colours[c] + through * images[k][c] for c in range(3)]
    total = functools.reduce(jnp.add, depths)
    out_ref[0], out_ref[1], out_ref[2] = colours
    small = total * polynomial(EXPM1, total)
    out_ref[3] = jnp.where(total < 0.5, small, 1.0 - jnp.exp(-total))


def call(kernel, out_shape, specs, scratch=(), cost=1.0, name=None, limit=VMEM_LIMIT):
    where = {"s": pltpu.SMEM, "v": pltpu.VMEM, "a": pl.ANY}
    return pl.pallas_call(
        kernel,
        out_shape=out_shape,
        in_specs=[pl.BlockSpec(memory_space=where[s]) for s in specs],
        out_specs=jax.tree.map(lambda _: pl.BlockSpec(memory_space=pltpu.VMEM), out_shape),
        scratch_shapes=list(scratch),
        compiler_params=pltpu.CompilerParams(vmem_limit_bytes=limit),
        cost_estimate=pl.CostEstimate(flops=0, bytes_accessed=int(cost * 3.0e6), transcendentals=0),
        name=name,
    )


def swap_pairs(first, second, axis):
    count = lax.axis_size(axis)
    one = lax.ppermute(first, axis, [(i, i ^ 1) for i in range(count)])
    if count == 2:
        return one, one
    ends = [(0, 0), (count - 1, count - 1)]
    return one, lax.ppermute(second, axis, ends + [(i, i + 1 if i % 2 else i - 1) for i in range(1, count - 1)])


def on_device(fields, material, depth_order, table):
    _, zs, xs, ys = fields.shape
    nx, nz = lax.axis_size("gx"), lax.axis_size("gz")
    block = xs + TILE
    part = xs // nz
    swaps = nz in (2, 4)
    groups = -(-zs // GROUP)
    f32 = lambda *shape: jax.ShapeDtypeStruct(shape, jnp.float32)

    def side(even_high):
        return call(functools.partial(rows_kernel, zs, xs, even_high), f32(FACE, zs, ys), "v", name="x_rows")(fields)

    x_a, x_b = swap_pairs(side(True), side(False) if nx > 2 else None, "gx")
    cell, strip = [jnp.asarray(m) for m in band_matrices(ys)]
    rows = call(functools.partial(cells_kernel, zs, xs), f32(6, zs, xs, ys), "vv", cost=1.0, name="cells")(fields, cell)
    held, ids, main, nearer = call(
        functools.partial(stage_kernel, zs, xs, swaps),
        (
            f32(4, zs, xs, ys),
            jax.ShapeDtypeStruct((zs, xs, ys), jnp.int32),
            f32(groups, xs, 128),
            f32(nz * nz, 1, 128),
        ),
        "saa",
        [pltpu.SemaphoreType.DMA((5,))],
        cost=2.0,
        name="stage",
    )(depth_order, fields, material)
    x_a, x_b, held, rows = lax.optimization_barrier((x_a, x_b, held, rows))

    halo, own = call(
        functools.partial(x_halo_kernel, zs, xs), (f32(4, zs, TILE, ys), f32(groups, block, 128)), "vvvv", name="x_halo"
    )(held, main, x_a, x_b)
    y_a, y_b = swap_pairs(own, own, "gy")
    looked = call(
        functools.partial(lookup_kernel, zs, xs),
        f32(4, zs, xs, ys),
        "vv",
        [pltpu.VMEM((4, 128), jnp.float32)],
        cost=2.0,
        name="lookup",
    )(table, ids)
    cross = call(
        functools.partial(cross_kernel, zs, xs),
        f32(7, zs, xs, ys),
        "vvv",
        [pltpu.VMEM((6, zs, TILE, ys), jnp.float32)],
        cost=1.0,
        name="cross",
    )(rows, halo, cell)
    y_a, y_b, looked, cross = lax.optimization_barrier((y_a, y_b, looked, cross))

    faces = f32((FACE + 1) * block, ys)
    merged, f_a, f_b = call(
        functools.partial(face_kernel, zs, xs), (f32(groups, block, 128), faces, faces), "vvvvv", name="faces"
    )(held, halo, own, y_a, y_b)
    z_a, z_b = swap_pairs(f_a, f_b, "gz")

    scale = 2.0 / (zs * nz)
    inner, full = call(
        functools.partial(inner_kernel, zs, xs, scale),
        (f32(5, xs, ys), f32(7, zs, xs, ys)),
        "vvvv",
        [pltpu.VMEM((3, groups, xs, 128), jnp.float32), pltpu.VMEM((6, 2, xs, ys), jnp.float32)],
        cost=4.0,
        name="inner",
    )(cross, merged, looked, strip)

    images = call(
        functools.partial(edge_kernel, zs, xs, scale),
        [f32(4, part, ys)] * nz if swaps else [f32(4, xs, ys)],
        "vvvvv",
        [
            pltpu.VMEM((7, 4, xs, ys), jnp.float32),
            pltpu.VMEM((2, 2, 6, block, ys), jnp.float32),
            pltpu.VMEM((4, xs, ys), jnp.float32),
        ],
        name="edges",
    )(z_a, z_b, full, looked, inner)

    if swaps:
        mine = [images[0]]
        for k in range(1, nz):
            mine.append(lax.ppermute(images[k], "gz", [(i, i ^ k) for i in range(nz)]))
    else:
        stacked = lax.all_to_all(images[0].reshape(4, nz, part, ys), "gz", split_axis=1, concat_axis=1)
        mine = [stacked[:, b] for b in range(nz)]
    return call(blend_kernel, f32(4, part, ys), "v" + "v" * nz, name="blend")(nearer, *mine)


def solution(mesh):
    return jax.shard_map(
        on_device,
        mesh=mesh,
        in_specs=(P(None, "gz", "gx", "gy"), P("gz", "gx", "gy"), P(), P()),
        out_specs=P(None, ("gx", "gz"), "gy"),
        check_vma=False,
    )
```

```python
import functools

import jax
import jax.numpy as jnp
import ml_dtypes
import numpy as np
from jax import lax
from jax.experimental import pallas as pl
from jax.experimental.pallas import tpu as pltpu
from jax.sharding import PartitionSpec as P

VMEM_LIMIT = 40 * 1024 * 1024
GROUP = 12
SLOT = 10
TILE = 8
FACE = 5
SPAN = 24

LOG1P = (
    0.9999995186059567, -0.49996356582563917, 0.33265255844036573, -0.24453388969978707, 0.17659864766821842,
    -0.10679931280022417, 0.043659288844443055, -0.008466410404849948,
)
EXPM1 = (
    1.0, -0.4999995231628418, 0.1666584461927414, -0.04160914570093155, 0.00814302358776331, -0.0010865303920581937,
)


def polynomial(coefficients, value):
    terms = list(coefficients)
    power = value
    while len(terms) > 1:
        paired = [terms[k] + terms[k + 1] * power for k in range(0, len(terms) - 1, 2)]
        terms = paired + ([terms[-1]] if len(terms) % 2 else [])
        power = power * power if len(terms) > 1 else power
    return terms[0]


BLUR, BLUR2, SLOPE = {-1: 1, 0: 2, 1: 1}, {-2: 1, -1: 4, 0: 6, 1: 4, 2: 1}, {-2: -1, -1: -2, 1: 2, 2: 1}


def strip_matrix(ysize):
    strips = np.zeros((128, 7 * ysize), np.float32)
    for block, (taps, field) in enumerate([(BLUR, f) for f in range(4)] + [(BLUR2, 0), (SLOPE, 0), (BLUR2, 0)]):
        first = slot_of(field)[0]
        outside = {-2: 0, -1: 1, ysize: 2, ysize + 1: 3} if field == 0 else {-1: first, ysize: first + 1}
        for out in range(ysize):
            for off, weight in taps.items():
                if not 0 <= out + off < ysize:
                    strips[outside[out + off], block * ysize + out] = weight
    return np.concatenate([strips, strips], axis=0).astype(ml_dtypes.bfloat16)


def make_cell_weights(out_ref):
    off = lax.broadcasted_iota(jnp.int32, (128, 128), 0) - lax.broadcasted_iota(jnp.int32, (128, 128), 1)
    for block, taps in enumerate((BLUR, BLUR2, SLOPE)):
        weights = jnp.zeros((128, 128), jnp.float32)
        for step, weight in taps.items():
            weights = jnp.where(off == step, float(weight), weights)
        for half in range(2):
            out_ref[128 * half : 128 * half + 128, 128 * block : 128 * block + 128] = weights.astype(jnp.bfloat16)


def halves(values):
    high = values.astype(jnp.bfloat16)
    low = (values - high.astype(jnp.float32)).astype(jnp.bfloat16)
    return jnp.concatenate([high, low], axis=1)


def place_of(axis):
    at = lax.axis_index(axis)
    return at == 0, at == lax.axis_size(axis) - 1, lax.rem(at, 2) == 1


def rows_kernel(zs, even_high, tile_ref, out_ref):
    high = (lax.rem(lax.axis_index("gx"), 2) == 0) == even_high
    for group in range(FACE):
        field = max(group - 1, 0)
        rows = tile_ref.at[field].reshape(zs * TILE, 128)
        low_row = group if group < 2 else 0
        high_row = TILE - 2 + group if group < 2 else TILE - 1
        out_ref[group] = rows[pl.ds(jnp.where(high, high_row, low_row), zs, stride=TILE), :]


def slot_of(field):
    return (0, 4) if field == 0 else (2 + 2 * field, 2)


def pack_strips(load, layers, lane, rows):
    packed = jnp.zeros((rows, 128), jnp.float32)
    for k, z in enumerate(layers):
        for field in range(4):
            first, count = slot_of(field)
            start = SLOT * k + first
            values = pltpu.roll(load(field, z), (start + count // 2) % 128, 1)
            packed = jnp.where((lane >= start) & (lane < start + count), values, packed)
    return packed


def stage_kernel(zs, xs, peers, order_ref, fields_ref, held_ref, pack_ref, near_ref, sems):
    copies = [pltpu.make_async_copy(fields_ref.at[f], held_ref.at[f], sems.at[f]) for f in range(4)]
    for copy in copies:
        copy.start()
    iz, count = lax.axis_index("gz"), lax.axis_size("gz")
    ranks = [order_ref[iz ^ k if peers else k] for k in range(count)]
    for k in range(count):
        for other in range(count):
            nearer = jnp.where(ranks[other] < ranks[k], 1.0, 0.0)
            near_ref[k * count + other] = jnp.full((1, 128), nearer, jnp.float32)
    lane = lax.broadcasted_iota(jnp.int32, (1, 128), 1)
    for group in range(pack_ref.shape[0]):
        layers = range(group * GROUP, min(zs, group * GROUP + GROUP))
        pack_ref[group] = pack_strips(lambda f, z: fields_ref[f, z], layers, lane, xs)
    for copy in copies:
        copy.wait()


def lookup_kernel(zs, xs, table_ref, ids_ref, looked_ref, tables_ref):
    tables_ref[...] = jnp.zeros_like(tables_ref)
    tables_ref[:, 0 : table_ref.shape[1]] = table_ref[...]
    tables = [jnp.broadcast_to(tables_ref[c : c + 1, :], (TILE, 128)) for c in range(4)]
    each = 8
    tiles = xs // TILE

    def step(k, carry):
        for j in range(each):
            z = k * each + j
            for t in range(tiles):
                ids = ids_ref[z, pl.ds(t, TILE, stride=tiles), :]
                for c in range(4):
                    looked_ref[c, z, t * TILE : t * TILE + TILE, :] = jnp.take_along_axis(
                        tables[c], ids, axis=1, mode="promise_in_bounds"
                    )
        return carry

    lax.fori_loop(0, zs // each, step, 0)


def x_halo_kernel(zs, xs, held_ref, main_ref, xa_ref, xb_ref, halo_ref, pack_ref):
    first, last, odd = place_of("gx")
    halo_ref[...] = jnp.zeros_like(halo_ref)
    for field in range(4):
        tiles = halo_ref.at[field].reshape(zs * TILE, 128)
        own = held_ref.at[field].reshape(zs * xs, 128)
        at = 0 if field == 0 else 1 + field
        below = jnp.where(odd, xa_ref[1 + field], xb_ref[1 + field])
        above = jnp.where(odd, xb_ref[at], xa_ref[at])
        tiles[pl.ds(0, zs, stride=TILE), :] = jnp.where(first, 0.0, below)
        tiles[pl.ds(TILE - 1, zs, stride=TILE), :] = jnp.where(last, 0.0, above)
        if field == 0:
            low, high = own[pl.ds(0, zs, stride=xs), :], own[pl.ds(xs - 1, zs, stride=xs), :]
            tiles[pl.ds(1, zs, stride=TILE), :] = jnp.where(first, -low, jnp.where(odd, xa_ref[0], xb_ref[0]))
            tiles[pl.ds(TILE - 2, zs, stride=TILE), :] = jnp.where(last, -high, jnp.where(odd, xb_ref[1], xa_ref[1]))
    lane = lax.broadcasted_iota(jnp.int32, (1, 128), 1)
    for group in range(pack_ref.shape[0]):
        layers = range(group * GROUP, min(zs, group * GROUP + GROUP))
        pack_ref[group, 0:TILE] = pack_strips(lambda f, z: halo_ref[f, z], layers, lane, TILE)
        pack_ref[group, TILE:] = main_ref[group]


def face_kernel(zs, xs, held_ref, halo_ref, own_ref, ya_ref, yb_ref, merged_ref, fa_ref, fb_ref):
    yfirst, ylast, yodd = place_of("gy")
    zodd = place_of("gz")[2]
    block = xs + TILE
    lane = lax.broadcasted_iota(jnp.int32, (1, 128), 1)
    place = lax.rem(lane, SLOT)
    from_left = (place < 2) | ((place >= 4) & (lax.rem(place, 2) == 0))
    for group in range(own_ref.shape[0]):
        own = own_ref[group]
        fill_left = jnp.where(place == 0, -pltpu.roll(own, 126, 1), 0.0)
        fill_right = jnp.where(place == 3, -pltpu.roll(own, 2, 1), 0.0)
        first, second = ya_ref[group], yb_ref[group]
        left = jnp.where(yfirst, fill_left, jnp.where(yodd, first, second))
        right = jnp.where(ylast, fill_right, jnp.where(yodd, second, first))
        merged_ref[group] = jnp.where(from_left, left, right)

    sub = lax.broadcasted_iota(jnp.int32, (TILE, 1), 0)
    ends = (sub < 2) | (sub >= TILE - 2)

    def put(start, low, high):
        for out_ref, swapped in ((fa_ref, False), (fb_ref, True)):
            out_ref[start : start + low.shape[0], :] = jnp.where(zodd != swapped, low, high)

    for j in range(FACE):
        put(j * xs, held_ref[max(j - 1, 0), j if j < 2 else 0], held_ref[max(j - 1, 0), zs - 2 + j if j < 2 else zs - 1])

    def density_rows(z):
        return jnp.where(ends, halo_ref[0, z], pltpu.roll(halo_ref[0, z + 1], TILE // 2, 0))

    def field_rows(z):
        rows = [pltpu.roll(halo_ref[f, z], 2 * f - 2, 0) if f > 1 else halo_ref[f, z] for f in (1, 2, 3)]
        mixed = jnp.where((sub == 0) | (sub == TILE - 1), rows[0], rows[1])
        return jnp.where((sub == 3) | (sub == 4), rows[2], mixed)

    def strips(z):
        group, k = divmod(z, GROUP)
        packed = jnp.zeros((TILE, 128), jnp.float32)
        for t in range(block // TILE):
            moved = pltpu.roll(merged_ref[group, t * TILE : t * TILE + TILE], (SPAN * t - SLOT * k) % 128, 1)
            packed = jnp.where((lane >= SPAN * t) & (lane < SPAN * t + SPAN), moved, packed)
        return packed

    put(FACE * xs, density_rows(0), density_rows(zs - 2))
    put(FACE * xs + TILE, field_rows(0), field_rows(zs - 1))
    put(FACE * xs + 2 * TILE, strips(0), strips(zs - 2))


def along_y(values, halo, lane, density):
    def shifted(off):
        mixed = jnp.where(lane >= 128 - off if off > 0 else lane < -off, halo, values)
        return pltpu.roll(mixed, off % 128, 1)

    m1, p1 = shifted(1), shifted(-1)
    near = m1 + p1
    blur = near + 2.0 * values
    if not density:
        return (blur,)
    m2, p2 = shifted(2), shifted(-2)
    return blur, (m2 + p2) + 4.0 * near + 6.0 * values, (p2 - m2) + 2.0 * (p1 - m1)


class Rows:
    def __init__(self, tiles, halo):
        self.tiles, self.halo = list(tiles), halo
        self.sub = lax.broadcasted_iota(jnp.int32, (TILE, 1), 0)
        self.made = {}

    def row(self, t):
        count = len(self.tiles)
        if 0 <= t < count:
            return self.tiles[t]
        if t not in self.made:
            down = t < 0
            step = -t - 1 if down else t - count
            halo = self.halo if step == 0 else pltpu.roll(self.halo, TILE - 1 if down else 1, 0)
            inner = pltpu.roll(self.tiles[t % count], 1 if down else TILE - 1, 0)
            self.made[t] = jnp.where(self.sub == (0 if down else TILE - 1), halo, inner)
        return self.made[t]

    def pair(self, level, t):
        if level == 0:
            return self.row(t)
        if (level, t) not in self.made:
            self.made[level, t] = self.pair(level - 1, t) + self.pair(level - 1, t + 1)
        return self.made[level, t]

    def blur(self):
        return [self.pair(2, t - 1) for t in range(len(self.tiles))]

    def blur2(self):
        return [self.pair(4, t - 2) for t in range(len(self.tiles))]

    def slope(self):
        return [self.pair(2, t) - self.pair(2, t - 2) for t in range(len(self.tiles))]


def cells_kernel(zs, xs, fields_ref, out_ref, cell_ref):
    each, tiles = 8, xs // TILE
    make_cell_weights(cell_ref)

    def step(k, carry):
        first = k * each
        for field in range(4):
            rows = [
                fields_ref[field, first + j, pl.ds(t, TILE, stride=tiles), :] for j in range(each) for t in range(tiles)
            ]
            weights = cell_ref[...] if field == 0 else cell_ref[:, 0:128]
            result = jnp.dot(halves(jnp.concatenate(rows, axis=0)), weights, preferred_element_type=jnp.float32)
            for part in (0, 1, 2) if field == 0 else (2 + field,):
                columns = slice(128 * part, 128 * part + 128) if field == 0 else slice(0, 128)
                out_ref[part, pl.ds(first, each)] = result[:, columns].reshape(each, xs, 128)
        return carry

    lax.fori_loop(0, zs // each, step, 0)


def cross_kernel(zs, xs, rows_ref, halo_ref, cell_ref, out_ref, edge_ref):
    each, tiles = 4, xs // TILE
    for field in range(4):
        weights = cell_ref[...] if field == 0 else cell_ref[:, 0:128]
        result = jnp.dot(
            halves(halo_ref[field].reshape(zs * TILE, 128)), weights, preferred_element_type=jnp.float32
        )
        for part in (0, 1, 2) if field == 0 else (2 + field,):
            columns = slice(128 * part, 128 * part + 128) if field == 0 else slice(0, 128)
            edge_ref[part] = result[:, columns].reshape(zs, TILE, 128)

    def step(k, carry):
        for j in range(each):
            z = k * each + j

            def part_rows(part):
                return Rows([rows_ref[part, z, t * TILE : t * TILE + TILE, :] for t in range(tiles)], edge_ref[part, z])

            twice, sloped = part_rows(1), part_rows(2)
            results = [part_rows(part).blur() for part in (0, 3, 4, 5)]
            results += [twice.blur2(), twice.slope(), sloped.blur2()]
            for part, values in enumerate(results):
                for t in range(tiles):
                    out_ref[part, z, t * TILE : t * TILE + TILE, :] = values[t]
        return carry

    lax.fori_loop(0, zs // each, step, 0)


def before_shade(load, z):
    def blur(part):
        return load(part, z - 1) + load(part, z + 1) + 2.0 * load(part, z)

    def blur2(part):
        return (load(part, z - 2) + load(part, z + 2)) + 4.0 * (load(part, z - 1) + load(part, z + 1)) + 6.0 * load(part, z)

    unit = 1.0 / 2048.0
    near = load(4, z + 1) - load(4, z - 1)
    grad_z = (load(4, z + 2) - load(4, z - 2)) + (near + near)
    grad_x = blur2(5)
    grad_y = blur2(6)
    facing = jnp.abs((0.8 * unit) * (grad_z + grad_y) + (0.4 * unit) * grad_x)
    square = grad_z * grad_z + grad_x * grad_x + grad_y * grad_y
    shading = 0.3 + facing * lax.rsqrt(square * (unit * unit) + 0.0025)
    density = (3.0 / 64.0) * blur(0)
    return [density, jnp.exp(-jnp.abs(density)), shading] + [blur(1 + c) for c in range(3)]


def shade(state, taken, looked, scale):
    density, t, shading = taken[:3]
    soft = jnp.maximum(density, 0.0) + t * polynomial(LOG1P, t)
    extinct = looked[3] * (soft * scale)
    passed, total, depth = state[0], state[1:4], state[4]
    weight = passed * (extinct * polynomial(EXPM1, extinct))
    lit = weight * shading
    colours = [
        total[c] + (looked[c] * lit) * (1.0 + 0.5 * jnp.tanh((1.0 / 64.0) * taken[3 + c])) for c in range(3)
    ]
    return (passed - weight, *colours, depth + extinct)


def inner_kernel(zs, xs, scale, cross_ref, merged_ref, looked_ref, strip_ref, inner_ref, full_ref, filtered_ref, taken_ref):
    tiles, each = xs // TILE, 8
    for group in range(merged_ref.shape[0]):
        rows = Rows([merged_ref[group, pl.ds(TILE + t, TILE, stride=tiles), :] for t in range(tiles)], merged_ref[group, 0:TILE])
        for k, values in enumerate((rows.blur(), rows.blur2(), rows.slope())):
            for t in range(tiles):
                filtered_ref[k, group, t * TILE : t * TILE + TILE, :] = values[t]

    def strip_step(step, carry):
        first = step * each
        for k, parts in enumerate(((0, 1, 2, 3), (4, 6), (5,))):
            strips = []
            for j in range(each):
                group = lax.div(first + j, GROUP)
                slot = first + j - group * GROUP
                strips.append(pltpu.roll(filtered_ref[k, group], lax.rem(128 - SLOT * slot, 128), 1))
            columns = slice((0, 512, 768)[k], (512, 768, 896)[k])
            result = jnp.dot(
                halves(jnp.concatenate(strips, axis=0)), strip_ref[:, columns], preferred_element_type=jnp.float32
            )
            for n, part in enumerate(parts):
                share = result[:, 128 * n : 128 * n + 128].reshape(each, xs, 128)
                full_ref[part, pl.ds(first, each)] = cross_ref[part, pl.ds(first, each)] + share
        return carry

    lax.fori_loop(0, zs // each, strip_step, 0)

    pairs = (zs - 4) // 2

    def take(step):
        for j in range(2):
            z = 2 + 2 * step + j
            for k, values in enumerate(before_shade(lambda part, z: full_ref[part, z], z)):
                taken_ref[k, j] = values

    def advance(step, state):
        for j in range(2):
            looked = [looked_ref[c, 2 + 2 * step + j] for c in range(4)]
            state = shade(state, [taken_ref[k, j] for k in range(6)], looked, scale)
        return state

    def z_step(step, state):
        state = advance(step, state)
        take(step + 1)
        return state

    zero = jnp.zeros((xs, 128), jnp.float32)
    take(0)
    state = lax.fori_loop(0, pairs - 1, z_step, (zero + 1.0, zero, zero, zero, zero))
    for k, values in enumerate(advance(pairs - 1, state)):
        inner_ref[k] = values


def edge_kernel(zs, xs, scale, fa_ref, fb_ref, cross_ref, looked_ref, inner_ref, *rest):
    out_refs, (near_ref, rows_ref, image_ref) = rest[:-3], rest[-3:]
    zfirst, zlast, zodd = place_of("gz")
    block = xs + TILE
    tiles = xs // TILE
    lane = lax.broadcasted_iota(jnp.int32, (1, 128), 1)
    for side in range(2):
        first, second = (fa_ref, fb_ref) if side == 0 else (fb_ref, fa_ref)

        def face(start, count):
            return jnp.where(zodd, first[start : start + count, :], second[start : start + count, :])

        ends = [face(FACE * xs, TILE), face(FACE * xs + TILE, TILE)]
        strips = face(FACE * xs + 2 * TILE, TILE)
        for j in range(FACE):
            field = max(j - 1, 0)
            layer = j if j < 2 else (1 if side == 0 else 0)
            turned = TILE // 2 * j if j < 2 else 2 * field - 2
            outer_rows = ends[min(field, 1)]
            if turned:
                outer_rows = pltpu.roll(outer_rows, TILE - turned, 0)
            at_lane = SLOT * layer + slot_of(field)[0]
            own = 126 if field == 0 else 127
            halo = [pltpu.roll(strips, (own - at_lane - SPAN * t) % 128, 1) for t in range(block // TILE)]
            values = jnp.concatenate([outer_rows, face(j * xs, xs)], axis=0)
            results = along_y(values, jnp.concatenate(halo, axis=0), lane, field == 0)
            for part, result in zip((0, 1, 2) if field == 0 else (2 + field,), results):
                rows_ref[side, layer, part] = result
    for side in range(2):
        edge = zfirst if side == 0 else zlast
        for layer in range(2):
            mirrored = 0 if side == 0 else zs - 1
            outer = layer == side

            def part_rows(part):
                ref = rows_ref.at[side, layer, part]
                return Rows([ref[pl.ds(TILE + t, TILE, stride=tiles), :] for t in range(tiles)], ref[0:TILE, :])

            twice, sloped = part_rows(1), part_rows(2)
            for part, values in zip((4, 5, 6), (twice.blur2(), twice.slope(), sloped.blur2())):
                for t in range(tiles):
                    rows = slice(t * TILE, t * TILE + TILE)
                    fill = -cross_ref[part, mirrored, rows] if outer else 0.0
                    near_ref[part, 2 * side + layer, rows] = jnp.where(edge, fill, values[t])
            if not outer:
                for part, source in enumerate((0, 3, 4, 5)):
                    for t, values in enumerate(part_rows(source).blur()):
                        near_ref[part, 2 * side + layer, t * TILE : t * TILE + TILE] = jnp.where(edge, 0.0, values)

    def load(part, z):
        if z < 0:
            return near_ref[part, z + 2]
        if z >= zs:
            return near_ref[part, z - zs + 2]
        return cross_ref[part, z]

    def behind(state, z):
        return shade(state, before_shade(load, z), [looked_ref[c, z] for c in range(4)], scale)

    zero = jnp.zeros((xs, 128), jnp.float32)
    state = behind(behind((zero + 1.0, zero, zero, zero, zero), 0), 1)
    passed = state[0]
    state = (
        passed * inner_ref[0],
        state[1] + passed * inner_ref[1],
        state[2] + passed * inner_ref[2],
        state[3] + passed * inner_ref[3],
        state[4] + inner_ref[4],
    )
    state = behind(behind(state, zs - 2), zs - 1)
    for c in range(4):
        for t in range(tiles):
            image_ref[c, pl.ds(t, TILE, stride=tiles), :] = state[1 + c][t * TILE : t * TILE + TILE]
    if len(out_refs) == 1:
        out_refs[0][...] = image_ref[...]
    else:
        part = xs // len(out_refs)
        for k, ref in enumerate(out_refs):
            ref[...] = image_ref[:, pl.ds(pl.multiple_of((lax.axis_index("gz") ^ k) * part, part), part), :]


def blend_kernel(near_ref, *refs):
    images, out_ref = refs[:-1], refs[-1]
    count = len(images)
    depths = [image[3] for image in images]
    colours = [jnp.zeros_like(depths[0])] * 3
    for k in range(count):
        prior = jnp.zeros_like(depths[0])
        for other in range(count):
            if other != k:
                prior += near_ref[k * count + other] * depths[other]
        through = jnp.exp(-prior)
        colours = [colours[c] + through * images[k][c] for c in range(3)]
    total = functools.reduce(jnp.add, depths)
    out_ref[0], out_ref[1], out_ref[2] = colours
    small = total * polynomial(EXPM1, total)
    out_ref[3] = jnp.where(total < 0.5, small, 1.0 - jnp.exp(-total))


def call(kernel, out_shape, specs, scratch=(), cost=1.0, name=None, limit=VMEM_LIMIT):
    where = {"s": pltpu.SMEM, "v": pltpu.VMEM, "a": pl.ANY}
    return pl.pallas_call(
        kernel,
        out_shape=out_shape,
        in_specs=[pl.BlockSpec(memory_space=where[s]) for s in specs],
        out_specs=jax.tree.map(lambda _: pl.BlockSpec(memory_space=pltpu.VMEM), out_shape),
        scratch_shapes=list(scratch),
        compiler_params=pltpu.CompilerParams(vmem_limit_bytes=limit),
        cost_estimate=pl.CostEstimate(flops=0, bytes_accessed=int(cost * 3.0e6), transcendentals=0),
        name=name,
    )


def swap_pairs(first, second, axis):
    count = lax.axis_size(axis)
    one = lax.ppermute(first, axis, [(i, i ^ 1) for i in range(count)])
    if count == 2:
        return one, one
    ends = [(0, 0), (count - 1, count - 1)]
    return one, lax.ppermute(second, axis, ends + [(i, i + 1 if i % 2 else i - 1) for i in range(1, count - 1)])


def on_device(fields, material, depth_order, table):
    _, zs, xs, ys = fields.shape
    nx, nz = lax.axis_size("gx"), lax.axis_size("gz")
    block = xs + TILE
    part = xs // nz
    swaps = nz in (2, 4)
    groups = -(-zs // GROUP)
    f32 = lambda *shape: jax.ShapeDtypeStruct(shape, jnp.float32)

    def side(even_high):
        high = (lax.axis_index("gx") % 2 == 0) == even_high
        tile = lax.dynamic_slice_in_dim(fields, jnp.where(high, xs - TILE, 0), TILE, axis=2)
        return call(functools.partial(rows_kernel, zs, even_high), f32(FACE, zs, ys), "v", name="x_rows")(tile)

    first = side(True)
    x_a, x_b = swap_pairs(first, side(False) if nx > 2 else None, "gx")
    fields, _ = lax.optimization_barrier((fields, first))
    strip = jnp.asarray(strip_matrix(ys))
    looked = call(
        functools.partial(lookup_kernel, zs, xs),
        f32(4, zs, xs, ys),
        "vv",
        [pltpu.VMEM((4, 128), jnp.float32)],
        cost=1.2,
        name="lookup",
    )(table, material)
    held, main, nearer = call(
        functools.partial(stage_kernel, zs, xs, swaps),
        (f32(4, zs, xs, ys), f32(groups, xs, 128), f32(nz * nz, 1, 128)),
        "sv",
        [pltpu.SemaphoreType.DMA((4,))],
        cost=1.0,
        name="stage",
    )(depth_order, fields)
    x_a, x_b, held, looked = lax.optimization_barrier((x_a, x_b, held, looked))

    halo, own = call(
        functools.partial(x_halo_kernel, zs, xs), (f32(4, zs, TILE, ys), f32(groups, block, 128)), "vvvv", name="x_halo"
    )(held, main, x_a, x_b)
    y_a, y_b = swap_pairs(own, own, "gy")
    rows, cell = call(
        functools.partial(cells_kernel, zs, xs),
        (f32(6, zs, xs, ys), jax.ShapeDtypeStruct((256, 3 * ys), jnp.bfloat16)),
        "v",
        cost=1.3,
        name="cells",
    )(held)
    cross = call(
        functools.partial(cross_kernel, zs, xs),
        f32(7, zs, xs, ys),
        "vvv",
        [pltpu.VMEM((6, zs, TILE, ys), jnp.float32)],
        cost=1.0,
        name="cross",
    )(rows, halo, cell)
    y_a, y_b, cross = lax.optimization_barrier((y_a, y_b, cross))

    faces = f32(FACE * xs + 3 * TILE, ys)
    merged, f_a, f_b = call(
        functools.partial(face_kernel, zs, xs), (f32(groups, block, 128), faces, faces), "vvvvv", name="faces"
    )(held, halo, own, y_a, y_b)
    z_a, z_b = swap_pairs(f_a, f_b, "gz")

    scale = 2.0 / (zs * nz)
    inner, full = call(
        functools.partial(inner_kernel, zs, xs, scale),
        (f32(5, xs, ys), f32(7, zs, xs, ys)),
        "vvvv",
        [pltpu.VMEM((3, groups, xs, 128), jnp.float32), pltpu.VMEM((6, 2, xs, ys), jnp.float32)],
        cost=4.0,
        name="inner",
    )(cross, merged, looked, strip)

    images = call(
        functools.partial(edge_kernel, zs, xs, scale),
        [f32(4, part, ys)] * nz if swaps else [f32(4, xs, ys)],
        "vvvvv",
        [
            pltpu.VMEM((7, 4, xs, ys), jnp.float32),
            pltpu.VMEM((2, 2, 6, block, ys), jnp.float32),
            pltpu.VMEM((4, xs, ys), jnp.float32),
        ],
        name="edges",
    )(z_a, z_b, full, looked, inner)

    if swaps:
        mine = [images[0]]
        for k in range(1, nz):
            mine.append(lax.ppermute(images[k], "gz", [(i, i ^ k) for i in range(nz)]))
    else:
        stacked = lax.all_to_all(images[0].reshape(4, nz, part, ys), "gz", split_axis=1, concat_axis=1)
        mine = [stacked[:, b] for b in range(nz)]
    return call(blend_kernel, f32(4, part, ys), "v" + "v" * nz, name="blend")(nearer, *mine)


def solution(mesh):
    return jax.shard_map(
        on_device,
        mesh=mesh,
        in_specs=(P(None, "gz", "gx", "gy"), P("gz", "gx", "gy"), P(), P()),
        out_specs=P(None, ("gx", "gz"), "gy"),
        check_vma=False,
    )
```

```python
import functools

import jax
import jax.numpy as jnp
import ml_dtypes
import numpy as np
from jax import lax
from jax.experimental import pallas as pl
from jax.experimental.pallas import tpu as pltpu
from jax.sharding import PartitionSpec as P

VMEM_LIMIT = 40 * 1024 * 1024
GROUP = 12
SLOT = 10
TILE = 8
FACE = 5
SPAN = 24

LOG1P = (
    0.9999995186059567, -0.49996356582563917, 0.33265255844036573, -0.24453388969978707, 0.17659864766821842,
    -0.10679931280022417, 0.043659288844443055, -0.008466410404849948,
)
EXPM1 = (
    1.0, -0.4999995231628418, 0.1666584461927414, -0.04160914570093155, 0.00814302358776331, -0.0010865303920581937,
)


def polynomial(coefficients, value):
    terms = list(coefficients)
    power = value
    while len(terms) > 1:
        paired = [terms[k] + terms[k + 1] * power for k in range(0, len(terms) - 1, 2)]
        terms = paired + ([terms[-1]] if len(terms) % 2 else [])
        power = power * power if len(terms) > 1 else power
    return terms[0]


BLUR, BLUR2, SLOPE = {-1: 1, 0: 2, 1: 1}, {-2: 1, -1: 4, 0: 6, 1: 4, 2: 1}, {-2: -1, -1: -2, 1: 2, 2: 1}


def strip_matrix(ysize):
    strips = np.zeros((128, 7 * ysize), np.float32)
    for block, (taps, field) in enumerate([(BLUR, f) for f in range(4)] + [(BLUR2, 0), (SLOPE, 0), (BLUR2, 0)]):
        first = slot_of(field)[0]
        outside = {-2: 0, -1: 1, ysize: 2, ysize + 1: 3} if field == 0 else {-1: first, ysize: first + 1}
        for out in range(ysize):
            for off, weight in taps.items():
                if not 0 <= out + off < ysize:
                    strips[outside[out + off], block * ysize + out] = weight
    return np.concatenate([strips, strips], axis=0).astype(ml_dtypes.bfloat16)


def make_cell_weights(out_ref):
    off = lax.broadcasted_iota(jnp.int32, (128, 128), 0) - lax.broadcasted_iota(jnp.int32, (128, 128), 1)
    for block, taps in enumerate((BLUR, BLUR2, SLOPE)):
        weights = jnp.zeros((128, 128), jnp.float32)
        for step, weight in taps.items():
            weights = jnp.where(off == step, float(weight), weights)
        for half in range(2):
            out_ref[128 * half : 128 * half + 128, 128 * block : 128 * block + 128] = weights.astype(jnp.bfloat16)


def halves(values):
    high = values.astype(jnp.bfloat16)
    low = (values - high.astype(jnp.float32)).astype(jnp.bfloat16)
    return jnp.concatenate([high, low], axis=1)


def place_of(axis):
    at = lax.axis_index(axis)
    return at == 0, at == lax.axis_size(axis) - 1, lax.rem(at, 2) == 1


def rows_kernel(zs, xs, even_high, fields_ref, out_ref):
    high = (lax.rem(lax.axis_index("gx"), 2) == 0) == even_high
    for group in range(FACE):
        field = max(group - 1, 0)
        rows = fields_ref.at[field].reshape(zs * xs, 128)
        low_row = group if group < 2 else 0
        high_row = xs - 2 + group if group < 2 else xs - 1
        out_ref[group] = rows[pl.ds(jnp.where(high, high_row, low_row), zs, stride=xs), :]


def slot_of(field):
    return (0, 4) if field == 0 else (2 + 2 * field, 2)


def pack_strips(load, layers, lane, rows):
    packed = jnp.zeros((rows, 128), jnp.float32)
    for k, z in enumerate(layers):
        for field in range(4):
            first, count = slot_of(field)
            start = SLOT * k + first
            values = pltpu.roll(load(field, z), (start + count // 2) % 128, 1)
            packed = jnp.where((lane >= start) & (lane < start + count), values, packed)
    return packed


def pack_kernel(zs, xs, fields_ref, pack_ref):
    lane = lax.broadcasted_iota(jnp.int32, (1, 128), 1)
    for group in range(pack_ref.shape[0]):
        layers = range(group * GROUP, min(zs, group * GROUP + GROUP))
        pack_ref[group] = pack_strips(lambda f, z: fields_ref[f, z], layers, lane, xs)


def lookup_kernel(zs, xs, table_ref, ids_ref, looked_ref, tables_ref):
    tables_ref[...] = jnp.zeros_like(tables_ref)
    tables_ref[:, 0 : table_ref.shape[1]] = table_ref[...]
    tables = [jnp.broadcast_to(tables_ref[c : c + 1, :], (TILE, 128)) for c in range(4)]
    each = 8
    tiles = xs // TILE

    def step(k, carry):
        for j in range(each):
            z = k * each + j
            for t in range(tiles):
                ids = ids_ref[z, pl.ds(t, TILE, stride=tiles), :]
                for c in range(4):
                    looked_ref[c, z, t * TILE : t * TILE + TILE, :] = jnp.take_along_axis(
                        tables[c], ids, axis=1, mode="promise_in_bounds"
                    )
        return carry

    lax.fori_loop(0, zs // each, step, 0)


def x_halo_kernel(zs, xs, fields_ref, main_ref, xa_ref, xb_ref, halo_ref, pack_ref):
    first, last, odd = place_of("gx")
    halo_ref[...] = jnp.zeros_like(halo_ref)
    for field in range(4):
        tiles = halo_ref.at[field].reshape(zs * TILE, 128)
        own = fields_ref.at[field].reshape(zs * xs, 128)
        at = 0 if field == 0 else 1 + field
        below = jnp.where(odd, xa_ref[1 + field], xb_ref[1 + field])
        above = jnp.where(odd, xb_ref[at], xa_ref[at])
        tiles[pl.ds(0, zs, stride=TILE), :] = jnp.where(first, 0.0, below)
        tiles[pl.ds(TILE - 1, zs, stride=TILE), :] = jnp.where(last, 0.0, above)
        if field == 0:
            low, high = own[pl.ds(0, zs, stride=xs), :], own[pl.ds(xs - 1, zs, stride=xs), :]
            tiles[pl.ds(1, zs, stride=TILE), :] = jnp.where(first, -low, jnp.where(odd, xa_ref[0], xb_ref[0]))
            tiles[pl.ds(TILE - 2, zs, stride=TILE), :] = jnp.where(last, -high, jnp.where(odd, xb_ref[1], xa_ref[1]))
    lane = lax.broadcasted_iota(jnp.int32, (1, 128), 1)
    for group in range(pack_ref.shape[0]):
        layers = range(group * GROUP, min(zs, group * GROUP + GROUP))
        pack_ref[group, 0:TILE] = pack_strips(lambda f, z: halo_ref[f, z], layers, lane, TILE)
        pack_ref[group, TILE:] = main_ref[group]


def face_kernel(zs, xs, fields_ref, halo_ref, own_ref, ya_ref, yb_ref, merged_ref, fa_ref, fb_ref):
    yfirst, ylast, yodd = place_of("gy")
    zodd = place_of("gz")[2]
    block = xs + TILE
    lane = lax.broadcasted_iota(jnp.int32, (1, 128), 1)
    place = lax.rem(lane, SLOT)
    from_left = (place < 2) | ((place >= 4) & (lax.rem(place, 2) == 0))
    for group in range(own_ref.shape[0]):
        own = own_ref[group]
        fill_left = jnp.where(place == 0, -pltpu.roll(own, 126, 1), 0.0)
        fill_right = jnp.where(place == 3, -pltpu.roll(own, 2, 1), 0.0)
        first, second = ya_ref[group], yb_ref[group]
        left = jnp.where(yfirst, fill_left, jnp.where(yodd, first, second))
        right = jnp.where(ylast, fill_right, jnp.where(yodd, second, first))
        merged_ref[group] = jnp.where(from_left, left, right)

    sub = lax.broadcasted_iota(jnp.int32, (TILE, 1), 0)
    ends = (sub < 2) | (sub >= TILE - 2)

    def put(start, low, high):
        for out_ref, swapped in ((fa_ref, False), (fb_ref, True)):
            out_ref[start : start + low.shape[0], :] = jnp.where(zodd != swapped, low, high)

    for j in range(FACE):
        put(j * xs, fields_ref[max(j - 1, 0), j if j < 2 else 0], fields_ref[max(j - 1, 0), zs - 2 + j if j < 2 else zs - 1])

    def density_rows(z):
        return jnp.where(ends, halo_ref[0, z], pltpu.roll(halo_ref[0, z + 1], TILE // 2, 0))

    def field_rows(z):
        rows = [pltpu.roll(halo_ref[f, z], 2 * f - 2, 0) if f > 1 else halo_ref[f, z] for f in (1, 2, 3)]
        mixed = jnp.where((sub == 0) | (sub == TILE - 1), rows[0], rows[1])
        return jnp.where((sub == 3) | (sub == 4), rows[2], mixed)

    def strips(z):
        group, k = divmod(z, GROUP)
        packed = jnp.zeros((TILE, 128), jnp.float32)
        for t in range(block // TILE):
            moved = pltpu.roll(merged_ref[group, t * TILE : t * TILE + TILE], (SPAN * t - SLOT * k) % 128, 1)
            packed = jnp.where((lane >= SPAN * t) & (lane < SPAN * t + SPAN), moved, packed)
        return packed

    put(FACE * xs, density_rows(0), density_rows(zs - 2))
    put(FACE * xs + TILE, field_rows(0), field_rows(zs - 1))
    put(FACE * xs + 2 * TILE, strips(0), strips(zs - 2))


def along_y(values, halo, lane, density):
    def shifted(off):
        mixed = jnp.where(lane >= 128 - off if off > 0 else lane < -off, halo, values)
        return pltpu.roll(mixed, off % 128, 1)

    m1, p1 = shifted(1), shifted(-1)
    near = m1 + p1
    blur = near + 2.0 * values
    if not density:
        return (blur,)
    m2, p2 = shifted(2), shifted(-2)
    return blur, (m2 + p2) + 4.0 * near + 6.0 * values, (p2 - m2) + 2.0 * (p1 - m1)


class Rows:
    def __init__(self, tiles, halo):
        self.tiles, self.halo = list(tiles), halo
        self.sub = lax.broadcasted_iota(jnp.int32, (TILE, 1), 0)
        self.made = {}

    def row(self, t):
        count = len(self.tiles)
        if 0 <= t < count:
            return self.tiles[t]
        if t not in self.made:
            down = t < 0
            step = -t - 1 if down else t - count
            halo = self.halo if step == 0 else pltpu.roll(self.halo, TILE - 1 if down else 1, 0)
            inner = pltpu.roll(self.tiles[t % count], 1 if down else TILE - 1, 0)
            self.made[t] = jnp.where(self.sub == (0 if down else TILE - 1), halo, inner)
        return self.made[t]

    def pair(self, level, t):
        if level == 0:
            return self.row(t)
        if (level, t) not in self.made:
            self.made[level, t] = self.pair(level - 1, t) + self.pair(level - 1, t + 1)
        return self.made[level, t]

    def blur(self):
        return [self.pair(2, t - 1) for t in range(len(self.tiles))]

    def blur2(self):
        return [self.pair(4, t - 2) for t in range(len(self.tiles))]

    def slope(self):
        return [self.pair(2, t) - self.pair(2, t - 2) for t in range(len(self.tiles))]


def cells_kernel(zs, xs, fields_ref, out_ref, cell_ref):
    each, tiles = 8, xs // TILE
    make_cell_weights(cell_ref)

    def step(k, carry):
        first = k * each
        for field in range(4):
            rows = [
                fields_ref[field, first + j, pl.ds(t, TILE, stride=tiles), :] for j in range(each) for t in range(tiles)
            ]
            weights = cell_ref[...] if field == 0 else cell_ref[:, 0:128]
            result = jnp.dot(halves(jnp.concatenate(rows, axis=0)), weights, preferred_element_type=jnp.float32)
            for part in (0, 1, 2) if field == 0 else (2 + field,):
                columns = slice(128 * part, 128 * part + 128) if field == 0 else slice(0, 128)
                out_ref[part, pl.ds(first, each)] = result[:, columns].reshape(each, xs, 128)
        return carry

    lax.fori_loop(0, zs // each, step, 0)


def cross_kernel(zs, xs, peers, order_ref, rows_ref, halo_ref, cell_ref, out_ref, near_ref, edge_ref):
    each, tiles = 4, xs // TILE
    iz, count = lax.axis_index("gz"), lax.axis_size("gz")
    ranks = [order_ref[iz ^ k if peers else k] for k in range(count)]
    for k in range(count):
        for other in range(count):
            nearer = jnp.where(ranks[other] < ranks[k], 1.0, 0.0)
            near_ref[k * count + other] = jnp.full((1, 128), nearer, jnp.float32)
    for field in range(4):
        weights = cell_ref[...] if field == 0 else cell_ref[:, 0:128]
        result = jnp.dot(
            halves(halo_ref[field].reshape(zs * TILE, 128)), weights, preferred_element_type=jnp.float32
        )
        for part in (0, 1, 2) if field == 0 else (2 + field,):
            columns = slice(128 * part, 128 * part + 128) if field == 0 else slice(0, 128)
            edge_ref[part] = result[:, columns].reshape(zs, TILE, 128)

    def step(k, carry):
        for j in range(each):
            z = k * each + j

            def part_rows(part):
                return Rows([rows_ref[part, z, t * TILE : t * TILE + TILE, :] for t in range(tiles)], edge_ref[part, z])

            twice, sloped = part_rows(1), part_rows(2)
            results = [part_rows(part).blur() for part in (0, 3, 4, 5)]
            results += [twice.blur2(), twice.slope(), sloped.blur2()]
            for part, values in enumerate(results):
                for t in range(tiles):
                    out_ref[part, z, t * TILE : t * TILE + TILE, :] = values[t]
        return carry

    lax.fori_loop(0, zs // each, step, 0)


def before_shade(load, z):
    def blur(part):
        return load(part, z - 1) + load(part, z + 1) + 2.0 * load(part, z)

    def blur2(part):
        return (load(part, z - 2) + load(part, z + 2)) + 4.0 * (load(part, z - 1) + load(part, z + 1)) + 6.0 * load(part, z)

    unit = 1.0 / 2048.0
    near = load(4, z + 1) - load(4, z - 1)
    grad_z = (load(4, z + 2) - load(4, z - 2)) + (near + near)
    grad_x = blur2(5)
    grad_y = blur2(6)
    facing = jnp.abs((0.8 * unit) * (grad_z + grad_y) + (0.4 * unit) * grad_x)
    square = grad_z * grad_z + grad_x * grad_x + grad_y * grad_y
    shading = 0.3 + facing * lax.rsqrt(square * (unit * unit) + 0.0025)
    density = (3.0 / 64.0) * blur(0)
    return [density, jnp.exp(-jnp.abs(density)), shading] + [blur(1 + c) for c in range(3)]


def shade(state, taken, looked, scale):
    density, t, shading = taken[:3]
    soft = jnp.maximum(density, 0.0) + t * polynomial(LOG1P, t)
    extinct = looked[3] * (soft * scale)
    passed, total, depth = state[0], state[1:4], state[4]
    weight = passed * (extinct * polynomial(EXPM1, extinct))
    lit = weight * shading
    colours = [
        total[c] + (looked[c] * lit) * (1.0 + 0.5 * jnp.tanh((1.0 / 64.0) * taken[3 + c])) for c in range(3)
    ]
    return (passed - weight, *colours, depth + extinct)


def inner_kernel(zs, xs, scale, cross_ref, merged_ref, looked_ref, strip_ref, inner_ref, full_ref, filtered_ref, taken_ref):
    tiles, each = xs // TILE, 8
    for group in range(merged_ref.shape[0]):
        rows = Rows([merged_ref[group, pl.ds(TILE + t, TILE, stride=tiles), :] for t in range(tiles)], merged_ref[group, 0:TILE])
        for k, values in enumerate((rows.blur(), rows.blur2(), rows.slope())):
            for t in range(tiles):
                filtered_ref[k, group, t * TILE : t * TILE + TILE, :] = values[t]

    def strip_step(step, carry):
        first = step * each
        for k, parts in enumerate(((0, 1, 2, 3), (4, 6), (5,))):
            strips = []
            for j in range(each):
                group = lax.div(first + j, GROUP)
                slot = first + j - group * GROUP
                strips.append(pltpu.roll(filtered_ref[k, group], lax.rem(128 - SLOT * slot, 128), 1))
            columns = slice((0, 512, 768)[k], (512, 768, 896)[k])
            result = jnp.dot(
                halves(jnp.concatenate(strips, axis=0)), strip_ref[:, columns], preferred_element_type=jnp.float32
            )
            for n, part in enumerate(parts):
                share = result[:, 128 * n : 128 * n + 128].reshape(each, xs, 128)
                full_ref[part, pl.ds(first, each)] = cross_ref[part, pl.ds(first, each)] + share
        return carry

    lax.fori_loop(0, zs // each, strip_step, 0)

    pairs = (zs - 4) // 2

    def take(step):
        for j in range(2):
            z = 2 + 2 * step + j
            for k, values in enumerate(before_shade(lambda part, z: full_ref[part, z], z)):
                taken_ref[k, j] = values

    def advance(step, state):
        for j in range(2):
            looked = [looked_ref[c, 2 + 2 * step + j] for c in range(4)]
            state = shade(state, [taken_ref[k, j] for k in range(6)], looked, scale)
        return state

    def z_step(step, state):
        state = advance(step, state)
        take(step + 1)
        return state

    zero = jnp.zeros((xs, 128), jnp.float32)
    take(0)
    state = lax.fori_loop(0, pairs - 1, z_step, (zero + 1.0, zero, zero, zero, zero))
    for k, values in enumerate(advance(pairs - 1, state)):
        inner_ref[k] = values


def edge_kernel(zs, xs, scale, fa_ref, fb_ref, cross_ref, looked_ref, inner_ref, *rest):
    out_refs, (near_ref, rows_ref, image_ref) = rest[:-3], rest[-3:]
    zfirst, zlast, zodd = place_of("gz")
    block = xs + TILE
    tiles = xs // TILE
    lane = lax.broadcasted_iota(jnp.int32, (1, 128), 1)
    for side in range(2):
        first, second = (fa_ref, fb_ref) if side == 0 else (fb_ref, fa_ref)

        def face(start, count):
            return jnp.where(zodd, first[start : start + count, :], second[start : start + count, :])

        ends = [face(FACE * xs, TILE), face(FACE * xs + TILE, TILE)]
        strips = face(FACE * xs + 2 * TILE, TILE)
        for j in range(FACE):
            field = max(j - 1, 0)
            layer = j if j < 2 else (1 if side == 0 else 0)
            turned = TILE // 2 * j if j < 2 else 2 * field - 2
            outer_rows = ends[min(field, 1)]
            if turned:
                outer_rows = pltpu.roll(outer_rows, TILE - turned, 0)
            at_lane = SLOT * layer + slot_of(field)[0]
            own = 126 if field == 0 else 127
            halo = [pltpu.roll(strips, (own - at_lane - SPAN * t) % 128, 1) for t in range(block // TILE)]
            values = jnp.concatenate([outer_rows, face(j * xs, xs)], axis=0)
            results = along_y(values, jnp.concatenate(halo, axis=0), lane, field == 0)
            for part, result in zip((0, 1, 2) if field == 0 else (2 + field,), results):
                rows_ref[side, layer, part] = result
    for side in range(2):
        edge = zfirst if side == 0 else zlast
        for layer in range(2):
            mirrored = 0 if side == 0 else zs - 1
            outer = layer == side

            def part_rows(part):
                ref = rows_ref.at[side, layer, part]
                return Rows([ref[pl.ds(TILE + t, TILE, stride=tiles), :] for t in range(tiles)], ref[0:TILE, :])

            twice, sloped = part_rows(1), part_rows(2)
            for part, values in zip((4, 5, 6), (twice.blur2(), twice.slope(), sloped.blur2())):
                for t in range(tiles):
                    rows = slice(t * TILE, t * TILE + TILE)
                    fill = -cross_ref[part, mirrored, rows] if outer else 0.0
                    near_ref[part, 2 * side + layer, rows] = jnp.where(edge, fill, values[t])
            if not outer:
                for part, source in enumerate((0, 3, 4, 5)):
                    for t, values in enumerate(part_rows(source).blur()):
                        near_ref[part, 2 * side + layer, t * TILE : t * TILE + TILE] = jnp.where(edge, 0.0, values)

    def load(part, z):
        if z < 0:
            return near_ref[part, z + 2]
        if z >= zs:
            return near_ref[part, z - zs + 2]
        return cross_ref[part, z]

    def behind(state, z):
        return shade(state, before_shade(load, z), [looked_ref[c, z] for c in range(4)], scale)

    zero = jnp.zeros((xs, 128), jnp.float32)
    state = behind(behind((zero + 1.0, zero, zero, zero, zero), 0), 1)
    passed = state[0]
    state = (
        passed * inner_ref[0],
        state[1] + passed * inner_ref[1],
        state[2] + passed * inner_ref[2],
        state[3] + passed * inner_ref[3],
        state[4] + inner_ref[4],
    )
    state = behind(behind(state, zs - 2), zs - 1)
    for c in range(4):
        for t in range(tiles):
            image_ref[c, pl.ds(t, TILE, stride=tiles), :] = state[1 + c][t * TILE : t * TILE + TILE]
    if len(out_refs) == 1:
        out_refs[0][...] = image_ref[...]
    else:
        part = xs // len(out_refs)
        for k, ref in enumerate(out_refs):
            ref[...] = image_ref[:, pl.ds(pl.multiple_of((lax.axis_index("gz") ^ k) * part, part), part), :]


def blend_kernel(near_ref, *refs):
    images, out_ref = refs[:-1], refs[-1]
    count = len(images)
    depths = [image[3] for image in images]
    colours = [jnp.zeros_like(depths[0])] * 3
    for k in range(count):
        prior = jnp.zeros_like(depths[0])
        for other in range(count):
            if other != k:
                prior += near_ref[k * count + other] * depths[other]
        through = jnp.exp(-prior)
        colours = [colours[c] + through * images[k][c] for c in range(3)]
    total = functools.reduce(jnp.add, depths)
    out_ref[0], out_ref[1], out_ref[2] = colours
    small = total * polynomial(EXPM1, total)
    out_ref[3] = jnp.where(total < 0.5, small, 1.0 - jnp.exp(-total))


def call(kernel, out_shape, specs, scratch=(), cost=1.0, name=None, limit=VMEM_LIMIT):
    where = {"s": pltpu.SMEM, "v": pltpu.VMEM, "a": pl.ANY}
    return pl.pallas_call(
        kernel,
        out_shape=out_shape,
        in_specs=[pl.BlockSpec(memory_space=where[s]) for s in specs],
        out_specs=jax.tree.map(lambda _: pl.BlockSpec(memory_space=pltpu.VMEM), out_shape),
        scratch_shapes=list(scratch),
        compiler_params=pltpu.CompilerParams(vmem_limit_bytes=limit),
        cost_estimate=pl.CostEstimate(flops=0, bytes_accessed=int(cost * 3.0e6), transcendentals=0),
        name=name,
    )


def swap_pairs(first, second, axis):
    count = lax.axis_size(axis)
    one = lax.ppermute(first, axis, [(i, i ^ 1) for i in range(count)])
    if count == 2:
        return one, one
    return one, lax.ppermute(second, axis, [(i, i + 1 if i % 2 else i - 1) for i in range(1, count - 1)])


def on_device(fields, material, depth_order, table):
    _, zs, xs, ys = fields.shape
    nx, nz = lax.axis_size("gx"), lax.axis_size("gz")
    block = xs + TILE
    part = xs // nz
    swaps = nz in (2, 4)
    groups = -(-zs // GROUP)
    f32 = lambda *shape: jax.ShapeDtypeStruct(shape, jnp.float32)

    def side(even_high):
        return call(functools.partial(rows_kernel, zs, xs, even_high), f32(FACE, zs, ys), "v", name="x_rows")(fields)

    x_a, x_b = swap_pairs(side(True), side(False) if nx > 2 else None, "gx")
    strip = jnp.asarray(strip_matrix(ys))
    looked = call(
        functools.partial(lookup_kernel, zs, xs),
        f32(4, zs, xs, ys),
        "vv",
        [pltpu.VMEM((4, 128), jnp.float32)],
        cost=1.2,
        name="lookup",
    )(table, material)
    main = call(functools.partial(pack_kernel, zs, xs), f32(groups, xs, 128), "v", cost=0.7, name="pack")(fields)
    x_a, x_b, main, looked = lax.optimization_barrier((x_a, x_b, main, looked))

    halo, own = call(
        functools.partial(x_halo_kernel, zs, xs), (f32(4, zs, TILE, ys), f32(groups, block, 128)), "vvvv", name="x_halo"
    )(fields, main, x_a, x_b)
    y_a, y_b = swap_pairs(own, own, "gy")
    rows, cell = call(
        functools.partial(cells_kernel, zs, xs),
        (f32(6, zs, xs, ys), jax.ShapeDtypeStruct((256, 3 * ys), jnp.bfloat16)),
        "v",
        cost=1.3,
        name="cells",
    )(fields)
    cross, nearer = call(
        functools.partial(cross_kernel, zs, xs, swaps),
        (f32(7, zs, xs, ys), f32(nz * nz, 1, 128)),
        "svvv",
        [pltpu.VMEM((6, zs, TILE, ys), jnp.float32)],
        cost=1.0,
        name="cross",
    )(depth_order, rows, halo, cell)
    y_a, y_b, cross = lax.optimization_barrier((y_a, y_b, cross))

    faces = f32(FACE * xs + 3 * TILE, ys)
    merged, f_a, f_b = call(
        functools.partial(face_kernel, zs, xs), (f32(groups, block, 128), faces, faces), "vvvvv", name="faces"
    )(fields, halo, own, y_a, y_b)
    z_a, z_b = swap_pairs(f_a, f_b, "gz")

    scale = 2.0 / (zs * nz)
    inner, full = call(
        functools.partial(inner_kernel, zs, xs, scale),
        (f32(5, xs, ys), f32(7, zs, xs, ys)),
        "vvvv",
        [pltpu.VMEM((3, groups, xs, 128), jnp.float32), pltpu.VMEM((6, 2, xs, ys), jnp.float32)],
        cost=4.0,
        name="inner",
    )(cross, merged, looked, strip)

    images = call(
        functools.partial(edge_kernel, zs, xs, scale),
        [f32(4, part, ys)] * nz if swaps else [f32(4, xs, ys)],
        "vvvvv",
        [
            pltpu.VMEM((7, 4, xs, ys), jnp.float32),
            pltpu.VMEM((2, 2, 6, block, ys), jnp.float32),
            pltpu.VMEM((4, xs, ys), jnp.float32),
        ],
        name="edges",
    )(z_a, z_b, full, looked, inner)

    if swaps:
        mine = [images[0]]
        for k in range(1, nz):
            mine.append(lax.ppermute(images[k], "gz", [(i, i ^ k) for i in range(nz)]))
    else:
        stacked = lax.all_to_all(images[0].reshape(4, nz, part, ys), "gz", split_axis=1, concat_axis=1)
        mine = [stacked[:, b] for b in range(nz)]
    return call(blend_kernel, f32(4, part, ys), "v" + "v" * nz, name="blend")(nearer, *mine)


def solution(mesh):
    return jax.shard_map(
        on_device,
        mesh=mesh,
        in_specs=(P(None, "gz", "gx", "gy"), P("gz", "gx", "gy"), P(), P()),
        out_specs=P(None, ("gx", "gz"), "gy"),
        check_vma=False,
    )
```

```python
import functools

import jax
import jax.numpy as jnp
import ml_dtypes
import numpy as np
from jax import lax
from jax.experimental import pallas as pl
from jax.experimental.pallas import tpu as pltpu
from jax.sharding import PartitionSpec as P

VMEM_LIMIT = 40 * 1024 * 1024
GROUP = 12
SLOT = 10
TILE = 8
FACE = 5
SPAN = 24

LOG1P = (
    0.9999995186059567, -0.49996356582563917, 0.33265255844036573, -0.24453388969978707, 0.17659864766821842,
    -0.10679931280022417, 0.043659288844443055, -0.008466410404849948,
)
EXPM1 = (
    1.0, -0.4999995231628418, 0.1666584461927414, -0.04160914570093155, 0.00814302358776331, -0.0010865303920581937,
)


def polynomial(coefficients, value):
    terms = list(coefficients)
    power = value
    while len(terms) > 1:
        paired = [terms[k] + terms[k + 1] * power for k in range(0, len(terms) - 1, 2)]
        terms = paired + ([terms[-1]] if len(terms) % 2 else [])
        power = power * power if len(terms) > 1 else power
    return terms[0]


BLUR, BLUR2, SLOPE = {-1: 1, 0: 2, 1: 1}, {-2: 1, -1: 4, 0: 6, 1: 4, 2: 1}, {-2: -1, -1: -2, 1: 2, 2: 1}


def strip_matrix(ysize):
    strips = np.zeros((128, 7 * ysize), np.float32)
    for block, (taps, field) in enumerate([(BLUR, f) for f in range(4)] + [(BLUR2, 0), (SLOPE, 0), (BLUR2, 0)]):
        first = slot_of(field)[0]
        outside = {-2: 0, -1: 1, ysize: 2, ysize + 1: 3} if field == 0 else {-1: first, ysize: first + 1}
        for out in range(ysize):
            for off, weight in taps.items():
                if not 0 <= out + off < ysize:
                    strips[outside[out + off], block * ysize + out] = weight
    return np.concatenate([strips, strips], axis=0).astype(ml_dtypes.bfloat16)


def make_cell_weights(out_ref):
    off = lax.broadcasted_iota(jnp.int32, (128, 128), 0) - lax.broadcasted_iota(jnp.int32, (128, 128), 1)
    for block, taps in enumerate((BLUR, BLUR2, SLOPE)):
        weights = jnp.zeros((128, 128), jnp.float32)
        for step, weight in taps.items():
            weights = jnp.where(off == step, float(weight), weights)
        for half in range(2):
            out_ref[128 * half : 128 * half + 128, 128 * block : 128 * block + 128] = weights.astype(jnp.bfloat16)


def halves(values):
    high = values.astype(jnp.bfloat16)
    low = (values - high.astype(jnp.float32)).astype(jnp.bfloat16)
    return jnp.concatenate([high, low], axis=1)


def place_of(axis):
    at = lax.axis_index(axis)
    return at == 0, at == lax.axis_size(axis) - 1, lax.rem(at, 2) == 1


def rows_kernel(zs, xs, even_high, fields_ref, out_ref):
    high = (lax.rem(lax.axis_index("gx"), 2) == 0) == even_high
    for group in range(FACE):
        field = max(group - 1, 0)
        rows = fields_ref.at[field].reshape(zs * xs, 128)
        low_row = group if group < 2 else 0
        high_row = xs - 2 + group if group < 2 else xs - 1
        out_ref[group] = rows[pl.ds(jnp.where(high, high_row, low_row), zs, stride=xs), :]


def slot_of(field):
    return (0, 4) if field == 0 else (2 + 2 * field, 2)


def pack_strips(load, layers, lane, rows):
    packed = jnp.zeros((rows, 128), jnp.float32)
    for k, z in enumerate(layers):
        for field in range(4):
            first, count = slot_of(field)
            start = SLOT * k + first
            values = pltpu.roll(load(field, z), (start + count // 2) % 128, 1)
            packed = jnp.where((lane >= start) & (lane < start + count), values, packed)
    return packed


def pack_kernel(zs, xs, fields_ref, pack_ref):
    lane = lax.broadcasted_iota(jnp.int32, (1, 128), 1)
    for group in range(pack_ref.shape[0]):
        layers = range(group * GROUP, min(zs, group * GROUP + GROUP))
        pack_ref[group] = pack_strips(lambda f, z: fields_ref[f, z], layers, lane, xs)


def lookup_kernel(zs, xs, peers, order_ref, table_ref, ids_ref, looked_ref, near_ref, tables_ref):
    iz, count = lax.axis_index("gz"), lax.axis_size("gz")
    ranks = [order_ref[iz ^ k if peers else k] for k in range(count)]
    for k in range(count):
        for other in range(count):
            nearer = jnp.where(ranks[other] < ranks[k], 1.0, 0.0)
            near_ref[k * count + other] = jnp.full((1, 128), nearer, jnp.float32)
    tables_ref[...] = jnp.zeros_like(tables_ref)
    tables_ref[:, 0 : table_ref.shape[1]] = table_ref[...]
    tables = [jnp.broadcast_to(tables_ref[c : c + 1, :], (TILE, 128)) for c in range(4)]
    each = 8
    tiles = xs // TILE

    def step(k, carry):
        for j in range(each):
            z = k * each + j
            for t in range(tiles):
                ids = ids_ref[z, pl.ds(t, TILE, stride=tiles), :]
                for c in range(4):
                    looked_ref[c, z, t * TILE : t * TILE + TILE, :] = jnp.take_along_axis(
                        tables[c], ids, axis=1, mode="promise_in_bounds"
                    )
        return carry

    lax.fori_loop(0, zs // each, step, 0)


def x_halo_kernel(zs, xs, fields_ref, main_ref, xa_ref, xb_ref, halo_ref, pack_ref):
    first, last, odd = place_of("gx")
    halo_ref[...] = jnp.zeros_like(halo_ref)
    for field in range(4):
        tiles = halo_ref.at[field].reshape(zs * TILE, 128)
        own = fields_ref.at[field].reshape(zs * xs, 128)
        at = 0 if field == 0 else 1 + field
        below = jnp.where(odd, xa_ref[1 + field], xb_ref[1 + field])
        above = jnp.where(odd, xb_ref[at], xa_ref[at])
        tiles[pl.ds(0, zs, stride=TILE), :] = jnp.where(first, 0.0, below)
        tiles[pl.ds(TILE - 1, zs, stride=TILE), :] = jnp.where(last, 0.0, above)
        if field == 0:
            low, high = own[pl.ds(0, zs, stride=xs), :], own[pl.ds(xs - 1, zs, stride=xs), :]
            tiles[pl.ds(1, zs, stride=TILE), :] = jnp.where(first, -low, jnp.where(odd, xa_ref[0], xb_ref[0]))
            tiles[pl.ds(TILE - 2, zs, stride=TILE), :] = jnp.where(last, -high, jnp.where(odd, xb_ref[1], xa_ref[1]))
    lane = lax.broadcasted_iota(jnp.int32, (1, 128), 1)
    for group in range(pack_ref.shape[0]):
        layers = range(group * GROUP, min(zs, group * GROUP + GROUP))
        pack_ref[group, 0:TILE] = pack_strips(lambda f, z: halo_ref[f, z], layers, lane, TILE)
        pack_ref[group, TILE:] = main_ref[group]


def face_kernel(zs, xs, fields_ref, halo_ref, own_ref, ya_ref, yb_ref, merged_ref, fa_ref, fb_ref):
    yfirst, ylast, yodd = place_of("gy")
    zodd = place_of("gz")[2]
    block = xs + TILE
    lane = lax.broadcasted_iota(jnp.int32, (1, 128), 1)
    place = lax.rem(lane, SLOT)
    from_left = (place < 2) | ((place >= 4) & (lax.rem(place, 2) == 0))
    for group in range(own_ref.shape[0]):
        own = own_ref[group]
        fill_left = jnp.where(place == 0, -pltpu.roll(own, 126, 1), 0.0)
        fill_right = jnp.where(place == 3, -pltpu.roll(own, 2, 1), 0.0)
        first, second = ya_ref[group], yb_ref[group]
        left = jnp.where(yfirst, fill_left, jnp.where(yodd, first, second))
        right = jnp.where(ylast, fill_right, jnp.where(yodd, second, first))
        merged_ref[group] = jnp.where(from_left, left, right)

    sub = lax.broadcasted_iota(jnp.int32, (TILE, 1), 0)
    ends = (sub < 2) | (sub >= TILE - 2)

    def put(start, low, high):
        for out_ref, swapped in ((fa_ref, False), (fb_ref, True)):
            out_ref[start : start + low.shape[0], :] = jnp.where(zodd != swapped, low, high)

    for j in range(FACE):
        put(j * xs, fields_ref[max(j - 1, 0), j if j < 2 else 0], fields_ref[max(j - 1, 0), zs - 2 + j if j < 2 else zs - 1])

    def density_rows(z):
        return jnp.where(ends, halo_ref[0, z], pltpu.roll(halo_ref[0, z + 1], TILE // 2, 0))

    def field_rows(z):
        rows = [pltpu.roll(halo_ref[f, z], 2 * f - 2, 0) if f > 1 else halo_ref[f, z] for f in (1, 2, 3)]
        mixed = jnp.where((sub == 0) | (sub == TILE - 1), rows[0], rows[1])
        return jnp.where((sub == 3) | (sub == 4), rows[2], mixed)

    def strips(z):
        group, k = divmod(z, GROUP)
        packed = jnp.zeros((TILE, 128), jnp.float32)
        for t in range(block // TILE):
            moved = pltpu.roll(merged_ref[group, t * TILE : t * TILE + TILE], (SPAN * t - SLOT * k) % 128, 1)
            packed = jnp.where((lane >= SPAN * t) & (lane < SPAN * t + SPAN), moved, packed)
        return packed

    put(FACE * xs, density_rows(0), density_rows(zs - 2))
    put(FACE * xs + TILE, field_rows(0), field_rows(zs - 1))
    put(FACE * xs + 2 * TILE, strips(0), strips(zs - 2))


def along_y(values, halo, lane, density):
    def shifted(off):
        mixed = jnp.where(lane >= 128 - off if off > 0 else lane < -off, halo, values)
        return pltpu.roll(mixed, off % 128, 1)

    m1, p1 = shifted(1), shifted(-1)
    near = m1 + p1
    blur = near + 2.0 * values
    if not density:
        return (blur,)
    m2, p2 = shifted(2), shifted(-2)
    return blur, (m2 + p2) + 4.0 * near + 6.0 * values, (p2 - m2) + 2.0 * (p1 - m1)


class Rows:
    def __init__(self, tiles, halo):
        self.tiles, self.halo = list(tiles), halo
        self.sub = lax.broadcasted_iota(jnp.int32, (TILE, 1), 0)
        self.made = {}

    def row(self, t):
        count = len(self.tiles)
        if 0 <= t < count:
            return self.tiles[t]
        if t not in self.made:
            down = t < 0
            step = -t - 1 if down else t - count
            halo = self.halo if step == 0 else pltpu.roll(self.halo, TILE - 1 if down else 1, 0)
            inner = pltpu.roll(self.tiles[t % count], 1 if down else TILE - 1, 0)
            self.made[t] = jnp.where(self.sub == (0 if down else TILE - 1), halo, inner)
        return self.made[t]

    def pair(self, level, t):
        if level == 0:
            return self.row(t)
        if (level, t) not in self.made:
            self.made[level, t] = self.pair(level - 1, t) + self.pair(level - 1, t + 1)
        return self.made[level, t]

    def blur(self):
        return [self.pair(2, t - 1) for t in range(len(self.tiles))]

    def blur2(self):
        return [self.pair(4, t - 2) for t in range(len(self.tiles))]

    def slope(self):
        return [self.pair(2, t) - self.pair(2, t - 2) for t in range(len(self.tiles))]


def cells_kernel(zs, xs, fields_ref, out_ref, cell_ref):
    each, tiles = 8, xs // TILE
    make_cell_weights(cell_ref)

    def step(k, carry):
        first = k * each
        for field in range(4):
            rows = [
                fields_ref[field, first + j, pl.ds(t, TILE, stride=tiles), :] for j in range(each) for t in range(tiles)
            ]
            weights = cell_ref[...] if field == 0 else cell_ref[:, 0:128]
            result = jnp.dot(halves(jnp.concatenate(rows, axis=0)), weights, preferred_element_type=jnp.float32)
            for part in (0, 1, 2) if field == 0 else (2 + field,):
                columns = slice(128 * part, 128 * part + 128) if field == 0 else slice(0, 128)
                out_ref[part, pl.ds(first, each)] = result[:, columns].reshape(each, xs, 128)
        return carry

    lax.fori_loop(0, zs // each, step, 0)


def cross_kernel(zs, xs, rows_ref, halo_ref, cell_ref, out_ref, edge_ref):
    each, tiles = 4, xs // TILE
    for field in range(4):
        weights = cell_ref[...] if field == 0 else cell_ref[:, 0:128]
        result = jnp.dot(
            halves(halo_ref[field].reshape(zs * TILE, 128)), weights, preferred_element_type=jnp.float32
        )
        for part in (0, 1, 2) if field == 0 else (2 + field,):
            columns = slice(128 * part, 128 * part + 128) if field == 0 else slice(0, 128)
            edge_ref[part] = result[:, columns].reshape(zs, TILE, 128)

    def step(k, carry):
        for j in range(each):
            z = k * each + j

            def part_rows(part):
                return Rows([rows_ref[part, z, t * TILE : t * TILE + TILE, :] for t in range(tiles)], edge_ref[part, z])

            twice, sloped = part_rows(1), part_rows(2)
            results = [part_rows(part).blur() for part in (0, 3, 4, 5)]
            results += [twice.blur2(), twice.slope(), sloped.blur2()]
            for part, values in enumerate(results):
                for t in range(tiles):
                    out_ref[part, z, t * TILE : t * TILE + TILE, :] = values[t]
        return carry

    lax.fori_loop(0, zs // each, step, 0)


def before_shade(load, z):
    def blur(part):
        return load(part, z - 1) + load(part, z + 1) + 2.0 * load(part, z)

    def blur2(part):
        return (load(part, z - 2) + load(part, z + 2)) + 4.0 * (load(part, z - 1) + load(part, z + 1)) + 6.0 * load(part, z)

    unit = 1.0 / 2048.0
    near = load(4, z + 1) - load(4, z - 1)
    grad_z = (load(4, z + 2) - load(4, z - 2)) + (near + near)
    grad_x = blur2(5)
    grad_y = blur2(6)
    facing = jnp.abs((0.8 * unit) * (grad_z + grad_y) + (0.4 * unit) * grad_x)
    square = grad_z * grad_z + grad_x * grad_x + grad_y * grad_y
    shading = 0.3 + facing * lax.rsqrt(square * (unit * unit) + 0.0025)
    density = (3.0 / 64.0) * blur(0)
    return [density, jnp.exp(-jnp.abs(density)), shading] + [blur(1 + c) for c in range(3)]


def shade(state, taken, looked, scale):
    density, t, shading = taken[:3]
    soft = jnp.maximum(density, 0.0) + t * polynomial(LOG1P, t)
    extinct = looked[3] * (soft * scale)
    passed, total, depth = state[0], state[1:4], state[4]
    weight = passed * (extinct * polynomial(EXPM1, extinct))
    lit = weight * shading
    colours = [
        total[c] + (looked[c] * lit) * (1.0 + 0.5 * jnp.tanh((1.0 / 64.0) * taken[3 + c])) for c in range(3)
    ]
    return (passed - weight, *colours, depth + extinct)


def inner_kernel(zs, xs, scale, cross_ref, merged_ref, looked_ref, strip_ref, inner_ref, full_ref, filtered_ref, taken_ref):
    tiles, each = xs // TILE, 8
    for group in range(merged_ref.shape[0]):
        rows = Rows([merged_ref[group, pl.ds(TILE + t, TILE, stride=tiles), :] for t in range(tiles)], merged_ref[group, 0:TILE])
        for k, values in enumerate((rows.blur(), rows.blur2(), rows.slope())):
            for t in range(tiles):
                filtered_ref[k, group, t * TILE : t * TILE + TILE, :] = values[t]

    def strip_step(step, carry):
        first = step * each
        for k, parts in enumerate(((0, 1, 2, 3), (4, 6), (5,))):
            strips = []
            for j in range(each):
                group = lax.div(first + j, GROUP)
                slot = first + j - group * GROUP
                strips.append(pltpu.roll(filtered_ref[k, group], lax.rem(128 - SLOT * slot, 128), 1))
            columns = slice((0, 512, 768)[k], (512, 768, 896)[k])
            result = jnp.dot(
                halves(jnp.concatenate(strips, axis=0)), strip_ref[:, columns], preferred_element_type=jnp.float32
            )
            for n, part in enumerate(parts):
                share = result[:, 128 * n : 128 * n + 128].reshape(each, xs, 128)
                full_ref[part, pl.ds(first, each)] = cross_ref[part, pl.ds(first, each)] + share
        return carry

    lax.fori_loop(0, zs // each, strip_step, 0)

    pairs = (zs - 4) // 2

    def take(step):
        for j in range(2):
            z = 2 + 2 * step + j
            for k, values in enumerate(before_shade(lambda part, z: full_ref[part, z], z)):
                taken_ref[k, j] = values

    def advance(step, state):
        for j in range(2):
            looked = [looked_ref[c, 2 + 2 * step + j] for c in range(4)]
            state = shade(state, [taken_ref[k, j] for k in range(6)], looked, scale)
        return state

    def z_step(step, state):
        state = advance(step, state)
        take(step + 1)
        return state

    zero = jnp.zeros((xs, 128), jnp.float32)
    take(0)
    state = lax.fori_loop(0, pairs - 1, z_step, (zero + 1.0, zero, zero, zero, zero))
    for k, values in enumerate(advance(pairs - 1, state)):
        inner_ref[k] = values


def edge_kernel(zs, xs, scale, fa_ref, fb_ref, cross_ref, looked_ref, inner_ref, *rest):
    out_refs, (near_ref, rows_ref, image_ref) = rest[:-3], rest[-3:]
    zfirst, zlast, zodd = place_of("gz")
    block = xs + TILE
    tiles = xs // TILE
    lane = lax.broadcasted_iota(jnp.int32, (1, 128), 1)
    for side in range(2):
        first, second = (fa_ref, fb_ref) if side == 0 else (fb_ref, fa_ref)

        def face(start, count):
            return jnp.where(zodd, first[start : start + count, :], second[start : start + count, :])

        ends = [face(FACE * xs, TILE), face(FACE * xs + TILE, TILE)]
        strips = face(FACE * xs + 2 * TILE, TILE)
        for j in range(FACE):
            field = max(j - 1, 0)
            layer = j if j < 2 else (1 if side == 0 else 0)
            turned = TILE // 2 * j if j < 2 else 2 * field - 2
            outer_rows = ends[min(field, 1)]
            if turned:
                outer_rows = pltpu.roll(outer_rows, TILE - turned, 0)
            at_lane = SLOT * layer + slot_of(field)[0]
            own = 126 if field == 0 else 127
            halo = [pltpu.roll(strips, (own - at_lane - SPAN * t) % 128, 1) for t in range(block // TILE)]
            values = jnp.concatenate([outer_rows, face(j * xs, xs)], axis=0)
            results = along_y(values, jnp.concatenate(halo, axis=0), lane, field == 0)
            for part, result in zip((0, 1, 2) if field == 0 else (2 + field,), results):
                rows_ref[side, layer, part] = result
    for side in range(2):
        edge = zfirst if side == 0 else zlast
        for layer in range(2):
            mirrored = 0 if side == 0 else zs - 1
            outer = layer == side

            def part_rows(part):
                ref = rows_ref.at[side, layer, part]
                return Rows([ref[pl.ds(TILE + t, TILE, stride=tiles), :] for t in range(tiles)], ref[0:TILE, :])

            twice, sloped = part_rows(1), part_rows(2)
            for part, values in zip((4, 5, 6), (twice.blur2(), twice.slope(), sloped.blur2())):
                for t in range(tiles):
                    rows = slice(t * TILE, t * TILE + TILE)
                    fill = -cross_ref[part, mirrored, rows] if outer else 0.0
                    near_ref[part, 2 * side + layer, rows] = jnp.where(edge, fill, values[t])
            if not outer:
                for part, source in enumerate((0, 3, 4, 5)):
                    for t, values in enumerate(part_rows(source).blur()):
                        near_ref[part, 2 * side + layer, t * TILE : t * TILE + TILE] = jnp.where(edge, 0.0, values)

    def load(part, z):
        if z < 0:
            return near_ref[part, z + 2]
        if z >= zs:
            return near_ref[part, z - zs + 2]
        return cross_ref[part, z]

    def behind(state, z):
        return shade(state, before_shade(load, z), [looked_ref[c, z] for c in range(4)], scale)

    zero = jnp.zeros((xs, 128), jnp.float32)
    state = behind(behind((zero + 1.0, zero, zero, zero, zero), 0), 1)
    passed = state[0]
    state = (
        passed * inner_ref[0],
        state[1] + passed * inner_ref[1],
        state[2] + passed * inner_ref[2],
        state[3] + passed * inner_ref[3],
        state[4] + inner_ref[4],
    )
    state = behind(behind(state, zs - 2), zs - 1)
    for c in range(4):
        for t in range(tiles):
            image_ref[c, pl.ds(t, TILE, stride=tiles), :] = state[1 + c][t * TILE : t * TILE + TILE]
    if len(out_refs) == 1:
        out_refs[0][...] = image_ref[...]
    else:
        part = xs // len(out_refs)
        for k, ref in enumerate(out_refs):
            ref[...] = image_ref[:, pl.ds(pl.multiple_of((lax.axis_index("gz") ^ k) * part, part), part), :]


def blend_kernel(near_ref, *refs):
    images, out_ref = refs[:-1], refs[-1]
    count = len(images)
    depths = [image[3] for image in images]
    colours = [jnp.zeros_like(depths[0])] * 3
    for k in range(count):
        prior = jnp.zeros_like(depths[0])
        for other in range(count):
            if other != k:
                prior += near_ref[k * count + other] * depths[other]
        through = jnp.exp(-prior)
        colours = [colours[c] + through * images[k][c] for c in range(3)]
    total = functools.reduce(jnp.add, depths)
    out_ref[0], out_ref[1], out_ref[2] = colours
    small = total * polynomial(EXPM1, total)
    out_ref[3] = jnp.where(total < 0.5, small, 1.0 - jnp.exp(-total))


def call(kernel, out_shape, specs, scratch=(), cost=1.0, name=None, limit=VMEM_LIMIT):
    where = {"s": pltpu.SMEM, "v": pltpu.VMEM, "a": pl.ANY}
    return pl.pallas_call(
        kernel,
        out_shape=out_shape,
        in_specs=[pl.BlockSpec(memory_space=where[s]) for s in specs],
        out_specs=jax.tree.map(lambda _: pl.BlockSpec(memory_space=pltpu.VMEM), out_shape),
        scratch_shapes=list(scratch),
        compiler_params=pltpu.CompilerParams(vmem_limit_bytes=limit),
        cost_estimate=pl.CostEstimate(flops=0, bytes_accessed=int(cost * 3.0e6), transcendentals=0),
        name=name,
    )


def swap_pairs(first, second, axis, idle):
    count, others = lax.axis_size(axis), lax.axis_size(idle)
    one = lax.ppermute(first, axis, [(i, i ^ 1) for i in range(count)])
    if count == 2:
        return one, one
    pairs = []
    for i in range(count):
        for j in range(others):
            end = i in (0, count - 1)
            to = (i if end else i + 1 if i % 2 else i - 1, j ^ 1 if end else j)
            if axis < idle:
                pairs.append((i * others + j, to[0] * others + to[1]))
            else:
                pairs.append((j * count + i, to[1] * count + to[0]))
    return one, lax.ppermute(second, tuple(sorted((axis, idle))), pairs)


def on_device(fields, material, depth_order, table):
    _, zs, xs, ys = fields.shape
    nx, nz = lax.axis_size("gx"), lax.axis_size("gz")
    block = xs + TILE
    part = xs // nz
    swaps = nz in (2, 4)
    groups = -(-zs // GROUP)
    f32 = lambda *shape: jax.ShapeDtypeStruct(shape, jnp.float32)

    def side(even_high):
        return call(functools.partial(rows_kernel, zs, xs, even_high), f32(FACE, zs, ys), "v", name="x_rows")(fields)

    x_a, x_b = swap_pairs(side(True), side(False) if nx > 2 else None, "gx", "gy")
    strip = jnp.asarray(strip_matrix(ys))
    looked, nearer = call(
        functools.partial(lookup_kernel, zs, xs, swaps),
        (f32(4, zs, xs, ys), f32(nz * nz, 1, 128)),
        "svv",
        [pltpu.VMEM((4, 128), jnp.float32)],
        cost=1.2,
        name="lookup",
    )(depth_order, table, material)
    main = call(functools.partial(pack_kernel, zs, xs), f32(groups, xs, 128), "v", cost=0.7, name="pack")(fields)
    x_a, x_b, main, looked = lax.optimization_barrier((x_a, x_b, main, looked))

    halo, own = call(
        functools.partial(x_halo_kernel, zs, xs), (f32(4, zs, TILE, ys), f32(groups, block, 128)), "vvvv", name="x_halo"
    )(fields, main, x_a, x_b)
    y_a, y_b = swap_pairs(own, own, "gy", "gx")
    rows, cell = call(
        functools.partial(cells_kernel, zs, xs),
        (f32(6, zs, xs, ys), jax.ShapeDtypeStruct((256, 3 * ys), jnp.bfloat16)),
        "v",
        cost=1.3,
        name="cells",
    )(fields)
    cross = call(
        functools.partial(cross_kernel, zs, xs),
        f32(7, zs, xs, ys),
        "vvv",
        [pltpu.VMEM((6, zs, TILE, ys), jnp.float32)],
        cost=1.0,
        name="cross",
    )(rows, halo, cell)
    y_a, y_b, cross = lax.optimization_barrier((y_a, y_b, cross))

    faces = f32(FACE * xs + 3 * TILE, ys)
    merged, f_a, f_b = call(
        functools.partial(face_kernel, zs, xs), (f32(groups, block, 128), faces, faces), "vvvvv", name="faces"
    )(fields, halo, own, y_a, y_b)
    z_a, z_b = swap_pairs(f_a, f_b, "gz", "gy")

    scale = 2.0 / (zs * nz)
    inner, full = call(
        functools.partial(inner_kernel, zs, xs, scale),
        (f32(5, xs, ys), f32(7, zs, xs, ys)),
        "vvvv",
        [pltpu.VMEM((3, groups, xs, 128), jnp.float32), pltpu.VMEM((6, 2, xs, ys), jnp.float32)],
        cost=4.0,
        name="inner",
    )(cross, merged, looked, strip)

    images = call(
        functools.partial(edge_kernel, zs, xs, scale),
        [f32(4, part, ys)] * nz if swaps else [f32(4, xs, ys)],
        "vvvvv",
        [
            pltpu.VMEM((7, 4, xs, ys), jnp.float32),
            pltpu.VMEM((2, 2, 6, block, ys), jnp.float32),
            pltpu.VMEM((4, xs, ys), jnp.float32),
        ],
        name="edges",
    )(z_a, z_b, full, looked, inner)

    if swaps:
        mine = [images[0]]
        for k in range(1, nz):
            mine.append(lax.ppermute(images[k], "gz", [(i, i ^ k) for i in range(nz)]))
    else:
        stacked = lax.all_to_all(images[0].reshape(4, nz, part, ys), "gz", split_axis=1, concat_axis=1)
        mine = [stacked[:, b] for b in range(nz)]
    return call(blend_kernel, f32(4, part, ys), "v" + "v" * nz, name="blend")(nearer, *mine)


def solution(mesh):
    return jax.shard_map(
        on_device,
        mesh=mesh,
        in_specs=(P(None, "gz", "gx", "gy"), P("gz", "gx", "gy"), P(), P()),
        out_specs=P(None, ("gx", "gz"), "gy"),
        check_vma=False,
    )
```

```python
import functools

import jax
import jax.numpy as jnp
import ml_dtypes
import numpy as np
from jax import lax
from jax.experimental import pallas as pl
from jax.experimental.pallas import tpu as pltpu
from jax.sharding import PartitionSpec as P

VMEM_LIMIT = 40 * 1024 * 1024
GROUP = 12
SLOT = 10
TILE = 8
FACE = 5
SPAN = 24

LOG1P = (
    0.9999995186059567, -0.49996356582563917, 0.33265255844036573, -0.24453388969978707, 0.17659864766821842,
    -0.10679931280022417, 0.043659288844443055, -0.008466410404849948,
)
EXPM1 = (
    1.0, -0.4999995231628418, 0.1666584461927414, -0.04160914570093155, 0.00814302358776331, -0.0010865303920581937,
)


def polynomial(coefficients, value):
    terms = list(coefficients)
    power = value
    while len(terms) > 1:
        paired = [terms[k] + terms[k + 1] * power for k in range(0, len(terms) - 1, 2)]
        terms = paired + ([terms[-1]] if len(terms) % 2 else [])
        power = power * power if len(terms) > 1 else power
    return terms[0]


BLUR, BLUR2, SLOPE = {-1: 1, 0: 2, 1: 1}, {-2: 1, -1: 4, 0: 6, 1: 4, 2: 1}, {-2: -1, -1: -2, 1: 2, 2: 1}


def strip_matrix(ysize):
    strips = np.zeros((128, 7 * ysize), np.float32)
    for block, (taps, field) in enumerate([(BLUR, f) for f in range(4)] + [(BLUR2, 0), (SLOPE, 0), (BLUR2, 0)]):
        first = slot_of(field)[0]
        outside = {-2: 0, -1: 1, ysize: 2, ysize + 1: 3} if field == 0 else {-1: first, ysize: first + 1}
        for out in range(ysize):
            for off, weight in taps.items():
                if not 0 <= out + off < ysize:
                    strips[outside[out + off], block * ysize + out] = weight
    return np.concatenate([strips, strips], axis=0).astype(ml_dtypes.bfloat16)


def make_cell_weights(out_ref):
    off = lax.broadcasted_iota(jnp.int32, (128, 128), 0) - lax.broadcasted_iota(jnp.int32, (128, 128), 1)
    for block, taps in enumerate((BLUR, BLUR2, SLOPE)):
        weights = jnp.zeros((128, 128), jnp.float32)
        for step, weight in taps.items():
            weights = jnp.where(off == step, float(weight), weights)
        for half in range(2):
            out_ref[128 * half : 128 * half + 128, 128 * block : 128 * block + 128] = weights.astype(jnp.bfloat16)


def halves(values):
    high = values.astype(jnp.bfloat16)
    low = (values - high.astype(jnp.float32)).astype(jnp.bfloat16)
    return jnp.concatenate([high, low], axis=1)


def place_of(axis):
    at = lax.axis_index(axis)
    return at == 0, at == lax.axis_size(axis) - 1, lax.rem(at, 2) == 1


def rows_kernel(zs, xs, even_high, fields_ref, out_ref):
    high = (lax.rem(lax.axis_index("gx"), 2) == 0) == even_high
    for group in range(FACE):
        field = max(group - 1, 0)
        rows = fields_ref.at[field].reshape(zs * xs, 128)
        low_row = group if group < 2 else 0
        high_row = xs - 2 + group if group < 2 else xs - 1
        out_ref[group] = rows[pl.ds(jnp.where(high, high_row, low_row), zs, stride=xs), :]


def slot_of(field):
    return (0, 4) if field == 0 else (2 + 2 * field, 2)


def pack_strips(load, layers, lane, rows):
    packed = jnp.zeros((rows, 128), jnp.float32)
    for k, z in enumerate(layers):
        for field in range(4):
            first, count = slot_of(field)
            start = SLOT * k + first
            values = pltpu.roll(load(field, z), (start + count // 2) % 128, 1)
            packed = jnp.where((lane >= start) & (lane < start + count), values, packed)
    return packed


def put_faces(zodd, out_refs, start, low, high):
    for ref, swapped in zip(out_refs, (False, True)):
        ref[start : start + low.shape[0], :] = jnp.where(zodd != swapped, low, high)


def pack_kernel(zs, xs, fields_ref, pack_ref, ma_ref, mb_ref):
    zodd = place_of("gz")[2]
    for j in range(FACE):
        field = max(j - 1, 0)
        low, high = fields_ref[field, j if j < 2 else 0], fields_ref[field, zs - 2 + j if j < 2 else zs - 1]
        put_faces(zodd, (ma_ref, mb_ref), j * xs, low, high)
    lane = lax.broadcasted_iota(jnp.int32, (1, 128), 1)
    for group in range(pack_ref.shape[0]):
        layers = range(group * GROUP, min(zs, group * GROUP + GROUP))
        pack_ref[group] = pack_strips(lambda f, z: fields_ref[f, z], layers, lane, xs)


def lookup_kernel(zs, xs, peers, order_ref, table_ref, ids_ref, looked_ref, near_ref, tables_ref):
    iz, count = lax.axis_index("gz"), lax.axis_size("gz")
    ranks = [order_ref[iz ^ k if peers else k] for k in range(count)]
    for k in range(count):
        for other in range(count):
            nearer = jnp.where(ranks[other] < ranks[k], 1.0, 0.0)
            near_ref[k * count + other] = jnp.full((1, 128), nearer, jnp.float32)
    tables_ref[...] = jnp.zeros_like(tables_ref)
    tables_ref[:, 0 : table_ref.shape[1]] = table_ref[...]
    tables = [jnp.broadcast_to(tables_ref[c : c + 1, :], (TILE, 128)) for c in range(4)]
    each = 8
    tiles = xs // TILE

    def step(k, carry):
        for j in range(each):
            z = k * each + j
            for t in range(tiles):
                ids = ids_ref[z, pl.ds(t, TILE, stride=tiles), :]
                for c in range(4):
                    looked_ref[c, z, t * TILE : t * TILE + TILE, :] = jnp.take_along_axis(
                        tables[c], ids, axis=1, mode="promise_in_bounds"
                    )
        return carry

    lax.fori_loop(0, zs // each, step, 0)


def x_halo_kernel(zs, xs, fields_ref, main_ref, xa_ref, xb_ref, halo_ref, pack_ref):
    first, last, odd = place_of("gx")
    halo_ref[...] = jnp.zeros_like(halo_ref)
    for field in range(4):
        tiles = halo_ref.at[field].reshape(zs * TILE, 128)
        own = fields_ref.at[field].reshape(zs * xs, 128)
        at = 0 if field == 0 else 1 + field
        below = jnp.where(odd, xa_ref[1 + field], xb_ref[1 + field])
        above = jnp.where(odd, xb_ref[at], xa_ref[at])
        tiles[pl.ds(0, zs, stride=TILE), :] = jnp.where(first, 0.0, below)
        tiles[pl.ds(TILE - 1, zs, stride=TILE), :] = jnp.where(last, 0.0, above)
        if field == 0:
            low, high = own[pl.ds(0, zs, stride=xs), :], own[pl.ds(xs - 1, zs, stride=xs), :]
            tiles[pl.ds(1, zs, stride=TILE), :] = jnp.where(first, -low, jnp.where(odd, xa_ref[0], xb_ref[0]))
            tiles[pl.ds(TILE - 2, zs, stride=TILE), :] = jnp.where(last, -high, jnp.where(odd, xb_ref[1], xa_ref[1]))
    lane = lax.broadcasted_iota(jnp.int32, (1, 128), 1)
    for group in range(pack_ref.shape[0]):
        layers = range(group * GROUP, min(zs, group * GROUP + GROUP))
        pack_ref[group, 0:TILE] = pack_strips(lambda f, z: halo_ref[f, z], layers, lane, TILE)
        pack_ref[group, TILE:] = main_ref[group]


def face_kernel(zs, xs, halo_ref, own_ref, ya_ref, yb_ref, merged_ref, fa_ref, fb_ref):
    yfirst, ylast, yodd = place_of("gy")
    zodd = place_of("gz")[2]
    block = xs + TILE
    lane = lax.broadcasted_iota(jnp.int32, (1, 128), 1)
    place = lax.rem(lane, SLOT)
    from_left = (place < 2) | ((place >= 4) & (lax.rem(place, 2) == 0))
    for group in range(own_ref.shape[0]):
        own = own_ref[group]
        fill_left = jnp.where(place == 0, -pltpu.roll(own, 126, 1), 0.0)
        fill_right = jnp.where(place == 3, -pltpu.roll(own, 2, 1), 0.0)
        first, second = ya_ref[group], yb_ref[group]
        left = jnp.where(yfirst, fill_left, jnp.where(yodd, first, second))
        right = jnp.where(ylast, fill_right, jnp.where(yodd, second, first))
        merged_ref[group] = jnp.where(from_left, left, right)

    sub = lax.broadcasted_iota(jnp.int32, (TILE, 1), 0)
    ends = (sub < 2) | (sub >= TILE - 2)

    def density_rows(z):
        return jnp.where(ends, halo_ref[0, z], pltpu.roll(halo_ref[0, z + 1], TILE // 2, 0))

    def field_rows(z):
        rows = [pltpu.roll(halo_ref[f, z], 2 * f - 2, 0) if f > 1 else halo_ref[f, z] for f in (1, 2, 3)]
        mixed = jnp.where((sub == 0) | (sub == TILE - 1), rows[0], rows[1])
        return jnp.where((sub == 3) | (sub == 4), rows[2], mixed)

    def strips(z):
        group, k = divmod(z, GROUP)
        packed = jnp.zeros((TILE, 128), jnp.float32)
        for t in range(block // TILE):
            moved = pltpu.roll(merged_ref[group, t * TILE : t * TILE + TILE], (SPAN * t - SLOT * k) % 128, 1)
            packed = jnp.where((lane >= SPAN * t) & (lane < SPAN * t + SPAN), moved, packed)
        return packed

    outs = (fa_ref, fb_ref)
    put_faces(zodd, outs, 0, density_rows(0), density_rows(zs - 2))
    put_faces(zodd, outs, TILE, field_rows(0), field_rows(zs - 1))
    put_faces(zodd, outs, 2 * TILE, strips(0), strips(zs - 2))


def along_y(values, halo, lane, density):
    def shifted(off):
        mixed = jnp.where(lane >= 128 - off if off > 0 else lane < -off, halo, values)
        return pltpu.roll(mixed, off % 128, 1)

    m1, p1 = shifted(1), shifted(-1)
    near = m1 + p1
    blur = near + 2.0 * values
    if not density:
        return (blur,)
    m2, p2 = shifted(2), shifted(-2)
    return blur, (m2 + p2) + 4.0 * near + 6.0 * values, (p2 - m2) + 2.0 * (p1 - m1)


class Rows:
    def __init__(self, tiles, halo):
        self.tiles, self.halo = list(tiles), halo
        self.sub = lax.broadcasted_iota(jnp.int32, (TILE, 1), 0)
        self.made = {}

    def row(self, t):
        count = len(self.tiles)
        if 0 <= t < count:
            return self.tiles[t]
        if t not in self.made:
            down = t < 0
            step = -t - 1 if down else t - count
            halo = self.halo if step == 0 else pltpu.roll(self.halo, TILE - 1 if down else 1, 0)
            inner = pltpu.roll(self.tiles[t % count], 1 if down else TILE - 1, 0)
            self.made[t] = jnp.where(self.sub == (0 if down else TILE - 1), halo, inner)
        return self.made[t]

    def pair(self, level, t):
        if level == 0:
            return self.row(t)
        if (level, t) not in self.made:
            self.made[level, t] = self.pair(level - 1, t) + self.pair(level - 1, t + 1)
        return self.made[level, t]

    def blur(self):
        return [self.pair(2, t - 1) for t in range(len(self.tiles))]

    def blur2(self):
        return [self.pair(4, t - 2) for t in range(len(self.tiles))]

    def slope(self):
        return [self.pair(2, t) - self.pair(2, t - 2) for t in range(len(self.tiles))]


def cells_kernel(zs, xs, fields_ref, out_ref, cell_ref):
    each, tiles = 8, xs // TILE
    make_cell_weights(cell_ref)

    def step(k, carry):
        first = k * each
        for field in range(4):
            rows = [
                fields_ref[field, first + j, pl.ds(t, TILE, stride=tiles), :] for j in range(each) for t in range(tiles)
            ]
            weights = cell_ref[...] if field == 0 else cell_ref[:, 0:128]
            result = jnp.dot(halves(jnp.concatenate(rows, axis=0)), weights, preferred_element_type=jnp.float32)
            for part in (0, 1, 2) if field == 0 else (2 + field,):
                columns = slice(128 * part, 128 * part + 128) if field == 0 else slice(0, 128)
                out_ref[part, pl.ds(first, each)] = result[:, columns].reshape(each, xs, 128)
        return carry

    lax.fori_loop(0, zs // each, step, 0)


def cross_kernel(zs, xs, rows_ref, halo_ref, cell_ref, out_ref, edge_ref):
    each, tiles = 4, xs // TILE
    for field in range(4):
        weights = cell_ref[...] if field == 0 else cell_ref[:, 0:128]
        result = jnp.dot(
            halves(halo_ref[field].reshape(zs * TILE, 128)), weights, preferred_element_type=jnp.float32
        )
        for part in (0, 1, 2) if field == 0 else (2 + field,):
            columns = slice(128 * part, 128 * part + 128) if field == 0 else slice(0, 128)
            edge_ref[part] = result[:, columns].reshape(zs, TILE, 128)

    def step(k, carry):
        for j in range(each):
            z = k * each + j

            def part_rows(part):
                return Rows([rows_ref[part, z, t * TILE : t * TILE + TILE, :] for t in range(tiles)], edge_ref[part, z])

            twice, sloped = part_rows(1), part_rows(2)
            results = [part_rows(part).blur() for part in (0, 3, 4, 5)]
            results += [twice.blur2(), twice.slope(), sloped.blur2()]
            for part, values in enumerate(results):
                for t in range(tiles):
                    out_ref[part, z, t * TILE : t * TILE + TILE, :] = values[t]
        return carry

    lax.fori_loop(0, zs // each, step, 0)


def before_shade(load, z):
    def blur(part):
        return load(part, z - 1) + load(part, z + 1) + 2.0 * load(part, z)

    def blur2(part):
        return (load(part, z - 2) + load(part, z + 2)) + 4.0 * (load(part, z - 1) + load(part, z + 1)) + 6.0 * load(part, z)

    unit = 1.0 / 2048.0
    near = load(4, z + 1) - load(4, z - 1)
    grad_z = (load(4, z + 2) - load(4, z - 2)) + (near + near)
    grad_x = blur2(5)
    grad_y = blur2(6)
    facing = jnp.abs((0.8 * unit) * (grad_z + grad_y) + (0.4 * unit) * grad_x)
    square = grad_z * grad_z + grad_x * grad_x + grad_y * grad_y
    shading = 0.3 + facing * lax.rsqrt(square * (unit * unit) + 0.0025)
    density = (3.0 / 64.0) * blur(0)
    return [density, jnp.exp(-jnp.abs(density)), shading] + [blur(1 + c) for c in range(3)]


def shade(state, taken, looked, scale):
    density, t, shading = taken[:3]
    soft = jnp.maximum(density, 0.0) + t * polynomial(LOG1P, t)
    extinct = looked[3] * (soft * scale)
    passed, total, depth = state[0], state[1:4], state[4]
    weight = passed * (extinct * polynomial(EXPM1, extinct))
    lit = weight * shading
    colours = [
        total[c] + (looked[c] * lit) * (1.0 + 0.5 * jnp.tanh((1.0 / 64.0) * taken[3 + c])) for c in range(3)
    ]
    return (passed - weight, *colours, depth + extinct)


def inner_kernel(zs, xs, scale, cross_ref, merged_ref, looked_ref, strip_ref, inner_ref, full_ref, filtered_ref, taken_ref):
    tiles, each = xs // TILE, 8
    for group in range(merged_ref.shape[0]):
        rows = Rows([merged_ref[group, pl.ds(TILE + t, TILE, stride=tiles), :] for t in range(tiles)], merged_ref[group, 0:TILE])
        for k, values in enumerate((rows.blur(), rows.blur2(), rows.slope())):
            for t in range(tiles):
                filtered_ref[k, group, t * TILE : t * TILE + TILE, :] = values[t]

    def strip_step(step, carry):
        first = step * each
        for k, parts in enumerate(((0, 1, 2, 3), (4, 6), (5,))):
            strips = []
            for j in range(each):
                group = lax.div(first + j, GROUP)
                slot = first + j - group * GROUP
                strips.append(pltpu.roll(filtered_ref[k, group], lax.rem(128 - SLOT * slot, 128), 1))
            columns = slice((0, 512, 768)[k], (512, 768, 896)[k])
            result = jnp.dot(
                halves(jnp.concatenate(strips, axis=0)), strip_ref[:, columns], preferred_element_type=jnp.float32
            )
            for n, part in enumerate(parts):
                share = result[:, 128 * n : 128 * n + 128].reshape(each, xs, 128)
                full_ref[part, pl.ds(first, each)] = cross_ref[part, pl.ds(first, each)] + share
        return carry

    lax.fori_loop(0, zs // each, strip_step, 0)

    pairs = (zs - 4) // 2

    def take(step):
        for j in range(2):
            z = 2 + 2 * step + j
            for k, values in enumerate(before_shade(lambda part, z: full_ref[part, z], z)):
                taken_ref[k, j] = values

    def advance(step, state):
        for j in range(2):
            looked = [looked_ref[c, 2 + 2 * step + j] for c in range(4)]
            state = shade(state, [taken_ref[k, j] for k in range(6)], looked, scale)
        return state

    def z_step(step, state):
        state = advance(step, state)
        take(step + 1)
        return state

    zero = jnp.zeros((xs, 128), jnp.float32)
    take(0)
    state = lax.fori_loop(0, pairs - 1, z_step, (zero + 1.0, zero, zero, zero, zero))
    for k, values in enumerate(advance(pairs - 1, state)):
        inner_ref[k] = values


def edge_kernel(zs, xs, scale, ma_ref, mb_ref, fa_ref, fb_ref, cross_ref, looked_ref, inner_ref, *rest):
    out_refs, (near_ref, rows_ref, image_ref) = rest[:-3], rest[-3:]
    zfirst, zlast, zodd = place_of("gz")
    block = xs + TILE
    tiles = xs // TILE
    lane = lax.broadcasted_iota(jnp.int32, (1, 128), 1)
    for side in range(2):

        def face(start, count, refs=(fa_ref, fb_ref)):
            first, second = refs if side == 0 else refs[::-1]
            return jnp.where(zodd, first[start : start + count, :], second[start : start + count, :])

        ends = [face(0, TILE), face(TILE, TILE)]
        strips = face(2 * TILE, TILE)
        for j in range(FACE):
            field = max(j - 1, 0)
            layer = j if j < 2 else (1 if side == 0 else 0)
            turned = TILE // 2 * j if j < 2 else 2 * field - 2
            outer_rows = ends[min(field, 1)]
            if turned:
                outer_rows = pltpu.roll(outer_rows, TILE - turned, 0)
            at_lane = SLOT * layer + slot_of(field)[0]
            own = 126 if field == 0 else 127
            halo = [pltpu.roll(strips, (own - at_lane - SPAN * t) % 128, 1) for t in range(block // TILE)]
            values = jnp.concatenate([outer_rows, face(j * xs, xs, (ma_ref, mb_ref))], axis=0)
            results = along_y(values, jnp.concatenate(halo, axis=0), lane, field == 0)
            for part, result in zip((0, 1, 2) if field == 0 else (2 + field,), results):
                rows_ref[side, layer, part] = result
    for side in range(2):
        edge = zfirst if side == 0 else zlast
        for layer in range(2):
            mirrored = 0 if side == 0 else zs - 1
            outer = layer == side

            def part_rows(part):
                ref = rows_ref.at[side, layer, part]
                return Rows([ref[pl.ds(TILE + t, TILE, stride=tiles), :] for t in range(tiles)], ref[0:TILE, :])

            twice, sloped = part_rows(1), part_rows(2)
            for part, values in zip((4, 5, 6), (twice.blur2(), twice.slope(), sloped.blur2())):
                for t in range(tiles):
                    rows = slice(t * TILE, t * TILE + TILE)
                    fill = -cross_ref[part, mirrored, rows] if outer else 0.0
                    near_ref[part, 2 * side + layer, rows] = jnp.where(edge, fill, values[t])
            if not outer:
                for part, source in enumerate((0, 3, 4, 5)):
                    for t, values in enumerate(part_rows(source).blur()):
                        near_ref[part, 2 * side + layer, t * TILE : t * TILE + TILE] = jnp.where(edge, 0.0, values)

    def load(part, z):
        if z < 0:
            return near_ref[part, z + 2]
        if z >= zs:
            return near_ref[part, z - zs + 2]
        return cross_ref[part, z]

    def behind(state, z):
        return shade(state, before_shade(load, z), [looked_ref[c, z] for c in range(4)], scale)

    zero = jnp.zeros((xs, 128), jnp.float32)
    state = behind(behind((zero + 1.0, zero, zero, zero, zero), 0), 1)
    passed = state[0]
    state = (
        passed * inner_ref[0],
        state[1] + passed * inner_ref[1],
        state[2] + passed * inner_ref[2],
        state[3] + passed * inner_ref[3],
        state[4] + inner_ref[4],
    )
    state = behind(behind(state, zs - 2), zs - 1)
    for c in range(4):
        for t in range(tiles):
            image_ref[c, pl.ds(t, TILE, stride=tiles), :] = state[1 + c][t * TILE : t * TILE + TILE]
    if len(out_refs) == 1:
        out_refs[0][...] = image_ref[...]
    else:
        part = xs // len(out_refs)
        for k, ref in enumerate(out_refs):
            ref[...] = image_ref[:, pl.ds(pl.multiple_of((lax.axis_index("gz") ^ k) * part, part), part), :]


def blend_kernel(near_ref, *refs):
    images, out_ref = refs[:-1], refs[-1]
    count = len(images)
    depths = [image[3] for image in images]
    colours = [jnp.zeros_like(depths[0])] * 3
    for k in range(count):
        prior = jnp.zeros_like(depths[0])
        for other in range(count):
            if other != k:
                prior += near_ref[k * count + other] * depths[other]
        through = jnp.exp(-prior)
        colours = [colours[c] + through * images[k][c] for c in range(3)]
    total = functools.reduce(jnp.add, depths)
    out_ref[0], out_ref[1], out_ref[2] = colours
    small = total * polynomial(EXPM1, total)
    out_ref[3] = jnp.where(total < 0.5, small, 1.0 - jnp.exp(-total))


def call(kernel, out_shape, specs, scratch=(), cost=1.0, name=None, limit=VMEM_LIMIT):
    where = {"s": pltpu.SMEM, "v": pltpu.VMEM, "a": pl.ANY}
    return pl.pallas_call(
        kernel,
        out_shape=out_shape,
        in_specs=[pl.BlockSpec(memory_space=where[s]) for s in specs],
        out_specs=jax.tree.map(lambda _: pl.BlockSpec(memory_space=pltpu.VMEM), out_shape),
        scratch_shapes=list(scratch),
        compiler_params=pltpu.CompilerParams(vmem_limit_bytes=limit),
        cost_estimate=pl.CostEstimate(flops=0, bytes_accessed=int(cost * 3.0e6), transcendentals=0),
        name=name,
    )


def swap_pairs(first, second, axis, idle):
    count, others = lax.axis_size(axis), lax.axis_size(idle)
    one = lax.ppermute(first, axis, [(i, i ^ 1) for i in range(count)])
    if count == 2:
        return one, one
    pairs = []
    for i in range(count):
        for j in range(others):
            end = i in (0, count - 1)
            to = (i if end else i + 1 if i % 2 else i - 1, j ^ 1 if end else j)
            if axis < idle:
                pairs.append((i * others + j, to[0] * others + to[1]))
            else:
                pairs.append((j * count + i, to[1] * count + to[0]))
    return one, lax.ppermute(second, tuple(sorted((axis, idle))), pairs)


def on_device(fields, material, depth_order, table):
    _, zs, xs, ys = fields.shape
    nx, nz = lax.axis_size("gx"), lax.axis_size("gz")
    block = xs + TILE
    part = xs // nz
    swaps = nz in (2, 4)
    groups = -(-zs // GROUP)
    f32 = lambda *shape: jax.ShapeDtypeStruct(shape, jnp.float32)

    def side(even_high):
        return call(functools.partial(rows_kernel, zs, xs, even_high), f32(FACE, zs, ys), "v", name="x_rows")(fields)

    x_a, x_b = swap_pairs(side(True), side(False) if nx > 2 else None, "gx", "gy")
    strip = jnp.asarray(strip_matrix(ys))
    looked, nearer = call(
        functools.partial(lookup_kernel, zs, xs, swaps),
        (f32(4, zs, xs, ys), f32(nz * nz, 1, 128)),
        "svv",
        [pltpu.VMEM((4, 128), jnp.float32)],
        cost=1.2,
        name="lookup",
    )(depth_order, table, material)
    main, m_a, m_b = call(
        functools.partial(pack_kernel, zs, xs),
        (f32(groups, xs, 128), f32(FACE * xs, ys), f32(FACE * xs, ys)),
        "v",
        cost=0.7,
        name="pack",
    )(fields)
    z_ma, z_mb = swap_pairs(m_a, m_b, "gz", "gy")
    x_a, x_b, main, looked = lax.optimization_barrier((x_a, x_b, main, looked))

    halo, own = call(
        functools.partial(x_halo_kernel, zs, xs), (f32(4, zs, TILE, ys), f32(groups, block, 128)), "vvvv", name="x_halo"
    )(fields, main, x_a, x_b)
    y_a, y_b = swap_pairs(own, own, "gy", "gx")
    rows, cell = call(
        functools.partial(cells_kernel, zs, xs),
        (f32(6, zs, xs, ys), jax.ShapeDtypeStruct((256, 3 * ys), jnp.bfloat16)),
        "v",
        cost=1.3,
        name="cells",
    )(fields)
    cross = call(
        functools.partial(cross_kernel, zs, xs),
        f32(7, zs, xs, ys),
        "vvv",
        [pltpu.VMEM((6, zs, TILE, ys), jnp.float32)],
        cost=1.0,
        name="cross",
    )(rows, halo, cell)
    y_a, y_b, cross = lax.optimization_barrier((y_a, y_b, cross))

    faces = f32(3 * TILE, ys)
    merged, f_a, f_b = call(
        functools.partial(face_kernel, zs, xs), (f32(groups, block, 128), faces, faces), "vvvv", name="faces"
    )(halo, own, y_a, y_b)
    z_a, z_b = swap_pairs(f_a, f_b, "gz", "gy")

    scale = 2.0 / (zs * nz)
    inner, full = call(
        functools.partial(inner_kernel, zs, xs, scale),
        (f32(5, xs, ys), f32(7, zs, xs, ys)),
        "vvvv",
        [pltpu.VMEM((3, groups, xs, 128), jnp.float32), pltpu.VMEM((6, 2, xs, ys), jnp.float32)],
        cost=4.0,
        name="inner",
    )(cross, merged, looked, strip)

    images = call(
        functools.partial(edge_kernel, zs, xs, scale),
        [f32(4, part, ys)] * nz if swaps else [f32(4, xs, ys)],
        "vvvvvvv",
        [
            pltpu.VMEM((7, 4, xs, ys), jnp.float32),
            pltpu.VMEM((2, 2, 6, block, ys), jnp.float32),
            pltpu.VMEM((4, xs, ys), jnp.float32),
        ],
        name="edges",
    )(z_ma, z_mb, z_a, z_b, full, looked, inner)

    if swaps:
        mine = [images[0]]
        for k in range(1, nz):
            mine.append(lax.ppermute(images[k], "gz", [(i, i ^ k) for i in range(nz)]))
    else:
        stacked = lax.all_to_all(images[0].reshape(4, nz, part, ys), "gz", split_axis=1, concat_axis=1)
        mine = [stacked[:, b] for b in range(nz)]
    return call(blend_kernel, f32(4, part, ys), "v" + "v" * nz, name="blend")(nearer, *mine)


def solution(mesh):
    return jax.shard_map(
        on_device,
        mesh=mesh,
        in_specs=(P(None, "gz", "gx", "gy"), P("gz", "gx", "gy"), P(), P()),
        out_specs=P(None, ("gx", "gz"), "gy"),
        check_vma=False,
    )
```

```python
import functools

import jax
import jax.numpy as jnp
import ml_dtypes
import numpy as np
from jax import lax
from jax.experimental import pallas as pl
from jax.experimental.pallas import tpu as pltpu
from jax.sharding import PartitionSpec as P

VMEM_LIMIT = 40 * 1024 * 1024
GROUP = 12
SLOT = 10
TILE = 8
FACE = 5
SPAN = 24

LOG1P = (
    0.9999995186059567, -0.49996356582563917, 0.33265255844036573, -0.24453388969978707, 0.17659864766821842,
    -0.10679931280022417, 0.043659288844443055, -0.008466410404849948,
)
EXPM1 = (
    1.0, -0.4999995231628418, 0.1666584461927414, -0.04160914570093155, 0.00814302358776331, -0.0010865303920581937,
)


def polynomial(coefficients, value):
    terms = list(coefficients)
    power = value
    while len(terms) > 1:
        paired = [terms[k] + terms[k + 1] * power for k in range(0, len(terms) - 1, 2)]
        terms = paired + ([terms[-1]] if len(terms) % 2 else [])
        power = power * power if len(terms) > 1 else power
    return terms[0]


BLUR, BLUR2, SLOPE = {-1: 1, 0: 2, 1: 1}, {-2: 1, -1: 4, 0: 6, 1: 4, 2: 1}, {-2: -1, -1: -2, 1: 2, 2: 1}


def strip_matrix(ysize):
    strips = np.zeros((128, 7 * ysize), np.float32)
    for block, (taps, field) in enumerate([(BLUR, f) for f in range(4)] + [(BLUR2, 0), (SLOPE, 0), (BLUR2, 0)]):
        first = slot_of(field)[0]
        outside = {-2: 0, -1: 1, ysize: 2, ysize + 1: 3} if field == 0 else {-1: first, ysize: first + 1}
        for out in range(ysize):
            for off, weight in taps.items():
                if not 0 <= out + off < ysize:
                    strips[outside[out + off], block * ysize + out] = weight
    return np.concatenate([strips, strips], axis=0).astype(ml_dtypes.bfloat16)


def make_cell_weights(out_ref):
    off = lax.broadcasted_iota(jnp.int32, (128, 128), 0) - lax.broadcasted_iota(jnp.int32, (128, 128), 1)
    for block, taps in enumerate((BLUR, BLUR2, SLOPE)):
        weights = jnp.zeros((128, 128), jnp.float32)
        for step, weight in taps.items():
            weights = jnp.where(off == step, float(weight), weights)
        for half in range(2):
            out_ref[128 * half : 128 * half + 128, 128 * block : 128 * block + 128] = weights.astype(jnp.bfloat16)


def halves(values):
    high = values.astype(jnp.bfloat16)
    low = (values - high.astype(jnp.float32)).astype(jnp.bfloat16)
    return jnp.concatenate([high, low], axis=1)


def place_of(axis):
    at = lax.axis_index(axis)
    return at == 0, at == lax.axis_size(axis) - 1, lax.rem(at, 2) == 1


def rows_kernel(zs, xs, even_high, fields_ref, out_ref):
    high = (lax.rem(lax.axis_index("gx"), 2) == 0) == even_high
    for group in range(FACE):
        field = max(group - 1, 0)
        rows = fields_ref.at[field].reshape(zs * xs, 128)
        low_row = group if group < 2 else 0
        high_row = xs - 2 + group if group < 2 else xs - 1
        out_ref[group] = rows[pl.ds(jnp.where(high, high_row, low_row), zs, stride=xs), :]


def slot_of(field):
    return (0, 4) if field == 0 else (2 + 2 * field, 2)


def pack_strips(load, layers, lane, rows):
    packed = jnp.zeros((rows, 128), jnp.float32)
    for k, z in enumerate(layers):
        for field in range(4):
            first, count = slot_of(field)
            start = SLOT * k + first
            values = pltpu.roll(load(field, z), (start + count // 2) % 128, 1)
            packed = jnp.where((lane >= start) & (lane < start + count), values, packed)
    return packed


def pack_kernel(zs, xs, fields_ref, pack_ref, ca_ref, cb_ref):
    xodd = place_of("gx")[2]
    lane = lax.broadcasted_iota(jnp.int32, (1, 128), 1)
    sub = lax.broadcasted_iota(jnp.int32, (TILE, 1), 0)
    for group in range(pack_ref.shape[0]):
        layers = range(group * GROUP, min(zs, group * GROUP + GROUP))
        packed = pack_strips(lambda f, z: fields_ref[f, z], layers, lane, xs)
        pack_ref[group] = packed
        first, last = packed[0:TILE], packed[xs - TILE :]
        low = jnp.where(sub == TILE - 1, pltpu.roll(first, TILE - 1, 0), pltpu.roll(first, TILE - 3, 0))
        high = jnp.where(sub == 0, pltpu.roll(last, 1, 0), pltpu.roll(last, 3, 0))
        ca_ref[group] = jnp.where(xodd, low, high)
        cb_ref[group] = jnp.where(xodd, high, low)


def lookup_kernel(zs, xs, peers, order_ref, table_ref, ids_ref, looked_ref, near_ref, tables_ref):
    iz, count = lax.axis_index("gz"), lax.axis_size("gz")
    order = order_ref[...].astype(jnp.float32)
    lane = lax.broadcasted_iota(jnp.int32, order.shape, 1)
    ranks = [
        jnp.sum(jnp.where(lane == (iz ^ k if peers else k), order, 0.0), axis=1, keepdims=True) for k in range(count)
    ]
    for k in range(count):
        for other in range(count):
            nearer = jnp.where(ranks[other] < ranks[k], 1.0, 0.0)
            near_ref[k * count + other] = jnp.broadcast_to(nearer, (1, 128))
    tables_ref[...] = jnp.zeros_like(tables_ref)
    tables_ref[:, 0 : table_ref.shape[1]] = table_ref[...]
    tables = [jnp.broadcast_to(tables_ref[c : c + 1, :], (TILE, 128)) for c in range(4)]
    each = 8
    tiles = xs // TILE

    def step(k, carry):
        for j in range(each):
            z = k * each + j
            for t in range(tiles):
                ids = ids_ref[z, pl.ds(t, TILE, stride=tiles), :]
                for c in range(4):
                    looked_ref[c, z, t * TILE : t * TILE + TILE, :] = jnp.take_along_axis(
                        tables[c], ids, axis=1, mode="promise_in_bounds"
                    )
        return carry

    lax.fori_loop(0, zs // each, step, 0)


def join_kernel(zs, xs, fields_ref, own_ref, xa_ref, xb_ref, ya_ref, yb_ref, *rest):
    corner_refs, (halo_ref, merged_ref, fa_ref, fb_ref) = rest[:-4], rest[-4:]
    xfirst, xlast, xodd = place_of("gx")
    yfirst, ylast, yodd = place_of("gy")
    zodd = place_of("gz")[2]
    halo_ref[...] = jnp.zeros_like(halo_ref)
    for field in range(4):
        tiles = halo_ref.at[field].reshape(zs * TILE, 128)
        own = fields_ref.at[field].reshape(zs * xs, 128)
        at = 0 if field == 0 else 1 + field
        below = jnp.where(xodd, xa_ref[1 + field], xb_ref[1 + field])
        above = jnp.where(xodd, xb_ref[at], xa_ref[at])
        tiles[pl.ds(0, zs, stride=TILE), :] = jnp.where(xfirst, 0.0, below)
        tiles[pl.ds(TILE - 1, zs, stride=TILE), :] = jnp.where(xlast, 0.0, above)
        if field == 0:
            low, high = own[pl.ds(0, zs, stride=xs), :], own[pl.ds(xs - 1, zs, stride=xs), :]
            tiles[pl.ds(1, zs, stride=TILE), :] = jnp.where(xfirst, -low, jnp.where(xodd, xa_ref[0], xb_ref[0]))
            tiles[pl.ds(TILE - 2, zs, stride=TILE), :] = jnp.where(xlast, -high, jnp.where(xodd, xb_ref[1], xa_ref[1]))

    block = xs + TILE
    lane = lax.broadcasted_iota(jnp.int32, (1, 128), 1)
    sub = lax.broadcasted_iota(jnp.int32, (TILE, 1), 0)
    place = lax.rem(lane, SLOT)
    from_left = (place < 2) | ((place >= 4) & (lax.rem(place, 2) == 0))

    def merge(own, first, second):
        fill_left = jnp.where(place == 0, -pltpu.roll(own, 126, 1), 0.0)
        fill_right = jnp.where(place == 3, -pltpu.roll(own, 2, 1), 0.0)
        left = jnp.where(yfirst, fill_left, jnp.where(yodd, first, second))
        right = jnp.where(ylast, fill_right, jnp.where(yodd, second, first))
        return jnp.where(from_left, left, right)

    for group in range(own_ref.shape[0]):
        main = merge(own_ref[group], ya_ref[group], yb_ref[group])
        merged_ref[group, TILE:] = main
        tiles = []
        for k in range(2):
            a, b = corner_refs[k][group], corner_refs[k - 2][group]
            tiles.append(jnp.where(sub < TILE // 2, jnp.where(xodd, a, b), jnp.where(xodd, b, a)))
        tile = merge(tiles[1], tiles[0], tiles[1])
        low = jnp.where(sub == 1, -pltpu.roll(main[0:TILE], 1, 0), 0.0)
        high = jnp.where(sub == TILE - 2, -pltpu.roll(main[xs - TILE :], TILE - 1, 0), 0.0)
        tile = jnp.where(xfirst & (sub < TILE // 2), low, tile)
        merged_ref[group, 0:TILE] = jnp.where(xlast & (sub >= TILE // 2), high, tile)

    def put(start, low, high):
        for out_ref, swapped in ((fa_ref, False), (fb_ref, True)):
            out_ref[start : start + low.shape[0], :] = jnp.where(zodd != swapped, low, high)

    for j in range(FACE):
        put(j * xs, fields_ref[max(j - 1, 0), j if j < 2 else 0], fields_ref[max(j - 1, 0), zs - 2 + j if j < 2 else zs - 1])

    ends = (sub < 2) | (sub >= TILE - 2)

    def density_rows(z):
        return jnp.where(ends, halo_ref[0, z], pltpu.roll(halo_ref[0, z + 1], TILE // 2, 0))

    def field_rows(z):
        rows = [pltpu.roll(halo_ref[f, z], 2 * f - 2, 0) if f > 1 else halo_ref[f, z] for f in (1, 2, 3)]
        mixed = jnp.where((sub == 0) | (sub == TILE - 1), rows[0], rows[1])
        return jnp.where((sub == 3) | (sub == 4), rows[2], mixed)

    def strips(z):
        group, k = divmod(z, GROUP)
        packed = jnp.zeros((TILE, 128), jnp.float32)
        for t in range(block // TILE):
            moved = pltpu.roll(merged_ref[group, t * TILE : t * TILE + TILE], (SPAN * t - SLOT * k) % 128, 1)
            packed = jnp.where((lane >= SPAN * t) & (lane < SPAN * t + SPAN), moved, packed)
        return packed

    put(FACE * xs, density_rows(0), density_rows(zs - 2))
    put(FACE * xs + TILE, field_rows(0), field_rows(zs - 1))
    put(FACE * xs + 2 * TILE, strips(0), strips(zs - 2))


def along_y(values, halo, lane, density):
    def shifted(off):
        mixed = jnp.where(lane >= 128 - off if off > 0 else lane < -off, halo, values)
        return pltpu.roll(mixed, off % 128, 1)

    m1, p1 = shifted(1), shifted(-1)
    near = m1 + p1
    blur = near + 2.0 * values
    if not density:
        return (blur,)
    m2, p2 = shifted(2), shifted(-2)
    return blur, (m2 + p2) + 4.0 * near + 6.0 * values, (p2 - m2) + 2.0 * (p1 - m1)


class Rows:
    def __init__(self, tiles, halo):
        self.tiles, self.halo = list(tiles), halo
        self.sub = lax.broadcasted_iota(jnp.int32, (TILE, 1), 0)
        self.made = {}

    def row(self, t):
        count = len(self.tiles)
        if 0 <= t < count:
            return self.tiles[t]
        if t not in self.made:
            down = t < 0
            step = -t - 1 if down else t - count
            halo = self.halo if step == 0 else pltpu.roll(self.halo, TILE - 1 if down else 1, 0)
            inner = pltpu.roll(self.tiles[t % count], 1 if down else TILE - 1, 0)
            self.made[t] = jnp.where(self.sub == (0 if down else TILE - 1), halo, inner)
        return self.made[t]

    def pair(self, level, t):
        if level == 0:
            return self.row(t)
        if (level, t) not in self.made:
            self.made[level, t] = self.pair(level - 1, t) + self.pair(level - 1, t + 1)
        return self.made[level, t]

    def blur(self):
        return [self.pair(2, t - 1) for t in range(len(self.tiles))]

    def blur2(self):
        return [self.pair(4, t - 2) for t in range(len(self.tiles))]

    def slope(self):
        return [self.pair(2, t) - self.pair(2, t - 2) for t in range(len(self.tiles))]


def cells_kernel(zs, xs, fields_ref, out_ref, cell_ref):
    each, tiles = 8, xs // TILE
    make_cell_weights(cell_ref)

    def step(k, carry):
        first = k * each
        for field in range(4):
            rows = [
                fields_ref[field, first + j, pl.ds(t, TILE, stride=tiles), :] for j in range(each) for t in range(tiles)
            ]
            weights = cell_ref[...] if field == 0 else cell_ref[:, 0:128]
            result = jnp.dot(halves(jnp.concatenate(rows, axis=0)), weights, preferred_element_type=jnp.float32)
            for part in (0, 1, 2) if field == 0 else (2 + field,):
                columns = slice(128 * part, 128 * part + 128) if field == 0 else slice(0, 128)
                out_ref[part, pl.ds(first, each)] = result[:, columns].reshape(each, xs, 128)
        return carry

    lax.fori_loop(0, zs // each, step, 0)


def cross_kernel(zs, xs, rows_ref, halo_ref, cell_ref, out_ref, edge_ref):
    each, tiles = 4, xs // TILE
    for field in range(4):
        weights = cell_ref[...] if field == 0 else cell_ref[:, 0:128]
        result = jnp.dot(
            halves(halo_ref[field].reshape(zs * TILE, 128)), weights, preferred_element_type=jnp.float32
        )
        for part in (0, 1, 2) if field == 0 else (2 + field,):
            columns = slice(128 * part, 128 * part + 128) if field == 0 else slice(0, 128)
            edge_ref[part] = result[:, columns].reshape(zs, TILE, 128)

    def step(k, carry):
        for j in range(each):
            z = k * each + j

            def part_rows(part):
                return Rows([rows_ref[part, z, t * TILE : t * TILE + TILE, :] for t in range(tiles)], edge_ref[part, z])

            twice, sloped = part_rows(1), part_rows(2)
            results = [part_rows(part).blur() for part in (0, 3, 4, 5)]
            results += [twice.blur2(), twice.slope(), sloped.blur2()]
            for part, values in enumerate(results):
                for t in range(tiles):
                    out_ref[part, z, t * TILE : t * TILE + TILE, :] = values[t]
        return carry

    lax.fori_loop(0, zs // each, step, 0)


def before_shade(load, z):
    def blur(part):
        return load(part, z - 1) + load(part, z + 1) + 2.0 * load(part, z)

    def blur2(part):
        return (load(part, z - 2) + load(part, z + 2)) + 4.0 * (load(part, z - 1) + load(part, z + 1)) + 6.0 * load(part, z)

    unit = 1.0 / 2048.0
    near = load(4, z + 1) - load(4, z - 1)
    grad_z = (load(4, z + 2) - load(4, z - 2)) + (near + near)
    grad_x = blur2(5)
    grad_y = blur2(6)
    facing = jnp.abs((0.8 * unit) * (grad_z + grad_y) + (0.4 * unit) * grad_x)
    square = grad_z * grad_z + grad_x * grad_x + grad_y * grad_y
    shading = 0.3 + facing * lax.rsqrt(square * (unit * unit) + 0.0025)
    density = (3.0 / 64.0) * blur(0)
    return [density, jnp.exp(-jnp.abs(density)), shading] + [blur(1 + c) for c in range(3)]


def shade(state, taken, looked, scale):
    density, t, shading = taken[:3]
    soft = jnp.maximum(density, 0.0) + t * polynomial(LOG1P, t)
    extinct = looked[3] * (soft * scale)
    passed, total, depth = state[0], state[1:4], state[4]
    weight = passed * (extinct * polynomial(EXPM1, extinct))
    lit = weight * shading
    colours = [
        total[c] + (looked[c] * lit) * (1.0 + 0.5 * jnp.tanh((1.0 / 64.0) * taken[3 + c])) for c in range(3)
    ]
    return (passed - weight, *colours, depth + extinct)


def inner_kernel(zs, xs, scale, cross_ref, merged_ref, looked_ref, strip_ref, inner_ref, full_ref, filtered_ref, taken_ref):
    tiles, each = xs // TILE, 8
    for group in range(merged_ref.shape[0]):
        rows = Rows([merged_ref[group, pl.ds(TILE + t, TILE, stride=tiles), :] for t in range(tiles)], merged_ref[group, 0:TILE])
        for k, values in enumerate((rows.blur(), rows.blur2(), rows.slope())):
            for t in range(tiles):
                filtered_ref[k, group, t * TILE : t * TILE + TILE, :] = values[t]

    def strip_step(step, carry):
        first = step * each
        for k, parts in enumerate(((0, 1, 2, 3), (4, 6), (5,))):
            strips = []
            for j in range(each):
                group = lax.div(first + j, GROUP)
                slot = first + j - group * GROUP
                strips.append(pltpu.roll(filtered_ref[k, group], lax.rem(128 - SLOT * slot, 128), 1))
            columns = slice((0, 512, 768)[k], (512, 768, 896)[k])
            result = jnp.dot(
                halves(jnp.concatenate(strips, axis=0)), strip_ref[:, columns], preferred_element_type=jnp.float32
            )
            for n, part in enumerate(parts):
                share = result[:, 128 * n : 128 * n + 128].reshape(each, xs, 128)
                full_ref[part, pl.ds(first, each)] = cross_ref[part, pl.ds(first, each)] + share
        return carry

    lax.fori_loop(0, zs // each, strip_step, 0)

    pairs = (zs - 4) // 2

    def take(step):
        for j in range(2):
            z = 2 + 2 * step + j
            for k, values in enumerate(before_shade(lambda part, z: full_ref[part, z], z)):
                taken_ref[k, j] = values

    def advance(step, state):
        for j in range(2):
            looked = [looked_ref[c, 2 + 2 * step + j] for c in range(4)]
            state = shade(state, [taken_ref[k, j] for k in range(6)], looked, scale)
        return state

    def z_step(step, state):
        state = advance(step, state)
        take(step + 1)
        return state

    zero = jnp.zeros((xs, 128), jnp.float32)
    take(0)
    state = lax.fori_loop(0, pairs - 1, z_step, (zero + 1.0, zero, zero, zero, zero))
    for k, values in enumerate(advance(pairs - 1, state)):
        inner_ref[k] = values


def edge_kernel(zs, xs, scale, fa_ref, fb_ref, cross_ref, looked_ref, inner_ref, *rest):
    out_refs, (near_ref, rows_ref, image_ref) = rest[:-3], rest[-3:]
    zfirst, zlast, zodd = place_of("gz")
    block = xs + TILE
    tiles = xs // TILE
    lane = lax.broadcasted_iota(jnp.int32, (1, 128), 1)
    for side in range(2):
        first, second = (fa_ref, fb_ref) if side == 0 else (fb_ref, fa_ref)

        def face(start, count):
            return jnp.where(zodd, first[start : start + count, :], second[start : start + count, :])

        ends = [face(FACE * xs, TILE), face(FACE * xs + TILE, TILE)]
        strips = face(FACE * xs + 2 * TILE, TILE)
        for j in range(FACE):
            field = max(j - 1, 0)
            layer = j if j < 2 else (1 if side == 0 else 0)
            turned = TILE // 2 * j if j < 2 else 2 * field - 2
            outer_rows = ends[min(field, 1)]
            if turned:
                outer_rows = pltpu.roll(outer_rows, TILE - turned, 0)
            at_lane = SLOT * layer + slot_of(field)[0]
            own = 126 if field == 0 else 127
            halo = [pltpu.roll(strips, (own - at_lane - SPAN * t) % 128, 1) for t in range(block // TILE)]
            values = jnp.concatenate([outer_rows, face(j * xs, xs)], axis=0)
            results = along_y(values, jnp.concatenate(halo, axis=0), lane, field == 0)
            for part, result in zip((0, 1, 2) if field == 0 else (2 + field,), results):
                rows_ref[side, layer, part] = result
    for side in range(2):
        edge = zfirst if side == 0 else zlast
        for layer in range(2):
            mirrored = 0 if side == 0 else zs - 1
            outer = layer == side

            def part_rows(part):
                ref = rows_ref.at[side, layer, part]
                return Rows([ref[pl.ds(TILE + t, TILE, stride=tiles), :] for t in range(tiles)], ref[0:TILE, :])

            twice, sloped = part_rows(1), part_rows(2)
            for part, values in zip((4, 5, 6), (twice.blur2(), twice.slope(), sloped.blur2())):
                for t in range(tiles):
                    rows = slice(t * TILE, t * TILE + TILE)
                    fill = -cross_ref[part, mirrored, rows] if outer else 0.0
                    near_ref[part, 2 * side + layer, rows] = jnp.where(edge, fill, values[t])
            if not outer:
                for part, source in enumerate((0, 3, 4, 5)):
                    for t, values in enumerate(part_rows(source).blur()):
                        near_ref[part, 2 * side + layer, t * TILE : t * TILE + TILE] = jnp.where(edge, 0.0, values)

    def load(part, z):
        if z < 0:
            return near_ref[part, z + 2]
        if z >= zs:
            return near_ref[part, z - zs + 2]
        return cross_ref[part, z]

    def behind(state, z):
        return shade(state, before_shade(load, z), [looked_ref[c, z] for c in range(4)], scale)

    zero = jnp.zeros((xs, 128), jnp.float32)
    state = behind(behind((zero + 1.0, zero, zero, zero, zero), 0), 1)
    passed = state[0]
    state = (
        passed * inner_ref[0],
        state[1] + passed * inner_ref[1],
        state[2] + passed * inner_ref[2],
        state[3] + passed * inner_ref[3],
        state[4] + inner_ref[4],
    )
    state = behind(behind(state, zs - 2), zs - 1)
    for c in range(4):
        for t in range(tiles):
            image_ref[c, pl.ds(t, TILE, stride=tiles), :] = state[1 + c][t * TILE : t * TILE + TILE]
    if len(out_refs) == 1:
        out_refs[0][...] = image_ref[...]
    else:
        part = xs // len(out_refs)
        for k, ref in enumerate(out_refs):
            ref[...] = image_ref[:, pl.ds(pl.multiple_of((lax.axis_index("gz") ^ k) * part, part), part), :]


def blend_kernel(near_ref, *refs):
    images, out_ref = refs[:-1], refs[-1]
    count = len(images)
    depths = [image[3] for image in images]
    colours = [jnp.zeros_like(depths[0])] * 3
    for k in range(count):
        prior = jnp.zeros_like(depths[0])
        for other in range(count):
            if other != k:
                prior += near_ref[k * count + other] * depths[other]
        through = jnp.exp(-prior)
        colours = [colours[c] + through * images[k][c] for c in range(3)]
    total = functools.reduce(jnp.add, depths)
    out_ref[0], out_ref[1], out_ref[2] = colours
    small = total * polynomial(EXPM1, total)
    out_ref[3] = jnp.where(total < 0.5, small, 1.0 - jnp.exp(-total))


def call(kernel, out_shape, specs, scratch=(), cost=1.0, name=None, limit=VMEM_LIMIT):
    where = {"s": pltpu.SMEM, "v": pltpu.VMEM, "a": pl.ANY}
    return pl.pallas_call(
        kernel,
        out_shape=out_shape,
        in_specs=[pl.BlockSpec(memory_space=where[s]) for s in specs],
        out_specs=jax.tree.map(lambda _: pl.BlockSpec(memory_space=pltpu.VMEM), out_shape),
        scratch_shapes=list(scratch),
        compiler_params=pltpu.CompilerParams(vmem_limit_bytes=limit),
        cost_estimate=pl.CostEstimate(flops=0, bytes_accessed=int(cost * 3.0e6), transcendentals=0),
        name=name,
    )


def swap_pairs(first, second, axis, idle):
    count, others = lax.axis_size(axis), lax.axis_size(idle)
    one = lax.ppermute(first, axis, [(i, i ^ 1) for i in range(count)])
    if count == 2:
        return one, one
    pairs = []
    for i in range(count):
        for j in range(others):
            end = i in (0, count - 1)
            to = (i if end else i + 1 if i % 2 else i - 1, j ^ 1 if end else j)
            if axis < idle:
                pairs.append((i * others + j, to[0] * others + to[1]))
            else:
                pairs.append((j * count + i, to[1] * count + to[0]))
    return one, lax.ppermute(second, tuple(sorted((axis, idle))), pairs)


def swap_corners(values, x_kind, y_kind):
    counts = [lax.axis_size(a) for a in ("gx", "gy")]

    def partner(at, count, kind):
        to = at ^ 1 if kind == 0 else at + 1 if at % 2 else at - 1
        return to if 0 <= to < count else at

    pairs = []
    for i in range(counts[0]):
        for j in range(counts[1]):
            to = partner(i, counts[0], x_kind), partner(j, counts[1], y_kind)
            pairs.append((i * counts[1] + j, to[0] * counts[1] + to[1]))
    return lax.ppermute(values, ("gx", "gy"), pairs)


def on_device(fields, material, depth_order, table):
    _, zs, xs, ys = fields.shape
    nx, nz = lax.axis_size("gx"), lax.axis_size("gz")
    block = xs + TILE
    part = xs // nz
    swaps = nz in (2, 4)
    groups = -(-zs // GROUP)
    f32 = lambda *shape: jax.ShapeDtypeStruct(shape, jnp.float32)

    def side(even_high):
        return call(functools.partial(rows_kernel, zs, xs, even_high), f32(FACE, zs, ys), "v", name="x_rows")(fields)

    x_a, x_b = swap_pairs(side(True), side(False) if nx > 2 else None, "gx", "gy")
    strip = jnp.asarray(strip_matrix(ys))
    looked, nearer = call(
        functools.partial(lookup_kernel, zs, xs, swaps),
        (f32(4, zs, xs, ys), f32(nz * nz, 1, 128)),
        "vvv",
        [pltpu.VMEM((4, 128), jnp.float32)],
        cost=1.2,
        name="lookup",
    )(depth_order[None], table, material)
    strips, corners = f32(groups, xs, 128), f32(groups, TILE, 128)
    main, c_a, c_b = call(
        functools.partial(pack_kernel, zs, xs), (strips, corners, corners), "v", cost=0.7, name="pack"
    )(fields)
    y_a, y_b = swap_pairs(main, main, "gy", "gx")
    d = [swap_corners(c, x_kind, y_kind) for x_kind, c in enumerate((c_a, c_b)[: 1 if nx == 2 else 2]) for y_kind in (0, 1)]
    rows, cell = call(
        functools.partial(cells_kernel, zs, xs),
        (f32(6, zs, xs, ys), jax.ShapeDtypeStruct((256, 3 * ys), jnp.bfloat16)),
        "v",
        cost=1.3,
        name="cells",
    )(fields)
    x_a, x_b, y_a, y_b, d, looked, rows = lax.optimization_barrier((x_a, x_b, y_a, y_b, d, looked, rows))

    faces = f32(FACE * xs + 3 * TILE, ys)
    halo, merged, f_a, f_b = call(
        functools.partial(join_kernel, zs, xs),
        (f32(4, zs, TILE, ys), f32(groups, block, 128), faces, faces),
        "v" * (6 + len(d)),
        name="join",
    )(fields, main, x_a, x_b, y_a, y_b, *d)
    z_a, z_b = swap_pairs(f_a, f_b, "gz", "gy")
    cross = call(
        functools.partial(cross_kernel, zs, xs),
        f32(7, zs, xs, ys),
        "vvv",
        [pltpu.VMEM((6, zs, TILE, ys), jnp.float32)],
        cost=1.0,
        name="cross",
    )(rows, halo, cell)

    scale = 2.0 / (zs * nz)
    inner, full = call(
        functools.partial(inner_kernel, zs, xs, scale),
        (f32(5, xs, ys), f32(7, zs, xs, ys)),
        "vvvv",
        [pltpu.VMEM((3, groups, xs, 128), jnp.float32), pltpu.VMEM((6, 2, xs, ys), jnp.float32)],
        cost=4.0,
        name="inner",
    )(cross, merged, looked, strip)

    images = call(
        functools.partial(edge_kernel, zs, xs, scale),
        [f32(4, part, ys)] * nz if swaps else [f32(4, xs, ys)],
        "vvvvv",
        [
            pltpu.VMEM((7, 4, xs, ys), jnp.float32),
            pltpu.VMEM((2, 2, 6, block, ys), jnp.float32),
            pltpu.VMEM((4, xs, ys), jnp.float32),
        ],
        name="edges",
    )(z_a, z_b, full, looked, inner)

    if swaps:
        mine = [images[0]]
        for k in range(1, nz):
            mine.append(lax.ppermute(images[k], "gz", [(i, i ^ k) for i in range(nz)]))
    else:
        stacked = lax.all_to_all(images[0].reshape(4, nz, part, ys), "gz", split_axis=1, concat_axis=1)
        mine = [stacked[:, b] for b in range(nz)]
    return call(blend_kernel, f32(4, part, ys), "v" + "v" * nz, name="blend")(nearer, *mine)


def solution(mesh):
    return jax.shard_map(
        on_device,
        mesh=mesh,
        in_specs=(P(None, "gz", "gx", "gy"), P("gz", "gx", "gy"), P(), P()),
        out_specs=P(None, ("gx", "gz"), "gy"),
        check_vma=False,
    )
```

```python
import functools

import jax
import jax.numpy as jnp
import ml_dtypes
import numpy as np
from jax import lax
from jax.experimental import pallas as pl
from jax.experimental.pallas import tpu as pltpu
from jax.sharding import PartitionSpec as P

VMEM_LIMIT = 40 * 1024 * 1024
GROUP = 12
SLOT = 10
TILE = 8
FACE = 5
SPAN = 24

LOG1P = (
    0.9999995186059567, -0.49996356582563917, 0.33265255844036573, -0.24453388969978707, 0.17659864766821842,
    -0.10679931280022417, 0.043659288844443055, -0.008466410404849948,
)
EXPM1 = (
    1.0, -0.4999995231628418, 0.1666584461927414, -0.04160914570093155, 0.00814302358776331, -0.0010865303920581937,
)


def polynomial(coefficients, value):
    terms = list(coefficients)
    power = value
    while len(terms) > 1:
        paired = [terms[k] + terms[k + 1] * power for k in range(0, len(terms) - 1, 2)]
        terms = paired + ([terms[-1]] if len(terms) % 2 else [])
        power = power * power if len(terms) > 1 else power
    return terms[0]


BLUR, BLUR2, SLOPE = {-1: 1, 0: 2, 1: 1}, {-2: 1, -1: 4, 0: 6, 1: 4, 2: 1}, {-2: -1, -1: -2, 1: 2, 2: 1}


def strip_matrix(ysize):
    strips = np.zeros((128, 7 * ysize), np.float32)
    for block, (taps, field) in enumerate([(BLUR, f) for f in range(4)] + [(BLUR2, 0), (SLOPE, 0), (BLUR2, 0)]):
        first = slot_of(field)[0]
        outside = {-2: 0, -1: 1, ysize: 2, ysize + 1: 3} if field == 0 else {-1: first, ysize: first + 1}
        for out in range(ysize):
            for off, weight in taps.items():
                if not 0 <= out + off < ysize:
                    strips[outside[out + off], block * ysize + out] = weight
    return np.concatenate([strips, strips], axis=0).astype(ml_dtypes.bfloat16)


def make_cell_weights(out_ref):
    off = lax.broadcasted_iota(jnp.int32, (128, 128), 0) - lax.broadcasted_iota(jnp.int32, (128, 128), 1)
    for block, taps in enumerate((BLUR, BLUR2, SLOPE)):
        weights = jnp.zeros((128, 128), jnp.float32)
        for step, weight in taps.items():
            weights = jnp.where(off == step, float(weight), weights)
        for half in range(2):
            out_ref[128 * half : 128 * half + 128, 128 * block : 128 * block + 128] = weights.astype(jnp.bfloat16)


def halves(values):
    high = values.astype(jnp.bfloat16)
    low = (values - high.astype(jnp.float32)).astype(jnp.bfloat16)
    return jnp.concatenate([high, low], axis=1)


def place_of(axis):
    at = lax.axis_index(axis)
    return at == 0, at == lax.axis_size(axis) - 1, lax.rem(at, 2) == 1


def rows_kernel(zs, xs, even_high, fields_ref, out_ref):
    high = (lax.rem(lax.axis_index("gx"), 2) == 0) == even_high
    for group in range(FACE):
        field = max(group - 1, 0)
        rows = fields_ref.at[field].reshape(zs * xs, 128)
        low_row = group if group < 2 else 0
        high_row = xs - 2 + group if group < 2 else xs - 1
        out_ref[group] = rows[pl.ds(jnp.where(high, high_row, low_row), zs, stride=xs), :]


def slot_of(field):
    return (0, 4) if field == 0 else (2 + 2 * field, 2)


def pack_strips(load, layers, lane, rows):
    packed = jnp.zeros((rows, 128), jnp.float32)
    for k, z in enumerate(layers):
        for field in range(4):
            first, count = slot_of(field)
            start = SLOT * k + first
            values = pltpu.roll(load(field, z), (start + count // 2) % 128, 1)
            packed = jnp.where((lane >= start) & (lane < start + count), values, packed)
    return packed


def pack_kernel(zs, xs, fields_ref, pack_ref, *corner_refs):
    xodd = place_of("gx")[2]
    lane = lax.broadcasted_iota(jnp.int32, (1, 128), 1)
    sub = lax.broadcasted_iota(jnp.int32, (TILE, 1), 0)
    for group in range(pack_ref.shape[0]):
        layers = range(group * GROUP, min(zs, group * GROUP + GROUP))
        packed = pack_strips(lambda f, z: fields_ref[f, z], layers, lane, xs)
        pack_ref[group] = packed
        first, last = packed[0:TILE], packed[xs - TILE :]
        low = jnp.where(sub == TILE - 1, pltpu.roll(first, TILE - 1, 0), pltpu.roll(first, TILE - 3, 0))
        high = jnp.where(sub == 0, pltpu.roll(last, 1, 0), pltpu.roll(last, 3, 0))
        for ref, swapped in zip(corner_refs, (False, True)):
            ref[group] = jnp.where(xodd != swapped, low, high)


def lookup_kernel(zs, xs, peers, order_ref, table_ref, ids_ref, looked_ref, near_ref, tables_ref):
    iz, count = lax.axis_index("gz"), lax.axis_size("gz")
    order = order_ref[...].astype(jnp.float32)
    lane = lax.broadcasted_iota(jnp.int32, order.shape, 1)
    ranks = [
        jnp.sum(jnp.where(lane == (iz ^ k if peers else k), order, 0.0), axis=1, keepdims=True) for k in range(count)
    ]
    for k in range(count):
        for other in range(count):
            nearer = jnp.where(ranks[other] < ranks[k], 1.0, 0.0)
            near_ref[k * count + other] = jnp.broadcast_to(nearer, (1, 128))
    tables_ref[...] = jnp.zeros_like(tables_ref)
    tables_ref[:, 0 : table_ref.shape[1]] = table_ref[...]
    tables = [jnp.broadcast_to(tables_ref[c : c + 1, :], (TILE, 128)) for c in range(4)]
    each = 8
    tiles = xs // TILE

    def step(k, carry):
        for j in range(each):
            z = k * each + j
            for t in range(tiles):
                ids = ids_ref[z, pl.ds(t, TILE, stride=tiles), :]
                for c in range(4):
                    looked_ref[c, z, t * TILE : t * TILE + TILE, :] = jnp.take_along_axis(
                        tables[c], ids, axis=1, mode="promise_in_bounds"
                    )
        return carry

    lax.fori_loop(0, zs // each, step, 0)


def join_kernel(zs, xs, fields_ref, own_ref, xa_ref, xb_ref, ya_ref, yb_ref, *rest):
    corner_refs, (halo_ref, merged_ref, fa_ref, fb_ref) = rest[:-4], rest[-4:]
    xfirst, xlast, xodd = place_of("gx")
    yfirst, ylast, yodd = place_of("gy")
    zodd = place_of("gz")[2]
    halo_ref[...] = jnp.zeros_like(halo_ref)
    for field in range(4):
        tiles = halo_ref.at[field].reshape(zs * TILE, 128)
        own = fields_ref.at[field].reshape(zs * xs, 128)
        at = 0 if field == 0 else 1 + field
        below = jnp.where(xodd, xa_ref[1 + field], xb_ref[1 + field])
        above = jnp.where(xodd, xb_ref[at], xa_ref[at])
        tiles[pl.ds(0, zs, stride=TILE), :] = jnp.where(xfirst, 0.0, below)
        tiles[pl.ds(TILE - 1, zs, stride=TILE), :] = jnp.where(xlast, 0.0, above)
        if field == 0:
            low, high = own[pl.ds(0, zs, stride=xs), :], own[pl.ds(xs - 1, zs, stride=xs), :]
            tiles[pl.ds(1, zs, stride=TILE), :] = jnp.where(xfirst, -low, jnp.where(xodd, xa_ref[0], xb_ref[0]))
            tiles[pl.ds(TILE - 2, zs, stride=TILE), :] = jnp.where(xlast, -high, jnp.where(xodd, xb_ref[1], xa_ref[1]))

    block = xs + TILE
    lane = lax.broadcasted_iota(jnp.int32, (1, 128), 1)
    sub = lax.broadcasted_iota(jnp.int32, (TILE, 1), 0)
    place = lax.rem(lane, SLOT)
    from_left = (place < 2) | ((place >= 4) & (lax.rem(place, 2) == 0))

    def merge(own, first, second):
        fill_left = jnp.where(place == 0, -pltpu.roll(own, 126, 1), 0.0)
        fill_right = jnp.where(place == 3, -pltpu.roll(own, 2, 1), 0.0)
        left = jnp.where(yfirst, fill_left, jnp.where(yodd, first, second))
        right = jnp.where(ylast, fill_right, jnp.where(yodd, second, first))
        return jnp.where(from_left, left, right)

    for group in range(own_ref.shape[0]):
        main = merge(own_ref[group], ya_ref[group], yb_ref[group])
        merged_ref[group, TILE:] = main
        tiles = []
        for k in range(2):
            a, b = corner_refs[k][group], corner_refs[k - 2][group]
            tiles.append(jnp.where(sub < TILE // 2, jnp.where(xodd, a, b), jnp.where(xodd, b, a)))
        tile = merge(tiles[1], tiles[0], tiles[1])
        low = jnp.where(sub == 1, -pltpu.roll(main[0:TILE], 1, 0), 0.0)
        high = jnp.where(sub == TILE - 2, -pltpu.roll(main[xs - TILE :], TILE - 1, 0), 0.0)
        tile = jnp.where(xfirst & (sub < TILE // 2), low, tile)
        merged_ref[group, 0:TILE] = jnp.where(xlast & (sub >= TILE // 2), high, tile)

    def put(start, low, high):
        for out_ref, swapped in ((fa_ref, False), (fb_ref, True)):
            out_ref[start : start + low.shape[0], :] = jnp.where(zodd != swapped, low, high)

    for j in range(FACE):
        put(j * xs, fields_ref[max(j - 1, 0), j if j < 2 else 0], fields_ref[max(j - 1, 0), zs - 2 + j if j < 2 else zs - 1])

    ends = (sub < 2) | (sub >= TILE - 2)

    def density_rows(z):
        return jnp.where(ends, halo_ref[0, z], pltpu.roll(halo_ref[0, z + 1], TILE // 2, 0))

    def field_rows(z):
        rows = [pltpu.roll(halo_ref[f, z], 2 * f - 2, 0) if f > 1 else halo_ref[f, z] for f in (1, 2, 3)]
        mixed = jnp.where((sub == 0) | (sub == TILE - 1), rows[0], rows[1])
        return jnp.where((sub == 3) | (sub == 4), rows[2], mixed)

    def strips(z):
        group, k = divmod(z, GROUP)
        packed = jnp.zeros((TILE, 128), jnp.float32)
        for t in range(block // TILE):
            moved = pltpu.roll(merged_ref[group, t * TILE : t * TILE + TILE], (SPAN * t - SLOT * k) % 128, 1)
            packed = jnp.where((lane >= SPAN * t) & (lane < SPAN * t + SPAN), moved, packed)
        return packed

    put(FACE * xs, density_rows(0), density_rows(zs - 2))
    put(FACE * xs + TILE, field_rows(0), field_rows(zs - 1))
    put(FACE * xs + 2 * TILE, strips(0), strips(zs - 2))


def along_y(values, halo, lane, density):
    def shifted(off):
        mixed = jnp.where(lane >= 128 - off if off > 0 else lane < -off, halo, values)
        return pltpu.roll(mixed, off % 128, 1)

    m1, p1 = shifted(1), shifted(-1)
    near = m1 + p1
    blur = near + 2.0 * values
    if not density:
        return (blur,)
    m2, p2 = shifted(2), shifted(-2)
    return blur, (m2 + p2) + 4.0 * near + 6.0 * values, (p2 - m2) + 2.0 * (p1 - m1)


class Rows:
    def __init__(self, tiles, halo):
        self.tiles, self.halo = list(tiles), halo
        self.sub = lax.broadcasted_iota(jnp.int32, (TILE, 1), 0)
        self.made = {}

    def row(self, t):
        count = len(self.tiles)
        if 0 <= t < count:
            return self.tiles[t]
        if t not in self.made:
            down = t < 0
            step = -t - 1 if down else t - count
            halo = self.halo if step == 0 else pltpu.roll(self.halo, TILE - 1 if down else 1, 0)
            inner = pltpu.roll(self.tiles[t % count], 1 if down else TILE - 1, 0)
            self.made[t] = jnp.where(self.sub == (0 if down else TILE - 1), halo, inner)
        return self.made[t]

    def pair(self, level, t):
        if level == 0:
            return self.row(t)
        if (level, t) not in self.made:
            self.made[level, t] = self.pair(level - 1, t) + self.pair(level - 1, t + 1)
        return self.made[level, t]

    def blur(self):
        return [self.pair(2, t - 1) for t in range(len(self.tiles))]

    def blur2(self):
        return [self.pair(4, t - 2) for t in range(len(self.tiles))]

    def slope(self):
        return [self.pair(2, t) - self.pair(2, t - 2) for t in range(len(self.tiles))]


def cells_kernel(zs, xs, fields_ref, out_ref, cell_ref):
    each, tiles = 8, xs // TILE
    make_cell_weights(cell_ref)

    def step(k, carry):
        first = k * each
        for field in range(4):
            rows = [
                fields_ref[field, first + j, pl.ds(t, TILE, stride=tiles), :] for j in range(each) for t in range(tiles)
            ]
            weights = cell_ref[...] if field == 0 else cell_ref[:, 0:128]
            result = jnp.dot(halves(jnp.concatenate(rows, axis=0)), weights, preferred_element_type=jnp.float32)
            for part in (0, 1, 2) if field == 0 else (2 + field,):
                columns = slice(128 * part, 128 * part + 128) if field == 0 else slice(0, 128)
                out_ref[part, pl.ds(first, each)] = result[:, columns].reshape(each, xs, 128)
        return carry

    lax.fori_loop(0, zs // each, step, 0)


def cross_kernel(zs, xs, rows_ref, halo_ref, cell_ref, out_ref, edge_ref):
    each, tiles = 4, xs // TILE
    for field in range(4):
        weights = cell_ref[...] if field == 0 else cell_ref[:, 0:128]
        result = jnp.dot(
            halves(halo_ref[field].reshape(zs * TILE, 128)), weights, preferred_element_type=jnp.float32
        )
        for part in (0, 1, 2) if field == 0 else (2 + field,):
            columns = slice(128 * part, 128 * part + 128) if field == 0 else slice(0, 128)
            edge_ref[part] = result[:, columns].reshape(zs, TILE, 128)

    def step(k, carry):
        for j in range(each):
            z = k * each + j

            def part_rows(part):
                return Rows([rows_ref[part, z, t * TILE : t * TILE + TILE, :] for t in range(tiles)], edge_ref[part, z])

            twice, sloped = part_rows(1), part_rows(2)
            results = [part_rows(part).blur() for part in (0, 3, 4, 5)]
            results += [twice.blur2(), twice.slope(), sloped.blur2()]
            for part, values in enumerate(results):
                for t in range(tiles):
                    out_ref[part, z, t * TILE : t * TILE + TILE, :] = values[t]
        return carry

    lax.fori_loop(0, zs // each, step, 0)


def before_shade(load, z):
    def blur(part):
        return load(part, z - 1) + load(part, z + 1) + 2.0 * load(part, z)

    def blur2(part):
        return (load(part, z - 2) + load(part, z + 2)) + 4.0 * (load(part, z - 1) + load(part, z + 1)) + 6.0 * load(part, z)

    unit = 1.0 / 2048.0
    near = load(4, z + 1) - load(4, z - 1)
    grad_z = (load(4, z + 2) - load(4, z - 2)) + (near + near)
    grad_x = blur2(5)
    grad_y = blur2(6)
    facing = jnp.abs((0.8 * unit) * (grad_z + grad_y) + (0.4 * unit) * grad_x)
    square = grad_z * grad_z + grad_x * grad_x + grad_y * grad_y
    shading = 0.3 + facing * lax.rsqrt(square * (unit * unit) + 0.0025)
    density = (3.0 / 64.0) * blur(0)
    return [density, jnp.exp(-jnp.abs(density)), shading] + [blur(1 + c) for c in range(3)]


def shade(state, taken, looked, scale):
    density, t, shading = taken[:3]
    soft = jnp.maximum(density, 0.0) + t * polynomial(LOG1P, t)
    extinct = looked[3] * (soft * scale)
    passed, total, depth = state[0], state[1:4], state[4]
    weight = passed * (extinct * polynomial(EXPM1, extinct))
    lit = weight * shading
    colours = [
        total[c] + (looked[c] * lit) * (1.0 + 0.5 * jnp.tanh((1.0 / 64.0) * taken[3 + c])) for c in range(3)
    ]
    return (passed - weight, *colours, depth + extinct)


def inner_kernel(zs, xs, scale, cross_ref, merged_ref, looked_ref, strip_ref, inner_ref, full_ref, filtered_ref, taken_ref):
    tiles, each = xs // TILE, 8
    for group in range(merged_ref.shape[0]):
        rows = Rows([merged_ref[group, pl.ds(TILE + t, TILE, stride=tiles), :] for t in range(tiles)], merged_ref[group, 0:TILE])
        for k, values in enumerate((rows.blur(), rows.blur2(), rows.slope())):
            for t in range(tiles):
                filtered_ref[k, group, t * TILE : t * TILE + TILE, :] = values[t]

    def strip_step(step, carry):
        first = step * each
        for k, parts in enumerate(((0, 1, 2, 3), (4, 6), (5,))):
            strips = []
            for j in range(each):
                group = lax.div(first + j, GROUP)
                slot = first + j - group * GROUP
                strips.append(pltpu.roll(filtered_ref[k, group], lax.rem(128 - SLOT * slot, 128), 1))
            columns = slice((0, 512, 768)[k], (512, 768, 896)[k])
            result = jnp.dot(
                halves(jnp.concatenate(strips, axis=0)), strip_ref[:, columns], preferred_element_type=jnp.float32
            )
            for n, part in enumerate(parts):
                share = result[:, 128 * n : 128 * n + 128].reshape(each, xs, 128)
                full_ref[part, pl.ds(first, each)] = cross_ref[part, pl.ds(first, each)] + share
        return carry

    lax.fori_loop(0, zs // each, strip_step, 0)

    pairs = (zs - 4) // 2

    def take(step):
        for j in range(2):
            z = 2 + 2 * step + j
            for k, values in enumerate(before_shade(lambda part, z: full_ref[part, z], z)):
                taken_ref[k, j] = values

    def advance(step, state):
        for j in range(2):
            looked = [looked_ref[c, 2 + 2 * step + j] for c in range(4)]
            state = shade(state, [taken_ref[k, j] for k in range(6)], looked, scale)
        return state

    def z_step(step, state):
        state = advance(step, state)
        take(step + 1)
        return state

    zero = jnp.zeros((xs, 128), jnp.float32)
    take(0)
    state = lax.fori_loop(0, pairs - 1, z_step, (zero + 1.0, zero, zero, zero, zero))
    for k, values in enumerate(advance(pairs - 1, state)):
        inner_ref[k] = values


def edge_kernel(zs, xs, scale, fb_ref, fa_ref, cross_ref, looked_ref, inner_ref, *rest):
    out_refs, (near_ref, rows_ref, image_ref) = rest[:-3], rest[-3:]
    zfirst, zlast, zodd = place_of("gz")
    block = xs + TILE
    tiles = xs // TILE
    lane = lax.broadcasted_iota(jnp.int32, (1, 128), 1)
    for side in range(2):
        first, second = (fa_ref, fb_ref) if side == 0 else (fb_ref, fa_ref)

        def face(start, count):
            return jnp.where(zodd, first[start : start + count, :], second[start : start + count, :])

        ends = [face(FACE * xs, TILE), face(FACE * xs + TILE, TILE)]
        strips = face(FACE * xs + 2 * TILE, TILE)
        for j in range(FACE):
            field = max(j - 1, 0)
            layer = j if j < 2 else (1 if side == 0 else 0)
            turned = TILE // 2 * j if j < 2 else 2 * field - 2
            outer_rows = ends[min(field, 1)]
            if turned:
                outer_rows = pltpu.roll(outer_rows, TILE - turned, 0)
            at_lane = SLOT * layer + slot_of(field)[0]
            own = 126 if field == 0 else 127
            halo = [pltpu.roll(strips, (own - at_lane - SPAN * t) % 128, 1) for t in range(block // TILE)]
            values = jnp.concatenate([outer_rows, face(j * xs, xs)], axis=0)
            results = along_y(values, jnp.concatenate(halo, axis=0), lane, field == 0)
            for part, result in zip((0, 1, 2) if field == 0 else (2 + field,), results):
                rows_ref[side, layer, part] = result
    for side in range(2):
        edge = zfirst if side == 0 else zlast
        for layer in range(2):
            mirrored = 0 if side == 0 else zs - 1
            outer = layer == side

            def part_rows(part):
                ref = rows_ref.at[side, layer, part]
                return Rows([ref[pl.ds(TILE + t, TILE, stride=tiles), :] for t in range(tiles)], ref[0:TILE, :])

            twice, sloped = part_rows(1), part_rows(2)
            for part, values in zip((4, 5, 6), (twice.blur2(), twice.slope(), sloped.blur2())):
                for t in range(tiles):
                    rows = slice(t * TILE, t * TILE + TILE)
                    fill = -cross_ref[part, mirrored, rows] if outer else 0.0
                    near_ref[part, 2 * side + layer, rows] = jnp.where(edge, fill, values[t])
            if not outer:
                for part, source in enumerate((0, 3, 4, 5)):
                    for t, values in enumerate(part_rows(source).blur()):
                        near_ref[part, 2 * side + layer, t * TILE : t * TILE + TILE] = jnp.where(edge, 0.0, values)

    def load(part, z):
        if z < 0:
            return near_ref[part, z + 2]
        if z >= zs:
            return near_ref[part, z - zs + 2]
        return cross_ref[part, z]

    def behind(state, z):
        return shade(state, before_shade(load, z), [looked_ref[c, z] for c in range(4)], scale)

    zero = jnp.zeros((xs, 128), jnp.float32)
    state = behind(behind((zero + 1.0, zero, zero, zero, zero), 0), 1)
    passed = state[0]
    state = (
        passed * inner_ref[0],
        state[1] + passed * inner_ref[1],
        state[2] + passed * inner_ref[2],
        state[3] + passed * inner_ref[3],
        state[4] + inner_ref[4],
    )
    state = behind(behind(state, zs - 2), zs - 1)
    for c in range(4):
        for t in range(tiles):
            image_ref[c, pl.ds(t, TILE, stride=tiles), :] = state[1 + c][t * TILE : t * TILE + TILE]
    if len(out_refs) == 1:
        out_refs[0][...] = image_ref[...]
    else:
        part = xs // len(out_refs)
        for k, ref in enumerate(out_refs):
            ref[...] = image_ref[:, pl.ds(pl.multiple_of((lax.axis_index("gz") ^ k) * part, part), part), :]


def blend_kernel(near_ref, *refs):
    images, out_ref = refs[:-1], refs[-1]
    count = len(images)
    depths = [image[3] for image in images]
    colours = [jnp.zeros_like(depths[0])] * 3
    for k in range(count):
        prior = jnp.zeros_like(depths[0])
        for other in range(count):
            if other != k:
                prior += near_ref[k * count + other] * depths[other]
        through = jnp.exp(-prior)
        colours = [colours[c] + through * images[k][c] for c in range(3)]
    total = functools.reduce(jnp.add, depths)
    out_ref[0], out_ref[1], out_ref[2] = colours
    small = total * polynomial(EXPM1, total)
    out_ref[3] = jnp.where(total < 0.5, small, 1.0 - jnp.exp(-total))


def call(kernel, out_shape, specs, scratch=(), cost=1.0, name=None, limit=VMEM_LIMIT):
    where = {"s": pltpu.SMEM, "v": pltpu.VMEM, "a": pl.ANY}
    return pl.pallas_call(
        kernel,
        out_shape=out_shape,
        in_specs=[pl.BlockSpec(memory_space=where[s]) for s in specs],
        out_specs=jax.tree.map(lambda _: pl.BlockSpec(memory_space=pltpu.VMEM), out_shape),
        scratch_shapes=list(scratch),
        compiler_params=pltpu.CompilerParams(vmem_limit_bytes=limit),
        cost_estimate=pl.CostEstimate(flops=0, bytes_accessed=int(cost * 3.0e6), transcendentals=0),
        name=name,
    )


def swap_pairs(first, second, axis, idle):
    count, others = lax.axis_size(axis), lax.axis_size(idle)
    even = [(i, i ^ 1) for i in range(count)]
    if count == 2:
        one = lax.ppermute(first, axis, even)
        return one, one
    pairs = []
    for i in range(count):
        for j in range(others):
            end = i in (0, count - 1)
            to = (i if end else i + 1 if i % 2 else i - 1, j ^ 1 if end else j)
            if axis < idle:
                pairs.append((i * others + j, to[0] * others + to[1]))
            else:
                pairs.append((j * count + i, to[1] * count + to[0]))
    two = lax.ppermute(second, tuple(sorted((axis, idle))), pairs)
    return lax.ppermute(first, axis, even), two


def swap_corners(values, x_kind, y_kind):
    counts = [lax.axis_size(a) for a in ("gx", "gy")]

    def partner(at, count, kind):
        to = at ^ 1 if kind == 0 else at + 1 if at % 2 else at - 1
        return to if 0 <= to < count else at

    pairs = []
    for i in range(counts[0]):
        for j in range(counts[1]):
            to = partner(i, counts[0], x_kind), partner(j, counts[1], y_kind)
            pairs.append((i * counts[1] + j, to[0] * counts[1] + to[1]))
    return lax.ppermute(values, ("gx", "gy"), pairs)


def on_device(fields, material, depth_order, table):
    _, zs, xs, ys = fields.shape
    nx, nz = lax.axis_size("gx"), lax.axis_size("gz")
    block = xs + TILE
    part = xs // nz
    swaps = nz in (2, 4)
    groups = -(-zs // GROUP)
    f32 = lambda *shape: jax.ShapeDtypeStruct(shape, jnp.float32)

    def side(even_high):
        return call(functools.partial(rows_kernel, zs, xs, even_high), f32(FACE, zs, ys), "v", name="x_rows")(fields)

    x_a, x_b = swap_pairs(side(True), side(False) if nx > 2 else None, "gx", "gy")
    strip = jnp.asarray(strip_matrix(ys))
    looked, nearer = call(
        functools.partial(lookup_kernel, zs, xs, swaps),
        (f32(4, zs, xs, ys), f32(nz * nz, 1, 128)),
        "vvv",
        [pltpu.VMEM((4, 128), jnp.float32)],
        cost=1.2,
        name="lookup",
    )(depth_order[None], table, material)
    strips, corners = f32(groups, xs, 128), f32(groups, TILE, 128)
    main, *c = call(
        functools.partial(pack_kernel, zs, xs), (strips,) + (corners,) * (1 if nx == 2 else 2), "v", cost=0.7, name="pack"
    )(fields)
    y_a, y_b = swap_pairs(main, main, "gy", "gx")
    d = [swap_corners(values, x_kind, y_kind) for x_kind, values in enumerate(c) for y_kind in (0, 1)]
    rows, cell = call(
        functools.partial(cells_kernel, zs, xs),
        (f32(6, zs, xs, ys), jax.ShapeDtypeStruct((256, 3 * ys), jnp.bfloat16)),
        "v",
        cost=1.3,
        name="cells",
    )(fields)
    x_a, x_b, y_a, y_b, d, looked, rows = lax.optimization_barrier((x_a, x_b, y_a, y_b, d, looked, rows))

    faces = f32(FACE * xs + 3 * TILE, ys)
    halo, merged, f_a, f_b = call(
        functools.partial(join_kernel, zs, xs),
        (f32(4, zs, TILE, ys), f32(groups, block, 128), faces, faces),
        "v" * (6 + len(d)),
        name="join",
    )(fields, main, x_a, x_b, y_a, y_b, *d)
    z_a, z_b = swap_pairs(f_a, f_b, "gz", "gy")
    cross = call(
        functools.partial(cross_kernel, zs, xs),
        f32(7, zs, xs, ys),
        "vvv",
        [pltpu.VMEM((6, zs, TILE, ys), jnp.float32)],
        cost=1.0,
        name="cross",
    )(rows, halo, cell)

    scale = 2.0 / (zs * nz)
    inner, full = call(
        functools.partial(inner_kernel, zs, xs, scale),
        (f32(5, xs, ys), f32(7, zs, xs, ys)),
        "vvvv",
        [pltpu.VMEM((3, groups, xs, 128), jnp.float32), pltpu.VMEM((6, 2, xs, ys), jnp.float32)],
        cost=4.0,
        name="inner",
    )(cross, merged, looked, strip)

    images = call(
        functools.partial(edge_kernel, zs, xs, scale),
        [f32(4, part, ys)] * nz if swaps else [f32(4, xs, ys)],
        "vvvvv",
        [
            pltpu.VMEM((7, 4, xs, ys), jnp.float32),
            pltpu.VMEM((2, 2, 6, block, ys), jnp.float32),
            pltpu.VMEM((4, xs, ys), jnp.float32),
        ],
        name="edges",
    )(z_b, z_a, full, looked, inner)

    if swaps:
        mine = [images[0]]
        for k in range(1, nz):
            mine.append(lax.ppermute(images[k], "gz", [(i, i ^ k) for i in range(nz)]))
    else:
        stacked = lax.all_to_all(images[0].reshape(4, nz, part, ys), "gz", split_axis=1, concat_axis=1)
        mine = [stacked[:, b] for b in range(nz)]
    return call(blend_kernel, f32(4, part, ys), "v" + "v" * nz, name="blend")(nearer, *mine)


def solution(mesh):
    return jax.shard_map(
        on_device,
        mesh=mesh,
        in_specs=(P(None, "gz", "gx", "gy"), P("gz", "gx", "gy"), P(), P()),
        out_specs=P(None, ("gx", "gz"), "gy"),
        check_vma=False,
    )
```

```python
import functools

import jax
import jax.numpy as jnp
import ml_dtypes
import numpy as np
from jax import lax
from jax.experimental import pallas as pl
from jax.experimental.pallas import tpu as pltpu
from jax.sharding import PartitionSpec as P

VMEM_LIMIT = 40 * 1024 * 1024
GROUP = 12
SLOT = 10
TILE = 8
FACE = 5
SPAN = 24

LOG1P = (
    0.9999995186059567, -0.49996356582563917, 0.33265255844036573, -0.24453388969978707, 0.17659864766821842,
    -0.10679931280022417, 0.043659288844443055, -0.008466410404849948,
)
EXPM1 = (
    1.0, -0.4999995231628418, 0.1666584461927414, -0.04160914570093155, 0.00814302358776331, -0.0010865303920581937,
)


def polynomial(coefficients, value):
    terms = list(coefficients)
    power = value
    while len(terms) > 1:
        paired = [terms[k] + terms[k + 1] * power for k in range(0, len(terms) - 1, 2)]
        terms = paired + ([terms[-1]] if len(terms) % 2 else [])
        power = power * power if len(terms) > 1 else power
    return terms[0]


BLUR, BLUR2, SLOPE = {-1: 1, 0: 2, 1: 1}, {-2: 1, -1: 4, 0: 6, 1: 4, 2: 1}, {-2: -1, -1: -2, 1: 2, 2: 1}


def strip_matrix(ysize):
    strips = np.zeros((128, 7 * ysize), np.float32)
    for block, (taps, field) in enumerate([(BLUR, f) for f in range(4)] + [(BLUR2, 0), (SLOPE, 0), (BLUR2, 0)]):
        first = slot_of(field)[0]
        outside = {-2: 0, -1: 1, ysize: 2, ysize + 1: 3} if field == 0 else {-1: first, ysize: first + 1}
        for out in range(ysize):
            for off, weight in taps.items():
                if not 0 <= out + off < ysize:
                    strips[outside[out + off], block * ysize + out] = weight
    return np.concatenate([strips, strips], axis=0).astype(ml_dtypes.bfloat16)


def make_cell_weights(out_ref):
    off = lax.broadcasted_iota(jnp.int32, (128, 128), 0) - lax.broadcasted_iota(jnp.int32, (128, 128), 1)
    for block, taps in enumerate((BLUR, BLUR2, SLOPE)):
        weights = jnp.zeros((128, 128), jnp.float32)
        for step, weight in taps.items():
            weights = jnp.where(off == step, float(weight), weights)
        for half in range(2):
            out_ref[128 * half : 128 * half + 128, 128 * block : 128 * block + 128] = weights.astype(jnp.bfloat16)


def halves(values):
    high = values.astype(jnp.bfloat16)
    low = (values - high.astype(jnp.float32)).astype(jnp.bfloat16)
    return jnp.concatenate([high, low], axis=1)


def place_of(axis):
    at = lax.axis_index(axis)
    return at == 0, at == lax.axis_size(axis) - 1, lax.rem(at, 2) == 1


def rows_kernel(zs, xs, even_high, fields_ref, out_ref):
    high = (lax.rem(lax.axis_index("gx"), 2) == 0) == even_high
    for group in range(FACE):
        field = max(group - 1, 0)
        rows = fields_ref.at[field].reshape(zs * xs, 128)
        low_row = group if group < 2 else 0
        high_row = xs - 2 + group if group < 2 else xs - 1
        out_ref[group] = rows[pl.ds(jnp.where(high, high_row, low_row), zs, stride=xs), :]


def slot_of(field):
    return (0, 4) if field == 0 else (2 + 2 * field, 2)


def pack_strips(load, layers, lane, rows):
    packed = jnp.zeros((rows, 128), jnp.float32)
    for k, z in enumerate(layers):
        for field in range(4):
            first, count = slot_of(field)
            start = SLOT * k + first
            values = pltpu.roll(load(field, z), (start + count // 2) % 128, 1)
            packed = jnp.where((lane >= start) & (lane < start + count), values, packed)
    return packed


def pack_kernel(zs, xs, fields_ref, pack_ref, *corner_refs):
    xodd = place_of("gx")[2]
    lane = lax.broadcasted_iota(jnp.int32, (1, 128), 1)
    sub = lax.broadcasted_iota(jnp.int32, (TILE, 1), 0)
    for group in range(pack_ref.shape[0]):
        layers = range(group * GROUP, min(zs, group * GROUP + GROUP))
        packed = pack_strips(lambda f, z: fields_ref[f, z], layers, lane, xs)
        pack_ref[group] = packed
        first, last = packed[0:TILE], packed[xs - TILE :]
        low = jnp.where(sub == TILE - 1, pltpu.roll(first, TILE - 1, 0), pltpu.roll(first, TILE - 3, 0))
        high = jnp.where(sub == 0, pltpu.roll(last, 1, 0), pltpu.roll(last, 3, 0))
        for ref, swapped in zip(corner_refs, (False, True)):
            ref[group] = jnp.where(xodd != swapped, low, high)


def lookup_kernel(zs, xs, peers, order_ref, table_ref, ids_ref, looked_ref, near_ref, tables_ref):
    iz, count = lax.axis_index("gz"), lax.axis_size("gz")
    order = order_ref[...].astype(jnp.float32)
    lane = lax.broadcasted_iota(jnp.int32, order.shape, 1)
    ranks = [
        jnp.sum(jnp.where(lane == (iz ^ k if peers else k), order, 0.0), axis=1, keepdims=True) for k in range(count)
    ]
    for k in range(count):
        for other in range(count):
            nearer = jnp.where(ranks[other] < ranks[k], 1.0, 0.0)
            near_ref[k * count + other] = jnp.broadcast_to(nearer, (1, 128))
    tables_ref[...] = jnp.zeros_like(tables_ref)
    tables_ref[:, 0 : table_ref.shape[1]] = table_ref[...]
    tables = [jnp.broadcast_to(tables_ref[c : c + 1, :], (TILE, 128)) for c in range(4)]
    each = 8
    tiles = xs // TILE

    def step(k, carry):
        for j in range(each):
            z = k * each + j
            for t in range(tiles):
                ids = ids_ref[z, pl.ds(t, TILE, stride=tiles), :]
                for c in range(4):
                    looked_ref[c, z, t * TILE : t * TILE + TILE, :] = jnp.take_along_axis(
                        tables[c], ids, axis=1, mode="promise_in_bounds"
                    )
        return carry

    lax.fori_loop(0, zs // each, step, 0)


def join_kernel(zs, xs, fields_ref, own_ref, xa_ref, xb_ref, ya_ref, yb_ref, *rest):
    corner_refs, (halo_ref, merged_ref, fa_ref, fb_ref) = rest[:-4], rest[-4:]
    xfirst, xlast, xodd = place_of("gx")
    yfirst, ylast, yodd = place_of("gy")
    zodd = place_of("gz")[2]
    halo_ref[...] = jnp.zeros_like(halo_ref)
    for field in range(4):
        tiles = halo_ref.at[field].reshape(zs * TILE, 128)
        own = fields_ref.at[field].reshape(zs * xs, 128)
        at = 0 if field == 0 else 1 + field
        below = jnp.where(xodd, xa_ref[1 + field], xb_ref[1 + field])
        above = jnp.where(xodd, xb_ref[at], xa_ref[at])
        tiles[pl.ds(0, zs, stride=TILE), :] = jnp.where(xfirst, 0.0, below)
        tiles[pl.ds(TILE - 1, zs, stride=TILE), :] = jnp.where(xlast, 0.0, above)
        if field == 0:
            low, high = own[pl.ds(0, zs, stride=xs), :], own[pl.ds(xs - 1, zs, stride=xs), :]
            tiles[pl.ds(1, zs, stride=TILE), :] = jnp.where(xfirst, -low, jnp.where(xodd, xa_ref[0], xb_ref[0]))
            tiles[pl.ds(TILE - 2, zs, stride=TILE), :] = jnp.where(xlast, -high, jnp.where(xodd, xb_ref[1], xa_ref[1]))

    block = xs + TILE
    lane = lax.broadcasted_iota(jnp.int32, (1, 128), 1)
    sub = lax.broadcasted_iota(jnp.int32, (TILE, 1), 0)
    place = lax.rem(lane, SLOT)
    from_left = (place < 2) | ((place >= 4) & (lax.rem(place, 2) == 0))

    def merge(own, first, second):
        fill_left = jnp.where(place == 0, -pltpu.roll(own, 126, 1), 0.0)
        fill_right = jnp.where(place == 3, -pltpu.roll(own, 2, 1), 0.0)
        left = jnp.where(yfirst, fill_left, jnp.where(yodd, first, second))
        right = jnp.where(ylast, fill_right, jnp.where(yodd, second, first))
        return jnp.where(from_left, left, right)

    for group in range(own_ref.shape[0]):
        main = merge(own_ref[group], ya_ref[group], yb_ref[group])
        merged_ref[group, TILE:] = main
        tiles = []
        for k in range(2):
            a, b = corner_refs[k][group], corner_refs[k - 2][group]
            tiles.append(jnp.where(sub < TILE // 2, jnp.where(xodd, a, b), jnp.where(xodd, b, a)))
        tile = merge(tiles[1], tiles[0], tiles[1])
        low = jnp.where(sub == 1, -pltpu.roll(main[0:TILE], 1, 0), 0.0)
        high = jnp.where(sub == TILE - 2, -pltpu.roll(main[xs - TILE :], TILE - 1, 0), 0.0)
        tile = jnp.where(xfirst & (sub < TILE // 2), low, tile)
        merged_ref[group, 0:TILE] = jnp.where(xlast & (sub >= TILE // 2), high, tile)

    def put(start, low, high):
        for out_ref, swapped in ((fa_ref, False), (fb_ref, True)):
            out_ref[start : start + low.shape[0], :] = jnp.where(zodd != swapped, low, high)

    for j in range(FACE):
        put(j * xs, fields_ref[max(j - 1, 0), j if j < 2 else 0], fields_ref[max(j - 1, 0), zs - 2 + j if j < 2 else zs - 1])

    ends = (sub < 2) | (sub >= TILE - 2)

    def density_rows(z):
        return jnp.where(ends, halo_ref[0, z], pltpu.roll(halo_ref[0, z + 1], TILE // 2, 0))

    def field_rows(z):
        rows = [pltpu.roll(halo_ref[f, z], 2 * f - 2, 0) if f > 1 else halo_ref[f, z] for f in (1, 2, 3)]
        mixed = jnp.where((sub == 0) | (sub == TILE - 1), rows[0], rows[1])
        return jnp.where((sub == 3) | (sub == 4), rows[2], mixed)

    def strips(z):
        group, k = divmod(z, GROUP)
        packed = jnp.zeros((TILE, 128), jnp.float32)
        for t in range(block // TILE):
            moved = pltpu.roll(merged_ref[group, t * TILE : t * TILE + TILE], (SPAN * t - SLOT * k) % 128, 1)
            packed = jnp.where((lane >= SPAN * t) & (lane < SPAN * t + SPAN), moved, packed)
        return packed

    put(FACE * xs, density_rows(0), density_rows(zs - 2))
    put(FACE * xs + TILE, field_rows(0), field_rows(zs - 1))
    put(FACE * xs + 2 * TILE, strips(0), strips(zs - 2))


def along_y(values, halo, lane, density):
    def shifted(off):
        mixed = jnp.where(lane >= 128 - off if off > 0 else lane < -off, halo, values)
        return pltpu.roll(mixed, off % 128, 1)

    m1, p1 = shifted(1), shifted(-1)
    near = m1 + p1
    blur = near + 2.0 * values
    if not density:
        return (blur,)
    m2, p2 = shifted(2), shifted(-2)
    return blur, (m2 + p2) + 4.0 * near + 6.0 * values, (p2 - m2) + 2.0 * (p1 - m1)


class Rows:
    def __init__(self, tiles, halo):
        self.tiles, self.halo = list(tiles), halo
        self.sub = lax.broadcasted_iota(jnp.int32, (TILE, 1), 0)
        self.made = {}

    def row(self, t):
        count = len(self.tiles)
        if 0 <= t < count:
            return self.tiles[t]
        if t not in self.made:
            down = t < 0
            step = -t - 1 if down else t - count
            halo = self.halo if step == 0 else pltpu.roll(self.halo, TILE - 1 if down else 1, 0)
            inner = pltpu.roll(self.tiles[t % count], 1 if down else TILE - 1, 0)
            self.made[t] = jnp.where(self.sub == (0 if down else TILE - 1), halo, inner)
        return self.made[t]

    def pair(self, level, t):
        if level == 0:
            return self.row(t)
        if (level, t) not in self.made:
            self.made[level, t] = self.pair(level - 1, t) + self.pair(level - 1, t + 1)
        return self.made[level, t]

    def blur(self):
        return [self.pair(2, t - 1) for t in range(len(self.tiles))]

    def blur2(self):
        return [self.pair(4, t - 2) for t in range(len(self.tiles))]

    def slope(self):
        return [self.pair(2, t) - self.pair(2, t - 2) for t in range(len(self.tiles))]


def cells_kernel(zs, xs, fields_ref, out_ref, cell_ref):
    each, tiles = 8, xs // TILE
    make_cell_weights(cell_ref)

    def step(k, carry):
        first = k * each
        for field in range(4):
            rows = [
                fields_ref[field, first + j, pl.ds(t, TILE, stride=tiles), :] for j in range(each) for t in range(tiles)
            ]
            weights = cell_ref[...] if field == 0 else cell_ref[:, 0:128]
            result = jnp.dot(halves(jnp.concatenate(rows, axis=0)), weights, preferred_element_type=jnp.float32)
            for part in (0, 1, 2) if field == 0 else (2 + field,):
                columns = slice(128 * part, 128 * part + 128) if field == 0 else slice(0, 128)
                out_ref[part, pl.ds(first, each)] = result[:, columns].reshape(each, xs, 128)
        return carry

    lax.fori_loop(0, zs // each, step, 0)


def cross_kernel(zs, xs, rows_ref, halo_ref, cell_ref, out_ref, edge_ref):
    each, tiles = 4, xs // TILE
    for field in range(4):
        weights = cell_ref[...] if field == 0 else cell_ref[:, 0:128]
        result = jnp.dot(
            halves(halo_ref[field].reshape(zs * TILE, 128)), weights, preferred_element_type=jnp.float32
        )
        for part in (0, 1, 2) if field == 0 else (2 + field,):
            columns = slice(128 * part, 128 * part + 128) if field == 0 else slice(0, 128)
            edge_ref[part] = result[:, columns].reshape(zs, TILE, 128)

    def step(k, carry):
        for j in range(each):
            z = k * each + j

            def part_rows(part):
                return Rows([rows_ref[part, z, t * TILE : t * TILE + TILE, :] for t in range(tiles)], edge_ref[part, z])

            twice, sloped = part_rows(1), part_rows(2)
            results = [part_rows(part).blur() for part in (0, 3, 4, 5)]
            results += [twice.blur2(), twice.slope(), sloped.blur2()]
            for part, values in enumerate(results):
                for t in range(tiles):
                    out_ref[part, z, t * TILE : t * TILE + TILE, :] = values[t]
        return carry

    lax.fori_loop(0, zs // each, step, 0)


def before_shade(load, z):
    def blur(part):
        return load(part, z - 1) + load(part, z + 1) + 2.0 * load(part, z)

    def blur2(part):
        return (load(part, z - 2) + load(part, z + 2)) + 4.0 * (load(part, z - 1) + load(part, z + 1)) + 6.0 * load(part, z)

    unit = 1.0 / 2048.0
    near = load(4, z + 1) - load(4, z - 1)
    grad_z = (load(4, z + 2) - load(4, z - 2)) + (near + near)
    grad_x = blur2(5)
    grad_y = blur2(6)
    facing = jnp.abs((0.8 * unit) * (grad_z + grad_y) + (0.4 * unit) * grad_x)
    square = grad_z * grad_z + grad_x * grad_x + grad_y * grad_y
    shading = 0.3 + facing * lax.rsqrt(square * (unit * unit) + 0.0025)
    density = (3.0 / 64.0) * blur(0)
    return [density, jnp.exp(-jnp.abs(density)), shading] + [blur(1 + c) for c in range(3)]


def shade(state, taken, looked, scale):
    density, t, shading = taken[:3]
    soft = jnp.maximum(density, 0.0) + t * polynomial(LOG1P, t)
    extinct = looked[3] * (soft * scale)
    passed, total, depth = state[0], state[1:4], state[4]
    weight = passed * (extinct * polynomial(EXPM1, extinct))
    lit = weight * shading
    colours = [
        total[c] + (looked[c] * lit) * (1.0 + 0.5 * jnp.tanh((1.0 / 64.0) * taken[3 + c])) for c in range(3)
    ]
    return (passed - weight, *colours, depth + extinct)


def inner_kernel(zs, xs, scale, cross_ref, merged_ref, looked_ref, strip_ref, inner_ref, full_ref, filtered_ref, taken_ref):
    tiles, each = xs // TILE, 8
    for group in range(merged_ref.shape[0]):
        rows = Rows([merged_ref[group, pl.ds(TILE + t, TILE, stride=tiles), :] for t in range(tiles)], merged_ref[group, 0:TILE])
        for k, values in enumerate((rows.blur(), rows.blur2(), rows.slope())):
            for t in range(tiles):
                filtered_ref[k, group, t * TILE : t * TILE + TILE, :] = values[t]

    def strip_step(step, carry):
        first = step * each
        for k, parts in enumerate(((0, 1, 2, 3), (4, 6), (5,))):
            strips = []
            for j in range(each):
                group = lax.div(first + j, GROUP)
                slot = first + j - group * GROUP
                strips.append(pltpu.roll(filtered_ref[k, group], lax.rem(128 - SLOT * slot, 128), 1))
            columns = slice((0, 512, 768)[k], (512, 768, 896)[k])
            result = jnp.dot(
                halves(jnp.concatenate(strips, axis=0)), strip_ref[:, columns], preferred_element_type=jnp.float32
            )
            for n, part in enumerate(parts):
                share = result[:, 128 * n : 128 * n + 128].reshape(each, xs, 128)
                full_ref[part, pl.ds(first, each)] = cross_ref[part, pl.ds(first, each)] + share
        return carry

    lax.fori_loop(0, zs // each, strip_step, 0)

    ahead = taken_ref.shape[1]
    steps = (zs - 4) // ahead

    def take(step):
        for j in range(ahead):
            z = 2 + ahead * step + j
            for k, values in enumerate(before_shade(lambda part, z: full_ref[part, z], z)):
                taken_ref[k, j] = values

    def advance(step, state):
        for j in range(ahead):
            looked = [looked_ref[c, 2 + ahead * step + j] for c in range(4)]
            state = shade(state, [taken_ref[k, j] for k in range(6)], looked, scale)
        return state

    def z_step(step, state):
        state = advance(step, state)
        take(step + 1)
        return state

    zero = jnp.zeros((xs, 128), jnp.float32)
    take(0)
    state = lax.fori_loop(0, steps - 1, z_step, (zero + 1.0, zero, zero, zero, zero))
    for k, values in enumerate(advance(steps - 1, state)):
        inner_ref[k] = values


def edge_kernel(zs, xs, scale, fb_ref, fa_ref, cross_ref, looked_ref, inner_ref, *rest):
    out_refs, (near_ref, rows_ref, image_ref) = rest[:-3], rest[-3:]
    zfirst, zlast, zodd = place_of("gz")
    block = xs + TILE
    tiles = xs // TILE
    lane = lax.broadcasted_iota(jnp.int32, (1, 128), 1)
    for side in range(2):
        first, second = (fa_ref, fb_ref) if side == 0 else (fb_ref, fa_ref)

        def face(start, count):
            return jnp.where(zodd, first[start : start + count, :], second[start : start + count, :])

        ends = [face(FACE * xs, TILE), face(FACE * xs + TILE, TILE)]
        strips = face(FACE * xs + 2 * TILE, TILE)
        for j in range(FACE):
            field = max(j - 1, 0)
            layer = j if j < 2 else (1 if side == 0 else 0)
            turned = TILE // 2 * j if j < 2 else 2 * field - 2
            outer_rows = ends[min(field, 1)]
            if turned:
                outer_rows = pltpu.roll(outer_rows, TILE - turned, 0)
            at_lane = SLOT * layer + slot_of(field)[0]
            own = 126 if field == 0 else 127
            halo = [pltpu.roll(strips, (own - at_lane - SPAN * t) % 128, 1) for t in range(block // TILE)]
            values = jnp.concatenate([outer_rows, face(j * xs, xs)], axis=0)
            results = along_y(values, jnp.concatenate(halo, axis=0), lane, field == 0)
            for part, result in zip((0, 1, 2) if field == 0 else (2 + field,), results):
                rows_ref[side, layer, part] = result
    for side in range(2):
        edge = zfirst if side == 0 else zlast
        for layer in range(2):
            mirrored = 0 if side == 0 else zs - 1
            outer = layer == side

            def part_rows(part):
                ref = rows_ref.at[side, layer, part]
                return Rows([ref[pl.ds(TILE + t, TILE, stride=tiles), :] for t in range(tiles)], ref[0:TILE, :])

            twice, sloped = part_rows(1), part_rows(2)
            for part, values in zip((4, 5, 6), (twice.blur2(), twice.slope(), sloped.blur2())):
                for t in range(tiles):
                    rows = slice(t * TILE, t * TILE + TILE)
                    fill = -cross_ref[part, mirrored, rows] if outer else 0.0
                    near_ref[part, 2 * side + layer, rows] = jnp.where(edge, fill, values[t])
            if not outer:
                for part, source in enumerate((0, 3, 4, 5)):
                    for t, values in enumerate(part_rows(source).blur()):
                        near_ref[part, 2 * side + layer, t * TILE : t * TILE + TILE] = jnp.where(edge, 0.0, values)

    def load(part, z):
        if z < 0:
            return near_ref[part, z + 2]
        if z >= zs:
            return near_ref[part, z - zs + 2]
        return cross_ref[part, z]

    def behind(state, z):
        return shade(state, before_shade(load, z), [looked_ref[c, z] for c in range(4)], scale)

    zero = jnp.zeros((xs, 128), jnp.float32)
    state = behind(behind((zero + 1.0, zero, zero, zero, zero), 0), 1)
    passed = state[0]
    state = (
        passed * inner_ref[0],
        state[1] + passed * inner_ref[1],
        state[2] + passed * inner_ref[2],
        state[3] + passed * inner_ref[3],
        state[4] + inner_ref[4],
    )
    state = behind(behind(state, zs - 2), zs - 1)
    for c in range(4):
        for t in range(tiles):
            image_ref[c, pl.ds(t, TILE, stride=tiles), :] = state[1 + c][t * TILE : t * TILE + TILE]
    if len(out_refs) == 1:
        out_refs[0][...] = image_ref[...]
    else:
        part = xs // len(out_refs)
        for k, ref in enumerate(out_refs):
            ref[...] = image_ref[:, pl.ds(pl.multiple_of((lax.axis_index("gz") ^ k) * part, part), part), :]


def blend_kernel(near_ref, *refs):
    images, out_ref = refs[:-1], refs[-1]
    count = len(images)
    depths = [image[3] for image in images]
    colours = [jnp.zeros_like(depths[0])] * 3
    for k in range(count):
        prior = jnp.zeros_like(depths[0])
        for other in range(count):
            if other != k:
                prior += near_ref[k * count + other] * depths[other]
        through = jnp.exp(-prior)
        colours = [colours[c] + through * images[k][c] for c in range(3)]
    total = functools.reduce(jnp.add, depths)
    out_ref[0], out_ref[1], out_ref[2] = colours
    small = total * polynomial(EXPM1, total)
    out_ref[3] = jnp.where(total < 0.5, small, 1.0 - jnp.exp(-total))


def call(kernel, out_shape, specs, scratch=(), cost=1.0, name=None, limit=VMEM_LIMIT):
    where = {"s": pltpu.SMEM, "v": pltpu.VMEM, "a": pl.ANY}
    return pl.pallas_call(
        kernel,
        out_shape=out_shape,
        in_specs=[pl.BlockSpec(memory_space=where[s]) for s in specs],
        out_specs=jax.tree.map(lambda _: pl.BlockSpec(memory_space=pltpu.VMEM), out_shape),
        scratch_shapes=list(scratch),
        compiler_params=pltpu.CompilerParams(vmem_limit_bytes=limit),
        cost_estimate=pl.CostEstimate(flops=0, bytes_accessed=int(cost * 3.0e6), transcendentals=0),
        name=name,
    )


def swap_pairs(first, second, axis, idle):
    count, others = lax.axis_size(axis), lax.axis_size(idle)
    even = [(i, i ^ 1) for i in range(count)]
    if count == 2:
        one = lax.ppermute(first, axis, even)
        return one, one
    pairs = []
    for i in range(count):
        for j in range(others):
            end = i in (0, count - 1)
            to = (i if end else i + 1 if i % 2 else i - 1, j ^ 1 if end else j)
            if axis < idle:
                pairs.append((i * others + j, to[0] * others + to[1]))
            else:
                pairs.append((j * count + i, to[1] * count + to[0]))
    two = lax.ppermute(second, tuple(sorted((axis, idle))), pairs)
    return lax.ppermute(first, axis, even), two


def swap_corners(values, x_kind, y_kind):
    counts = [lax.axis_size(a) for a in ("gx", "gy")]

    def partner(at, count, kind):
        to = at ^ 1 if kind == 0 else at + 1 if at % 2 else at - 1
        return to if 0 <= to < count else at

    pairs = []
    for i in range(counts[0]):
        for j in range(counts[1]):
            to = partner(i, counts[0], x_kind), partner(j, counts[1], y_kind)
            pairs.append((i * counts[1] + j, to[0] * counts[1] + to[1]))
    return lax.ppermute(values, ("gx", "gy"), pairs)


def on_device(fields, material, depth_order, table):
    _, zs, xs, ys = fields.shape
    nx, nz = lax.axis_size("gx"), lax.axis_size("gz")
    block = xs + TILE
    part = xs // nz
    swaps = nz in (2, 4)
    groups = -(-zs // GROUP)
    f32 = lambda *shape: jax.ShapeDtypeStruct(shape, jnp.float32)

    def side(even_high):
        return call(functools.partial(rows_kernel, zs, xs, even_high), f32(FACE, zs, ys), "v", name="x_rows")(fields)

    x_a, x_b = swap_pairs(side(True), side(False) if nx > 2 else None, "gx", "gy")
    strip = jnp.asarray(strip_matrix(ys))
    looked, nearer = call(
        functools.partial(lookup_kernel, zs, xs, swaps),
        (f32(4, zs, xs, ys), f32(nz * nz, 1, 128)),
        "vvv",
        [pltpu.VMEM((4, 128), jnp.float32)],
        cost=1.2,
        name="lookup",
    )(depth_order[None], table, material)
    strips, corners = f32(groups, xs, 128), f32(groups, TILE, 128)
    main, *c = call(
        functools.partial(pack_kernel, zs, xs), (strips,) + (corners,) * (1 if nx == 2 else 2), "v", cost=0.7, name="pack"
    )(fields)
    y_a, y_b = swap_pairs(main, main, "gy", "gx")
    d = [swap_corners(values, x_kind, y_kind) for x_kind, values in enumerate(c) for y_kind in (0, 1)]
    rows, cell = call(
        functools.partial(cells_kernel, zs, xs),
        (f32(6, zs, xs, ys), jax.ShapeDtypeStruct((256, 3 * ys), jnp.bfloat16)),
        "v",
        cost=1.3,
        name="cells",
    )(fields)
    x_a, x_b, y_a, y_b, d, looked, rows = lax.optimization_barrier((x_a, x_b, y_a, y_b, d, looked, rows))

    faces = f32(FACE * xs + 3 * TILE, ys)
    halo, merged, f_a, f_b = call(
        functools.partial(join_kernel, zs, xs),
        (f32(4, zs, TILE, ys), f32(groups, block, 128), faces, faces),
        "v" * (6 + len(d)),
        name="join",
    )(fields, main, x_a, x_b, y_a, y_b, *d)
    z_a, z_b = swap_pairs(f_a, f_b, "gz", "gy")
    cross = call(
        functools.partial(cross_kernel, zs, xs),
        f32(7, zs, xs, ys),
        "vvv",
        [pltpu.VMEM((6, zs, TILE, ys), jnp.float32)],
        cost=1.0,
        name="cross",
    )(rows, halo, cell)

    scale = 2.0 / (zs * nz)
    inner, full = call(
        functools.partial(inner_kernel, zs, xs, scale),
        (f32(5, xs, ys), f32(7, zs, xs, ys)),
        "vvvv",
        [pltpu.VMEM((3, groups, xs, 128), jnp.float32), pltpu.VMEM((6, 4, xs, ys), jnp.float32)],
        cost=4.0,
        name="inner",
    )(cross, merged, looked, strip)

    images = call(
        functools.partial(edge_kernel, zs, xs, scale),
        [f32(4, part, ys)] * nz if swaps else [f32(4, xs, ys)],
        "vvvvv",
        [
            pltpu.VMEM((7, 4, xs, ys), jnp.float32),
            pltpu.VMEM((2, 2, 6, block, ys), jnp.float32),
            pltpu.VMEM((4, xs, ys), jnp.float32),
        ],
        name="edges",
    )(z_b, z_a, full, looked, inner)

    if swaps:
        mine = [images[0]]
        for k in range(1, nz):
            mine.append(lax.ppermute(images[k], "gz", [(i, i ^ k) for i in range(nz)]))
    else:
        stacked = lax.all_to_all(images[0].reshape(4, nz, part, ys), "gz", split_axis=1, concat_axis=1)
        mine = [stacked[:, b] for b in range(nz)]
    return call(blend_kernel, f32(4, part, ys), "v" + "v" * nz, name="blend")(nearer, *mine)


def solution(mesh):
    return jax.shard_map(
        on_device,
        mesh=mesh,
        in_specs=(P(None, "gz", "gx", "gy"), P("gz", "gx", "gy"), P(), P()),
        out_specs=P(None, ("gx", "gz"), "gy"),
        check_vma=False,
    )
```

```python
import functools

import jax
import jax.numpy as jnp
import ml_dtypes
import numpy as np
from jax import lax
from jax.experimental import pallas as pl
from jax.experimental.pallas import tpu as pltpu
from jax.sharding import PartitionSpec as P

VMEM_LIMIT = 40 * 1024 * 1024
GROUP = 12
SLOT = 10
TILE = 8
FACE = 5
SPAN = 24

LOG1P = (
    0.9999995186059567, -0.49996356582563917, 0.33265255844036573, -0.24453388969978707, 0.17659864766821842,
    -0.10679931280022417, 0.043659288844443055, -0.008466410404849948,
)
EXPM1 = (
    1.0, -0.4999995231628418, 0.1666584461927414, -0.04160914570093155, 0.00814302358776331, -0.0010865303920581937,
)


def polynomial(coefficients, value):
    terms = list(coefficients)
    power = value
    while len(terms) > 1:
        paired = [terms[k] + terms[k + 1] * power for k in range(0, len(terms) - 1, 2)]
        terms = paired + ([terms[-1]] if len(terms) % 2 else [])
        power = power * power if len(terms) > 1 else power
    return terms[0]


BLUR, BLUR2, SLOPE = {-1: 1, 0: 2, 1: 1}, {-2: 1, -1: 4, 0: 6, 1: 4, 2: 1}, {-2: -1, -1: -2, 1: 2, 2: 1}


def strip_matrix(ysize):
    strips = np.zeros((128, 7 * ysize), np.float32)
    for block, (taps, field) in enumerate([(BLUR, f) for f in range(4)] + [(BLUR2, 0), (SLOPE, 0), (BLUR2, 0)]):
        first = slot_of(field)[0]
        outside = {-2: 0, -1: 1, ysize: 2, ysize + 1: 3} if field == 0 else {-1: first, ysize: first + 1}
        for out in range(ysize):
            for off, weight in taps.items():
                if not 0 <= out + off < ysize:
                    strips[outside[out + off], block * ysize + out] = weight
    return np.concatenate([strips, strips], axis=0).astype(ml_dtypes.bfloat16)


def make_cell_weights(out_ref):
    off = lax.broadcasted_iota(jnp.int32, (128, 128), 0) - lax.broadcasted_iota(jnp.int32, (128, 128), 1)
    for block, taps in enumerate((BLUR, BLUR2, SLOPE)):
        weights = jnp.zeros((128, 128), jnp.float32)
        for step, weight in taps.items():
            weights = jnp.where(off == step, float(weight), weights)
        for half in range(2):
            out_ref[128 * half : 128 * half + 128, 128 * block : 128 * block + 128] = weights.astype(jnp.bfloat16)


def halves(values):
    high = values.astype(jnp.bfloat16)
    low = (values - high.astype(jnp.float32)).astype(jnp.bfloat16)
    return jnp.concatenate([high, low], axis=1)


def place_of(axis):
    at = lax.axis_index(axis)
    return at == 0, at == lax.axis_size(axis) - 1, lax.rem(at, 2) == 1


def rows_kernel(zs, xs, even_high, fields_ref, out_ref):
    high = (lax.rem(lax.axis_index("gx"), 2) == 0) == even_high
    for group in range(FACE):
        field = max(group - 1, 0)
        rows = fields_ref.at[field].reshape(zs * xs, 128)
        low_row = group if group < 2 else 0
        high_row = xs - 2 + group if group < 2 else xs - 1
        out_ref[group] = rows[pl.ds(jnp.where(high, high_row, low_row), zs, stride=xs), :]


def slot_of(field):
    return (0, 4) if field == 0 else (2 + 2 * field, 2)


def pack_strips(load, layers, lane, rows):
    packed = jnp.zeros((rows, 128), jnp.float32)
    for k, z in enumerate(layers):
        for field in range(4):
            first, count = slot_of(field)
            start = SLOT * k + first
            values = pltpu.roll(load(field, z), (start + count // 2) % 128, 1)
            packed = jnp.where((lane >= start) & (lane < start + count), values, packed)
    return packed


def pack_kernel(zs, xs, fields_ref, pack_ref, *corner_refs):
    xodd = place_of("gx")[2]
    lane = lax.broadcasted_iota(jnp.int32, (1, 128), 1)
    sub = lax.broadcasted_iota(jnp.int32, (TILE, 1), 0)
    for group in range(pack_ref.shape[0]):
        layers = range(group * GROUP, min(zs, group * GROUP + GROUP))
        packed = pack_strips(lambda f, z: fields_ref[f, z], layers, lane, xs)
        pack_ref[group] = packed
        first, last = packed[0:TILE], packed[xs - TILE :]
        low = jnp.where(sub == TILE - 1, pltpu.roll(first, TILE - 1, 0), pltpu.roll(first, TILE - 3, 0))
        high = jnp.where(sub == 0, pltpu.roll(last, 1, 0), pltpu.roll(last, 3, 0))
        for ref, swapped in zip(corner_refs, (False, True)):
            ref[group] = jnp.where(xodd != swapped, low, high)


def nearer_layers(peers, order_ref, near_ref):
    iz, count = lax.axis_index("gz"), lax.axis_size("gz")
    order = order_ref[...].astype(jnp.float32)
    lane = lax.broadcasted_iota(jnp.int32, order.shape, 1)
    ranks = [
        jnp.sum(jnp.where(lane == (iz ^ k if peers else k), order, 0.0), axis=1, keepdims=True) for k in range(count)
    ]
    for k in range(count):
        for other in range(count):
            nearer = jnp.where(ranks[other] < ranks[k], 1.0, 0.0)
            near_ref[k * count + other] = jnp.broadcast_to(nearer, (1, 128))


def tables_of(table_ref, wide_ref):
    wide_ref[...] = jnp.zeros_like(wide_ref)
    wide_ref[:, 0 : table_ref.shape[1]] = table_ref[...]
    return [jnp.broadcast_to(wide_ref[c : c + 1, :], (TILE, 128)) for c in range(4)]


def look_up(tables, ids_ref, z, t, tiles):
    ids = ids_ref[z, pl.ds(t, TILE, stride=tiles), :]
    return [jnp.take_along_axis(row, ids, axis=1, mode="promise_in_bounds") for row in tables]


def x_halo_kernel(zs, xs, fields_ref, xa_ref, xb_ref, halo_ref):
    xfirst, xlast, xodd = place_of("gx")
    halo_ref[...] = jnp.zeros_like(halo_ref)
    for field in range(4):
        tiles = halo_ref.at[field].reshape(zs * TILE, 128)
        own = fields_ref.at[field].reshape(zs * xs, 128)
        at = 0 if field == 0 else 1 + field
        below = jnp.where(xodd, xa_ref[1 + field], xb_ref[1 + field])
        above = jnp.where(xodd, xb_ref[at], xa_ref[at])
        tiles[pl.ds(0, zs, stride=TILE), :] = jnp.where(xfirst, 0.0, below)
        tiles[pl.ds(TILE - 1, zs, stride=TILE), :] = jnp.where(xlast, 0.0, above)
        if field == 0:
            low, high = own[pl.ds(0, zs, stride=xs), :], own[pl.ds(xs - 1, zs, stride=xs), :]
            tiles[pl.ds(1, zs, stride=TILE), :] = jnp.where(xfirst, -low, jnp.where(xodd, xa_ref[0], xb_ref[0]))
            tiles[pl.ds(TILE - 2, zs, stride=TILE), :] = jnp.where(xlast, -high, jnp.where(xodd, xb_ref[1], xa_ref[1]))


def join_kernel(zs, xs, fields_ref, halo_ref, own_ref, ya_ref, yb_ref, *rest):
    corner_refs, (merged_ref, fa_ref, fb_ref) = rest[:-3], rest[-3:]
    xfirst, xlast, xodd = place_of("gx")
    yfirst, ylast, yodd = place_of("gy")
    zodd = place_of("gz")[2]
    block = xs + TILE
    lane = lax.broadcasted_iota(jnp.int32, (1, 128), 1)
    sub = lax.broadcasted_iota(jnp.int32, (TILE, 1), 0)
    place = lax.rem(lane, SLOT)
    from_left = (place < 2) | ((place >= 4) & (lax.rem(place, 2) == 0))

    def merge(own, first, second):
        fill_left = jnp.where(place == 0, -pltpu.roll(own, 126, 1), 0.0)
        fill_right = jnp.where(place == 3, -pltpu.roll(own, 2, 1), 0.0)
        left = jnp.where(yfirst, fill_left, jnp.where(yodd, first, second))
        right = jnp.where(ylast, fill_right, jnp.where(yodd, second, first))
        return jnp.where(from_left, left, right)

    for group in range(own_ref.shape[0]):
        main = merge(own_ref[group], ya_ref[group], yb_ref[group])
        merged_ref[group, TILE:] = main
        tiles = []
        for k in range(2):
            a, b = corner_refs[k][group], corner_refs[k - 2][group]
            tiles.append(jnp.where(sub < TILE // 2, jnp.where(xodd, a, b), jnp.where(xodd, b, a)))
        tile = merge(tiles[1], tiles[0], tiles[1])
        low = jnp.where(sub == 1, -pltpu.roll(main[0:TILE], 1, 0), 0.0)
        high = jnp.where(sub == TILE - 2, -pltpu.roll(main[xs - TILE :], TILE - 1, 0), 0.0)
        tile = jnp.where(xfirst & (sub < TILE // 2), low, tile)
        merged_ref[group, 0:TILE] = jnp.where(xlast & (sub >= TILE // 2), high, tile)

    def put(start, low, high):
        for out_ref, swapped in ((fa_ref, False), (fb_ref, True)):
            out_ref[start : start + low.shape[0], :] = jnp.where(zodd != swapped, low, high)

    for j in range(FACE):
        put(j * xs, fields_ref[max(j - 1, 0), j if j < 2 else 0], fields_ref[max(j - 1, 0), zs - 2 + j if j < 2 else zs - 1])

    ends = (sub < 2) | (sub >= TILE - 2)

    def density_rows(z):
        return jnp.where(ends, halo_ref[0, z], pltpu.roll(halo_ref[0, z + 1], TILE // 2, 0))

    def field_rows(z):
        rows = [pltpu.roll(halo_ref[f, z], 2 * f - 2, 0) if f > 1 else halo_ref[f, z] for f in (1, 2, 3)]
        mixed = jnp.where((sub == 0) | (sub == TILE - 1), rows[0], rows[1])
        return jnp.where((sub == 3) | (sub == 4), rows[2], mixed)

    def strips(z):
        group, k = divmod(z, GROUP)
        packed = jnp.zeros((TILE, 128), jnp.float32)
        for t in range(block // TILE):
            moved = pltpu.roll(merged_ref[group, t * TILE : t * TILE + TILE], (SPAN * t - SLOT * k) % 128, 1)
            packed = jnp.where((lane >= SPAN * t) & (lane < SPAN * t + SPAN), moved, packed)
        return packed

    put(FACE * xs, density_rows(0), density_rows(zs - 2))
    put(FACE * xs + TILE, field_rows(0), field_rows(zs - 1))
    put(FACE * xs + 2 * TILE, strips(0), strips(zs - 2))


def along_y(values, halo, lane, density):
    def shifted(off):
        mixed = jnp.where(lane >= 128 - off if off > 0 else lane < -off, halo, values)
        return pltpu.roll(mixed, off % 128, 1)

    m1, p1 = shifted(1), shifted(-1)
    near = m1 + p1
    blur = near + 2.0 * values
    if not density:
        return (blur,)
    m2, p2 = shifted(2), shifted(-2)
    return blur, (m2 + p2) + 4.0 * near + 6.0 * values, (p2 - m2) + 2.0 * (p1 - m1)


class Rows:
    def __init__(self, tiles, halo):
        self.tiles, self.halo = list(tiles), halo
        self.sub = lax.broadcasted_iota(jnp.int32, (TILE, 1), 0)
        self.made = {}

    def row(self, t):
        count = len(self.tiles)
        if 0 <= t < count:
            return self.tiles[t]
        if t not in self.made:
            down = t < 0
            step = -t - 1 if down else t - count
            halo = self.halo if step == 0 else pltpu.roll(self.halo, TILE - 1 if down else 1, 0)
            inner = pltpu.roll(self.tiles[t % count], 1 if down else TILE - 1, 0)
            self.made[t] = jnp.where(self.sub == (0 if down else TILE - 1), halo, inner)
        return self.made[t]

    def pair(self, level, t):
        if level == 0:
            return self.row(t)
        if (level, t) not in self.made:
            self.made[level, t] = self.pair(level - 1, t) + self.pair(level - 1, t + 1)
        return self.made[level, t]

    def blur(self):
        return [self.pair(2, t - 1) for t in range(len(self.tiles))]

    def blur2(self):
        return [self.pair(4, t - 2) for t in range(len(self.tiles))]

    def slope(self):
        return [self.pair(2, t) - self.pair(2, t - 2) for t in range(len(self.tiles))]


def cells_kernel(zs, xs, fields_ref, out_ref, cell_ref):
    each, tiles = 8, xs // TILE
    make_cell_weights(cell_ref)

    def step(k, carry):
        first = k * each
        for field in range(4):
            rows = [
                fields_ref[field, first + j, pl.ds(t, TILE, stride=tiles), :] for j in range(each) for t in range(tiles)
            ]
            weights = cell_ref[...] if field == 0 else cell_ref[:, 0:128]
            result = jnp.dot(halves(jnp.concatenate(rows, axis=0)), weights, preferred_element_type=jnp.float32)
            for part in (0, 1, 2) if field == 0 else (2 + field,):
                columns = slice(128 * part, 128 * part + 128) if field == 0 else slice(0, 128)
                out_ref[part, pl.ds(first, each)] = result[:, columns].reshape(each, xs, 128)
        return carry

    lax.fori_loop(0, zs // each, step, 0)


def cross_kernel(zs, xs, peers, order_ref, rows_ref, halo_ref, cell_ref, out_ref, near_ref, edge_ref):
    each, tiles = 4, xs // TILE
    nearer_layers(peers, order_ref, near_ref)
    for field in range(4):
        weights = cell_ref[...] if field == 0 else cell_ref[:, 0:128]
        result = jnp.dot(
            halves(halo_ref[field].reshape(zs * TILE, 128)), weights, preferred_element_type=jnp.float32
        )
        for part in (0, 1, 2) if field == 0 else (2 + field,):
            columns = slice(128 * part, 128 * part + 128) if field == 0 else slice(0, 128)
            edge_ref[part] = result[:, columns].reshape(zs, TILE, 128)

    def step(k, carry):
        for j in range(each):
            z = k * each + j

            def part_rows(part):
                return Rows([rows_ref[part, z, t * TILE : t * TILE + TILE, :] for t in range(tiles)], edge_ref[part, z])

            twice, sloped = part_rows(1), part_rows(2)
            results = [part_rows(part).blur() for part in (0, 3, 4, 5)]
            results += [twice.blur2(), twice.slope(), sloped.blur2()]
            for part, values in enumerate(results):
                for t in range(tiles):
                    out_ref[part, z, t * TILE : t * TILE + TILE, :] = values[t]
        return carry

    lax.fori_loop(0, zs // each, step, 0)


def before_shade(load, z):
    def blur(part):
        return load(part, z - 1) + load(part, z + 1) + 2.0 * load(part, z)

    def blur2(part):
        return (load(part, z - 2) + load(part, z + 2)) + 4.0 * (load(part, z - 1) + load(part, z + 1)) + 6.0 * load(part, z)

    unit = 1.0 / 2048.0
    near = load(4, z + 1) - load(4, z - 1)
    grad_z = (load(4, z + 2) - load(4, z - 2)) + (near + near)
    grad_x = blur2(5)
    grad_y = blur2(6)
    facing = jnp.abs((0.8 * unit) * (grad_z + grad_y) + (0.4 * unit) * grad_x)
    square = grad_z * grad_z + grad_x * grad_x + grad_y * grad_y
    shading = 0.3 + facing * lax.rsqrt(square * (unit * unit) + 0.0025)
    density = (3.0 / 64.0) * blur(0)
    return [density, jnp.exp(-jnp.abs(density)), shading] + [blur(1 + c) for c in range(3)]


def shade(state, taken, looked, scale):
    density, t, shading = taken[:3]
    soft = jnp.maximum(density, 0.0) + t * polynomial(LOG1P, t)
    extinct = looked[3] * (soft * scale)
    passed, total, depth = state[0], state[1:4], state[4]
    weight = passed * (extinct * polynomial(EXPM1, extinct))
    lit = weight * shading
    colours = [
        total[c] + (looked[c] * lit) * (1.0 + 0.5 * jnp.tanh((1.0 / 64.0) * taken[3 + c])) for c in range(3)
    ]
    return (passed - weight, *colours, depth + extinct)


def inner_kernel(zs, xs, scale, cross_ref, merged_ref, table_ref, ids_ref, strip_ref, inner_ref, full_ref, filtered_ref, taken_ref, wide_ref):
    tiles, each = xs // TILE, 8
    tables = tables_of(table_ref, wide_ref)
    for group in range(merged_ref.shape[0]):
        rows = Rows([merged_ref[group, pl.ds(TILE + t, TILE, stride=tiles), :] for t in range(tiles)], merged_ref[group, 0:TILE])
        for k, values in enumerate((rows.blur(), rows.blur2(), rows.slope())):
            for t in range(tiles):
                filtered_ref[k, group, t * TILE : t * TILE + TILE, :] = values[t]

    def strip_step(step, carry):
        first = step * each
        for k, parts in enumerate(((0, 1, 2, 3), (4, 6), (5,))):
            strips = []
            for j in range(each):
                group = lax.div(first + j, GROUP)
                slot = first + j - group * GROUP
                strips.append(pltpu.roll(filtered_ref[k, group], lax.rem(128 - SLOT * slot, 128), 1))
            columns = slice((0, 512, 768)[k], (512, 768, 896)[k])
            result = jnp.dot(
                halves(jnp.concatenate(strips, axis=0)), strip_ref[:, columns], preferred_element_type=jnp.float32
            )
            for n, part in enumerate(parts):
                share = result[:, 128 * n : 128 * n + 128].reshape(each, xs, 128)
                full_ref[part, pl.ds(first, each)] = cross_ref[part, pl.ds(first, each)] + share
        return carry

    lax.fori_loop(0, zs // each, strip_step, 0)

    ahead = taken_ref.shape[1]
    steps = (zs - 4) // ahead

    def take(step):
        for j in range(ahead):
            z = 2 + ahead * step + j
            for k, values in enumerate(before_shade(lambda part, z: full_ref[part, z], z)):
                taken_ref[k, j] = values
            for t in range(tiles):
                for c, values in enumerate(look_up(tables, ids_ref, z, t, tiles)):
                    taken_ref[6 + c, j, t * TILE : t * TILE + TILE, :] = values

    def advance(step, state):
        for j in range(ahead):
            taken = [taken_ref[k, j] for k in range(10)]
            state = shade(state, taken[:6], taken[6:], scale)
        return state

    def z_step(step, state):
        state = advance(step, state)
        take(step + 1)
        return state

    zero = jnp.zeros((xs, 128), jnp.float32)
    take(0)
    state = lax.fori_loop(0, steps - 1, z_step, (zero + 1.0, zero, zero, zero, zero))
    for k, values in enumerate(advance(steps - 1, state)):
        inner_ref[k] = values


def edge_kernel(zs, xs, scale, fb_ref, fa_ref, cross_ref, table_ref, ids_ref, inner_ref, *rest):
    out_refs, (near_ref, rows_ref, image_ref, wide_ref) = rest[:-4], rest[-4:]
    tables = tables_of(table_ref, wide_ref)
    zfirst, zlast, zodd = place_of("gz")
    block = xs + TILE
    tiles = xs // TILE
    lane = lax.broadcasted_iota(jnp.int32, (1, 128), 1)
    for side in range(2):
        first, second = (fa_ref, fb_ref) if side == 0 else (fb_ref, fa_ref)

        def face(start, count):
            return jnp.where(zodd, first[start : start + count, :], second[start : start + count, :])

        ends = [face(FACE * xs, TILE), face(FACE * xs + TILE, TILE)]
        strips = face(FACE * xs + 2 * TILE, TILE)
        for j in range(FACE):
            field = max(j - 1, 0)
            layer = j if j < 2 else (1 if side == 0 else 0)
            turned = TILE // 2 * j if j < 2 else 2 * field - 2
            outer_rows = ends[min(field, 1)]
            if turned:
                outer_rows = pltpu.roll(outer_rows, TILE - turned, 0)
            at_lane = SLOT * layer + slot_of(field)[0]
            own = 126 if field == 0 else 127
            halo = [pltpu.roll(strips, (own - at_lane - SPAN * t) % 128, 1) for t in range(block // TILE)]
            values = jnp.concatenate([outer_rows, face(j * xs, xs)], axis=0)
            results = along_y(values, jnp.concatenate(halo, axis=0), lane, field == 0)
            for part, result in zip((0, 1, 2) if field == 0 else (2 + field,), results):
                rows_ref[side, layer, part] = result
    for side in range(2):
        edge = zfirst if side == 0 else zlast
        for layer in range(2):
            mirrored = 0 if side == 0 else zs - 1
            outer = layer == side

            def part_rows(part):
                ref = rows_ref.at[side, layer, part]
                return Rows([ref[pl.ds(TILE + t, TILE, stride=tiles), :] for t in range(tiles)], ref[0:TILE, :])

            twice, sloped = part_rows(1), part_rows(2)
            for part, values in zip((4, 5, 6), (twice.blur2(), twice.slope(), sloped.blur2())):
                for t in range(tiles):
                    rows = slice(t * TILE, t * TILE + TILE)
                    fill = -cross_ref[part, mirrored, rows] if outer else 0.0
                    near_ref[part, 2 * side + layer, rows] = jnp.where(edge, fill, values[t])
            if not outer:
                for part, source in enumerate((0, 3, 4, 5)):
                    for t, values in enumerate(part_rows(source).blur()):
                        near_ref[part, 2 * side + layer, t * TILE : t * TILE + TILE] = jnp.where(edge, 0.0, values)

    def load(part, z):
        if z < 0:
            return near_ref[part, z + 2]
        if z >= zs:
            return near_ref[part, z - zs + 2]
        return cross_ref[part, z]

    def behind(state, z):
        parts = [look_up(tables, ids_ref, z, t, tiles) for t in range(tiles)]
        looked = [jnp.concatenate([part[c] for part in parts], axis=0) for c in range(4)]
        return shade(state, before_shade(load, z), looked, scale)

    zero = jnp.zeros((xs, 128), jnp.float32)
    state = behind(behind((zero + 1.0, zero, zero, zero, zero), 0), 1)
    passed = state[0]
    state = (
        passed * inner_ref[0],
        state[1] + passed * inner_ref[1],
        state[2] + passed * inner_ref[2],
        state[3] + passed * inner_ref[3],
        state[4] + inner_ref[4],
    )
    state = behind(behind(state, zs - 2), zs - 1)
    for c in range(4):
        for t in range(tiles):
            image_ref[c, pl.ds(t, TILE, stride=tiles), :] = state[1 + c][t * TILE : t * TILE + TILE]
    if len(out_refs) == 1:
        out_refs[0][...] = image_ref[...]
    else:
        part = xs // len(out_refs)
        for k, ref in enumerate(out_refs):
            ref[...] = image_ref[:, pl.ds(pl.multiple_of((lax.axis_index("gz") ^ k) * part, part), part), :]


def blend_kernel(near_ref, *refs):
    images, out_ref = refs[:-1], refs[-1]
    count = len(images)
    depths = [image[3] for image in images]
    colours = [jnp.zeros_like(depths[0])] * 3
    for k in range(count):
        prior = jnp.zeros_like(depths[0])
        for other in range(count):
            if other != k:
                prior += near_ref[k * count + other] * depths[other]
        through = jnp.exp(-prior)
        colours = [colours[c] + through * images[k][c] for c in range(3)]
    total = functools.reduce(jnp.add, depths)
    out_ref[0], out_ref[1], out_ref[2] = colours
    small = total * polynomial(EXPM1, total)
    out_ref[3] = jnp.where(total < 0.5, small, 1.0 - jnp.exp(-total))


def call(kernel, out_shape, specs, scratch=(), cost=1.0, name=None, limit=VMEM_LIMIT):
    where = {"s": pltpu.SMEM, "v": pltpu.VMEM, "a": pl.ANY}
    return pl.pallas_call(
        kernel,
        out_shape=out_shape,
        in_specs=[pl.BlockSpec(memory_space=where[s]) for s in specs],
        out_specs=jax.tree.map(lambda _: pl.BlockSpec(memory_space=pltpu.VMEM), out_shape),
        scratch_shapes=list(scratch),
        compiler_params=pltpu.CompilerParams(vmem_limit_bytes=limit),
        cost_estimate=pl.CostEstimate(flops=0, bytes_accessed=int(cost * 3.0e6), transcendentals=0),
        name=name,
    )


def swap_pairs(first, second, axis, idle):
    count, others = lax.axis_size(axis), lax.axis_size(idle)
    even = [(i, i ^ 1) for i in range(count)]
    if count == 2:
        one = lax.ppermute(first, axis, even)
        return one, one
    pairs = []
    for i in range(count):
        for j in range(others):
            end = i in (0, count - 1)
            to = (i if end else i + 1 if i % 2 else i - 1, j ^ 1 if end else j)
            if axis < idle:
                pairs.append((i * others + j, to[0] * others + to[1]))
            else:
                pairs.append((j * count + i, to[1] * count + to[0]))
    two = lax.ppermute(second, tuple(sorted((axis, idle))), pairs)
    return lax.ppermute(first, axis, even), two


def swap_corners(values, x_kind, y_kind):
    counts = [lax.axis_size(a) for a in ("gx", "gy")]

    def partner(at, count, kind):
        to = at ^ 1 if kind == 0 else at + 1 if at % 2 else at - 1
        return to if 0 <= to < count else at

    pairs = []
    for i in range(counts[0]):
        for j in range(counts[1]):
            to = partner(i, counts[0], x_kind), partner(j, counts[1], y_kind)
            pairs.append((i * counts[1] + j, to[0] * counts[1] + to[1]))
    return lax.ppermute(values, ("gx", "gy"), pairs)


def on_device(fields, material, depth_order, table):
    _, zs, xs, ys = fields.shape
    nx, nz = lax.axis_size("gx"), lax.axis_size("gz")
    block = xs + TILE
    part = xs // nz
    swaps = nz in (2, 4)
    groups = -(-zs // GROUP)
    f32 = lambda *shape: jax.ShapeDtypeStruct(shape, jnp.float32)

    def side(even_high):
        return call(functools.partial(rows_kernel, zs, xs, even_high), f32(FACE, zs, ys), "v", name="x_rows")(fields)

    x_a, x_b = swap_pairs(side(True), side(False) if nx > 2 else None, "gx", "gy")
    strip = jnp.asarray(strip_matrix(ys))
    strips, corners = f32(groups, xs, 128), f32(groups, TILE, 128)
    main, *c = call(
        functools.partial(pack_kernel, zs, xs), (strips,) + (corners,) * (1 if nx == 2 else 2), "v", cost=0.7, name="pack"
    )(fields)
    y_a, y_b = swap_pairs(main, main, "gy", "gx")
    d = [swap_corners(values, x_kind, y_kind) for x_kind, values in enumerate(c) for y_kind in (0, 1)]
    rows, cell = call(
        functools.partial(cells_kernel, zs, xs),
        (f32(6, zs, xs, ys), jax.ShapeDtypeStruct((256, 3 * ys), jnp.bfloat16)),
        "v",
        cost=1.3,
        name="cells",
    )(fields)
    halo = call(functools.partial(x_halo_kernel, zs, xs), f32(4, zs, TILE, ys), "vvv", cost=0.2, name="x_halo")(
        fields, x_a, x_b
    )
    cross, nearer = call(
        functools.partial(cross_kernel, zs, xs, swaps),
        (f32(7, zs, xs, ys), f32(nz * nz, 1, 128)),
        "vvvv",
        [pltpu.VMEM((6, zs, TILE, ys), jnp.float32)],
        cost=1.0,
        name="cross",
    )(depth_order[None], rows, halo, cell)
    y_a, y_b, d, cross = lax.optimization_barrier((y_a, y_b, d, cross))

    faces = f32(FACE * xs + 3 * TILE, ys)
    merged, f_a, f_b = call(
        functools.partial(join_kernel, zs, xs),
        (f32(groups, block, 128), faces, faces),
        "v" * (5 + len(d)),
        name="join",
    )(fields, halo, main, y_a, y_b, *d)
    z_a, z_b = swap_pairs(f_a, f_b, "gz", "gy")

    scale = 2.0 / (zs * nz)
    inner, full = call(
        functools.partial(inner_kernel, zs, xs, scale),
        (f32(5, xs, ys), f32(7, zs, xs, ys)),
        "vvvvv",
        [
            pltpu.VMEM((3, groups, xs, 128), jnp.float32),
            pltpu.VMEM((10, 4, xs, ys), jnp.float32),
            pltpu.VMEM((4, 128), jnp.float32),
        ],
        cost=4.0,
        name="inner",
    )(cross, merged, table, material, strip)

    images = call(
        functools.partial(edge_kernel, zs, xs, scale),
        [f32(4, part, ys)] * nz if swaps else [f32(4, xs, ys)],
        "vvvvvv",
        [
            pltpu.VMEM((7, 4, xs, ys), jnp.float32),
            pltpu.VMEM((2, 2, 6, block, ys), jnp.float32),
            pltpu.VMEM((4, xs, ys), jnp.float32),
            pltpu.VMEM((4, 128), jnp.float32),
        ],
        name="edges",
    )(z_b, z_a, full, table, material, inner)

    if swaps:
        mine = [images[0]]
        for k in range(1, nz):
            mine.append(lax.ppermute(images[k], "gz", [(i, i ^ k) for i in range(nz)]))
    else:
        stacked = lax.all_to_all(images[0].reshape(4, nz, part, ys), "gz", split_axis=1, concat_axis=1)
        mine = [stacked[:, b] for b in range(nz)]
    return call(blend_kernel, f32(4, part, ys), "v" + "v" * nz, name="blend")(nearer, *mine)


def solution(mesh):
    return jax.shard_map(
        on_device,
        mesh=mesh,
        in_specs=(P(None, "gz", "gx", "gy"), P("gz", "gx", "gy"), P(), P()),
        out_specs=P(None, ("gx", "gz"), "gy"),
        check_vma=False,
    )
```

```python
import functools

import jax
import jax.numpy as jnp
import ml_dtypes
import numpy as np
from jax import lax
from jax.experimental import pallas as pl
from jax.experimental.pallas import tpu as pltpu
from jax.sharding import PartitionSpec as P

VMEM_LIMIT = 40 * 1024 * 1024
GROUP = 12
SLOT = 10
TILE = 8
FACE = 5
SPAN = 24

LOG1P = (
    0.9999995186059567, -0.49996356582563917, 0.33265255844036573, -0.24453388969978707, 0.17659864766821842,
    -0.10679931280022417, 0.043659288844443055, -0.008466410404849948,
)
EXPM1 = (
    1.0, -0.4999995231628418, 0.1666584461927414, -0.04160914570093155, 0.00814302358776331, -0.0010865303920581937,
)


def polynomial(coefficients, value):
    terms = list(coefficients)
    power = value
    while len(terms) > 1:
        paired = [terms[k] + terms[k + 1] * power for k in range(0, len(terms) - 1, 2)]
        terms = paired + ([terms[-1]] if len(terms) % 2 else [])
        power = power * power if len(terms) > 1 else power
    return terms[0]


BLUR, BLUR2, SLOPE = {-1: 1, 0: 2, 1: 1}, {-2: 1, -1: 4, 0: 6, 1: 4, 2: 1}, {-2: -1, -1: -2, 1: 2, 2: 1}


def strip_matrix(ysize):
    strips = np.zeros((128, 7 * ysize), np.float32)
    for block, (taps, field) in enumerate([(BLUR, f) for f in range(4)] + [(BLUR2, 0), (SLOPE, 0), (BLUR2, 0)]):
        first = slot_of(field)[0]
        outside = {-2: 0, -1: 1, ysize: 2, ysize + 1: 3} if field == 0 else {-1: first, ysize: first + 1}
        for out in range(ysize):
            for off, weight in taps.items():
                if not 0 <= out + off < ysize:
                    strips[outside[out + off], block * ysize + out] = weight
    return np.concatenate([strips, strips], axis=0).astype(ml_dtypes.bfloat16)


def make_cell_weights(out_ref):
    off = lax.broadcasted_iota(jnp.int32, (128, 128), 0) - lax.broadcasted_iota(jnp.int32, (128, 128), 1)
    for block, taps in enumerate((BLUR, BLUR2, SLOPE)):
        weights = jnp.zeros((128, 128), jnp.float32)
        for step, weight in taps.items():
            weights = jnp.where(off == step, float(weight), weights)
        for half in range(2):
            out_ref[128 * half : 128 * half + 128, 128 * block : 128 * block + 128] = weights.astype(jnp.bfloat16)


def halves(values):
    high = values.astype(jnp.bfloat16)
    low = (values - high.astype(jnp.float32)).astype(jnp.bfloat16)
    return jnp.concatenate([high, low], axis=1)


def place_of(axis):
    at = lax.axis_index(axis)
    return at == 0, at == lax.axis_size(axis) - 1, lax.rem(at, 2) == 1


def rows_kernel(zs, xs, even_high, fields_ref, out_ref):
    high = (lax.rem(lax.axis_index("gx"), 2) == 0) == even_high
    for group in range(FACE):
        field = max(group - 1, 0)
        rows = fields_ref.at[field].reshape(zs * xs, 128)
        low_row = group if group < 2 else 0
        high_row = xs - 2 + group if group < 2 else xs - 1
        out_ref[group] = rows[pl.ds(jnp.where(high, high_row, low_row), zs, stride=xs), :]


def slot_of(field):
    return (0, 4) if field == 0 else (2 + 2 * field, 2)


def pack_strips(load, layers, lane, rows):
    packed = jnp.zeros((rows, 128), jnp.float32)
    for k, z in enumerate(layers):
        for field in range(4):
            first, count = slot_of(field)
            start = SLOT * k + first
            values = pltpu.roll(load(field, z), (start + count // 2) % 128, 1)
            packed = jnp.where((lane >= start) & (lane < start + count), values, packed)
    return packed


def put_faces(zodd, out_refs, start, low, high):
    for ref, swapped in zip(out_refs, (False, True)):
        ref[start : start + low.shape[0], :] = jnp.where(zodd != swapped, low, high)


def pack_kernel(zs, xs, fields_ref, pack_ref, ma_ref, mb_ref, *corner_refs):
    zodd = place_of("gz")[2]
    for j in range(FACE):
        field = max(j - 1, 0)
        low, high = fields_ref[field, j if j < 2 else 0], fields_ref[field, zs - 2 + j if j < 2 else zs - 1]
        put_faces(zodd, (ma_ref, mb_ref), j * xs, low, high)
    xodd = place_of("gx")[2]
    lane = lax.broadcasted_iota(jnp.int32, (1, 128), 1)
    sub = lax.broadcasted_iota(jnp.int32, (TILE, 1), 0)
    for group in range(pack_ref.shape[0]):
        layers = range(group * GROUP, min(zs, group * GROUP + GROUP))
        packed = pack_strips(lambda f, z: fields_ref[f, z], layers, lane, xs)
        pack_ref[group] = packed
        first, last = packed[0:TILE], packed[xs - TILE :]
        low = jnp.where(sub == TILE - 1, pltpu.roll(first, TILE - 1, 0), pltpu.roll(first, TILE - 3, 0))
        high = jnp.where(sub == 0, pltpu.roll(last, 1, 0), pltpu.roll(last, 3, 0))
        for ref, swapped in zip(corner_refs, (False, True)):
            ref[group] = jnp.where(xodd != swapped, low, high)


def nearer_layers(offsets, order_ref, near_ref):
    iz, count = lax.axis_index("gz"), lax.axis_size("gz")
    order = order_ref[...].astype(jnp.float32)
    lane = lax.broadcasted_iota(jnp.int32, order.shape, 1)
    ranks = [
        jnp.sum(jnp.where(lane == (iz ^ offsets[k] if offsets else k), order, 0.0), axis=1, keepdims=True)
        for k in range(count)
    ]
    for k in range(count):
        for other in range(count):
            nearer = jnp.where(ranks[other] < ranks[k], 1.0, 0.0)
            near_ref[k * count + other] = jnp.broadcast_to(nearer, (1, 128))


def tables_of(table_ref, wide_ref):
    wide_ref[...] = jnp.zeros_like(wide_ref)
    wide_ref[:, 0 : table_ref.shape[1]] = table_ref[...]
    return [jnp.broadcast_to(wide_ref[c : c + 1, :], (TILE, 128)) for c in range(4)]


def look_up(tables, ids_ref, z, t, tiles):
    ids = ids_ref[z, pl.ds(t, TILE, stride=tiles), :]
    return [jnp.take_along_axis(row, ids, axis=1, mode="promise_in_bounds") for row in tables]


def x_halo_kernel(zs, xs, fields_ref, xa_ref, xb_ref, halo_ref):
    xfirst, xlast, xodd = place_of("gx")
    halo_ref[...] = jnp.zeros_like(halo_ref)
    for field in range(4):
        tiles = halo_ref.at[field].reshape(zs * TILE, 128)
        own = fields_ref.at[field].reshape(zs * xs, 128)
        at = 0 if field == 0 else 1 + field
        below = jnp.where(xodd, xa_ref[1 + field], xb_ref[1 + field])
        above = jnp.where(xodd, xb_ref[at], xa_ref[at])
        tiles[pl.ds(0, zs, stride=TILE), :] = jnp.where(xfirst, 0.0, below)
        tiles[pl.ds(TILE - 1, zs, stride=TILE), :] = jnp.where(xlast, 0.0, above)
        if field == 0:
            low, high = own[pl.ds(0, zs, stride=xs), :], own[pl.ds(xs - 1, zs, stride=xs), :]
            tiles[pl.ds(1, zs, stride=TILE), :] = jnp.where(xfirst, -low, jnp.where(xodd, xa_ref[0], xb_ref[0]))
            tiles[pl.ds(TILE - 2, zs, stride=TILE), :] = jnp.where(xlast, -high, jnp.where(xodd, xb_ref[1], xa_ref[1]))


def join_kernel(zs, xs, ma_ref, mb_ref, halo_ref, own_ref, ya_ref, yb_ref, *rest):
    corner_refs, (merged_ref, fa_ref, fb_ref) = rest[:-3], rest[-3:]
    xfirst, xlast, xodd = place_of("gx")
    yfirst, ylast, yodd = place_of("gy")
    zodd = place_of("gz")[2]
    block = xs + TILE
    lane = lax.broadcasted_iota(jnp.int32, (1, 128), 1)
    sub = lax.broadcasted_iota(jnp.int32, (TILE, 1), 0)
    place = lax.rem(lane, SLOT)
    from_left = (place < 2) | ((place >= 4) & (lax.rem(place, 2) == 0))

    def merge(own, first, second):
        fill_left = jnp.where(place == 0, -pltpu.roll(own, 126, 1), 0.0)
        fill_right = jnp.where(place == 3, -pltpu.roll(own, 2, 1), 0.0)
        left = jnp.where(yfirst, fill_left, jnp.where(yodd, first, second))
        right = jnp.where(ylast, fill_right, jnp.where(yodd, second, first))
        return jnp.where(from_left, left, right)

    for group in range(own_ref.shape[0]):
        main = merge(own_ref[group], ya_ref[group], yb_ref[group])
        merged_ref[group, TILE:] = main
        tiles = []
        for k in range(2):
            a, b = corner_refs[k][group], corner_refs[k - 2][group]
            tiles.append(jnp.where(sub < TILE // 2, jnp.where(xodd, a, b), jnp.where(xodd, b, a)))
        tile = merge(tiles[1], tiles[0], tiles[1])
        low = jnp.where(sub == 1, -pltpu.roll(main[0:TILE], 1, 0), 0.0)
        high = jnp.where(sub == TILE - 2, -pltpu.roll(main[xs - TILE :], TILE - 1, 0), 0.0)
        tile = jnp.where(xfirst & (sub < TILE // 2), low, tile)
        merged_ref[group, 0:TILE] = jnp.where(xlast & (sub >= TILE // 2), high, tile)

    ends = (sub < 2) | (sub >= TILE - 2)

    def density_rows(z):
        return jnp.where(ends, halo_ref[0, z], pltpu.roll(halo_ref[0, z + 1], TILE // 2, 0))

    def field_rows(z):
        rows = [pltpu.roll(halo_ref[f, z], 2 * f - 2, 0) if f > 1 else halo_ref[f, z] for f in (1, 2, 3)]
        mixed = jnp.where((sub == 0) | (sub == TILE - 1), rows[0], rows[1])
        return jnp.where((sub == 3) | (sub == 4), rows[2], mixed)

    def strips(z):
        group, k = divmod(z, GROUP)
        packed = jnp.zeros((TILE, 128), jnp.float32)
        for t in range(block // TILE):
            moved = pltpu.roll(merged_ref[group, t * TILE : t * TILE + TILE], (SPAN * t - SLOT * k) % 128, 1)
            packed = jnp.where((lane >= SPAN * t) & (lane < SPAN * t + SPAN), moved, packed)
        return packed

    outs, start = (fa_ref, fb_ref), FACE * xs
    fa_ref[0:start, :] = ma_ref[...]
    fb_ref[0:start, :] = mb_ref[...]
    put_faces(zodd, outs, start, density_rows(0), density_rows(zs - 2))
    put_faces(zodd, outs, start + TILE, field_rows(0), field_rows(zs - 1))
    put_faces(zodd, outs, start + 2 * TILE, strips(0), strips(zs - 2))


def along_y(values, halo, lane, density):
    def shifted(off):
        mixed = jnp.where(lane >= 128 - off if off > 0 else lane < -off, halo, values)
        return pltpu.roll(mixed, off % 128, 1)

    m1, p1 = shifted(1), shifted(-1)
    near = m1 + p1
    blur = near + 2.0 * values
    if not density:
        return (blur,)
    m2, p2 = shifted(2), shifted(-2)
    return blur, (m2 + p2) + 4.0 * near + 6.0 * values, (p2 - m2) + 2.0 * (p1 - m1)


class Rows:
    def __init__(self, tiles, halo):
        self.tiles, self.halo = list(tiles), halo
        self.sub = lax.broadcasted_iota(jnp.int32, (TILE, 1), 0)
        self.made = {}

    def row(self, t):
        count = len(self.tiles)
        if 0 <= t < count:
            return self.tiles[t]
        if t not in self.made:
            down = t < 0
            step = -t - 1 if down else t - count
            halo = self.halo if step == 0 else pltpu.roll(self.halo, TILE - 1 if down else 1, 0)
            inner = pltpu.roll(self.tiles[t % count], 1 if down else TILE - 1, 0)
            self.made[t] = jnp.where(self.sub == (0 if down else TILE - 1), halo, inner)
        return self.made[t]

    def pair(self, level, t):
        if level == 0:
            return self.row(t)
        if (level, t) not in self.made:
            self.made[level, t] = self.pair(level - 1, t) + self.pair(level - 1, t + 1)
        return self.made[level, t]

    def blur(self):
        return [self.pair(2, t - 1) for t in range(len(self.tiles))]

    def blur2(self):
        return [self.pair(4, t - 2) for t in range(len(self.tiles))]

    def slope(self):
        return [self.pair(2, t) - self.pair(2, t - 2) for t in range(len(self.tiles))]


def cells_kernel(zs, xs, fields_ref, out_ref, cell_ref):
    each, tiles = 8, xs // TILE
    make_cell_weights(cell_ref)

    def step(k, carry):
        first = k * each
        for field in range(4):
            rows = [
                fields_ref[field, first + j, pl.ds(t, TILE, stride=tiles), :] for j in range(each) for t in range(tiles)
            ]
            weights = cell_ref[...] if field == 0 else cell_ref[:, 0:128]
            result = jnp.dot(halves(jnp.concatenate(rows, axis=0)), weights, preferred_element_type=jnp.float32)
            for part in (0, 1, 2) if field == 0 else (2 + field,):
                columns = slice(128 * part, 128 * part + 128) if field == 0 else slice(0, 128)
                out_ref[part, pl.ds(first, each)] = result[:, columns].reshape(each, xs, 128)
        return carry

    lax.fori_loop(0, zs // each, step, 0)


def cross_kernel(zs, xs, offsets, order_ref, rows_ref, halo_ref, cell_ref, out_ref, near_ref, edge_ref):
    each, tiles = 4, xs // TILE
    nearer_layers(offsets, order_ref, near_ref)
    for field in range(4):
        weights = cell_ref[...] if field == 0 else cell_ref[:, 0:128]
        result = jnp.dot(
            halves(halo_ref[field].reshape(zs * TILE, 128)), weights, preferred_element_type=jnp.float32
        )
        for part in (0, 1, 2) if field == 0 else (2 + field,):
            columns = slice(128 * part, 128 * part + 128) if field == 0 else slice(0, 128)
            edge_ref[part] = result[:, columns].reshape(zs, TILE, 128)

    def step(k, carry):
        for j in range(each):
            z = k * each + j

            def part_rows(part):
                return Rows([rows_ref[part, z, t * TILE : t * TILE + TILE, :] for t in range(tiles)], edge_ref[part, z])

            twice, sloped = part_rows(1), part_rows(2)
            results = [part_rows(part).blur() for part in (0, 3, 4, 5)]
            results += [twice.blur2(), twice.slope(), sloped.blur2()]
            for part, values in enumerate(results):
                for t in range(tiles):
                    out_ref[part, z, t * TILE : t * TILE + TILE, :] = values[t]
        return carry

    lax.fori_loop(0, zs // each, step, 0)


def before_shade(load, z):
    def blur(part):
        return load(part, z - 1) + load(part, z + 1) + 2.0 * load(part, z)

    def blur2(part):
        return (load(part, z - 2) + load(part, z + 2)) + 4.0 * (load(part, z - 1) + load(part, z + 1)) + 6.0 * load(part, z)

    unit = 1.0 / 2048.0
    near = load(4, z + 1) - load(4, z - 1)
    grad_z = (load(4, z + 2) - load(4, z - 2)) + (near + near)
    grad_x = blur2(5)
    grad_y = blur2(6)
    facing = jnp.abs((0.8 * unit) * (grad_z + grad_y) + (0.4 * unit) * grad_x)
    square = grad_z * grad_z + grad_x * grad_x + grad_y * grad_y
    shading = 0.3 + facing * lax.rsqrt(square * (unit * unit) + 0.0025)
    density = (3.0 / 64.0) * blur(0)
    return [density, jnp.exp(-jnp.abs(density)), shading] + [blur(1 + c) for c in range(3)]


def shade(state, taken, looked, scale):
    density, t, shading = taken[:3]
    soft = jnp.maximum(density, 0.0) + t * polynomial(LOG1P, t)
    extinct = looked[3] * (soft * scale)
    passed, total, depth = state[0], state[1:4], state[4]
    weight = passed * (extinct * polynomial(EXPM1, extinct))
    lit = weight * shading
    colours = [
        total[c] + (looked[c] * lit) * (1.0 + 0.5 * jnp.tanh((1.0 / 64.0) * taken[3 + c])) for c in range(3)
    ]
    return (passed - weight, *colours, depth + extinct)


def inner_kernel(zs, xs, scale, cross_ref, merged_ref, table_ref, ids_ref, strip_ref, inner_ref, full_ref, looked_ref, filtered_ref, taken_ref, wide_ref):
    tiles, each = xs // TILE, 8
    tables = tables_of(table_ref, wide_ref)
    for group in range(merged_ref.shape[0]):
        rows = Rows([merged_ref[group, pl.ds(TILE + t, TILE, stride=tiles), :] for t in range(tiles)], merged_ref[group, 0:TILE])
        for k, values in enumerate((rows.blur(), rows.blur2(), rows.slope())):
            for t in range(tiles):
                filtered_ref[k, group, t * TILE : t * TILE + TILE, :] = values[t]

    def strip_step(step, carry):
        first = step * each
        for k, parts in enumerate(((0, 1, 2, 3), (4, 6), (5,))):
            strips = []
            for j in range(each):
                group = lax.div(first + j, GROUP)
                slot = first + j - group * GROUP
                strips.append(pltpu.roll(filtered_ref[k, group], lax.rem(128 - SLOT * slot, 128), 1))
            columns = slice((0, 512, 768)[k], (512, 768, 896)[k])
            result = jnp.dot(
                halves(jnp.concatenate(strips, axis=0)), strip_ref[:, columns], preferred_element_type=jnp.float32
            )
            for n, part in enumerate(parts):
                share = result[:, 128 * n : 128 * n + 128].reshape(each, xs, 128)
                full_ref[part, pl.ds(first, each)] = cross_ref[part, pl.ds(first, each)] + share
        return carry

    lax.fori_loop(0, zs // each, strip_step, 0)

    ahead = taken_ref.shape[1]
    steps = (zs - 4) // ahead

    def take(step):
        for j in range(ahead):
            z = 2 + ahead * step + j
            for k, values in enumerate(before_shade(lambda part, z: full_ref[part, z], z)):
                taken_ref[k, j] = values
            for t in range(tiles):
                for c, values in enumerate(look_up(tables, ids_ref, z, t, tiles)):
                    taken_ref[6 + c, j, t * TILE : t * TILE + TILE, :] = values

    def advance(step, state):
        for j in range(ahead):
            taken = [taken_ref[k, j] for k in range(10)]
            state = shade(state, taken[:6], taken[6:], scale)
        return state

    def z_step(step, state):
        state = advance(step, state)
        take(step + 1)
        return state

    for k, z in enumerate((0, 1, zs - 2, zs - 1)):
        for t in range(tiles):
            for c, values in enumerate(look_up(tables, ids_ref, z, t, tiles)):
                looked_ref[c, k, t * TILE : t * TILE + TILE, :] = values
    zero = jnp.zeros((xs, 128), jnp.float32)
    take(0)
    state = lax.fori_loop(0, steps - 1, z_step, (zero + 1.0, zero, zero, zero, zero))
    for k, values in enumerate(advance(steps - 1, state)):
        inner_ref[k] = values


def edge_kernel(zs, xs, scale, fb_ref, fa_ref, cross_ref, looked_ref, inner_ref, *rest):
    out_refs, (near_ref, rows_ref, image_ref) = rest[:-3], rest[-3:]
    zfirst, zlast, zodd = place_of("gz")
    block = xs + TILE
    tiles = xs // TILE
    lane = lax.broadcasted_iota(jnp.int32, (1, 128), 1)
    for side in range(2):
        first, second = (fa_ref, fb_ref) if side == 0 else (fb_ref, fa_ref)

        def face(start, count):
            return jnp.where(zodd, first[start : start + count, :], second[start : start + count, :])

        ends = [face(FACE * xs, TILE), face(FACE * xs + TILE, TILE)]
        strips = face(FACE * xs + 2 * TILE, TILE)
        for j in range(FACE):
            field = max(j - 1, 0)
            layer = j if j < 2 else (1 if side == 0 else 0)
            turned = TILE // 2 * j if j < 2 else 2 * field - 2
            outer_rows = ends[min(field, 1)]
            if turned:
                outer_rows = pltpu.roll(outer_rows, TILE - turned, 0)
            at_lane = SLOT * layer + slot_of(field)[0]
            own = 126 if field == 0 else 127
            halo = [pltpu.roll(strips, (own - at_lane - SPAN * t) % 128, 1) for t in range(block // TILE)]
            values = jnp.concatenate([outer_rows, face(j * xs, xs)], axis=0)
            results = along_y(values, jnp.concatenate(halo, axis=0), lane, field == 0)
            for part, result in zip((0, 1, 2) if field == 0 else (2 + field,), results):
                rows_ref[side, layer, part] = result
    for side in range(2):
        edge = zfirst if side == 0 else zlast
        for layer in range(2):
            mirrored = 0 if side == 0 else zs - 1
            outer = layer == side

            def part_rows(part):
                ref = rows_ref.at[side, layer, part]
                return Rows([ref[pl.ds(TILE + t, TILE, stride=tiles), :] for t in range(tiles)], ref[0:TILE, :])

            twice, sloped = part_rows(1), part_rows(2)
            for part, values in zip((4, 5, 6), (twice.blur2(), twice.slope(), sloped.blur2())):
                for t in range(tiles):
                    rows = slice(t * TILE, t * TILE + TILE)
                    fill = -cross_ref[part, mirrored, rows] if outer else 0.0
                    near_ref[part, 2 * side + layer, rows] = jnp.where(edge, fill, values[t])
            if not outer:
                for part, source in enumerate((0, 3, 4, 5)):
                    for t, values in enumerate(part_rows(source).blur()):
                        near_ref[part, 2 * side + layer, t * TILE : t * TILE + TILE] = jnp.where(edge, 0.0, values)

    def load(part, z):
        if z < 0:
            return near_ref[part, z + 2]
        if z >= zs:
            return near_ref[part, z - zs + 2]
        return cross_ref[part, z]

    def behind(state, z):
        looked = [looked_ref[c, z if z < 2 else z - zs + 4] for c in range(4)]
        return shade(state, before_shade(load, z), looked, scale)

    zero = jnp.zeros((xs, 128), jnp.float32)
    state = behind(behind((zero + 1.0, zero, zero, zero, zero), 0), 1)
    passed = state[0]
    state = (
        passed * inner_ref[0],
        state[1] + passed * inner_ref[1],
        state[2] + passed * inner_ref[2],
        state[3] + passed * inner_ref[3],
        state[4] + inner_ref[4],
    )
    state = behind(behind(state, zs - 2), zs - 1)
    for c in range(4):
        for t in range(tiles):
            image_ref[c, pl.ds(t, TILE, stride=tiles), :] = state[1 + c][t * TILE : t * TILE + TILE]
    if len(out_refs) == 1:
        out_refs[0][...] = image_ref[...]
    else:
        part = xs // len(out_refs)
        for k, ref in enumerate(out_refs):
            ref[...] = image_ref[:, pl.ds(pl.multiple_of((lax.axis_index("gz") ^ k) * part, part), part), :]


def blend_kernel(near_ref, *refs):
    images, out_ref = refs[:-1], refs[-1]
    count = len(images)
    depths = [image[3] for image in images]
    colours = [jnp.zeros_like(depths[0])] * 3
    for k in range(count):
        prior = jnp.zeros_like(depths[0])
        for other in range(count):
            if other != k:
                prior += near_ref[k * count + other] * depths[other]
        through = jnp.exp(-prior)
        colours = [colours[c] + through * images[k][c] for c in range(3)]
    total = functools.reduce(jnp.add, depths)
    out_ref[0], out_ref[1], out_ref[2] = colours
    small = total * polynomial(EXPM1, total)
    out_ref[3] = jnp.where(total < 0.5, small, 1.0 - jnp.exp(-total))


def call(kernel, out_shape, specs, scratch=(), cost=1.0, name=None, limit=VMEM_LIMIT):
    where = {"s": pltpu.SMEM, "v": pltpu.VMEM, "a": pl.ANY}
    return pl.pallas_call(
        kernel,
        out_shape=out_shape,
        in_specs=[pl.BlockSpec(memory_space=where[s]) for s in specs],
        out_specs=jax.tree.map(lambda _: pl.BlockSpec(memory_space=pltpu.VMEM), out_shape),
        scratch_shapes=list(scratch),
        compiler_params=pltpu.CompilerParams(vmem_limit_bytes=limit),
        cost_estimate=pl.CostEstimate(flops=0, bytes_accessed=int(cost * 3.0e6), transcendentals=0),
        name=name,
    )


def swap_pairs(first, second, axis, idle):
    count, others = lax.axis_size(axis), lax.axis_size(idle)
    even = [(i, i ^ 1) for i in range(count)]
    if count == 2:
        one = lax.ppermute(first, axis, even)
        return one, one
    pairs = []
    for i in range(count):
        for j in range(others):
            end = i in (0, count - 1)
            to = (i if end else i + 1 if i % 2 else i - 1, j ^ 1 if end else j)
            if axis < idle:
                pairs.append((i * others + j, to[0] * others + to[1]))
            else:
                pairs.append((j * count + i, to[1] * count + to[0]))
    two = lax.ppermute(second, tuple(sorted((axis, idle))), pairs)
    return lax.ppermute(first, axis, even), two


def swap_corners(values, x_kind, y_kind):
    counts = [lax.axis_size(a) for a in ("gx", "gy")]

    def partner(at, count, kind):
        to = at ^ 1 if kind == 0 else at + 1 if at % 2 else at - 1
        return to if 0 <= to < count else at

    pairs = []
    for i in range(counts[0]):
        for j in range(counts[1]):
            to = partner(i, counts[0], x_kind), partner(j, counts[1], y_kind)
            pairs.append((i * counts[1] + j, to[0] * counts[1] + to[1]))
    return lax.ppermute(values, ("gx", "gy"), pairs)


def on_device(fields, material, depth_order, table):
    _, zs, xs, ys = fields.shape
    nx, nz = lax.axis_size("gx"), lax.axis_size("gz")
    block = xs + TILE
    part = xs // nz
    swaps = nz in (2, 4)
    offsets = [0] + list(range(nz - 1, 0, -1)) if swaps else None
    groups = -(-zs // GROUP)
    f32 = lambda *shape: jax.ShapeDtypeStruct(shape, jnp.float32)

    def side(even_high):
        return call(functools.partial(rows_kernel, zs, xs, even_high), f32(FACE, zs, ys), "v", name="x_rows")(fields)

    x_a, x_b = swap_pairs(side(True), side(False) if nx > 2 else None, "gx", "gy")
    strip = jnp.asarray(strip_matrix(ys))
    strips, corners = f32(groups, xs, 128), f32(groups, TILE, 128)
    faces = f32(FACE * xs, ys)
    main, m_a, m_b, *c = call(
        functools.partial(pack_kernel, zs, xs),
        (strips, faces, faces) + (corners,) * (1 if nx == 2 else 2),
        "v",
        cost=0.7,
        name="pack",
    )(fields)
    y_a, y_b = swap_pairs(main, main, "gy", "gx")
    d = [swap_corners(values, x_kind, y_kind) for x_kind, values in enumerate(c) for y_kind in (0, 1)]
    rows, cell = call(
        functools.partial(cells_kernel, zs, xs),
        (f32(6, zs, xs, ys), jax.ShapeDtypeStruct((256, 3 * ys), jnp.bfloat16)),
        "v",
        cost=1.3,
        name="cells",
    )(fields)
    halo = call(functools.partial(x_halo_kernel, zs, xs), f32(4, zs, TILE, ys), "vvv", cost=0.2, name="x_halo")(
        fields, x_a, x_b
    )
    cross, nearer = call(
        functools.partial(cross_kernel, zs, xs, offsets),
        (f32(7, zs, xs, ys), f32(nz * nz, 1, 128)),
        "vvvv",
        [pltpu.VMEM((6, zs, TILE, ys), jnp.float32)],
        cost=1.0,
        name="cross",
    )(depth_order[None], rows, halo, cell)
    y_a, y_b, d, cross = lax.optimization_barrier((y_a, y_b, d, cross))

    faces = f32(FACE * xs + 3 * TILE, ys)
    merged, f_a, f_b = call(
        functools.partial(join_kernel, zs, xs),
        (f32(groups, block, 128), faces, faces),
        "v" * (6 + len(d)),
        name="join",
    )(m_a, m_b, halo, main, y_a, y_b, *d)
    z_a, z_b = swap_pairs(f_a, f_b, "gz", "gy")

    scale = 2.0 / (zs * nz)
    inner, full, looked = call(
        functools.partial(inner_kernel, zs, xs, scale),
        (f32(5, xs, ys), f32(7, zs, xs, ys), f32(4, 4, xs, ys)),
        "vvvvv",
        [
            pltpu.VMEM((3, groups, xs, 128), jnp.float32),
            pltpu.VMEM((10, 4, xs, ys), jnp.float32),
            pltpu.VMEM((4, 128), jnp.float32),
        ],
        cost=4.0,
        name="inner",
    )(cross, merged, table, material, strip)

    images = call(
        functools.partial(edge_kernel, zs, xs, scale),
        [f32(4, part, ys)] * nz if swaps else [f32(4, xs, ys)],
        "vvvvv",
        [
            pltpu.VMEM((7, 4, xs, ys), jnp.float32),
            pltpu.VMEM((2, 2, 6, block, ys), jnp.float32),
            pltpu.VMEM((4, xs, ys), jnp.float32),
        ],
        name="edges",
    )(z_b, z_a, full, looked, inner)

    if swaps:
        mine = [images[0]]
        for k in offsets[1:]:
            mine.append(lax.ppermute(images[k], "gz", [(i, i ^ k) for i in range(nz)]))
    else:
        stacked = lax.all_to_all(images[0].reshape(4, nz, part, ys), "gz", split_axis=1, concat_axis=1)
        mine = [stacked[:, b] for b in range(nz)]
    return call(blend_kernel, f32(4, part, ys), "v" + "v" * nz, name="blend")(nearer, *mine)


def solution(mesh):
    return jax.shard_map(
        on_device,
        mesh=mesh,
        in_specs=(P(None, "gz", "gx", "gy"), P("gz", "gx", "gy"), P(), P()),
        out_specs=P(None, ("gx", "gz"), "gy"),
        check_vma=False,
    )
```

```python
import functools

import jax
import jax.numpy as jnp
import ml_dtypes
import numpy as np
from jax import lax
from jax.experimental import pallas as pl
from jax.experimental.pallas import tpu as pltpu
from jax.sharding import PartitionSpec as P

VMEM_LIMIT = 40 * 1024 * 1024
GROUP = 12
SLOT = 10
TILE = 8
FACE = 5
SPAN = 24

LOG1P = (
    0.9999995186059567, -0.49996356582563917, 0.33265255844036573, -0.24453388969978707, 0.17659864766821842,
    -0.10679931280022417, 0.043659288844443055, -0.008466410404849948,
)
EXPM1 = (
    1.0, -0.4999995231628418, 0.1666584461927414, -0.04160914570093155, 0.00814302358776331, -0.0010865303920581937,
)


def polynomial(coefficients, value):
    terms = list(coefficients)
    power = value
    while len(terms) > 1:
        paired = [terms[k] + terms[k + 1] * power for k in range(0, len(terms) - 1, 2)]
        terms = paired + ([terms[-1]] if len(terms) % 2 else [])
        power = power * power if len(terms) > 1 else power
    return terms[0]


BLUR = {off: weight / 64 for off, weight in ((-1, 1), (0, 2), (1, 1))}
BLUR2 = {off: weight / 2048 for off, weight in ((-2, 1), (-1, 4), (0, 6), (1, 4), (2, 1))}
SLOPE = {off: weight / 2048 for off, weight in ((-2, -1), (-1, -2), (1, 2), (2, 1))}


def strip_matrix(ysize):
    strips = np.zeros((128, 7 * ysize), np.float32)
    for block, (taps, field) in enumerate([(BLUR, f) for f in range(4)] + [(BLUR2, 0), (SLOPE, 0), (BLUR2, 0)]):
        first = slot_of(field)[0]
        outside = {-2: 0, -1: 1, ysize: 2, ysize + 1: 3} if field == 0 else {-1: first, ysize: first + 1}
        for out in range(ysize):
            for off, weight in taps.items():
                if not 0 <= out + off < ysize:
                    strips[outside[out + off], block * ysize + out] = weight
    return np.concatenate([strips, strips], axis=0).astype(ml_dtypes.bfloat16)


def make_cell_weights(out_ref):
    off = lax.broadcasted_iota(jnp.int32, (128, 128), 0) - lax.broadcasted_iota(jnp.int32, (128, 128), 1)
    for block, taps in enumerate((BLUR, BLUR2, SLOPE)):
        weights = jnp.zeros((128, 128), jnp.float32)
        for step, weight in taps.items():
            weights = jnp.where(off == step, float(weight), weights)
        for half in range(2):
            out_ref[128 * half : 128 * half + 128, 128 * block : 128 * block + 128] = weights.astype(jnp.bfloat16)


def halves(values):
    high = values.astype(jnp.bfloat16)
    low = (values - high.astype(jnp.float32)).astype(jnp.bfloat16)
    return jnp.concatenate([high, low], axis=1)


def place_of(axis):
    at = lax.axis_index(axis)
    return at == 0, at == lax.axis_size(axis) - 1, lax.rem(at, 2) == 1


def rows_kernel(zs, xs, even_high, fields_ref, out_ref):
    high = (lax.rem(lax.axis_index("gx"), 2) == 0) == even_high
    for group in range(FACE):
        field = max(group - 1, 0)
        rows = fields_ref.at[field].reshape(zs * xs, 128)
        low_row = group if group < 2 else 0
        high_row = xs - 2 + group if group < 2 else xs - 1
        out_ref[group] = rows[pl.ds(jnp.where(high, high_row, low_row), zs, stride=xs), :]


def slot_of(field):
    return (0, 4) if field == 0 else (2 + 2 * field, 2)


def pack_strips(load, layers, lane, rows):
    packed = jnp.zeros((rows, 128), jnp.float32)
    for k, z in enumerate(layers):
        for field in range(4):
            first, count = slot_of(field)
            start = SLOT * k + first
            values = pltpu.roll(load(field, z), (start + count // 2) % 128, 1)
            packed = jnp.where((lane >= start) & (lane < start + count), values, packed)
    return packed


def put_faces(zodd, out_refs, start, low, high):
    for ref, swapped in zip(out_refs, (False, True)):
        ref[start : start + low.shape[0], :] = jnp.where(zodd != swapped, low, high)


def pack_kernel(zs, xs, fields_ref, pack_ref, ma_ref, mb_ref, *corner_refs):
    zodd = place_of("gz")[2]
    for j in range(FACE):
        field = max(j - 1, 0)
        low, high = fields_ref[field, j if j < 2 else 0], fields_ref[field, zs - 2 + j if j < 2 else zs - 1]
        put_faces(zodd, (ma_ref, mb_ref), j * xs, low, high)
    xodd = place_of("gx")[2]
    lane = lax.broadcasted_iota(jnp.int32, (1, 128), 1)
    sub = lax.broadcasted_iota(jnp.int32, (TILE, 1), 0)
    for group in range(pack_ref.shape[0]):
        layers = range(group * GROUP, min(zs, group * GROUP + GROUP))
        packed = pack_strips(lambda f, z: fields_ref[f, z], layers, lane, xs)
        pack_ref[group] = packed
        first, last = packed[0:TILE], packed[xs - TILE :]
        low = jnp.where(sub == TILE - 1, pltpu.roll(first, TILE - 1, 0), pltpu.roll(first, TILE - 3, 0))
        high = jnp.where(sub == 0, pltpu.roll(last, 1, 0), pltpu.roll(last, 3, 0))
        for ref, swapped in zip(corner_refs, (False, True)):
            ref[group] = jnp.where(xodd != swapped, low, high)


def nearer_layers(offsets, order_ref, near_ref):
    iz, count = lax.axis_index("gz"), lax.axis_size("gz")
    order = order_ref[...].astype(jnp.float32)
    lane = lax.broadcasted_iota(jnp.int32, order.shape, 1)
    ranks = [
        jnp.sum(jnp.where(lane == (iz ^ offsets[k] if offsets else k), order, 0.0), axis=1, keepdims=True)
        for k in range(count)
    ]
    for k in range(count):
        for other in range(count):
            nearer = jnp.where(ranks[other] < ranks[k], 1.0, 0.0)
            near_ref[k * count + other] = jnp.broadcast_to(nearer, (1, 128))


def tables_of(table_ref, wide_ref, scale):
    wide_ref[...] = jnp.zeros_like(wide_ref)
    wide_ref[:, 0 : table_ref.shape[1]] = table_ref[...]
    return [jnp.broadcast_to(wide_ref[c : c + 1, :] * (0.5 if c < 3 else scale), (TILE, 128)) for c in range(4)]


def look_up(tables, ids_ref, z, t, tiles):
    ids = ids_ref[z, pl.ds(t, TILE, stride=tiles), :]
    return [jnp.take_along_axis(row, ids, axis=1, mode="promise_in_bounds") for row in tables]


def x_halo_kernel(zs, xs, fields_ref, xa_ref, xb_ref, halo_ref):
    xfirst, xlast, xodd = place_of("gx")
    halo_ref[...] = jnp.zeros_like(halo_ref)
    for field in range(4):
        tiles = halo_ref.at[field].reshape(zs * TILE, 128)
        own = fields_ref.at[field].reshape(zs * xs, 128)
        at = 0 if field == 0 else 1 + field
        below = jnp.where(xodd, xa_ref[1 + field], xb_ref[1 + field])
        above = jnp.where(xodd, xb_ref[at], xa_ref[at])
        tiles[pl.ds(0, zs, stride=TILE), :] = jnp.where(xfirst, 0.0, below)
        tiles[pl.ds(TILE - 1, zs, stride=TILE), :] = jnp.where(xlast, 0.0, above)
        if field == 0:
            low, high = own[pl.ds(0, zs, stride=xs), :], own[pl.ds(xs - 1, zs, stride=xs), :]
            tiles[pl.ds(1, zs, stride=TILE), :] = jnp.where(xfirst, -low, jnp.where(xodd, xa_ref[0], xb_ref[0]))
            tiles[pl.ds(TILE - 2, zs, stride=TILE), :] = jnp.where(xlast, -high, jnp.where(xodd, xb_ref[1], xa_ref[1]))


def join_kernel(zs, xs, ma_ref, mb_ref, halo_ref, own_ref, ya_ref, yb_ref, *rest):
    corner_refs, (merged_ref, fa_ref, fb_ref) = rest[:-3], rest[-3:]
    xfirst, xlast, xodd = place_of("gx")
    yfirst, ylast, yodd = place_of("gy")
    zodd = place_of("gz")[2]
    block = xs + TILE
    lane = lax.broadcasted_iota(jnp.int32, (1, 128), 1)
    sub = lax.broadcasted_iota(jnp.int32, (TILE, 1), 0)
    place = lax.rem(lane, SLOT)
    from_left = (place < 2) | ((place >= 4) & (lax.rem(place, 2) == 0))

    def merge(own, first, second):
        fill_left = jnp.where(place == 0, -pltpu.roll(own, 126, 1), 0.0)
        fill_right = jnp.where(place == 3, -pltpu.roll(own, 2, 1), 0.0)
        left = jnp.where(yfirst, fill_left, jnp.where(yodd, first, second))
        right = jnp.where(ylast, fill_right, jnp.where(yodd, second, first))
        return jnp.where(from_left, left, right)

    for group in range(own_ref.shape[0]):
        main = merge(own_ref[group], ya_ref[group], yb_ref[group])
        merged_ref[group, TILE:] = main
        tiles = []
        for k in range(2):
            a, b = corner_refs[k][group], corner_refs[k - 2][group]
            tiles.append(jnp.where(sub < TILE // 2, jnp.where(xodd, a, b), jnp.where(xodd, b, a)))
        tile = merge(tiles[1], tiles[0], tiles[1])
        low = jnp.where(sub == 1, -pltpu.roll(main[0:TILE], 1, 0), 0.0)
        high = jnp.where(sub == TILE - 2, -pltpu.roll(main[xs - TILE :], TILE - 1, 0), 0.0)
        tile = jnp.where(xfirst & (sub < TILE // 2), low, tile)
        merged_ref[group, 0:TILE] = jnp.where(xlast & (sub >= TILE // 2), high, tile)

    ends = (sub < 2) | (sub >= TILE - 2)

    def density_rows(z):
        return jnp.where(ends, halo_ref[0, z], pltpu.roll(halo_ref[0, z + 1], TILE // 2, 0))

    def field_rows(z):
        rows = [pltpu.roll(halo_ref[f, z], 2 * f - 2, 0) if f > 1 else halo_ref[f, z] for f in (1, 2, 3)]
        mixed = jnp.where((sub == 0) | (sub == TILE - 1), rows[0], rows[1])
        return jnp.where((sub == 3) | (sub == 4), rows[2], mixed)

    def strips(z):
        group, k = divmod(z, GROUP)
        packed = jnp.zeros((TILE, 128), jnp.float32)
        for t in range(block // TILE):
            moved = pltpu.roll(merged_ref[group, t * TILE : t * TILE + TILE], (SPAN * t - SLOT * k) % 128, 1)
            packed = jnp.where((lane >= SPAN * t) & (lane < SPAN * t + SPAN), moved, packed)
        return packed

    outs, start = (fa_ref, fb_ref), FACE * xs
    fa_ref[0:start, :] = ma_ref[...]
    fb_ref[0:start, :] = mb_ref[...]
    put_faces(zodd, outs, start, density_rows(0), density_rows(zs - 2))
    put_faces(zodd, outs, start + TILE, field_rows(0), field_rows(zs - 1))
    put_faces(zodd, outs, start + 2 * TILE, strips(0), strips(zs - 2))


def along_y(values, halo, lane, density):
    def shifted(off):
        mixed = jnp.where(lane >= 128 - off if off > 0 else lane < -off, halo, values)
        return pltpu.roll(mixed, off % 128, 1)

    m1, p1 = shifted(1), shifted(-1)
    near = m1 + p1
    blur = BLUR[1] * near + BLUR[0] * values
    if not density:
        return (blur,)
    m2, p2 = shifted(2), shifted(-2)
    twice = BLUR2[2] * (m2 + p2) + BLUR2[1] * near + BLUR2[0] * values
    return blur, twice, SLOPE[2] * (p2 - m2) + SLOPE[1] * (p1 - m1)


class Rows:
    def __init__(self, tiles, halo):
        self.tiles, self.halo = list(tiles), halo
        self.sub = lax.broadcasted_iota(jnp.int32, (TILE, 1), 0)
        self.made = {}

    def row(self, t):
        count = len(self.tiles)
        if 0 <= t < count:
            return self.tiles[t]
        if t not in self.made:
            down = t < 0
            step = -t - 1 if down else t - count
            halo = self.halo if step == 0 else pltpu.roll(self.halo, TILE - 1 if down else 1, 0)
            inner = pltpu.roll(self.tiles[t % count], 1 if down else TILE - 1, 0)
            self.made[t] = jnp.where(self.sub == (0 if down else TILE - 1), halo, inner)
        return self.made[t]

    def pair(self, level, t):
        if level == 0:
            return self.row(t)
        if (level, t) not in self.made:
            self.made[level, t] = self.pair(level - 1, t) + self.pair(level - 1, t + 1)
        return self.made[level, t]

    def blur(self):
        return [self.pair(2, t - 1) for t in range(len(self.tiles))]

    def blur2(self):
        return [self.pair(4, t - 2) for t in range(len(self.tiles))]

    def slope(self):
        return [self.pair(2, t) - self.pair(2, t - 2) for t in range(len(self.tiles))]


def cells_kernel(zs, xs, fields_ref, out_ref, cell_ref):
    each, tiles = 8, xs // TILE
    make_cell_weights(cell_ref)

    def step(k, carry):
        first = k * each
        for field in range(4):
            rows = [
                fields_ref[field, first + j, pl.ds(t, TILE, stride=tiles), :] for j in range(each) for t in range(tiles)
            ]
            weights = cell_ref[...] if field == 0 else cell_ref[:, 0:128]
            result = jnp.dot(halves(jnp.concatenate(rows, axis=0)), weights, preferred_element_type=jnp.float32)
            for part in (0, 1, 2) if field == 0 else (2 + field,):
                columns = slice(128 * part, 128 * part + 128) if field == 0 else slice(0, 128)
                out_ref[part, pl.ds(first, each)] = result[:, columns].reshape(each, xs, 128)
        return carry

    lax.fori_loop(0, zs // each, step, 0)


def cross_kernel(zs, xs, offsets, order_ref, rows_ref, halo_ref, cell_ref, out_ref, near_ref, edge_ref):
    each, tiles = 4, xs // TILE
    nearer_layers(offsets, order_ref, near_ref)
    for field in range(4):
        weights = cell_ref[...] if field == 0 else cell_ref[:, 0:128]
        result = jnp.dot(
            halves(halo_ref[field].reshape(zs * TILE, 128)), weights, preferred_element_type=jnp.float32
        )
        for part in (0, 1, 2) if field == 0 else (2 + field,):
            columns = slice(128 * part, 128 * part + 128) if field == 0 else slice(0, 128)
            edge_ref[part] = result[:, columns].reshape(zs, TILE, 128)

    def step(k, carry):
        for j in range(each):
            z = k * each + j

            def part_rows(part):
                return Rows([rows_ref[part, z, t * TILE : t * TILE + TILE, :] for t in range(tiles)], edge_ref[part, z])

            twice, sloped = part_rows(1), part_rows(2)
            results = [part_rows(part).blur() for part in (0, 3, 4, 5)]
            results += [twice.blur2(), twice.slope(), sloped.blur2()]
            for part, values in enumerate(results):
                for t in range(tiles):
                    out_ref[part, z, t * TILE : t * TILE + TILE, :] = values[t]
        return carry

    lax.fori_loop(0, zs // each, step, 0)


def before_shade(load, z):
    def blur(part):
        return load(part, z - 1) + load(part, z + 1) + 2.0 * load(part, z)

    def blur2(part):
        return (load(part, z - 2) + load(part, z + 2)) + 4.0 * (load(part, z - 1) + load(part, z + 1)) + 6.0 * load(part, z)

    near = load(4, z + 1) - load(4, z - 1)
    grad_z = (load(4, z + 2) - load(4, z - 2)) + (near + near)
    grad_x = blur2(5)
    grad_y = blur2(6)
    facing = jnp.abs(0.8 * (grad_z + grad_y) + 0.4 * grad_x)
    square = grad_z * grad_z + grad_x * grad_x + grad_y * grad_y
    shading = 0.3 + facing * lax.rsqrt(square + 0.0025)
    density = 3.0 * blur(0)
    return [density, jnp.exp(-jnp.abs(density)), shading] + [blur(1 + c) for c in range(3)]


def shade(state, taken, looked):
    density, t, shading = taken[:3]
    soft = jnp.maximum(density, 0.0) + t * polynomial(LOG1P, t)
    extinct = looked[3] * soft
    passed, total, depth = state[0], state[1:4], state[4]
    weight = passed * (extinct * polynomial(EXPM1, extinct))
    lit = weight * shading
    colours = [
        total[c] + (looked[c] * lit) * (2.0 + jnp.tanh(taken[3 + c])) for c in range(3)
    ]
    return (passed - weight, *colours, depth + extinct)


def inner_kernel(zs, xs, scale, cross_ref, merged_ref, table_ref, ids_ref, strip_ref, inner_ref, full_ref, looked_ref, filtered_ref, taken_ref, wide_ref):
    tiles, each = xs // TILE, 8
    tables = tables_of(table_ref, wide_ref, scale)
    for group in range(merged_ref.shape[0]):
        rows = Rows([merged_ref[group, pl.ds(TILE + t, TILE, stride=tiles), :] for t in range(tiles)], merged_ref[group, 0:TILE])
        for k, values in enumerate((rows.blur(), rows.blur2(), rows.slope())):
            for t in range(tiles):
                filtered_ref[k, group, t * TILE : t * TILE + TILE, :] = values[t]

    def strip_step(step, carry):
        first = step * each
        for k, parts in enumerate(((0, 1, 2, 3), (4, 6), (5,))):
            strips = []
            for j in range(each):
                group = lax.div(first + j, GROUP)
                slot = first + j - group * GROUP
                strips.append(pltpu.roll(filtered_ref[k, group], lax.rem(128 - SLOT * slot, 128), 1))
            columns = slice((0, 512, 768)[k], (512, 768, 896)[k])
            result = jnp.dot(
                halves(jnp.concatenate(strips, axis=0)), strip_ref[:, columns], preferred_element_type=jnp.float32
            )
            for n, part in enumerate(parts):
                share = result[:, 128 * n : 128 * n + 128].reshape(each, xs, 128)
                full_ref[part, pl.ds(first, each)] = cross_ref[part, pl.ds(first, each)] + share
        return carry

    lax.fori_loop(0, zs // each, strip_step, 0)

    ahead = taken_ref.shape[1]
    steps = (zs - 4) // ahead

    def take(step):
        first = 2 + ahead * step
        for t in range(tiles):
            rows = slice(t * TILE, t * TILE + TILE)
            held = {}

            def load(part, j):
                if (part, j) not in held:
                    held[part, j] = full_ref[part, first + j, rows]
                return held[part, j]

            for j in range(ahead):
                taken = before_shade(load, j) + look_up(tables, ids_ref, first + j, t, tiles)
                for k, values in enumerate(taken):
                    taken_ref[k, j, rows] = values

    def advance(step, state):
        for j in range(ahead):
            taken = [taken_ref[k, j] for k in range(10)]
            state = shade(state, taken[:6], taken[6:])
        return state

    def z_step(step, state):
        state = advance(step, state)
        take(step + 1)
        return state

    for k, z in enumerate((0, 1, zs - 2, zs - 1)):
        for t in range(tiles):
            for c, values in enumerate(look_up(tables, ids_ref, z, t, tiles)):
                looked_ref[c, k, t * TILE : t * TILE + TILE, :] = values
    zero = jnp.zeros((xs, 128), jnp.float32)
    take(0)
    state = lax.fori_loop(0, steps - 1, z_step, (zero + 1.0, zero, zero, zero, zero))
    for k, values in enumerate(advance(steps - 1, state)):
        inner_ref[k] = values


def edge_kernel(zs, xs, fb_ref, fa_ref, cross_ref, looked_ref, inner_ref, *rest):
    out_refs, (near_ref, rows_ref, image_ref) = rest[:-3], rest[-3:]
    zfirst, zlast, zodd = place_of("gz")
    block = xs + TILE
    tiles = xs // TILE
    lane = lax.broadcasted_iota(jnp.int32, (1, 128), 1)
    for side in range(2):
        first, second = (fa_ref, fb_ref) if side == 0 else (fb_ref, fa_ref)

        def face(start, count):
            return jnp.where(zodd, first[start : start + count, :], second[start : start + count, :])

        ends = [face(FACE * xs, TILE), face(FACE * xs + TILE, TILE)]
        strips = face(FACE * xs + 2 * TILE, TILE)
        for j in range(FACE):
            field = max(j - 1, 0)
            layer = j if j < 2 else (1 if side == 0 else 0)
            turned = TILE // 2 * j if j < 2 else 2 * field - 2
            outer_rows = ends[min(field, 1)]
            if turned:
                outer_rows = pltpu.roll(outer_rows, TILE - turned, 0)
            at_lane = SLOT * layer + slot_of(field)[0]
            own = 126 if field == 0 else 127
            halo = [pltpu.roll(strips, (own - at_lane - SPAN * t) % 128, 1) for t in range(block // TILE)]
            values = jnp.concatenate([outer_rows, face(j * xs, xs)], axis=0)
            results = along_y(values, jnp.concatenate(halo, axis=0), lane, field == 0)
            for part, result in zip((0, 1, 2) if field == 0 else (2 + field,), results):
                rows_ref[side, layer, part] = result
    for side in range(2):
        edge = zfirst if side == 0 else zlast
        for layer in range(2):
            mirrored = 0 if side == 0 else zs - 1
            outer = layer == side

            def part_rows(part):
                ref = rows_ref.at[side, layer, part]
                return Rows([ref[pl.ds(TILE + t, TILE, stride=tiles), :] for t in range(tiles)], ref[0:TILE, :])

            twice, sloped = part_rows(1), part_rows(2)
            for part, values in zip((4, 5, 6), (twice.blur2(), twice.slope(), sloped.blur2())):
                for t in range(tiles):
                    rows = slice(t * TILE, t * TILE + TILE)
                    fill = -cross_ref[part, mirrored, rows] if outer else 0.0
                    near_ref[part, 2 * side + layer, rows] = jnp.where(edge, fill, values[t])
            if not outer:
                for part, source in enumerate((0, 3, 4, 5)):
                    for t, values in enumerate(part_rows(source).blur()):
                        near_ref[part, 2 * side + layer, t * TILE : t * TILE + TILE] = jnp.where(edge, 0.0, values)

    def load(part, z):
        if z < 0:
            return near_ref[part, z + 2]
        if z >= zs:
            return near_ref[part, z - zs + 2]
        return cross_ref[part, z]

    def behind(state, z):
        looked = [looked_ref[c, z if z < 2 else z - zs + 4] for c in range(4)]
        return shade(state, before_shade(load, z), looked)

    zero = jnp.zeros((xs, 128), jnp.float32)
    state = behind(behind((zero + 1.0, zero, zero, zero, zero), 0), 1)
    passed = state[0]
    state = (
        passed * inner_ref[0],
        state[1] + passed * inner_ref[1],
        state[2] + passed * inner_ref[2],
        state[3] + passed * inner_ref[3],
        state[4] + inner_ref[4],
    )
    state = behind(behind(state, zs - 2), zs - 1)
    for c in range(4):
        for t in range(tiles):
            image_ref[c, pl.ds(t, TILE, stride=tiles), :] = state[1 + c][t * TILE : t * TILE + TILE]
    if len(out_refs) == 1:
        out_refs[0][...] = image_ref[...]
    else:
        part = xs // len(out_refs)
        for k, ref in enumerate(out_refs):
            ref[...] = image_ref[:, pl.ds(pl.multiple_of((lax.axis_index("gz") ^ k) * part, part), part), :]


def blend_kernel(near_ref, *refs):
    images, out_ref = refs[:-1], refs[-1]
    count = len(images)
    depths = [image[3] for image in images]
    colours = [jnp.zeros_like(depths[0])] * 3
    for k in range(count):
        prior = jnp.zeros_like(depths[0])
        for other in range(count):
            if other != k:
                prior += near_ref[k * count + other] * depths[other]
        through = jnp.exp(-prior)
        colours = [colours[c] + through * images[k][c] for c in range(3)]
    total = functools.reduce(jnp.add, depths)
    out_ref[0], out_ref[1], out_ref[2] = colours
    small = total * polynomial(EXPM1, total)
    out_ref[3] = jnp.where(total < 0.5, small, 1.0 - jnp.exp(-total))


def call(kernel, out_shape, specs, scratch=(), cost=1.0, name=None, limit=VMEM_LIMIT):
    where = {"s": pltpu.SMEM, "v": pltpu.VMEM, "a": pl.ANY}
    return pl.pallas_call(
        kernel,
        out_shape=out_shape,
        in_specs=[pl.BlockSpec(memory_space=where[s]) for s in specs],
        out_specs=jax.tree.map(lambda _: pl.BlockSpec(memory_space=pltpu.VMEM), out_shape),
        scratch_shapes=list(scratch),
        compiler_params=pltpu.CompilerParams(vmem_limit_bytes=limit),
        cost_estimate=pl.CostEstimate(flops=0, bytes_accessed=int(cost * 3.0e6), transcendentals=0),
        name=name,
    )


def swap_pairs(first, second, axis, idle):
    count, others = lax.axis_size(axis), lax.axis_size(idle)
    even = [(i, i ^ 1) for i in range(count)]
    if count == 2:
        one = lax.ppermute(first, axis, even)
        return one, one
    pairs = []
    for i in range(count):
        for j in range(others):
            end = i in (0, count - 1)
            to = (i if end else i + 1 if i % 2 else i - 1, j ^ 1 if end else j)
            if axis < idle:
                pairs.append((i * others + j, to[0] * others + to[1]))
            else:
                pairs.append((j * count + i, to[1] * count + to[0]))
    two = lax.ppermute(second, tuple(sorted((axis, idle))), pairs)
    return lax.ppermute(first, axis, even), two


def swap_corners(values, x_kind, y_kind):
    counts = [lax.axis_size(a) for a in ("gx", "gy")]

    def partner(at, count, kind):
        to = at ^ 1 if kind == 0 else at + 1 if at % 2 else at - 1
        return to if 0 <= to < count else at

    pairs = []
    for i in range(counts[0]):
        for j in range(counts[1]):
            to = partner(i, counts[0], x_kind), partner(j, counts[1], y_kind)
            pairs.append((i * counts[1] + j, to[0] * counts[1] + to[1]))
    return lax.ppermute(values, ("gx", "gy"), pairs)


def on_device(fields, material, depth_order, table):
    _, zs, xs, ys = fields.shape
    nx, nz = lax.axis_size("gx"), lax.axis_size("gz")
    block = xs + TILE
    part = xs // nz
    swaps = nz in (2, 4)
    offsets = [0] + list(range(nz - 1, 0, -1)) if swaps else None
    groups = -(-zs // GROUP)
    f32 = lambda *shape: jax.ShapeDtypeStruct(shape, jnp.float32)

    def side(even_high):
        return call(functools.partial(rows_kernel, zs, xs, even_high), f32(FACE, zs, ys), "v", name="x_rows")(fields)

    x_a, x_b = swap_pairs(side(True), side(False) if nx > 2 else None, "gx", "gy")
    strip = jnp.asarray(strip_matrix(ys))
    strips, corners = f32(groups, xs, 128), f32(groups, TILE, 128)
    faces = f32(FACE * xs, ys)
    main, m_a, m_b, *c = call(
        functools.partial(pack_kernel, zs, xs),
        (strips, faces, faces) + (corners,) * (1 if nx == 2 else 2),
        "v",
        cost=0.7,
        name="pack",
    )(fields)
    y_a, y_b = swap_pairs(main, main, "gy", "gx")
    d = [swap_corners(values, x_kind, y_kind) for x_kind, values in enumerate(c) for y_kind in (0, 1)]
    rows, cell = call(
        functools.partial(cells_kernel, zs, xs),
        (f32(6, zs, xs, ys), jax.ShapeDtypeStruct((256, 3 * ys), jnp.bfloat16)),
        "v",
        cost=1.3,
        name="cells",
    )(fields)
    halo = call(functools.partial(x_halo_kernel, zs, xs), f32(4, zs, TILE, ys), "vvv", cost=0.2, name="x_halo")(
        fields, x_a, x_b
    )
    cross, nearer = call(
        functools.partial(cross_kernel, zs, xs, offsets),
        (f32(7, zs, xs, ys), f32(nz * nz, 1, 128)),
        "vvvv",
        [pltpu.VMEM((6, zs, TILE, ys), jnp.float32)],
        cost=1.0,
        name="cross",
    )(depth_order[None], rows, halo, cell)
    y_a, y_b, d, cross = lax.optimization_barrier((y_a, y_b, d, cross))

    faces = f32(FACE * xs + 3 * TILE, ys)
    merged, f_a, f_b = call(
        functools.partial(join_kernel, zs, xs),
        (f32(groups, block, 128), faces, faces),
        "v" * (6 + len(d)),
        name="join",
    )(m_a, m_b, halo, main, y_a, y_b, *d)
    z_a, z_b = swap_pairs(f_a, f_b, "gz", "gy")

    scale = 2.0 / (zs * nz)
    inner, full, looked = call(
        functools.partial(inner_kernel, zs, xs, scale),
        (f32(5, xs, ys), f32(7, zs, xs, ys), f32(4, 4, xs, ys)),
        "vvvvv",
        [
            pltpu.VMEM((3, groups, xs, 128), jnp.float32),
            pltpu.VMEM((10, 4, xs, ys), jnp.float32),
            pltpu.VMEM((4, 128), jnp.float32),
        ],
        cost=4.0,
        name="inner",
    )(cross, merged, table, material, strip)

    images = call(
        functools.partial(edge_kernel, zs, xs),
        [f32(4, part, ys)] * nz if swaps else [f32(4, xs, ys)],
        "vvvvv",
        [
            pltpu.VMEM((7, 4, xs, ys), jnp.float32),
            pltpu.VMEM((2, 2, 6, block, ys), jnp.float32),
            pltpu.VMEM((4, xs, ys), jnp.float32),
        ],
        name="edges",
    )(z_b, z_a, full, looked, inner)

    if swaps:
        mine = [images[0]]
        for k in offsets[1:]:
            mine.append(lax.ppermute(images[k], "gz", [(i, i ^ k) for i in range(nz)]))
    else:
        stacked = lax.all_to_all(images[0].reshape(4, nz, part, ys), "gz", split_axis=1, concat_axis=1)
        mine = [stacked[:, b] for b in range(nz)]
    return call(blend_kernel, f32(4, part, ys), "v" + "v" * nz, name="blend")(nearer, *mine)


def solution(mesh):
    return jax.shard_map(
        on_device,
        mesh=mesh,
        in_specs=(P(None, "gz", "gx", "gy"), P("gz", "gx", "gy"), P(), P()),
        out_specs=P(None, ("gx", "gz"), "gy"),
        check_vma=False,
    )
```

```python
import functools

import jax
import jax.numpy as jnp
import ml_dtypes
import numpy as np
from jax import lax
from jax.experimental import pallas as pl
from jax.experimental.pallas import tpu as pltpu
from jax.sharding import PartitionSpec as P

VMEM_LIMIT = 40 * 1024 * 1024
GROUP = 12
SLOT = 10
TILE = 8
FACE = 5
SPAN = 24

LOG1P = (
    0.9999995186059567, -0.49996356582563917, 0.33265255844036573, -0.24453388969978707, 0.17659864766821842,
    -0.10679931280022417, 0.043659288844443055, -0.008466410404849948,
)
EXPM1 = (
    1.0, -0.4999995231628418, 0.1666584461927414, -0.04160914570093155, 0.00814302358776331, -0.0010865303920581937,
)


def polynomial(coefficients, value):
    terms = list(coefficients)
    power = value
    while len(terms) > 1:
        paired = [terms[k] + terms[k + 1] * power for k in range(0, len(terms) - 1, 2)]
        terms = paired + ([terms[-1]] if len(terms) % 2 else [])
        power = power * power if len(terms) > 1 else power
    return terms[0]


BLUR = {off: weight / 64 for off, weight in ((-1, 1), (0, 2), (1, 1))}
BLUR2 = {off: weight / 2048 for off, weight in ((-2, 1), (-1, 4), (0, 6), (1, 4), (2, 1))}
SLOPE = {off: weight / 2048 for off, weight in ((-2, -1), (-1, -2), (1, 2), (2, 1))}


def strip_matrix(ysize):
    strips = np.zeros((128, 7 * ysize), np.float32)
    for block, (taps, field) in enumerate([(BLUR, f) for f in range(4)] + [(BLUR2, 0), (SLOPE, 0), (BLUR2, 0)]):
        first = slot_of(field)[0]
        outside = {-2: 0, -1: 1, ysize: 2, ysize + 1: 3} if field == 0 else {-1: first, ysize: first + 1}
        for out in range(ysize):
            for off, weight in taps.items():
                if not 0 <= out + off < ysize:
                    strips[outside[out + off], block * ysize + out] = weight
    return np.concatenate([strips, strips], axis=0).astype(ml_dtypes.bfloat16)


def make_cell_weights(out_ref):
    off = lax.broadcasted_iota(jnp.int32, (128, 128), 0) - lax.broadcasted_iota(jnp.int32, (128, 128), 1)
    for block, taps in enumerate((BLUR, BLUR2, SLOPE)):
        weights = jnp.zeros((128, 128), jnp.float32)
        for step, weight in taps.items():
            weights = jnp.where(off == step, float(weight), weights)
        for half in range(2):
            out_ref[128 * half : 128 * half + 128, 128 * block : 128 * block + 128] = weights.astype(jnp.bfloat16)


def halves(values):
    high = values.astype(jnp.bfloat16)
    low = (values - high.astype(jnp.float32)).astype(jnp.bfloat16)
    return jnp.concatenate([high, low], axis=1)


def place_of(axis):
    at = lax.axis_index(axis)
    return at == 0, at == lax.axis_size(axis) - 1, lax.rem(at, 2) == 1


class Fields:
    def __init__(self, refs):
        self.at = refs

    def __getitem__(self, index):
        return self.at[index[0]][index[1:]]


def on_fields(kernel):
    return lambda *refs: kernel(Fields(refs[:4]), *refs[4:])


def rows_kernel(zs, xs, even_high, fields_ref, out_ref):
    high = (lax.rem(lax.axis_index("gx"), 2) == 0) == even_high
    for group in range(FACE):
        field = max(group - 1, 0)
        rows = fields_ref.at[field].reshape(zs * xs, 128)
        low_row = group if group < 2 else 0
        high_row = xs - 2 + group if group < 2 else xs - 1
        out_ref[group] = rows[pl.ds(jnp.where(high, high_row, low_row), zs, stride=xs), :]


def slot_of(field):
    return (0, 4) if field == 0 else (2 + 2 * field, 2)


def pack_strips(load, layers, lane, rows):
    packed = jnp.zeros((rows, 128), jnp.float32)
    for k, z in enumerate(layers):
        for field in range(4):
            first, count = slot_of(field)
            start = SLOT * k + first
            values = pltpu.roll(load(field, z), (start + count // 2) % 128, 1)
            packed = jnp.where((lane >= start) & (lane < start + count), values, packed)
    return packed


def put_faces(zodd, out_refs, start, low, high):
    for ref, swapped in zip(out_refs, (False, True)):
        ref[start : start + low.shape[0], :] = jnp.where(zodd != swapped, low, high)


def pack_kernel(zs, xs, fields_ref, pack_ref, ma_ref, mb_ref, *corner_refs):
    zodd = place_of("gz")[2]
    for j in range(FACE):
        field = max(j - 1, 0)
        low, high = fields_ref[field, j if j < 2 else 0], fields_ref[field, zs - 2 + j if j < 2 else zs - 1]
        put_faces(zodd, (ma_ref, mb_ref), j * xs, low, high)
    xodd = place_of("gx")[2]
    lane = lax.broadcasted_iota(jnp.int32, (1, 128), 1)
    sub = lax.broadcasted_iota(jnp.int32, (TILE, 1), 0)
    for group in range(pack_ref.shape[0]):
        layers = range(group * GROUP, min(zs, group * GROUP + GROUP))
        packed = pack_strips(lambda f, z: fields_ref[f, z], layers, lane, xs)
        pack_ref[group] = packed
        first, last = packed[0:TILE], packed[xs - TILE :]
        low = jnp.where(sub == TILE - 1, pltpu.roll(first, TILE - 1, 0), pltpu.roll(first, TILE - 3, 0))
        high = jnp.where(sub == 0, pltpu.roll(last, 1, 0), pltpu.roll(last, 3, 0))
        for ref, swapped in zip(corner_refs, (False, True)):
            ref[group] = jnp.where(xodd != swapped, low, high)


def nearer_layers(offsets, order_ref, near_ref):
    iz, count = lax.axis_index("gz"), lax.axis_size("gz")
    order = order_ref[...].astype(jnp.float32)
    lane = lax.broadcasted_iota(jnp.int32, order.shape, 1)
    ranks = [
        jnp.sum(jnp.where(lane == (iz ^ offsets[k] if offsets else k), order, 0.0), axis=1, keepdims=True)
        for k in range(count)
    ]
    for k in range(count):
        for other in range(count):
            nearer = jnp.where(ranks[other] < ranks[k], 1.0, 0.0)
            near_ref[k * count + other] = jnp.broadcast_to(nearer, (1, 128))


def tables_of(table_ref, wide_ref, scale):
    wide_ref[...] = jnp.zeros_like(wide_ref)
    wide_ref[:, 0 : table_ref.shape[1]] = table_ref[...]
    return [jnp.broadcast_to(wide_ref[c : c + 1, :] * (0.5 if c < 3 else scale), (TILE, 128)) for c in range(4)]


def look_up(tables, ids_ref, z, t, tiles):
    ids = ids_ref[z, pl.ds(t, TILE, stride=tiles), :]
    return [jnp.take_along_axis(row, ids, axis=1, mode="promise_in_bounds") for row in tables]


def x_halo_kernel(zs, xs, fields_ref, xa_ref, xb_ref, halo_ref):
    xfirst, xlast, xodd = place_of("gx")
    halo_ref[...] = jnp.zeros_like(halo_ref)
    for field in range(4):
        tiles = halo_ref.at[field].reshape(zs * TILE, 128)
        own = fields_ref.at[field].reshape(zs * xs, 128)
        at = 0 if field == 0 else 1 + field
        below = jnp.where(xodd, xa_ref[1 + field], xb_ref[1 + field])
        above = jnp.where(xodd, xb_ref[at], xa_ref[at])
        tiles[pl.ds(0, zs, stride=TILE), :] = jnp.where(xfirst, 0.0, below)
        tiles[pl.ds(TILE - 1, zs, stride=TILE), :] = jnp.where(xlast, 0.0, above)
        if field == 0:
            low, high = own[pl.ds(0, zs, stride=xs), :], own[pl.ds(xs - 1, zs, stride=xs), :]
            tiles[pl.ds(1, zs, stride=TILE), :] = jnp.where(xfirst, -low, jnp.where(xodd, xa_ref[0], xb_ref[0]))
            tiles[pl.ds(TILE - 2, zs, stride=TILE), :] = jnp.where(xlast, -high, jnp.where(xodd, xb_ref[1], xa_ref[1]))


def join_kernel(zs, xs, ma_ref, mb_ref, halo_ref, own_ref, ya_ref, yb_ref, *rest):
    corner_refs, (merged_ref, fa_ref, fb_ref) = rest[:-3], rest[-3:]
    xfirst, xlast, xodd = place_of("gx")
    yfirst, ylast, yodd = place_of("gy")
    zodd = place_of("gz")[2]
    block = xs + TILE
    lane = lax.broadcasted_iota(jnp.int32, (1, 128), 1)
    sub = lax.broadcasted_iota(jnp.int32, (TILE, 1), 0)
    place = lax.rem(lane, SLOT)
    from_left = (place < 2) | ((place >= 4) & (lax.rem(place, 2) == 0))

    def merge(own, first, second):
        fill_left = jnp.where(place == 0, -pltpu.roll(own, 126, 1), 0.0)
        fill_right = jnp.where(place == 3, -pltpu.roll(own, 2, 1), 0.0)
        left = jnp.where(yfirst, fill_left, jnp.where(yodd, first, second))
        right = jnp.where(ylast, fill_right, jnp.where(yodd, second, first))
        return jnp.where(from_left, left, right)

    for group in range(own_ref.shape[0]):
        main = merge(own_ref[group], ya_ref[group], yb_ref[group])
        merged_ref[group, TILE:] = main
        tiles = []
        for k in range(2):
            a, b = corner_refs[k][group], corner_refs[k - 2][group]
            tiles.append(jnp.where(sub < TILE // 2, jnp.where(xodd, a, b), jnp.where(xodd, b, a)))
        tile = merge(tiles[1], tiles[0], tiles[1])
        low = jnp.where(sub == 1, -pltpu.roll(main[0:TILE], 1, 0), 0.0)
        high = jnp.where(sub == TILE - 2, -pltpu.roll(main[xs - TILE :], TILE - 1, 0), 0.0)
        tile = jnp.where(xfirst & (sub < TILE // 2), low, tile)
        merged_ref[group, 0:TILE] = jnp.where(xlast & (sub >= TILE // 2), high, tile)

    ends = (sub < 2) | (sub >= TILE - 2)

    def density_rows(z):
        return jnp.where(ends, halo_ref[0, z], pltpu.roll(halo_ref[0, z + 1], TILE // 2, 0))

    def field_rows(z):
        rows = [pltpu.roll(halo_ref[f, z], 2 * f - 2, 0) if f > 1 else halo_ref[f, z] for f in (1, 2, 3)]
        mixed = jnp.where((sub == 0) | (sub == TILE - 1), rows[0], rows[1])
        return jnp.where((sub == 3) | (sub == 4), rows[2], mixed)

    def strips(z):
        group, k = divmod(z, GROUP)
        packed = jnp.zeros((TILE, 128), jnp.float32)
        for t in range(block // TILE):
            moved = pltpu.roll(merged_ref[group, t * TILE : t * TILE + TILE], (SPAN * t - SLOT * k) % 128, 1)
            packed = jnp.where((lane >= SPAN * t) & (lane < SPAN * t + SPAN), moved, packed)
        return packed

    outs, start = (fa_ref, fb_ref), FACE * xs
    fa_ref[0:start, :] = ma_ref[...]
    fb_ref[0:start, :] = mb_ref[...]
    put_faces(zodd, outs, start, density_rows(0), density_rows(zs - 2))
    put_faces(zodd, outs, start + TILE, field_rows(0), field_rows(zs - 1))
    put_faces(zodd, outs, start + 2 * TILE, strips(0), strips(zs - 2))


def along_y(values, halo, lane, density):
    def shifted(off):
        mixed = jnp.where(lane >= 128 - off if off > 0 else lane < -off, halo, values)
        return pltpu.roll(mixed, off % 128, 1)

    m1, p1 = shifted(1), shifted(-1)
    near = m1 + p1
    blur = BLUR[1] * near + BLUR[0] * values
    if not density:
        return (blur,)
    m2, p2 = shifted(2), shifted(-2)
    twice = BLUR2[2] * (m2 + p2) + BLUR2[1] * near + BLUR2[0] * values
    return blur, twice, SLOPE[2] * (p2 - m2) + SLOPE[1] * (p1 - m1)


class Rows:
    def __init__(self, tiles, halo):
        self.tiles, self.halo = list(tiles), halo
        self.sub = lax.broadcasted_iota(jnp.int32, (TILE, 1), 0)
        self.made = {}

    def row(self, t):
        count = len(self.tiles)
        if 0 <= t < count:
            return self.tiles[t]
        if t not in self.made:
            down = t < 0
            step = -t - 1 if down else t - count
            halo = self.halo if step == 0 else pltpu.roll(self.halo, TILE - 1 if down else 1, 0)
            inner = pltpu.roll(self.tiles[t % count], 1 if down else TILE - 1, 0)
            self.made[t] = jnp.where(self.sub == (0 if down else TILE - 1), halo, inner)
        return self.made[t]

    def pair(self, level, t):
        if level == 0:
            return self.row(t)
        if (level, t) not in self.made:
            self.made[level, t] = self.pair(level - 1, t) + self.pair(level - 1, t + 1)
        return self.made[level, t]

    def blur(self):
        return [self.pair(2, t - 1) for t in range(len(self.tiles))]

    def blur2(self):
        return [self.pair(4, t - 2) for t in range(len(self.tiles))]

    def slope(self):
        return [self.pair(2, t) - self.pair(2, t - 2) for t in range(len(self.tiles))]


def cells_kernel(zs, xs, fields_ref, out_ref, cell_ref):
    each, tiles = 8, xs // TILE
    make_cell_weights(cell_ref)

    def step(k, carry):
        first = k * each
        for field in range(4):
            rows = [
                fields_ref[field, first + j, pl.ds(t, TILE, stride=tiles), :] for j in range(each) for t in range(tiles)
            ]
            weights = cell_ref[...] if field == 0 else cell_ref[:, 0:128]
            result = jnp.dot(halves(jnp.concatenate(rows, axis=0)), weights, preferred_element_type=jnp.float32)
            for part in (0, 1, 2) if field == 0 else (2 + field,):
                columns = slice(128 * part, 128 * part + 128) if field == 0 else slice(0, 128)
                out_ref[part, pl.ds(first, each)] = result[:, columns].reshape(each, xs, 128)
        return carry

    lax.fori_loop(0, zs // each, step, 0)


def cross_kernel(zs, xs, offsets, order_ref, rows_ref, halo_ref, cell_ref, out_ref, near_ref, edge_ref):
    each, tiles = 4, xs // TILE
    nearer_layers(offsets, order_ref, near_ref)
    for field in range(4):
        weights = cell_ref[...] if field == 0 else cell_ref[:, 0:128]
        result = jnp.dot(
            halves(halo_ref[field].reshape(zs * TILE, 128)), weights, preferred_element_type=jnp.float32
        )
        for part in (0, 1, 2) if field == 0 else (2 + field,):
            columns = slice(128 * part, 128 * part + 128) if field == 0 else slice(0, 128)
            edge_ref[part] = result[:, columns].reshape(zs, TILE, 128)

    def step(k, carry):
        for j in range(each):
            z = k * each + j

            def part_rows(part):
                return Rows([rows_ref[part, z, t * TILE : t * TILE + TILE, :] for t in range(tiles)], edge_ref[part, z])

            twice, sloped = part_rows(1), part_rows(2)
            results = [part_rows(part).blur() for part in (0, 3, 4, 5)]
            results += [twice.blur2(), twice.slope(), sloped.blur2()]
            for part, values in enumerate(results):
                for t in range(tiles):
                    out_ref[part, z, t * TILE : t * TILE + TILE, :] = values[t]
        return carry

    lax.fori_loop(0, zs // each, step, 0)


def before_shade(load, z):
    def blur(part):
        return load(part, z - 1) + load(part, z + 1) + 2.0 * load(part, z)

    def blur2(part):
        return (load(part, z - 2) + load(part, z + 2)) + 4.0 * (load(part, z - 1) + load(part, z + 1)) + 6.0 * load(part, z)

    near = load(4, z + 1) - load(4, z - 1)
    grad_z = (load(4, z + 2) - load(4, z - 2)) + (near + near)
    grad_x = blur2(5)
    grad_y = blur2(6)
    facing = jnp.abs(0.8 * (grad_z + grad_y) + 0.4 * grad_x)
    square = grad_z * grad_z + grad_x * grad_x + grad_y * grad_y
    shading = 0.3 + facing * lax.rsqrt(square + 0.0025)
    density = 3.0 * blur(0)
    return [density, jnp.exp(-jnp.abs(density)), shading] + [blur(1 + c) for c in range(3)]


def shade(state, taken, looked):
    density, t, shading = taken[:3]
    soft = jnp.maximum(density, 0.0) + t * polynomial(LOG1P, t)
    extinct = looked[3] * soft
    passed, total, depth = state[0], state[1:4], state[4]
    weight = passed * (extinct * polynomial(EXPM1, extinct))
    lit = weight * shading
    colours = [
        total[c] + (looked[c] * lit) * (2.0 + jnp.tanh(taken[3 + c])) for c in range(3)
    ]
    return (passed - weight, *colours, depth + extinct)


def inner_kernel(zs, xs, scale, cross_ref, merged_ref, table_ref, ids_ref, strip_ref, inner_ref, full_ref, looked_ref, filtered_ref, taken_ref, wide_ref):
    tiles, each = xs // TILE, 8
    tables = tables_of(table_ref, wide_ref, scale)
    for group in range(merged_ref.shape[0]):
        rows = Rows([merged_ref[group, pl.ds(TILE + t, TILE, stride=tiles), :] for t in range(tiles)], merged_ref[group, 0:TILE])
        for k, values in enumerate((rows.blur(), rows.blur2(), rows.slope())):
            for t in range(tiles):
                filtered_ref[k, group, t * TILE : t * TILE + TILE, :] = values[t]

    def strip_step(step, carry):
        first = step * each
        for k, parts in enumerate(((0, 1, 2, 3), (4, 6), (5,))):
            strips = []
            for j in range(each):
                group = lax.div(first + j, GROUP)
                slot = first + j - group * GROUP
                strips.append(pltpu.roll(filtered_ref[k, group], lax.rem(128 - SLOT * slot, 128), 1))
            columns = slice((0, 512, 768)[k], (512, 768, 896)[k])
            result = jnp.dot(
                halves(jnp.concatenate(strips, axis=0)), strip_ref[:, columns], preferred_element_type=jnp.float32
            )
            for n, part in enumerate(parts):
                share = result[:, 128 * n : 128 * n + 128].reshape(each, xs, 128)
                full_ref[part, pl.ds(first, each)] = cross_ref[part, pl.ds(first, each)] + share
        return carry

    lax.fori_loop(0, zs // each, strip_step, 0)

    ahead = taken_ref.shape[1]
    steps = (zs - 4) // ahead

    def take(step):
        first = 2 + ahead * step
        for t in range(tiles):
            rows = slice(t * TILE, t * TILE + TILE)
            held = {}

            def load(part, j):
                if (part, j) not in held:
                    held[part, j] = full_ref[part, first + j, rows]
                return held[part, j]

            for j in range(ahead):
                taken = before_shade(load, j) + look_up(tables, ids_ref, first + j, t, tiles)
                for k, values in enumerate(taken):
                    taken_ref[k, j, rows] = values

    def advance(step, state):
        for j in range(ahead):
            taken = [taken_ref[k, j] for k in range(10)]
            state = shade(state, taken[:6], taken[6:])
        return state

    def z_step(step, state):
        state = advance(step, state)
        take(step + 1)
        return state

    for k, z in enumerate((0, 1, zs - 2, zs - 1)):
        for t in range(tiles):
            for c, values in enumerate(look_up(tables, ids_ref, z, t, tiles)):
                looked_ref[c, k, t * TILE : t * TILE + TILE, :] = values
    zero = jnp.zeros((xs, 128), jnp.float32)
    take(0)
    state = lax.fori_loop(0, steps - 1, z_step, (zero + 1.0, zero, zero, zero, zero))
    for k, values in enumerate(advance(steps - 1, state)):
        inner_ref[k] = values


def edge_kernel(zs, xs, fb_ref, fa_ref, cross_ref, looked_ref, inner_ref, *rest):
    out_refs, (near_ref, rows_ref, image_ref) = rest[:-3], rest[-3:]
    zfirst, zlast, zodd = place_of("gz")
    block = xs + TILE
    tiles = xs // TILE
    lane = lax.broadcasted_iota(jnp.int32, (1, 128), 1)
    for side in range(2):
        first, second = (fa_ref, fb_ref) if side == 0 else (fb_ref, fa_ref)

        def face(start, count):
            return jnp.where(zodd, first[start : start + count, :], second[start : start + count, :])

        ends = [face(FACE * xs, TILE), face(FACE * xs + TILE, TILE)]
        strips = face(FACE * xs + 2 * TILE, TILE)
        for j in range(FACE):
            field = max(j - 1, 0)
            layer = j if j < 2 else (1 if side == 0 else 0)
            turned = TILE // 2 * j if j < 2 else 2 * field - 2
            outer_rows = ends[min(field, 1)]
            if turned:
                outer_rows = pltpu.roll(outer_rows, TILE - turned, 0)
            at_lane = SLOT * layer + slot_of(field)[0]
            own = 126 if field == 0 else 127
            halo = [pltpu.roll(strips, (own - at_lane - SPAN * t) % 128, 1) for t in range(block // TILE)]
            values = jnp.concatenate([outer_rows, face(j * xs, xs)], axis=0)
            results = along_y(values, jnp.concatenate(halo, axis=0), lane, field == 0)
            for part, result in zip((0, 1, 2) if field == 0 else (2 + field,), results):
                rows_ref[side, layer, part] = result
    for side in range(2):
        edge = zfirst if side == 0 else zlast
        for layer in range(2):
            mirrored = 0 if side == 0 else zs - 1
            outer = layer == side

            def part_rows(part):
                ref = rows_ref.at[side, layer, part]
                return Rows([ref[pl.ds(TILE + t, TILE, stride=tiles), :] for t in range(tiles)], ref[0:TILE, :])

            twice, sloped = part_rows(1), part_rows(2)
            for part, values in zip((4, 5, 6), (twice.blur2(), twice.slope(), sloped.blur2())):
                for t in range(tiles):
                    rows = slice(t * TILE, t * TILE + TILE)
                    fill = -cross_ref[part, mirrored, rows] if outer else 0.0
                    near_ref[part, 2 * side + layer, rows] = jnp.where(edge, fill, values[t])
            if not outer:
                for part, source in enumerate((0, 3, 4, 5)):
                    for t, values in enumerate(part_rows(source).blur()):
                        near_ref[part, 2 * side + layer, t * TILE : t * TILE + TILE] = jnp.where(edge, 0.0, values)

    def load(part, z):
        if z < 0:
            return near_ref[part, z + 2]
        if z >= zs:
            return near_ref[part, z - zs + 2]
        return cross_ref[part, z]

    def behind(state, z):
        looked = [looked_ref[c, z if z < 2 else z - zs + 4] for c in range(4)]
        return shade(state, before_shade(load, z), looked)

    zero = jnp.zeros((xs, 128), jnp.float32)
    state = behind(behind((zero + 1.0, zero, zero, zero, zero), 0), 1)
    passed = state[0]
    state = (
        passed * inner_ref[0],
        state[1] + passed * inner_ref[1],
        state[2] + passed * inner_ref[2],
        state[3] + passed * inner_ref[3],
        state[4] + inner_ref[4],
    )
    state = behind(behind(state, zs - 2), zs - 1)
    for c in range(4):
        for t in range(tiles):
            image_ref[c, pl.ds(t, TILE, stride=tiles), :] = state[1 + c][t * TILE : t * TILE + TILE]
    if len(out_refs) == 1:
        out_refs[0][...] = image_ref[...]
    else:
        part = xs // len(out_refs)
        for k, ref in enumerate(out_refs):
            ref[...] = image_ref[:, pl.ds(pl.multiple_of((lax.axis_index("gz") ^ k) * part, part), part), :]


def blend_kernel(near_ref, *refs):
    images, out_ref = refs[:-1], refs[-1]
    count = len(images)
    depths = [image[3] for image in images]
    colours = [jnp.zeros_like(depths[0])] * 3
    for k in range(count):
        prior = jnp.zeros_like(depths[0])
        for other in range(count):
            if other != k:
                prior += near_ref[k * count + other] * depths[other]
        through = jnp.exp(-prior)
        colours = [colours[c] + through * images[k][c] for c in range(3)]
    total = functools.reduce(jnp.add, depths)
    out_ref[0], out_ref[1], out_ref[2] = colours
    small = total * polynomial(EXPM1, total)
    out_ref[3] = jnp.where(total < 0.5, small, 1.0 - jnp.exp(-total))


def call(kernel, out_shape, specs, scratch=(), cost=1.0, name=None, limit=VMEM_LIMIT):
    where = {"s": pltpu.SMEM, "v": pltpu.VMEM, "a": pl.ANY}
    return pl.pallas_call(
        kernel,
        out_shape=out_shape,
        in_specs=[pl.BlockSpec(memory_space=where[s]) for s in specs],
        out_specs=jax.tree.map(lambda _: pl.BlockSpec(memory_space=pltpu.VMEM), out_shape),
        scratch_shapes=list(scratch),
        compiler_params=pltpu.CompilerParams(vmem_limit_bytes=limit),
        cost_estimate=pl.CostEstimate(flops=0, bytes_accessed=int(cost * 3.0e6), transcendentals=0),
        name=name,
    )


def swap_pairs(first, second, axis, idle):
    count, others = lax.axis_size(axis), lax.axis_size(idle)
    even = [(i, i ^ 1) for i in range(count)]
    if count == 2:
        one = lax.ppermute(first, axis, even)
        return one, one
    pairs = []
    for i in range(count):
        for j in range(others):
            end = i in (0, count - 1)
            to = (i if end else i + 1 if i % 2 else i - 1, j ^ 1 if end else j)
            if axis < idle:
                pairs.append((i * others + j, to[0] * others + to[1]))
            else:
                pairs.append((j * count + i, to[1] * count + to[0]))
    two = lax.ppermute(second, tuple(sorted((axis, idle))), pairs)
    return lax.ppermute(first, axis, even), two


def swap_corners(values, x_kind, y_kind):
    counts = [lax.axis_size(a) for a in ("gx", "gy")]

    def partner(at, count, kind):
        to = at ^ 1 if kind == 0 else at + 1 if at % 2 else at - 1
        return to if 0 <= to < count else at

    pairs = []
    for i in range(counts[0]):
        for j in range(counts[1]):
            to = partner(i, counts[0], x_kind), partner(j, counts[1], y_kind)
            pairs.append((i * counts[1] + j, to[0] * counts[1] + to[1]))
    return lax.ppermute(values, ("gx", "gy"), pairs)


def on_device(fields, material, depth_order, table):
    _, zs, xs, ys = fields.shape
    nx, nz = lax.axis_size("gx"), lax.axis_size("gz")
    block = xs + TILE
    part = xs // nz
    swaps = nz in (2, 4)
    offsets = [0] + list(range(nz - 1, 0, -1)) if swaps else None
    groups = -(-zs // GROUP)
    fields = [fields[k] for k in range(4)]
    f32 = lambda *shape: jax.ShapeDtypeStruct(shape, jnp.float32)

    def side(even_high):
        return call(
            on_fields(functools.partial(rows_kernel, zs, xs, even_high)), f32(FACE, zs, ys), "vvvv", name="x_rows"
        )(*fields)

    x_a, x_b = swap_pairs(side(True), side(False) if nx > 2 else None, "gx", "gy")
    strip = jnp.asarray(strip_matrix(ys))
    strips, corners = f32(groups, xs, 128), f32(groups, TILE, 128)
    faces = f32(FACE * xs, ys)
    main, m_a, m_b, *c = call(
        on_fields(functools.partial(pack_kernel, zs, xs)),
        (strips, faces, faces) + (corners,) * (1 if nx == 2 else 2),
        "vvvv",
        cost=0.7,
        name="pack",
    )(*fields)
    y_a, y_b = swap_pairs(main, main, "gy", "gx")
    d = [swap_corners(values, x_kind, y_kind) for x_kind, values in enumerate(c) for y_kind in (0, 1)]
    rows, cell = call(
        on_fields(functools.partial(cells_kernel, zs, xs)),
        (f32(6, zs, xs, ys), jax.ShapeDtypeStruct((256, 3 * ys), jnp.bfloat16)),
        "vvvv",
        cost=1.3,
        name="cells",
    )(*fields)
    halo = call(
        on_fields(functools.partial(x_halo_kernel, zs, xs)), f32(4, zs, TILE, ys), "vvvvvv", cost=0.2, name="x_halo"
    )(*fields, x_a, x_b)
    cross, nearer = call(
        functools.partial(cross_kernel, zs, xs, offsets),
        (f32(7, zs, xs, ys), f32(nz * nz, 1, 128)),
        "vvvv",
        [pltpu.VMEM((6, zs, TILE, ys), jnp.float32)],
        cost=1.0,
        name="cross",
    )(depth_order[None], rows, halo, cell)
    y_a, y_b, d, cross = lax.optimization_barrier((y_a, y_b, d, cross))

    faces = f32(FACE * xs + 3 * TILE, ys)
    merged, f_a, f_b = call(
        functools.partial(join_kernel, zs, xs),
        (f32(groups, block, 128), faces, faces),
        "v" * (6 + len(d)),
        name="join",
    )(m_a, m_b, halo, main, y_a, y_b, *d)
    z_a, z_b = swap_pairs(f_a, f_b, "gz", "gy")

    scale = 2.0 / (zs * nz)
    inner, full, looked = call(
        functools.partial(inner_kernel, zs, xs, scale),
        (f32(5, xs, ys), f32(7, zs, xs, ys), f32(4, 4, xs, ys)),
        "vvvvv",
        [
            pltpu.VMEM((3, groups, xs, 128), jnp.float32),
            pltpu.VMEM((10, 4, xs, ys), jnp.float32),
            pltpu.VMEM((4, 128), jnp.float32),
        ],
        cost=4.0,
        name="inner",
    )(cross, merged, table, material, strip)

    images = call(
        functools.partial(edge_kernel, zs, xs),
        [f32(4, part, ys)] * nz if swaps else [f32(4, xs, ys)],
        "vvvvv",
        [
            pltpu.VMEM((7, 4, xs, ys), jnp.float32),
            pltpu.VMEM((2, 2, 6, block, ys), jnp.float32),
            pltpu.VMEM((4, xs, ys), jnp.float32),
        ],
        name="edges",
    )(z_b, z_a, full, looked, inner)

    if swaps:
        mine = [images[0]]
        for k in offsets[1:]:
            mine.append(lax.ppermute(images[k], "gz", [(i, i ^ k) for i in range(nz)]))
    else:
        stacked = lax.all_to_all(images[0].reshape(4, nz, part, ys), "gz", split_axis=1, concat_axis=1)
        mine = [stacked[:, b] for b in range(nz)]
    return call(blend_kernel, f32(4, part, ys), "v" + "v" * nz, name="blend")(nearer, *mine)


def solution(mesh):
    return jax.shard_map(
        on_device,
        mesh=mesh,
        in_specs=(P(None, "gz", "gx", "gy"), P("gz", "gx", "gy"), P(), P()),
        out_specs=P(None, ("gx", "gz"), "gy"),
        check_vma=False,
    )
```

```python
import functools

import jax
import jax.numpy as jnp
import ml_dtypes
import numpy as np
from jax import lax
from jax.experimental import pallas as pl
from jax.experimental.pallas import tpu as pltpu
from jax.sharding import PartitionSpec as P

VMEM_LIMIT = 40 * 1024 * 1024
GROUP = 12
SLOT = 10
TILE = 8
FACE = 5
SPAN = 24

LOG1P = (
    0.9999995186059567, -0.49996356582563917, 0.33265255844036573, -0.24453388969978707, 0.17659864766821842,
    -0.10679931280022417, 0.043659288844443055, -0.008466410404849948,
)
EXPM1 = (
    1.0, -0.4999995231628418, 0.1666584461927414, -0.04160914570093155, 0.00814302358776331, -0.0010865303920581937,
)


def polynomial(coefficients, value):
    terms = list(coefficients)
    power = value
    while len(terms) > 1:
        paired = [terms[k] + terms[k + 1] * power for k in range(0, len(terms) - 1, 2)]
        terms = paired + ([terms[-1]] if len(terms) % 2 else [])
        power = power * power if len(terms) > 1 else power
    return terms[0]


BLUR = {off: weight / 64 for off, weight in ((-1, 1), (0, 2), (1, 1))}
BLUR2 = {off: weight / 2048 for off, weight in ((-2, 1), (-1, 4), (0, 6), (1, 4), (2, 1))}
SLOPE = {off: weight / 2048 for off, weight in ((-2, -1), (-1, -2), (1, 2), (2, 1))}


def strip_matrix(ysize):
    strips = np.zeros((128, 7 * ysize), np.float32)
    for block, (taps, field) in enumerate([(BLUR, f) for f in range(4)] + [(BLUR2, 0), (SLOPE, 0), (BLUR2, 0)]):
        first = slot_of(field)[0]
        outside = {-2: 0, -1: 1, ysize: 2, ysize + 1: 3} if field == 0 else {-1: first, ysize: first + 1}
        for out in range(ysize):
            for off, weight in taps.items():
                if not 0 <= out + off < ysize:
                    strips[outside[out + off], block * ysize + out] = weight
    return np.concatenate([strips, strips], axis=0).astype(ml_dtypes.bfloat16)


def make_cell_weights(out_ref):
    off = lax.broadcasted_iota(jnp.int32, (128, 128), 0) - lax.broadcasted_iota(jnp.int32, (128, 128), 1)
    for block, taps in enumerate((BLUR, BLUR2, SLOPE)):
        weights = jnp.zeros((128, 128), jnp.float32)
        for step, weight in taps.items():
            weights = jnp.where(off == step, float(weight), weights)
        for half in range(2):
            out_ref[128 * half : 128 * half + 128, 128 * block : 128 * block + 128] = weights.astype(jnp.bfloat16)


def halves(values):
    high = values.astype(jnp.bfloat16)
    low = (values - high.astype(jnp.float32)).astype(jnp.bfloat16)
    return jnp.concatenate([high, low], axis=1)


def place_of(axis):
    at = lax.axis_index(axis)
    return at == 0, at == lax.axis_size(axis) - 1, lax.rem(at, 2) == 1


def rows_kernel(zs, xs, even_high, fields_ref, out_ref):
    high = (lax.rem(lax.axis_index("gx"), 2) == 0) == even_high
    for group in range(FACE):
        field = max(group - 1, 0)
        rows = fields_ref.at[field].reshape(zs * xs, 128)
        low_row = group if group < 2 else 0
        high_row = xs - 2 + group if group < 2 else xs - 1
        out_ref[group] = rows[pl.ds(jnp.where(high, high_row, low_row), zs, stride=xs), :]


def slot_of(field):
    return (0, 4) if field == 0 else (2 + 2 * field, 2)


def pack_strips(load, layers, lane, rows):
    packed = jnp.zeros((rows, 128), jnp.float32)
    for k, z in enumerate(layers):
        for field in range(4):
            first, count = slot_of(field)
            start = SLOT * k + first
            values = pltpu.roll(load(field, z), (start + count // 2) % 128, 1)
            packed = jnp.where((lane >= start) & (lane < start + count), values, packed)
    return packed


def put_faces(zodd, out_refs, start, low, high):
    for ref, swapped in zip(out_refs, (False, True)):
        ref[start : start + low.shape[0], :] = jnp.where(zodd != swapped, low, high)


def pack_kernel(zs, xs, fields_ref, pack_ref, ma_ref, mb_ref, *corner_refs):
    zodd = place_of("gz")[2]
    for j in range(FACE):
        field = max(j - 1, 0)
        low, high = fields_ref[field, j if j < 2 else 0], fields_ref[field, zs - 2 + j if j < 2 else zs - 1]
        put_faces(zodd, (ma_ref, mb_ref), j * xs, low, high)
    xodd = place_of("gx")[2]
    lane = lax.broadcasted_iota(jnp.int32, (1, 128), 1)
    sub = lax.broadcasted_iota(jnp.int32, (TILE, 1), 0)
    for group in range(pack_ref.shape[0]):
        layers = range(group * GROUP, min(zs, group * GROUP + GROUP))
        packed = pack_strips(lambda f, z: fields_ref[f, z], layers, lane, xs)
        pack_ref[group] = packed
        first, last = packed[0:TILE], packed[xs - TILE :]
        low = jnp.where(sub == TILE - 1, pltpu.roll(first, TILE - 1, 0), pltpu.roll(first, TILE - 3, 0))
        high = jnp.where(sub == 0, pltpu.roll(last, 1, 0), pltpu.roll(last, 3, 0))
        for ref, swapped in zip(corner_refs, (False, True)):
            ref[group] = jnp.where(xodd != swapped, low, high)


def nearer_layers(offsets, order_ref, near_ref):
    iz, count = lax.axis_index("gz"), lax.axis_size("gz")
    order = order_ref[...].astype(jnp.float32)
    lane = lax.broadcasted_iota(jnp.int32, order.shape, 1)
    ranks = [
        jnp.sum(jnp.where(lane == (iz ^ offsets[k] if offsets else k), order, 0.0), axis=1, keepdims=True)
        for k in range(count)
    ]
    for k in range(count):
        for other in range(count):
            nearer = jnp.where(ranks[other] < ranks[k], 1.0, 0.0)
            near_ref[k * count + other] = jnp.broadcast_to(nearer, (1, 128))


def tables_of(table_ref, wide_ref, scale):
    wide_ref[...] = jnp.zeros_like(wide_ref)
    wide_ref[:, 0 : table_ref.shape[1]] = table_ref[...]
    return [jnp.broadcast_to(wide_ref[c : c + 1, :] * (0.5 if c < 3 else scale), (TILE, 128)) for c in range(4)]


def look_up(tables, ids_ref, z, t, tiles):
    ids = ids_ref[z, pl.ds(t, TILE, stride=tiles), :]
    return [jnp.take_along_axis(row, ids, axis=1, mode="promise_in_bounds") for row in tables]


def x_halo_kernel(zs, xs, fields_ref, xa_ref, xb_ref, halo_ref):
    xfirst, xlast, xodd = place_of("gx")
    halo_ref[...] = jnp.zeros_like(halo_ref)
    for field in range(4):
        tiles = halo_ref.at[field].reshape(zs * TILE, 128)
        own = fields_ref.at[field].reshape(zs * xs, 128)
        at = 0 if field == 0 else 1 + field
        below = jnp.where(xodd, xa_ref[1 + field], xb_ref[1 + field])
        above = jnp.where(xodd, xb_ref[at], xa_ref[at])
        tiles[pl.ds(0, zs, stride=TILE), :] = jnp.where(xfirst, 0.0, below)
        tiles[pl.ds(TILE - 1, zs, stride=TILE), :] = jnp.where(xlast, 0.0, above)
        if field == 0:
            low, high = own[pl.ds(0, zs, stride=xs), :], own[pl.ds(xs - 1, zs, stride=xs), :]
            tiles[pl.ds(1, zs, stride=TILE), :] = jnp.where(xfirst, -low, jnp.where(xodd, xa_ref[0], xb_ref[0]))
            tiles[pl.ds(TILE - 2, zs, stride=TILE), :] = jnp.where(xlast, -high, jnp.where(xodd, xb_ref[1], xa_ref[1]))


def join_kernel(zs, xs, ma_ref, mb_ref, halo_ref, own_ref, ya_ref, yb_ref, *rest):
    corner_refs, (cross_ref, strip_ref, merged_ref, fa_ref, fb_ref, full_ref, filtered_ref) = rest[:-7], rest[-7:]
    xfirst, xlast, xodd = place_of("gx")
    yfirst, ylast, yodd = place_of("gy")
    zfirst, zlast, zodd = place_of("gz")
    block = xs + TILE
    lane = lax.broadcasted_iota(jnp.int32, (1, 128), 1)
    sub = lax.broadcasted_iota(jnp.int32, (TILE, 1), 0)
    place = lax.rem(lane, SLOT)
    from_left = (place < 2) | ((place >= 4) & (lax.rem(place, 2) == 0))

    def merge(own, first, second):
        fill_left = jnp.where(place == 0, -pltpu.roll(own, 126, 1), 0.0)
        fill_right = jnp.where(place == 3, -pltpu.roll(own, 2, 1), 0.0)
        left = jnp.where(yfirst, fill_left, jnp.where(yodd, first, second))
        right = jnp.where(ylast, fill_right, jnp.where(yodd, second, first))
        return jnp.where(from_left, left, right)

    for group in range(own_ref.shape[0]):
        main = merge(own_ref[group], ya_ref[group], yb_ref[group])
        merged_ref[group, TILE:] = main
        tiles = []
        for k in range(2):
            a, b = corner_refs[k][group], corner_refs[k - 2][group]
            tiles.append(jnp.where(sub < TILE // 2, jnp.where(xodd, a, b), jnp.where(xodd, b, a)))
        tile = merge(tiles[1], tiles[0], tiles[1])
        low = jnp.where(sub == 1, -pltpu.roll(main[0:TILE], 1, 0), 0.0)
        high = jnp.where(sub == TILE - 2, -pltpu.roll(main[xs - TILE :], TILE - 1, 0), 0.0)
        tile = jnp.where(xfirst & (sub < TILE // 2), low, tile)
        merged_ref[group, 0:TILE] = jnp.where(xlast & (sub >= TILE // 2), high, tile)

    ends = (sub < 2) | (sub >= TILE - 2)

    def density_rows(z):
        return jnp.where(ends, halo_ref[0, z], pltpu.roll(halo_ref[0, z + 1], TILE // 2, 0))

    def field_rows(z):
        rows = [pltpu.roll(halo_ref[f, z], 2 * f - 2, 0) if f > 1 else halo_ref[f, z] for f in (1, 2, 3)]
        mixed = jnp.where((sub == 0) | (sub == TILE - 1), rows[0], rows[1])
        return jnp.where((sub == 3) | (sub == 4), rows[2], mixed)

    def strips(z):
        group, k = divmod(z, GROUP)
        packed = jnp.zeros((TILE, 128), jnp.float32)
        for t in range(block // TILE):
            moved = pltpu.roll(merged_ref[group, t * TILE : t * TILE + TILE], (SPAN * t - SLOT * k) % 128, 1)
            packed = jnp.where((lane >= SPAN * t) & (lane < SPAN * t + SPAN), moved, packed)
        return packed

    outs, start = (fa_ref, fb_ref), FACE * xs
    fa_ref[0:start, :] = ma_ref[...]
    fb_ref[0:start, :] = mb_ref[...]
    put_faces(zodd, outs, start, density_rows(0), density_rows(zs - 2))
    put_faces(zodd, outs, start + TILE, field_rows(0), field_rows(zs - 1))
    put_faces(zodd, outs, start + 2 * TILE, strips(0), strips(zs - 2))

    @pl.when(zfirst | zlast)
    def _():
        add_strips(zs, xs, cross_ref, merged_ref, strip_ref, full_ref, filtered_ref)


def along_y(values, halo, lane, density):
    def shifted(off):
        mixed = jnp.where(lane >= 128 - off if off > 0 else lane < -off, halo, values)
        return pltpu.roll(mixed, off % 128, 1)

    m1, p1 = shifted(1), shifted(-1)
    near = m1 + p1
    blur = BLUR[1] * near + BLUR[0] * values
    if not density:
        return (blur,)
    m2, p2 = shifted(2), shifted(-2)
    twice = BLUR2[2] * (m2 + p2) + BLUR2[1] * near + BLUR2[0] * values
    return blur, twice, SLOPE[2] * (p2 - m2) + SLOPE[1] * (p1 - m1)


class Rows:
    def __init__(self, tiles, halo):
        self.tiles, self.halo = list(tiles), halo
        self.sub = lax.broadcasted_iota(jnp.int32, (TILE, 1), 0)
        self.made = {}

    def row(self, t):
        count = len(self.tiles)
        if 0 <= t < count:
            return self.tiles[t]
        if t not in self.made:
            down = t < 0
            step = -t - 1 if down else t - count
            halo = self.halo if step == 0 else pltpu.roll(self.halo, TILE - 1 if down else 1, 0)
            inner = pltpu.roll(self.tiles[t % count], 1 if down else TILE - 1, 0)
            self.made[t] = jnp.where(self.sub == (0 if down else TILE - 1), halo, inner)
        return self.made[t]

    def pair(self, level, t):
        if level == 0:
            return self.row(t)
        if (level, t) not in self.made:
            self.made[level, t] = self.pair(level - 1, t) + self.pair(level - 1, t + 1)
        return self.made[level, t]

    def blur(self):
        return [self.pair(2, t - 1) for t in range(len(self.tiles))]

    def blur2(self):
        return [self.pair(4, t - 2) for t in range(len(self.tiles))]

    def slope(self):
        return [self.pair(2, t) - self.pair(2, t - 2) for t in range(len(self.tiles))]


def cells_kernel(zs, xs, fields_ref, out_ref, cell_ref):
    each, tiles = 8, xs // TILE
    make_cell_weights(cell_ref)

    def step(k, carry):
        first = k * each
        for field in range(4):
            rows = [
                fields_ref[field, first + j, pl.ds(t, TILE, stride=tiles), :] for j in range(each) for t in range(tiles)
            ]
            weights = cell_ref[...] if field == 0 else cell_ref[:, 0:128]
            result = jnp.dot(halves(jnp.concatenate(rows, axis=0)), weights, preferred_element_type=jnp.float32)
            for part in (0, 1, 2) if field == 0 else (2 + field,):
                columns = slice(128 * part, 128 * part + 128) if field == 0 else slice(0, 128)
                out_ref[part, pl.ds(first, each)] = result[:, columns].reshape(each, xs, 128)
        return carry

    lax.fori_loop(0, zs // each, step, 0)


def cross_kernel(zs, xs, offsets, order_ref, rows_ref, halo_ref, cell_ref, out_ref, near_ref, edge_ref):
    each, tiles = 4, xs // TILE
    nearer_layers(offsets, order_ref, near_ref)
    for field in range(4):
        weights = cell_ref[...] if field == 0 else cell_ref[:, 0:128]
        result = jnp.dot(
            halves(halo_ref[field].reshape(zs * TILE, 128)), weights, preferred_element_type=jnp.float32
        )
        for part in (0, 1, 2) if field == 0 else (2 + field,):
            columns = slice(128 * part, 128 * part + 128) if field == 0 else slice(0, 128)
            edge_ref[part] = result[:, columns].reshape(zs, TILE, 128)

    def step(k, carry):
        for j in range(each):
            z = k * each + j

            def part_rows(part):
                return Rows([rows_ref[part, z, t * TILE : t * TILE + TILE, :] for t in range(tiles)], edge_ref[part, z])

            twice, sloped = part_rows(1), part_rows(2)
            results = [part_rows(part).blur() for part in (0, 3, 4, 5)]
            results += [twice.blur2(), twice.slope(), sloped.blur2()]
            for part, values in enumerate(results):
                for t in range(tiles):
                    out_ref[part, z, t * TILE : t * TILE + TILE, :] = values[t]
        return carry

    lax.fori_loop(0, zs // each, step, 0)


def before_shade(load, z):
    def blur(part):
        return load(part, z - 1) + load(part, z + 1) + 2.0 * load(part, z)

    def blur2(part):
        return (load(part, z - 2) + load(part, z + 2)) + 4.0 * (load(part, z - 1) + load(part, z + 1)) + 6.0 * load(part, z)

    near = load(4, z + 1) - load(4, z - 1)
    grad_z = (load(4, z + 2) - load(4, z - 2)) + (near + near)
    grad_x = blur2(5)
    grad_y = blur2(6)
    facing = jnp.abs(0.8 * (grad_z + grad_y) + 0.4 * grad_x)
    square = grad_z * grad_z + grad_x * grad_x + grad_y * grad_y
    shading = 0.3 + facing * lax.rsqrt(square + 0.0025)
    density = 3.0 * blur(0)
    return [density, jnp.exp(-jnp.abs(density)), shading] + [blur(1 + c) for c in range(3)]


def shade(state, taken, looked):
    density, t, shading = taken[:3]
    soft = jnp.maximum(density, 0.0) + t * polynomial(LOG1P, t)
    extinct = looked[3] * soft
    passed, total, depth = state[0], state[1:4], state[4]
    weight = passed * (extinct * polynomial(EXPM1, extinct))
    lit = weight * shading
    colours = [
        total[c] + (looked[c] * lit) * (2.0 + jnp.tanh(taken[3 + c])) for c in range(3)
    ]
    return (passed - weight, *colours, depth + extinct)


def add_strips(zs, xs, cross_ref, merged_ref, strip_ref, full_ref, filtered_ref):
    tiles, each = xs // TILE, 8
    for group in range(merged_ref.shape[0]):
        rows = Rows([merged_ref[group, pl.ds(TILE + t, TILE, stride=tiles), :] for t in range(tiles)], merged_ref[group, 0:TILE])
        for k, values in enumerate((rows.blur(), rows.blur2(), rows.slope())):
            for t in range(tiles):
                filtered_ref[k, group, t * TILE : t * TILE + TILE, :] = values[t]

    def strip_step(step, carry):
        first = step * each
        for k, parts in enumerate(((0, 1, 2, 3), (4, 6), (5,))):
            strips = []
            for j in range(each):
                group = lax.div(first + j, GROUP)
                slot = first + j - group * GROUP
                strips.append(pltpu.roll(filtered_ref[k, group], lax.rem(128 - SLOT * slot, 128), 1))
            columns = slice((0, 512, 768)[k], (512, 768, 896)[k])
            result = jnp.dot(
                halves(jnp.concatenate(strips, axis=0)), strip_ref[:, columns], preferred_element_type=jnp.float32
            )
            for n, part in enumerate(parts):
                share = result[:, 128 * n : 128 * n + 128].reshape(each, xs, 128)
                full_ref[part, pl.ds(first, each)] = cross_ref[part, pl.ds(first, each)] + share
        return carry

    lax.fori_loop(0, zs // each, strip_step, 0)


def inner_kernel(zs, xs, scale, cross_ref, merged_ref, early_ref, table_ref, ids_ref, strip_ref, inner_ref, rim_ref, looked_ref, full_ref, filtered_ref, taken_ref, wide_ref):
    tiles = xs // TILE
    tables = tables_of(table_ref, wide_ref, scale)
    for k, z in enumerate((0, 1, zs - 2, zs - 1)):
        for t in range(tiles):
            for c, values in enumerate(look_up(tables, ids_ref, z, t, tiles)):
                looked_ref[c, k, t * TILE : t * TILE + TILE, :] = values
    zfirst, zlast, _ = place_of("gz")
    end = zfirst | zlast

    @pl.when(end)
    def _():
        shade_inner(zs, xs, early_ref, tables, ids_ref, inner_ref, rim_ref, taken_ref)

    @pl.when(jnp.logical_not(end))
    def _():
        add_strips(zs, xs, cross_ref, merged_ref, strip_ref, full_ref, filtered_ref)
        shade_inner(zs, xs, full_ref, tables, ids_ref, inner_ref, rim_ref, taken_ref)


def shade_inner(zs, xs, full_ref, tables, ids_ref, inner_ref, rim_ref, taken_ref):
    tiles = xs // TILE
    for part in range(7):
        rim_ref[part, 0:4] = full_ref[part, 0:4]
        rim_ref[part, 4:8] = full_ref[part, zs - 4 : zs]
    ahead = taken_ref.shape[1]
    steps = (zs - 4) // ahead

    def take(step):
        first = 2 + ahead * step
        for t in range(tiles):
            rows = slice(t * TILE, t * TILE + TILE)
            held = {}

            def load(part, j):
                if (part, j) not in held:
                    held[part, j] = full_ref[part, first + j, rows]
                return held[part, j]

            for j in range(ahead):
                taken = before_shade(load, j) + look_up(tables, ids_ref, first + j, t, tiles)
                for k, values in enumerate(taken):
                    taken_ref[k, j, rows] = values

    def advance(step, state):
        for j in range(ahead):
            taken = [taken_ref[k, j] for k in range(10)]
            state = shade(state, taken[:6], taken[6:])
        return state

    def z_step(step, state):
        state = advance(step, state)
        take(step + 1)
        return state

    zero = jnp.zeros((xs, 128), jnp.float32)
    take(0)
    state = lax.fori_loop(0, steps - 1, z_step, (zero + 1.0, zero, zero, zero, zero))
    for k, values in enumerate(advance(steps - 1, state)):
        inner_ref[k] = values


def edge_kernel(zs, xs, fb_ref, fa_ref, cross_ref, looked_ref, inner_ref, *rest):
    out_refs, (near_ref, rows_ref, image_ref) = rest[:-3], rest[-3:]
    zfirst, zlast, zodd = place_of("gz")
    block = xs + TILE
    tiles = xs // TILE
    lane = lax.broadcasted_iota(jnp.int32, (1, 128), 1)
    for side in range(2):
        first, second = (fa_ref, fb_ref) if side == 0 else (fb_ref, fa_ref)

        def face(start, count):
            return jnp.where(zodd, first[start : start + count, :], second[start : start + count, :])

        ends = [face(FACE * xs, TILE), face(FACE * xs + TILE, TILE)]
        strips = face(FACE * xs + 2 * TILE, TILE)
        for j in range(FACE):
            field = max(j - 1, 0)
            layer = j if j < 2 else (1 if side == 0 else 0)
            turned = TILE // 2 * j if j < 2 else 2 * field - 2
            outer_rows = ends[min(field, 1)]
            if turned:
                outer_rows = pltpu.roll(outer_rows, TILE - turned, 0)
            at_lane = SLOT * layer + slot_of(field)[0]
            own = 126 if field == 0 else 127
            halo = [pltpu.roll(strips, (own - at_lane - SPAN * t) % 128, 1) for t in range(block // TILE)]
            values = jnp.concatenate([outer_rows, face(j * xs, xs)], axis=0)
            results = along_y(values, jnp.concatenate(halo, axis=0), lane, field == 0)
            for part, result in zip((0, 1, 2) if field == 0 else (2 + field,), results):
                rows_ref[side, layer, part] = result
    for side in range(2):
        edge = zfirst if side == 0 else zlast
        for layer in range(2):
            mirrored = 0 if side == 0 else 7
            outer = layer == side

            def part_rows(part):
                ref = rows_ref.at[side, layer, part]
                return Rows([ref[pl.ds(TILE + t, TILE, stride=tiles), :] for t in range(tiles)], ref[0:TILE, :])

            twice, sloped = part_rows(1), part_rows(2)
            for part, values in zip((4, 5, 6), (twice.blur2(), twice.slope(), sloped.blur2())):
                for t in range(tiles):
                    rows = slice(t * TILE, t * TILE + TILE)
                    fill = -cross_ref[part, mirrored, rows] if outer else 0.0
                    near_ref[part, 2 * side + layer, rows] = jnp.where(edge, fill, values[t])
            if not outer:
                for part, source in enumerate((0, 3, 4, 5)):
                    for t, values in enumerate(part_rows(source).blur()):
                        near_ref[part, 2 * side + layer, t * TILE : t * TILE + TILE] = jnp.where(edge, 0.0, values)

    def load(part, z):
        if z < 0:
            return near_ref[part, z + 2]
        if z >= zs:
            return near_ref[part, z - zs + 2]
        return cross_ref[part, z if z < 4 else z - zs + 8]

    def behind(state, z):
        looked = [looked_ref[c, z if z < 2 else z - zs + 4] for c in range(4)]
        return shade(state, before_shade(load, z), looked)

    zero = jnp.zeros((xs, 128), jnp.float32)
    state = behind(behind((zero + 1.0, zero, zero, zero, zero), 0), 1)
    passed = state[0]
    state = (
        passed * inner_ref[0],
        state[1] + passed * inner_ref[1],
        state[2] + passed * inner_ref[2],
        state[3] + passed * inner_ref[3],
        state[4] + inner_ref[4],
    )
    state = behind(behind(state, zs - 2), zs - 1)
    for c in range(4):
        for t in range(tiles):
            image_ref[c, pl.ds(t, TILE, stride=tiles), :] = state[1 + c][t * TILE : t * TILE + TILE]
    if len(out_refs) == 1:
        out_refs[0][...] = image_ref[...]
    else:
        part = xs // len(out_refs)
        for k, ref in enumerate(out_refs):
            ref[...] = image_ref[:, pl.ds(pl.multiple_of((lax.axis_index("gz") ^ k) * part, part), part), :]


def blend_kernel(near_ref, *refs):
    images, out_ref = refs[:-1], refs[-1]
    count = len(images)
    depths = [image[3] for image in images]
    colours = [jnp.zeros_like(depths[0])] * 3
    for k in range(count):
        prior = jnp.zeros_like(depths[0])
        for other in range(count):
            if other != k:
                prior += near_ref[k * count + other] * depths[other]
        through = jnp.exp(-prior)
        colours = [colours[c] + through * images[k][c] for c in range(3)]
    total = functools.reduce(jnp.add, depths)
    out_ref[0], out_ref[1], out_ref[2] = colours
    small = total * polynomial(EXPM1, total)
    out_ref[3] = jnp.where(total < 0.5, small, 1.0 - jnp.exp(-total))


def call(kernel, out_shape, specs, scratch=(), cost=1.0, name=None, limit=VMEM_LIMIT):
    where = {"s": pltpu.SMEM, "v": pltpu.VMEM, "a": pl.ANY}
    return pl.pallas_call(
        kernel,
        out_shape=out_shape,
        in_specs=[pl.BlockSpec(memory_space=where[s]) for s in specs],
        out_specs=jax.tree.map(lambda _: pl.BlockSpec(memory_space=pltpu.VMEM), out_shape),
        scratch_shapes=list(scratch),
        compiler_params=pltpu.CompilerParams(vmem_limit_bytes=limit),
        cost_estimate=pl.CostEstimate(flops=0, bytes_accessed=int(cost * 3.0e6), transcendentals=0),
        name=name,
    )


def swap_pairs(first, second, axis, idle):
    count, others = lax.axis_size(axis), lax.axis_size(idle)
    even = [(i, i ^ 1) for i in range(count)]
    if count == 2:
        one = lax.ppermute(first, axis, even)
        return one, one
    pairs = []
    for i in range(count):
        for j in range(others):
            end = i in (0, count - 1)
            to = (i if end else i + 1 if i % 2 else i - 1, j ^ 1 if end else j)
            if axis < idle:
                pairs.append((i * others + j, to[0] * others + to[1]))
            else:
                pairs.append((j * count + i, to[1] * count + to[0]))
    two = lax.ppermute(second, tuple(sorted((axis, idle))), pairs)
    return lax.ppermute(first, axis, even), two


def swap_corners(values, x_kind, y_kind):
    counts = [lax.axis_size(a) for a in ("gx", "gy")]

    def partner(at, count, kind):
        to = at ^ 1 if kind == 0 else at + 1 if at % 2 else at - 1
        return to if 0 <= to < count else at

    pairs = []
    for i in range(counts[0]):
        for j in range(counts[1]):
            to = partner(i, counts[0], x_kind), partner(j, counts[1], y_kind)
            pairs.append((i * counts[1] + j, to[0] * counts[1] + to[1]))
    return lax.ppermute(values, ("gx", "gy"), pairs)


def on_device(fields, material, depth_order, table):
    _, zs, xs, ys = fields.shape
    nx, nz = lax.axis_size("gx"), lax.axis_size("gz")
    block = xs + TILE
    part = xs // nz
    swaps = nz in (2, 4)
    offsets = [0] + list(range(nz - 1, 0, -1)) if swaps else None
    groups = -(-zs // GROUP)
    f32 = lambda *shape: jax.ShapeDtypeStruct(shape, jnp.float32)

    def side(even_high):
        return call(functools.partial(rows_kernel, zs, xs, even_high), f32(FACE, zs, ys), "v", name="x_rows")(fields)

    x_a, x_b = swap_pairs(side(True), side(False) if nx > 2 else None, "gx", "gy")
    strip = jnp.asarray(strip_matrix(ys))
    strips, corners = f32(groups, xs, 128), f32(groups, TILE, 128)
    faces = f32(FACE * xs, ys)
    main, m_a, m_b, *c = call(
        functools.partial(pack_kernel, zs, xs),
        (strips, faces, faces) + (corners,) * (1 if nx == 2 else 2),
        "v",
        cost=0.7,
        name="pack",
    )(fields)
    y_a, y_b = swap_pairs(main, main, "gy", "gx")
    d = [swap_corners(values, x_kind, y_kind) for x_kind, values in enumerate(c) for y_kind in (0, 1)]
    rows, cell = call(
        functools.partial(cells_kernel, zs, xs),
        (f32(6, zs, xs, ys), jax.ShapeDtypeStruct((256, 3 * ys), jnp.bfloat16)),
        "v",
        cost=1.3,
        name="cells",
    )(fields)
    halo = call(functools.partial(x_halo_kernel, zs, xs), f32(4, zs, TILE, ys), "vvv", cost=0.2, name="x_halo")(
        fields, x_a, x_b
    )
    cross, nearer = call(
        functools.partial(cross_kernel, zs, xs, offsets),
        (f32(7, zs, xs, ys), f32(nz * nz, 1, 128)),
        "vvvv",
        [pltpu.VMEM((6, zs, TILE, ys), jnp.float32)],
        cost=1.0,
        name="cross",
    )(depth_order[None], rows, halo, cell)
    y_a, y_b, d, cross = lax.optimization_barrier((y_a, y_b, d, cross))

    faces = f32(FACE * xs + 3 * TILE, ys)
    merged, f_a, f_b, early = call(
        functools.partial(join_kernel, zs, xs),
        (f32(groups, block, 128), faces, faces, f32(7, zs, xs, ys)),
        "v" * (8 + len(d)),
        [pltpu.VMEM((3, groups, xs, 128), jnp.float32)],
        name="join",
    )(m_a, m_b, halo, main, y_a, y_b, *d, cross, strip)
    z_a, z_b = swap_pairs(f_a, f_b, "gz", "gy")

    scale = 2.0 / (zs * nz)
    inner, rim, looked = call(
        functools.partial(inner_kernel, zs, xs, scale),
        (f32(5, xs, ys), f32(7, 8, xs, ys), f32(4, 4, xs, ys)),
        "vvvvvv",
        [
            pltpu.VMEM((7, zs, xs, ys), jnp.float32),
            pltpu.VMEM((3, groups, xs, 128), jnp.float32),
            pltpu.VMEM((10, 4, xs, ys), jnp.float32),
            pltpu.VMEM((4, 128), jnp.float32),
        ],
        cost=4.0,
        name="inner",
    )(cross, merged, early, table, material, strip)

    images = call(
        functools.partial(edge_kernel, zs, xs),
        [f32(4, part, ys)] * nz if swaps else [f32(4, xs, ys)],
        "vvvvv",
        [
            pltpu.VMEM((7, 4, xs, ys), jnp.float32),
            pltpu.VMEM((2, 2, 6, block, ys), jnp.float32),
            pltpu.VMEM((4, xs, ys), jnp.float32),
        ],
        name="edges",
    )(z_b, z_a, rim, looked, inner)

    if swaps:
        mine = [images[0]]
        for k in offsets[1:]:
            mine.append(lax.ppermute(images[k], "gz", [(i, i ^ k) for i in range(nz)]))
    else:
        stacked = lax.all_to_all(images[0].reshape(4, nz, part, ys), "gz", split_axis=1, concat_axis=1)
        mine = [stacked[:, b] for b in range(nz)]
    return call(blend_kernel, f32(4, part, ys), "v" + "v" * nz, name="blend")(nearer, *mine)


def solution(mesh):
    return jax.shard_map(
        on_device,
        mesh=mesh,
        in_specs=(P(None, "gz", "gx", "gy"), P("gz", "gx", "gy"), P(), P()),
        out_specs=P(None, ("gx", "gz"), "gy"),
        check_vma=False,
    )
```

```python
import functools

import jax
import jax.numpy as jnp
import ml_dtypes
import numpy as np
from jax import lax
from jax.experimental import pallas as pl
from jax.experimental.pallas import tpu as pltpu
from jax.sharding import PartitionSpec as P

VMEM_LIMIT = 40 * 1024 * 1024
GROUP = 12
SLOT = 10
TILE = 8
FACE = 5
SPAN = 24

LOG1P = (
    0.9999995186059567, -0.49996356582563917, 0.33265255844036573, -0.24453388969978707, 0.17659864766821842,
    -0.10679931280022417, 0.043659288844443055, -0.008466410404849948,
)
EXPM1 = (
    1.0, -0.4999995231628418, 0.1666584461927414, -0.04160914570093155, 0.00814302358776331, -0.0010865303920581937,
)


def polynomial(coefficients, value):
    terms = list(coefficients)
    power = value
    while len(terms) > 1:
        paired = [terms[k] + terms[k + 1] * power for k in range(0, len(terms) - 1, 2)]
        terms = paired + ([terms[-1]] if len(terms) % 2 else [])
        power = power * power if len(terms) > 1 else power
    return terms[0]


BLUR = {off: weight / 64 for off, weight in ((-1, 1), (0, 2), (1, 1))}
BLUR2 = {off: weight / 2048 for off, weight in ((-2, 1), (-1, 4), (0, 6), (1, 4), (2, 1))}
SLOPE = {off: weight / 2048 for off, weight in ((-2, -1), (-1, -2), (1, 2), (2, 1))}


def strip_matrix(ysize):
    strips = np.zeros((128, 7 * ysize), np.float32)
    for block, (taps, field) in enumerate([(BLUR, f) for f in range(4)] + [(BLUR2, 0), (SLOPE, 0), (BLUR2, 0)]):
        first = slot_of(field)[0]
        outside = {-2: 0, -1: 1, ysize: 2, ysize + 1: 3} if field == 0 else {-1: first, ysize: first + 1}
        for out in range(ysize):
            for off, weight in taps.items():
                if not 0 <= out + off < ysize:
                    strips[outside[out + off], block * ysize + out] = weight
    return np.concatenate([strips, strips], axis=0).astype(ml_dtypes.bfloat16)


def make_cell_weights(out_ref):
    off = lax.broadcasted_iota(jnp.int32, (128, 128), 0) - lax.broadcasted_iota(jnp.int32, (128, 128), 1)
    for block, taps in enumerate((BLUR, BLUR2, SLOPE)):
        weights = jnp.zeros((128, 128), jnp.float32)
        for step, weight in taps.items():
            weights = jnp.where(off == step, float(weight), weights)
        for half in range(2):
            out_ref[128 * half : 128 * half + 128, 128 * block : 128 * block + 128] = weights.astype(jnp.bfloat16)


def halves(values):
    high = values.astype(jnp.bfloat16)
    low = (values - high.astype(jnp.float32)).astype(jnp.bfloat16)
    return jnp.concatenate([high, low], axis=1)


def place_of(axis):
    at = lax.axis_index(axis)
    return at == 0, at == lax.axis_size(axis) - 1, lax.rem(at, 2) == 1


def rows_kernel(zs, xs, even_high, fields_ref, out_ref):
    high = (lax.rem(lax.axis_index("gx"), 2) == 0) == even_high
    for group in range(FACE):
        field = max(group - 1, 0)
        rows = fields_ref.at[field].reshape(zs * xs, 128)
        low_row = group if group < 2 else 0
        high_row = xs - 2 + group if group < 2 else xs - 1
        out_ref[group] = rows[pl.ds(jnp.where(high, high_row, low_row), zs, stride=xs), :]


def slot_of(field):
    return (0, 4) if field == 0 else (2 + 2 * field, 2)


def pack_strips(load, layers, lane, rows):
    packed = jnp.zeros((rows, 128), jnp.float32)
    for k, z in enumerate(layers):
        for field in range(4):
            first, count = slot_of(field)
            start = SLOT * k + first
            values = pltpu.roll(load(field, z), (start + count // 2) % 128, 1)
            packed = jnp.where((lane >= start) & (lane < start + count), values, packed)
    return packed


def put_faces(zodd, out_refs, start, low, high):
    for ref, swapped in zip(out_refs, (False, True)):
        ref[start : start + low.shape[0], :] = jnp.where(zodd != swapped, low, high)


def pack_kernel(zs, xs, fields_ref, pack_ref, ma_ref, mb_ref, *corner_refs):
    zodd = place_of("gz")[2]
    for j in range(FACE):
        field = max(j - 1, 0)
        low, high = fields_ref[field, j if j < 2 else 0], fields_ref[field, zs - 2 + j if j < 2 else zs - 1]
        put_faces(zodd, (ma_ref, mb_ref), j * xs, low, high)
    xodd = place_of("gx")[2]
    lane = lax.broadcasted_iota(jnp.int32, (1, 128), 1)
    sub = lax.broadcasted_iota(jnp.int32, (TILE, 1), 0)
    for group in range(pack_ref.shape[0]):
        layers = range(group * GROUP, min(zs, group * GROUP + GROUP))
        packed = pack_strips(lambda f, z: fields_ref[f, z], layers, lane, xs)
        pack_ref[group] = packed
        first, last = packed[0:TILE], packed[xs - TILE :]
        low = jnp.where(sub == TILE - 1, pltpu.roll(first, TILE - 1, 0), pltpu.roll(first, TILE - 3, 0))
        high = jnp.where(sub == 0, pltpu.roll(last, 1, 0), pltpu.roll(last, 3, 0))
        for ref, swapped in zip(corner_refs, (False, True)):
            ref[group] = jnp.where(xodd != swapped, low, high)


def nearer_layers(offsets, order_ref, near_ref):
    iz, count = lax.axis_index("gz"), lax.axis_size("gz")
    order = order_ref[...].astype(jnp.float32)
    lane = lax.broadcasted_iota(jnp.int32, order.shape, 1)
    ranks = [
        jnp.sum(jnp.where(lane == (iz ^ offsets[k] if offsets else k), order, 0.0), axis=1, keepdims=True)
        for k in range(count)
    ]
    for k in range(count):
        for other in range(count):
            nearer = jnp.where(ranks[other] < ranks[k], 1.0, 0.0)
            near_ref[k * count + other] = jnp.broadcast_to(nearer, (1, 128))


def tables_of(table_ref, wide_ref, scale):
    wide_ref[...] = jnp.zeros_like(wide_ref)
    wide_ref[:, 0 : table_ref.shape[1]] = table_ref[...]
    return [jnp.broadcast_to(wide_ref[c : c + 1, :] * (0.5 if c < 3 else scale), (TILE, 128)) for c in range(4)]


def look_up(tables, ids_ref, z, t, tiles):
    ids = ids_ref[z, pl.ds(t, TILE, stride=tiles), :]
    return [jnp.take_along_axis(row, ids, axis=1, mode="promise_in_bounds") for row in tables]


def x_halo_kernel(zs, xs, fields_ref, xa_ref, xb_ref, halo_ref):
    xfirst, xlast, xodd = place_of("gx")
    halo_ref[...] = jnp.zeros_like(halo_ref)
    for field in range(4):
        tiles = halo_ref.at[field].reshape(zs * TILE, 128)
        own = fields_ref.at[field].reshape(zs * xs, 128)
        at = 0 if field == 0 else 1 + field
        below = jnp.where(xodd, xa_ref[1 + field], xb_ref[1 + field])
        above = jnp.where(xodd, xb_ref[at], xa_ref[at])
        tiles[pl.ds(0, zs, stride=TILE), :] = jnp.where(xfirst, 0.0, below)
        tiles[pl.ds(TILE - 1, zs, stride=TILE), :] = jnp.where(xlast, 0.0, above)
        if field == 0:
            low, high = own[pl.ds(0, zs, stride=xs), :], own[pl.ds(xs - 1, zs, stride=xs), :]
            tiles[pl.ds(1, zs, stride=TILE), :] = jnp.where(xfirst, -low, jnp.where(xodd, xa_ref[0], xb_ref[0]))
            tiles[pl.ds(TILE - 2, zs, stride=TILE), :] = jnp.where(xlast, -high, jnp.where(xodd, xb_ref[1], xa_ref[1]))


def join_kernel(zs, xs, ma_ref, mb_ref, halo_ref, own_ref, ya_ref, yb_ref, *rest):
    corner_refs, (merged_ref, fa_ref, fb_ref) = rest[:-3], rest[-3:]
    xfirst, xlast, xodd = place_of("gx")
    yfirst, ylast, yodd = place_of("gy")
    zodd = place_of("gz")[2]
    block = xs + TILE
    lane = lax.broadcasted_iota(jnp.int32, (1, 128), 1)
    sub = lax.broadcasted_iota(jnp.int32, (TILE, 1), 0)
    place = lax.rem(lane, SLOT)
    from_left = (place < 2) | ((place >= 4) & (lax.rem(place, 2) == 0))

    def merge(own, first, second):
        fill_left = jnp.where(place == 0, -pltpu.roll(own, 126, 1), 0.0)
        fill_right = jnp.where(place == 3, -pltpu.roll(own, 2, 1), 0.0)
        left = jnp.where(yfirst, fill_left, jnp.where(yodd, first, second))
        right = jnp.where(ylast, fill_right, jnp.where(yodd, second, first))
        return jnp.where(from_left, left, right)

    for group in range(own_ref.shape[0]):
        main = merge(own_ref[group], ya_ref[group], yb_ref[group])
        merged_ref[group, TILE:] = main
        tiles = []
        for k in range(2):
            a, b = corner_refs[k][group], corner_refs[k - 2][group]
            tiles.append(jnp.where(sub < TILE // 2, jnp.where(xodd, a, b), jnp.where(xodd, b, a)))
        tile = merge(tiles[1], tiles[0], tiles[1])
        low = jnp.where(sub == 1, -pltpu.roll(main[0:TILE], 1, 0), 0.0)
        high = jnp.where(sub == TILE - 2, -pltpu.roll(main[xs - TILE :], TILE - 1, 0), 0.0)
        tile = jnp.where(xfirst & (sub < TILE // 2), low, tile)
        merged_ref[group, 0:TILE] = jnp.where(xlast & (sub >= TILE // 2), high, tile)

    ends = (sub < 2) | (sub >= TILE - 2)

    def density_rows(z):
        return jnp.where(ends, halo_ref[0, z], pltpu.roll(halo_ref[0, z + 1], TILE // 2, 0))

    def field_rows(z):
        rows = [pltpu.roll(halo_ref[f, z], 2 * f - 2, 0) if f > 1 else halo_ref[f, z] for f in (1, 2, 3)]
        mixed = jnp.where((sub == 0) | (sub == TILE - 1), rows[0], rows[1])
        return jnp.where((sub == 3) | (sub == 4), rows[2], mixed)

    def strips(z):
        group, k = divmod(z, GROUP)
        packed = jnp.zeros((TILE, 128), jnp.float32)
        for t in range(block // TILE):
            moved = pltpu.roll(merged_ref[group, t * TILE : t * TILE + TILE], (SPAN * t - SLOT * k) % 128, 1)
            packed = jnp.where((lane >= SPAN * t) & (lane < SPAN * t + SPAN), moved, packed)
        return packed

    outs, start = (fa_ref, fb_ref), FACE * xs
    fa_ref[0:start, :] = ma_ref[...]
    fb_ref[0:start, :] = mb_ref[...]
    put_faces(zodd, outs, start, density_rows(0), density_rows(zs - 2))
    put_faces(zodd, outs, start + TILE, field_rows(0), field_rows(zs - 1))
    put_faces(zodd, outs, start + 2 * TILE, strips(0), strips(zs - 2))


def along_y(values, halo, lane, density):
    def shifted(off):
        mixed = jnp.where(lane >= 128 - off if off > 0 else lane < -off, halo, values)
        return pltpu.roll(mixed, off % 128, 1)

    m1, p1 = shifted(1), shifted(-1)
    near = m1 + p1
    blur = BLUR[1] * near + BLUR[0] * values
    if not density:
        return (blur,)
    m2, p2 = shifted(2), shifted(-2)
    twice = BLUR2[2] * (m2 + p2) + BLUR2[1] * near + BLUR2[0] * values
    return blur, twice, SLOPE[2] * (p2 - m2) + SLOPE[1] * (p1 - m1)


class Rows:
    def __init__(self, tiles, halo):
        self.tiles, self.halo = list(tiles), halo
        self.sub = lax.broadcasted_iota(jnp.int32, (TILE, 1), 0)
        self.made = {}

    def row(self, t):
        count = len(self.tiles)
        if 0 <= t < count:
            return self.tiles[t]
        if t not in self.made:
            down = t < 0
            step = -t - 1 if down else t - count
            halo = self.halo if step == 0 else pltpu.roll(self.halo, TILE - 1 if down else 1, 0)
            inner = pltpu.roll(self.tiles[t % count], 1 if down else TILE - 1, 0)
            self.made[t] = jnp.where(self.sub == (0 if down else TILE - 1), halo, inner)
        return self.made[t]

    def pair(self, level, t):
        if level == 0:
            return self.row(t)
        if (level, t) not in self.made:
            self.made[level, t] = self.pair(level - 1, t) + self.pair(level - 1, t + 1)
        return self.made[level, t]

    def blur(self):
        return [self.pair(2, t - 1) for t in range(len(self.tiles))]

    def blur2(self):
        return [self.pair(4, t - 2) for t in range(len(self.tiles))]

    def slope(self):
        return [self.pair(2, t) - self.pair(2, t - 2) for t in range(len(self.tiles))]


def cells_kernel(zs, xs, fields_ref, out_ref, cell_ref):
    each, tiles = 16, xs // TILE
    make_cell_weights(cell_ref)

    def step(k, carry):
        first = k * each
        for field in range(4):
            rows = [
                fields_ref[field, first + j, pl.ds(t, TILE, stride=tiles), :] for j in range(each) for t in range(tiles)
            ]
            weights = cell_ref[...] if field == 0 else cell_ref[:, 0:128]
            result = jnp.dot(halves(jnp.concatenate(rows, axis=0)), weights, preferred_element_type=jnp.float32)
            for part in (0, 1, 2) if field == 0 else (2 + field,):
                columns = slice(128 * part, 128 * part + 128) if field == 0 else slice(0, 128)
                out_ref[part, pl.ds(first, each)] = result[:, columns].reshape(each, xs, 128)
        return carry

    lax.fori_loop(0, zs // each, step, 0)


def cross_kernel(zs, xs, offsets, order_ref, rows_ref, halo_ref, cell_ref, out_ref, near_ref, edge_ref):
    each, tiles = 4, xs // TILE
    nearer_layers(offsets, order_ref, near_ref)
    for field in range(4):
        weights = cell_ref[...] if field == 0 else cell_ref[:, 0:128]
        result = jnp.dot(
            halves(halo_ref[field].reshape(zs * TILE, 128)), weights, preferred_element_type=jnp.float32
        )
        for part in (0, 1, 2) if field == 0 else (2 + field,):
            columns = slice(128 * part, 128 * part + 128) if field == 0 else slice(0, 128)
            edge_ref[part] = result[:, columns].reshape(zs, TILE, 128)

    def step(k, carry):
        for j in range(each):
            z = k * each + j

            def part_rows(part):
                return Rows([rows_ref[part, z, t * TILE : t * TILE + TILE, :] for t in range(tiles)], edge_ref[part, z])

            twice, sloped = part_rows(1), part_rows(2)
            results = [part_rows(part).blur() for part in (0, 3, 4, 5)]
            results += [twice.blur2(), twice.slope(), sloped.blur2()]
            for part, values in enumerate(results):
                for t in range(tiles):
                    out_ref[part, z, t * TILE : t * TILE + TILE, :] = values[t]
        return carry

    lax.fori_loop(0, zs // each, step, 0)


def before_shade(load, z):
    def blur(part):
        return load(part, z - 1) + load(part, z + 1) + 2.0 * load(part, z)

    def blur2(part):
        return (load(part, z - 2) + load(part, z + 2)) + 4.0 * (load(part, z - 1) + load(part, z + 1)) + 6.0 * load(part, z)

    near = load(4, z + 1) - load(4, z - 1)
    grad_z = (load(4, z + 2) - load(4, z - 2)) + (near + near)
    grad_x = blur2(5)
    grad_y = blur2(6)
    facing = jnp.abs(0.8 * (grad_z + grad_y) + 0.4 * grad_x)
    square = grad_z * grad_z + grad_x * grad_x + grad_y * grad_y
    shading = 0.3 + facing * lax.rsqrt(square + 0.0025)
    density = 3.0 * blur(0)
    return [density, jnp.exp(-jnp.abs(density)), shading] + [blur(1 + c) for c in range(3)]


def shade(state, taken, looked):
    density, t, shading = taken[:3]
    soft = jnp.maximum(density, 0.0) + t * polynomial(LOG1P, t)
    extinct = looked[3] * soft
    passed, total, depth = state[0], state[1:4], state[4]
    weight = passed * (extinct * polynomial(EXPM1, extinct))
    lit = weight * shading
    colours = [
        total[c] + (looked[c] * lit) * (2.0 + jnp.tanh(taken[3 + c])) for c in range(3)
    ]
    return (passed - weight, *colours, depth + extinct)


def inner_kernel(zs, xs, scale, cross_ref, merged_ref, table_ref, ids_ref, strip_ref, inner_ref, full_ref, looked_ref, filtered_ref, taken_ref, wide_ref):
    tiles, each = xs // TILE, 16
    tables = tables_of(table_ref, wide_ref, scale)
    for group in range(merged_ref.shape[0]):
        rows = Rows([merged_ref[group, pl.ds(TILE + t, TILE, stride=tiles), :] for t in range(tiles)], merged_ref[group, 0:TILE])
        for k, values in enumerate((rows.blur(), rows.blur2(), rows.slope())):
            for t in range(tiles):
                filtered_ref[k, group, t * TILE : t * TILE + TILE, :] = values[t]

    def strip_step(step, carry):
        first = step * each
        for k, parts in enumerate(((0, 1, 2, 3), (4, 6), (5,))):
            strips = []
            for j in range(each):
                group = lax.div(first + j, GROUP)
                slot = first + j - group * GROUP
                strips.append(pltpu.roll(filtered_ref[k, group], lax.rem(128 - SLOT * slot, 128), 1))
            columns = slice((0, 512, 768)[k], (512, 768, 896)[k])
            result = jnp.dot(
                halves(jnp.concatenate(strips, axis=0)), strip_ref[:, columns], preferred_element_type=jnp.float32
            )
            for n, part in enumerate(parts):
                share = result[:, 128 * n : 128 * n + 128].reshape(each, xs, 128)
                full_ref[part, pl.ds(first, each)] = cross_ref[part, pl.ds(first, each)] + share
        return carry

    lax.fori_loop(0, zs // each, strip_step, 0)

    ahead = taken_ref.shape[1]
    steps = (zs - 4) // ahead

    def take(step):
        first = 2 + ahead * step
        for t in range(tiles):
            rows = slice(t * TILE, t * TILE + TILE)
            held = {}

            def load(part, j):
                if (part, j) not in held:
                    held[part, j] = full_ref[part, first + j, rows]
                return held[part, j]

            for j in range(ahead):
                taken = before_shade(load, j) + look_up(tables, ids_ref, first + j, t, tiles)
                for k, values in enumerate(taken):
                    taken_ref[k, j, rows] = values

    def advance(step, state):
        for j in range(ahead):
            taken = [taken_ref[k, j] for k in range(10)]
            state = shade(state, taken[:6], taken[6:])
        return state

    def z_step(step, state):
        state = advance(step, state)
        take(step + 1)
        return state

    for k, z in enumerate((0, 1, zs - 2, zs - 1)):
        for t in range(tiles):
            for c, values in enumerate(look_up(tables, ids_ref, z, t, tiles)):
                looked_ref[c, k, t * TILE : t * TILE + TILE, :] = values
    zero = jnp.zeros((xs, 128), jnp.float32)
    take(0)
    state = lax.fori_loop(0, steps - 1, z_step, (zero + 1.0, zero, zero, zero, zero))
    for k, values in enumerate(advance(steps - 1, state)):
        inner_ref[k] = values


def edge_kernel(zs, xs, fb_ref, fa_ref, cross_ref, looked_ref, inner_ref, *rest):
    out_refs, (near_ref, rows_ref, image_ref) = rest[:-3], rest[-3:]
    zfirst, zlast, zodd = place_of("gz")
    block = xs + TILE
    tiles = xs // TILE
    lane = lax.broadcasted_iota(jnp.int32, (1, 128), 1)
    for side in range(2):
        first, second = (fa_ref, fb_ref) if side == 0 else (fb_ref, fa_ref)

        def face(start, count):
            return jnp.where(zodd, first[start : start + count, :], second[start : start + count, :])

        ends = [face(FACE * xs, TILE), face(FACE * xs + TILE, TILE)]
        strips = face(FACE * xs + 2 * TILE, TILE)
        for j in range(FACE):
            field = max(j - 1, 0)
            layer = j if j < 2 else (1 if side == 0 else 0)
            turned = TILE // 2 * j if j < 2 else 2 * field - 2
            outer_rows = ends[min(field, 1)]
            if turned:
                outer_rows = pltpu.roll(outer_rows, TILE - turned, 0)
            at_lane = SLOT * layer + slot_of(field)[0]
            own = 126 if field == 0 else 127
            halo = [pltpu.roll(strips, (own - at_lane - SPAN * t) % 128, 1) for t in range(block // TILE)]
            values = jnp.concatenate([outer_rows, face(j * xs, xs)], axis=0)
            results = along_y(values, jnp.concatenate(halo, axis=0), lane, field == 0)
            for part, result in zip((0, 1, 2) if field == 0 else (2 + field,), results):
                rows_ref[side, layer, part] = result
    for side in range(2):
        edge = zfirst if side == 0 else zlast
        for layer in range(2):
            mirrored = 0 if side == 0 else zs - 1
            outer = layer == side

            def part_rows(part):
                ref = rows_ref.at[side, layer, part]
                return Rows([ref[pl.ds(TILE + t, TILE, stride=tiles), :] for t in range(tiles)], ref[0:TILE, :])

            twice, sloped = part_rows(1), part_rows(2)
            for part, values in zip((4, 5, 6), (twice.blur2(), twice.slope(), sloped.blur2())):
                for t in range(tiles):
                    rows = slice(t * TILE, t * TILE + TILE)
                    fill = -cross_ref[part, mirrored, rows] if outer else 0.0
                    near_ref[part, 2 * side + layer, rows] = jnp.where(edge, fill, values[t])
            if not outer:
                for part, source in enumerate((0, 3, 4, 5)):
                    for t, values in enumerate(part_rows(source).blur()):
                        near_ref[part, 2 * side + layer, t * TILE : t * TILE + TILE] = jnp.where(edge, 0.0, values)

    def load(part, z):
        if z < 0:
            return near_ref[part, z + 2]
        if z >= zs:
            return near_ref[part, z - zs + 2]
        return cross_ref[part, z]

    def behind(state, z):
        looked = [looked_ref[c, z if z < 2 else z - zs + 4] for c in range(4)]
        return shade(state, before_shade(load, z), looked)

    zero = jnp.zeros((xs, 128), jnp.float32)
    state = behind(behind((zero + 1.0, zero, zero, zero, zero), 0), 1)
    passed = state[0]
    state = (
        passed * inner_ref[0],
        state[1] + passed * inner_ref[1],
        state[2] + passed * inner_ref[2],
        state[3] + passed * inner_ref[3],
        state[4] + inner_ref[4],
    )
    state = behind(behind(state, zs - 2), zs - 1)
    for c in range(4):
        for t in range(tiles):
            image_ref[c, pl.ds(t, TILE, stride=tiles), :] = state[1 + c][t * TILE : t * TILE + TILE]
    if len(out_refs) == 1:
        out_refs[0][...] = image_ref[...]
    else:
        part = xs // len(out_refs)
        for k, ref in enumerate(out_refs):
            ref[...] = image_ref[:, pl.ds(pl.multiple_of((lax.axis_index("gz") ^ k) * part, part), part), :]


def blend_kernel(near_ref, *refs):
    images, out_ref = refs[:-1], refs[-1]
    count = len(images)
    depths = [image[3] for image in images]
    colours = [jnp.zeros_like(depths[0])] * 3
    for k in range(count):
        prior = jnp.zeros_like(depths[0])
        for other in range(count):
            if other != k:
                prior += near_ref[k * count + other] * depths[other]
        through = jnp.exp(-prior)
        colours = [colours[c] + through * images[k][c] for c in range(3)]
    total = functools.reduce(jnp.add, depths)
    out_ref[0], out_ref[1], out_ref[2] = colours
    small = total * polynomial(EXPM1, total)
    out_ref[3] = jnp.where(total < 0.5, small, 1.0 - jnp.exp(-total))


def call(kernel, out_shape, specs, scratch=(), cost=1.0, name=None, limit=VMEM_LIMIT):
    where = {"s": pltpu.SMEM, "v": pltpu.VMEM, "a": pl.ANY}
    return pl.pallas_call(
        kernel,
        out_shape=out_shape,
        in_specs=[pl.BlockSpec(memory_space=where[s]) for s in specs],
        out_specs=jax.tree.map(lambda _: pl.BlockSpec(memory_space=pltpu.VMEM), out_shape),
        scratch_shapes=list(scratch),
        compiler_params=pltpu.CompilerParams(vmem_limit_bytes=limit),
        cost_estimate=pl.CostEstimate(flops=0, bytes_accessed=int(cost * 3.0e6), transcendentals=0),
        name=name,
    )


def swap_pairs(first, second, axis, idle):
    count, others = lax.axis_size(axis), lax.axis_size(idle)
    even = [(i, i ^ 1) for i in range(count)]
    if count == 2:
        one = lax.ppermute(first, axis, even)
        return one, one
    pairs = []
    for i in range(count):
        for j in range(others):
            end = i in (0, count - 1)
            to = (i if end else i + 1 if i % 2 else i - 1, j ^ 1 if end else j)
            if axis < idle:
                pairs.append((i * others + j, to[0] * others + to[1]))
            else:
                pairs.append((j * count + i, to[1] * count + to[0]))
    two = lax.ppermute(second, tuple(sorted((axis, idle))), pairs)
    return lax.ppermute(first, axis, even), two


def swap_corners(values, x_kind, y_kind):
    counts = [lax.axis_size(a) for a in ("gx", "gy")]

    def partner(at, count, kind):
        to = at ^ 1 if kind == 0 else at + 1 if at % 2 else at - 1
        return to if 0 <= to < count else at

    pairs = []
    for i in range(counts[0]):
        for j in range(counts[1]):
            to = partner(i, counts[0], x_kind), partner(j, counts[1], y_kind)
            pairs.append((i * counts[1] + j, to[0] * counts[1] + to[1]))
    return lax.ppermute(values, ("gx", "gy"), pairs)


def on_device(fields, material, depth_order, table):
    _, zs, xs, ys = fields.shape
    nx, nz = lax.axis_size("gx"), lax.axis_size("gz")
    block = xs + TILE
    part = xs // nz
    swaps = nz in (2, 4)
    offsets = [0] + list(range(nz - 1, 0, -1)) if swaps else None
    groups = -(-zs // GROUP)
    f32 = lambda *shape: jax.ShapeDtypeStruct(shape, jnp.float32)

    def side(even_high):
        return call(functools.partial(rows_kernel, zs, xs, even_high), f32(FACE, zs, ys), "v", name="x_rows")(fields)

    x_a, x_b = swap_pairs(side(True), side(False) if nx > 2 else None, "gx", "gy")
    strip = jnp.asarray(strip_matrix(ys))
    strips, corners = f32(groups, xs, 128), f32(groups, TILE, 128)
    faces = f32(FACE * xs, ys)
    main, m_a, m_b, *c = call(
        functools.partial(pack_kernel, zs, xs),
        (strips, faces, faces) + (corners,) * (1 if nx == 2 else 2),
        "v",
        cost=0.7,
        name="pack",
    )(fields)
    y_a, y_b = swap_pairs(main, main, "gy", "gx")
    d = [swap_corners(values, x_kind, y_kind) for x_kind, values in enumerate(c) for y_kind in (0, 1)]
    rows, cell = call(
        functools.partial(cells_kernel, zs, xs),
        (f32(6, zs, xs, ys), jax.ShapeDtypeStruct((256, 3 * ys), jnp.bfloat16)),
        "v",
        cost=1.3,
        name="cells",
    )(fields)
    halo = call(functools.partial(x_halo_kernel, zs, xs), f32(4, zs, TILE, ys), "vvv", cost=0.2, name="x_halo")(
        fields, x_a, x_b
    )
    cross, nearer = call(
        functools.partial(cross_kernel, zs, xs, offsets),
        (f32(7, zs, xs, ys), f32(nz * nz, 1, 128)),
        "vvvv",
        [pltpu.VMEM((6, zs, TILE, ys), jnp.float32)],
        cost=1.0,
        name="cross",
    )(depth_order[None], rows, halo, cell)
    y_a, y_b, d, cross = lax.optimization_barrier((y_a, y_b, d, cross))

    faces = f32(FACE * xs + 3 * TILE, ys)
    merged, f_a, f_b = call(
        functools.partial(join_kernel, zs, xs),
        (f32(groups, block, 128), faces, faces),
        "v" * (6 + len(d)),
        name="join",
    )(m_a, m_b, halo, main, y_a, y_b, *d)
    z_a, z_b = swap_pairs(f_a, f_b, "gz", "gy")

    scale = 2.0 / (zs * nz)
    inner, full, looked = call(
        functools.partial(inner_kernel, zs, xs, scale),
        (f32(5, xs, ys), f32(7, zs, xs, ys), f32(4, 4, xs, ys)),
        "vvvvv",
        [
            pltpu.VMEM((3, groups, xs, 128), jnp.float32),
            pltpu.VMEM((10, 4, xs, ys), jnp.float32),
            pltpu.VMEM((4, 128), jnp.float32),
        ],
        cost=4.0,
        name="inner",
    )(cross, merged, table, material, strip)

    images = call(
        functools.partial(edge_kernel, zs, xs),
        [f32(4, part, ys)] * nz if swaps else [f32(4, xs, ys)],
        "vvvvv",
        [
            pltpu.VMEM((7, 4, xs, ys), jnp.float32),
            pltpu.VMEM((2, 2, 6, block, ys), jnp.float32),
            pltpu.VMEM((4, xs, ys), jnp.float32),
        ],
        name="edges",
    )(z_b, z_a, full, looked, inner)

    if swaps:
        mine = [images[0]]
        for k in offsets[1:]:
            mine.append(lax.ppermute(images[k], "gz", [(i, i ^ k) for i in range(nz)]))
    else:
        stacked = lax.all_to_all(images[0].reshape(4, nz, part, ys), "gz", split_axis=1, concat_axis=1)
        mine = [stacked[:, b] for b in range(nz)]
    return call(blend_kernel, f32(4, part, ys), "v" + "v" * nz, name="blend")(nearer, *mine)


def solution(mesh):
    return jax.shard_map(
        on_device,
        mesh=mesh,
        in_specs=(P(None, "gz", "gx", "gy"), P("gz", "gx", "gy"), P(), P()),
        out_specs=P(None, ("gx", "gz"), "gy"),
        check_vma=False,
    )
```

```python
import functools

import jax
import jax.numpy as jnp
import ml_dtypes
import numpy as np
from jax import lax
from jax.experimental import pallas as pl
from jax.experimental.pallas import tpu as pltpu
from jax.sharding import PartitionSpec as P

VMEM_LIMIT = 40 * 1024 * 1024
GROUP = 12
SLOT = 10
TILE = 8
FACE = 5
SPAN = 24

LOG1P = (
    0.9999995186059567, -0.49996356582563917, 0.33265255844036573, -0.24453388969978707, 0.17659864766821842,
    -0.10679931280022417, 0.043659288844443055, -0.008466410404849948,
)
EXPM1 = (
    1.0, -0.4999995231628418, 0.1666584461927414, -0.04160914570093155, 0.00814302358776331, -0.0010865303920581937,
)


def polynomial(coefficients, value):
    terms = list(coefficients)
    power = value
    while len(terms) > 1:
        paired = [terms[k] + terms[k + 1] * power for k in range(0, len(terms) - 1, 2)]
        terms = paired + ([terms[-1]] if len(terms) % 2 else [])
        power = power * power if len(terms) > 1 else power
    return terms[0]


BLUR = {off: weight / 64 for off, weight in ((-1, 1), (0, 2), (1, 1))}
BLUR2 = {off: weight / 2048 for off, weight in ((-2, 1), (-1, 4), (0, 6), (1, 4), (2, 1))}
SLOPE = {off: weight / 2048 for off, weight in ((-2, -1), (-1, -2), (1, 2), (2, 1))}


def strip_matrix(ysize):
    strips = np.zeros((128, 7 * ysize), np.float32)
    for block, (taps, field) in enumerate([(BLUR, f) for f in range(4)] + [(BLUR2, 0), (SLOPE, 0), (BLUR2, 0)]):
        first = slot_of(field)[0]
        outside = {-2: 0, -1: 1, ysize: 2, ysize + 1: 3} if field == 0 else {-1: first, ysize: first + 1}
        for out in range(ysize):
            for off, weight in taps.items():
                if not 0 <= out + off < ysize:
                    strips[outside[out + off], block * ysize + out] = weight
    return np.concatenate([strips, strips], axis=0).astype(ml_dtypes.bfloat16)


def make_cell_weights(out_ref):
    off = lax.broadcasted_iota(jnp.int32, (128, 128), 0) - lax.broadcasted_iota(jnp.int32, (128, 128), 1)
    for block, taps in enumerate((BLUR, BLUR2, SLOPE)):
        weights = jnp.zeros((128, 128), jnp.float32)
        for step, weight in taps.items():
            weights = jnp.where(off == step, float(weight), weights)
        for half in range(2):
            out_ref[128 * half : 128 * half + 128, 128 * block : 128 * block + 128] = weights.astype(jnp.bfloat16)


def halves(values):
    high = values.astype(jnp.bfloat16)
    low = (values - high.astype(jnp.float32)).astype(jnp.bfloat16)
    return jnp.concatenate([high, low], axis=1)


def place_of(axis):
    at = lax.axis_index(axis)
    return at == 0, at == lax.axis_size(axis) - 1, lax.rem(at, 2) == 1


def rows_kernel(zs, xs, even_high, fields_ref, out_ref):
    high = (lax.rem(lax.axis_index("gx"), 2) == 0) == even_high
    for group in range(FACE):
        field = max(group - 1, 0)
        rows = fields_ref.at[field].reshape(zs * xs, 128)
        low_row = group if group < 2 else 0
        high_row = xs - 2 + group if group < 2 else xs - 1
        out_ref[group] = rows[pl.ds(jnp.where(high, high_row, low_row), zs, stride=xs), :]


def slot_of(field):
    return (0, 4) if field == 0 else (2 + 2 * field, 2)


def pack_strips(load, layers, lane, rows):
    packed = jnp.zeros((rows, 128), jnp.float32)
    for k, z in enumerate(layers):
        for field in range(4):
            first, count = slot_of(field)
            start = SLOT * k + first
            values = pltpu.roll(load(field, z), (start + count // 2) % 128, 1)
            packed = jnp.where((lane >= start) & (lane < start + count), values, packed)
    return packed


def put_faces(zodd, out_refs, start, low, high):
    for ref, swapped in zip(out_refs, (False, True)):
        ref[start : start + low.shape[0], :] = jnp.where(zodd != swapped, low, high)


def pack_kernel(zs, xs, fields_ref, pack_ref, ma_ref, mb_ref, *corner_refs):
    zodd = place_of("gz")[2]
    for j in range(FACE):
        field = max(j - 1, 0)
        low, high = fields_ref[field, j if j < 2 else 0], fields_ref[field, zs - 2 + j if j < 2 else zs - 1]
        put_faces(zodd, (ma_ref, mb_ref), j * xs, low, high)
    xodd = place_of("gx")[2]
    lane = lax.broadcasted_iota(jnp.int32, (1, 128), 1)
    sub = lax.broadcasted_iota(jnp.int32, (TILE, 1), 0)
    for group in range(pack_ref.shape[0]):
        layers = range(group * GROUP, min(zs, group * GROUP + GROUP))
        packed = pack_strips(lambda f, z: fields_ref[f, z], layers, lane, xs)
        pack_ref[group] = packed
        first, last = packed[0:TILE], packed[xs - TILE :]
        low = jnp.where(sub == TILE - 1, pltpu.roll(first, TILE - 1, 0), pltpu.roll(first, TILE - 3, 0))
        high = jnp.where(sub == 0, pltpu.roll(last, 1, 0), pltpu.roll(last, 3, 0))
        for ref, swapped in zip(corner_refs, (False, True)):
            ref[group] = jnp.where(xodd != swapped, low, high)


def nearer_layers(offsets, order_ref, near_ref):
    iz, count = lax.axis_index("gz"), lax.axis_size("gz")
    order = order_ref[...].astype(jnp.float32)
    lane = lax.broadcasted_iota(jnp.int32, order.shape, 1)
    ranks = [
        jnp.sum(jnp.where(lane == (iz ^ offsets[k] if offsets else k), order, 0.0), axis=1, keepdims=True)
        for k in range(count)
    ]
    for k in range(count):
        for other in range(count):
            nearer = jnp.where(ranks[other] < ranks[k], 1.0, 0.0)
            near_ref[k * count + other] = jnp.broadcast_to(nearer, (1, 128))


def tables_of(table_ref, wide_ref, scale):
    wide_ref[...] = jnp.zeros_like(wide_ref)
    wide_ref[:, 0 : table_ref.shape[1]] = table_ref[...]
    return [jnp.broadcast_to(wide_ref[c : c + 1, :] * (0.5 if c < 3 else scale), (TILE, 128)) for c in range(4)]


def look_up(tables, ids_ref, z, t, tiles):
    ids = ids_ref[z, pl.ds(t, TILE, stride=tiles), :]
    return [jnp.take_along_axis(row, ids, axis=1, mode="promise_in_bounds") for row in tables]


def x_halo_kernel(zs, xs, fields_ref, xa_ref, xb_ref, halo_ref):
    xfirst, xlast, xodd = place_of("gx")
    halo_ref[...] = jnp.zeros_like(halo_ref)
    for field in range(4):
        tiles = halo_ref.at[field].reshape(zs * TILE, 128)
        own = fields_ref.at[field].reshape(zs * xs, 128)
        at = 0 if field == 0 else 1 + field
        below = jnp.where(xodd, xa_ref[1 + field], xb_ref[1 + field])
        above = jnp.where(xodd, xb_ref[at], xa_ref[at])
        tiles[pl.ds(0, zs, stride=TILE), :] = jnp.where(xfirst, 0.0, below)
        tiles[pl.ds(TILE - 1, zs, stride=TILE), :] = jnp.where(xlast, 0.0, above)
        if field == 0:
            low, high = own[pl.ds(0, zs, stride=xs), :], own[pl.ds(xs - 1, zs, stride=xs), :]
            tiles[pl.ds(1, zs, stride=TILE), :] = jnp.where(xfirst, -low, jnp.where(xodd, xa_ref[0], xb_ref[0]))
            tiles[pl.ds(TILE - 2, zs, stride=TILE), :] = jnp.where(xlast, -high, jnp.where(xodd, xb_ref[1], xa_ref[1]))


def join_kernel(zs, xs, ma_ref, mb_ref, halo_ref, own_ref, ya_ref, yb_ref, *rest):
    corner_refs, (merged_ref, fa_ref, fb_ref) = rest[:-3], rest[-3:]
    xfirst, xlast, xodd = place_of("gx")
    yfirst, ylast, yodd = place_of("gy")
    zodd = place_of("gz")[2]
    block = xs + TILE
    lane = lax.broadcasted_iota(jnp.int32, (1, 128), 1)
    sub = lax.broadcasted_iota(jnp.int32, (TILE, 1), 0)
    place = lax.rem(lane, SLOT)
    from_left = (place < 2) | ((place >= 4) & (lax.rem(place, 2) == 0))

    def merge(own, first, second):
        fill_left = jnp.where(place == 0, -pltpu.roll(own, 126, 1), 0.0)
        fill_right = jnp.where(place == 3, -pltpu.roll(own, 2, 1), 0.0)
        left = jnp.where(yfirst, fill_left, jnp.where(yodd, first, second))
        right = jnp.where(ylast, fill_right, jnp.where(yodd, second, first))
        return jnp.where(from_left, left, right)

    for group in range(own_ref.shape[0]):
        main = merge(own_ref[group], ya_ref[group], yb_ref[group])
        merged_ref[group, TILE:] = main
        tiles = []
        for k in range(2):
            a, b = corner_refs[k][group], corner_refs[k - 2][group]
            tiles.append(jnp.where(sub < TILE // 2, jnp.where(xodd, a, b), jnp.where(xodd, b, a)))
        tile = merge(tiles[1], tiles[0], tiles[1])
        low = jnp.where(sub == 1, -pltpu.roll(main[0:TILE], 1, 0), 0.0)
        high = jnp.where(sub == TILE - 2, -pltpu.roll(main[xs - TILE :], TILE - 1, 0), 0.0)
        tile = jnp.where(xfirst & (sub < TILE // 2), low, tile)
        merged_ref[group, 0:TILE] = jnp.where(xlast & (sub >= TILE // 2), high, tile)

    ends = (sub < 2) | (sub >= TILE - 2)

    def density_rows(z):
        return jnp.where(ends, halo_ref[0, z], pltpu.roll(halo_ref[0, z + 1], TILE // 2, 0))

    def field_rows(z):
        rows = [pltpu.roll(halo_ref[f, z], 2 * f - 2, 0) if f > 1 else halo_ref[f, z] for f in (1, 2, 3)]
        mixed = jnp.where((sub == 0) | (sub == TILE - 1), rows[0], rows[1])
        return jnp.where((sub == 3) | (sub == 4), rows[2], mixed)

    def strips(z):
        group, k = divmod(z, GROUP)
        packed = jnp.zeros((TILE, 128), jnp.float32)
        for t in range(block // TILE):
            moved = pltpu.roll(merged_ref[group, t * TILE : t * TILE + TILE], (SPAN * t - SLOT * k) % 128, 1)
            packed = jnp.where((lane >= SPAN * t) & (lane < SPAN * t + SPAN), moved, packed)
        return packed

    outs, start = (fa_ref, fb_ref), FACE * xs
    fa_ref[0:start, :] = ma_ref[...]
    fb_ref[0:start, :] = mb_ref[...]
    put_faces(zodd, outs, start, density_rows(0), density_rows(zs - 2))
    put_faces(zodd, outs, start + TILE, field_rows(0), field_rows(zs - 1))
    put_faces(zodd, outs, start + 2 * TILE, strips(0), strips(zs - 2))


def along_y(values, halo, lane, density):
    def shifted(off):
        mixed = jnp.where(lane >= 128 - off if off > 0 else lane < -off, halo, values)
        return pltpu.roll(mixed, off % 128, 1)

    m1, p1 = shifted(1), shifted(-1)
    near = m1 + p1
    blur = BLUR[1] * near + BLUR[0] * values
    if not density:
        return (blur,)
    m2, p2 = shifted(2), shifted(-2)
    twice = BLUR2[2] * (m2 + p2) + BLUR2[1] * near + BLUR2[0] * values
    return blur, twice, SLOPE[2] * (p2 - m2) + SLOPE[1] * (p1 - m1)


class Rows:
    def __init__(self, tiles, halo):
        self.tiles, self.halo = list(tiles), halo
        self.sub = lax.broadcasted_iota(jnp.int32, (TILE, 1), 0)
        self.made = {}

    def row(self, t):
        count = len(self.tiles)
        if 0 <= t < count:
            return self.tiles[t]
        if t not in self.made:
            down = t < 0
            step = -t - 1 if down else t - count
            halo = self.halo if step == 0 else pltpu.roll(self.halo, TILE - 1 if down else 1, 0)
            inner = pltpu.roll(self.tiles[t % count], 1 if down else TILE - 1, 0)
            self.made[t] = jnp.where(self.sub == (0 if down else TILE - 1), halo, inner)
        return self.made[t]

    def pair(self, level, t):
        if level == 0:
            return self.row(t)
        if (level, t) not in self.made:
            self.made[level, t] = self.pair(level - 1, t) + self.pair(level - 1, t + 1)
        return self.made[level, t]

    def blur(self):
        return [self.pair(2, t - 1) for t in range(len(self.tiles))]

    def blur2(self):
        return [self.pair(4, t - 2) for t in range(len(self.tiles))]

    def slope(self):
        return [self.pair(2, t) - self.pair(2, t - 2) for t in range(len(self.tiles))]


def cells_kernel(zs, xs, fields_ref, out_ref, cell_ref):
    each, tiles = 32, xs // TILE
    make_cell_weights(cell_ref)

    def step(k, carry):
        first = k * each
        for field in range(4):
            rows = [
                fields_ref[field, first + j, pl.ds(t, TILE, stride=tiles), :] for j in range(each) for t in range(tiles)
            ]
            weights = cell_ref[...] if field == 0 else cell_ref[:, 0:128]
            result = jnp.dot(halves(jnp.concatenate(rows, axis=0)), weights, preferred_element_type=jnp.float32)
            for part in (0, 1, 2) if field == 0 else (2 + field,):
                columns = slice(128 * part, 128 * part + 128) if field == 0 else slice(0, 128)
                out_ref[part, pl.ds(first, each)] = result[:, columns].reshape(each, xs, 128)
        return carry

    lax.fori_loop(0, zs // each, step, 0)


def cross_kernel(zs, xs, offsets, order_ref, rows_ref, halo_ref, cell_ref, out_ref, near_ref, edge_ref):
    each, tiles = 4, xs // TILE
    nearer_layers(offsets, order_ref, near_ref)
    for field in range(4):
        weights = cell_ref[...] if field == 0 else cell_ref[:, 0:128]
        result = jnp.dot(
            halves(halo_ref[field].reshape(zs * TILE, 128)), weights, preferred_element_type=jnp.float32
        )
        for part in (0, 1, 2) if field == 0 else (2 + field,):
            columns = slice(128 * part, 128 * part + 128) if field == 0 else slice(0, 128)
            edge_ref[part] = result[:, columns].reshape(zs, TILE, 128)

    def step(k, carry):
        for j in range(each):
            z = k * each + j

            def part_rows(part):
                return Rows([rows_ref[part, z, t * TILE : t * TILE + TILE, :] for t in range(tiles)], edge_ref[part, z])

            twice, sloped = part_rows(1), part_rows(2)
            results = [part_rows(part).blur() for part in (0, 3, 4, 5)]
            results += [twice.blur2(), twice.slope(), sloped.blur2()]
            for part, values in enumerate(results):
                for t in range(tiles):
                    out_ref[part, z, t * TILE : t * TILE + TILE, :] = values[t]
        return carry

    lax.fori_loop(0, zs // each, step, 0)


def before_shade(load, z):
    def blur(part):
        return load(part, z - 1) + load(part, z + 1) + 2.0 * load(part, z)

    def blur2(part):
        return (load(part, z - 2) + load(part, z + 2)) + 4.0 * (load(part, z - 1) + load(part, z + 1)) + 6.0 * load(part, z)

    near = load(4, z + 1) - load(4, z - 1)
    grad_z = (load(4, z + 2) - load(4, z - 2)) + (near + near)
    grad_x = blur2(5)
    grad_y = blur2(6)
    facing = jnp.abs(0.8 * (grad_z + grad_y) + 0.4 * grad_x)
    square = grad_z * grad_z + grad_x * grad_x + grad_y * grad_y
    shading = 0.3 + facing * lax.rsqrt(square + 0.0025)
    density = 3.0 * blur(0)
    return [density, jnp.exp(-jnp.abs(density)), shading] + [blur(1 + c) for c in range(3)]


def shade(state, taken, looked):
    density, t, shading = taken[:3]
    soft = jnp.maximum(density, 0.0) + t * polynomial(LOG1P, t)
    extinct = looked[3] * soft
    passed, total, depth = state[0], state[1:4], state[4]
    weight = passed * (extinct * polynomial(EXPM1, extinct))
    lit = weight * shading
    colours = [
        total[c] + (looked[c] * lit) * (2.0 + jnp.tanh(taken[3 + c])) for c in range(3)
    ]
    return (passed - weight, *colours, depth + extinct)


def inner_kernel(zs, xs, scale, cross_ref, merged_ref, table_ref, ids_ref, strip_ref, inner_ref, full_ref, looked_ref, filtered_ref, taken_ref, wide_ref):
    tiles, each = xs // TILE, 32
    tables = tables_of(table_ref, wide_ref, scale)
    for group in range(merged_ref.shape[0]):
        rows = Rows([merged_ref[group, pl.ds(TILE + t, TILE, stride=tiles), :] for t in range(tiles)], merged_ref[group, 0:TILE])
        for k, values in enumerate((rows.blur(), rows.blur2(), rows.slope())):
            for t in range(tiles):
                filtered_ref[k, group, t * TILE : t * TILE + TILE, :] = values[t]

    def strip_step(step, carry):
        first = step * each
        for k, parts in enumerate(((0, 1, 2, 3), (4, 6), (5,))):
            strips = []
            for j in range(each):
                group = lax.div(first + j, GROUP)
                slot = first + j - group * GROUP
                strips.append(pltpu.roll(filtered_ref[k, group], lax.rem(128 - SLOT * slot, 128), 1))
            columns = slice((0, 512, 768)[k], (512, 768, 896)[k])
            result = jnp.dot(
                halves(jnp.concatenate(strips, axis=0)), strip_ref[:, columns], preferred_element_type=jnp.float32
            )
            for n, part in enumerate(parts):
                share = result[:, 128 * n : 128 * n + 128].reshape(each, xs, 128)
                full_ref[part, pl.ds(first, each)] = cross_ref[part, pl.ds(first, each)] + share
        return carry

    lax.fori_loop(0, zs // each, strip_step, 0)

    ahead = taken_ref.shape[1]
    steps = (zs - 4) // ahead

    def take(step):
        first = 2 + ahead * step
        for t in range(tiles):
            rows = slice(t * TILE, t * TILE + TILE)
            held = {}

            def load(part, j):
                if (part, j) not in held:
                    held[part, j] = full_ref[part, first + j, rows]
                return held[part, j]

            for j in range(ahead):
                taken = before_shade(load, j) + look_up(tables, ids_ref, first + j, t, tiles)
                for k, values in enumerate(taken):
                    taken_ref[k, j, rows] = values

    def advance(step, state):
        for j in range(ahead):
            taken = [taken_ref[k, j] for k in range(10)]
            state = shade(state, taken[:6], taken[6:])
        return state

    def z_step(step, state):
        state = advance(step, state)
        take(step + 1)
        return state

    for k, z in enumerate((0, 1, zs - 2, zs - 1)):
        for t in range(tiles):
            for c, values in enumerate(look_up(tables, ids_ref, z, t, tiles)):
                looked_ref[c, k, t * TILE : t * TILE + TILE, :] = values
    zero = jnp.zeros((xs, 128), jnp.float32)
    take(0)
    state = lax.fori_loop(0, steps - 1, z_step, (zero + 1.0, zero, zero, zero, zero))
    for k, values in enumerate(advance(steps - 1, state)):
        inner_ref[k] = values


def edge_kernel(zs, xs, fb_ref, fa_ref, cross_ref, looked_ref, inner_ref, *rest):
    out_refs, (near_ref, rows_ref, image_ref) = rest[:-3], rest[-3:]
    zfirst, zlast, zodd = place_of("gz")
    block = xs + TILE
    tiles = xs // TILE
    lane = lax.broadcasted_iota(jnp.int32, (1, 128), 1)
    for side in range(2):
        first, second = (fa_ref, fb_ref) if side == 0 else (fb_ref, fa_ref)

        def face(start, count):
            return jnp.where(zodd, first[start : start + count, :], second[start : start + count, :])

        ends = [face(FACE * xs, TILE), face(FACE * xs + TILE, TILE)]
        strips = face(FACE * xs + 2 * TILE, TILE)
        for j in range(FACE):
            field = max(j - 1, 0)
            layer = j if j < 2 else (1 if side == 0 else 0)
            turned = TILE // 2 * j if j < 2 else 2 * field - 2
            outer_rows = ends[min(field, 1)]
            if turned:
                outer_rows = pltpu.roll(outer_rows, TILE - turned, 0)
            at_lane = SLOT * layer + slot_of(field)[0]
            own = 126 if field == 0 else 127
            halo = [pltpu.roll(strips, (own - at_lane - SPAN * t) % 128, 1) for t in range(block // TILE)]
            values = jnp.concatenate([outer_rows, face(j * xs, xs)], axis=0)
            results = along_y(values, jnp.concatenate(halo, axis=0), lane, field == 0)
            for part, result in zip((0, 1, 2) if field == 0 else (2 + field,), results):
                rows_ref[side, layer, part] = result
    for side in range(2):
        edge = zfirst if side == 0 else zlast
        for layer in range(2):
            mirrored = 0 if side == 0 else zs - 1
            outer = layer == side

            def part_rows(part):
                ref = rows_ref.at[side, layer, part]
                return Rows([ref[pl.ds(TILE + t, TILE, stride=tiles), :] for t in range(tiles)], ref[0:TILE, :])

            twice, sloped = part_rows(1), part_rows(2)
            for part, values in zip((4, 5, 6), (twice.blur2(), twice.slope(), sloped.blur2())):
                for t in range(tiles):
                    rows = slice(t * TILE, t * TILE + TILE)
                    fill = -cross_ref[part, mirrored, rows] if outer else 0.0
                    near_ref[part, 2 * side + layer, rows] = jnp.where(edge, fill, values[t])
            if not outer:
                for part, source in enumerate((0, 3, 4, 5)):
                    for t, values in enumerate(part_rows(source).blur()):
                        near_ref[part, 2 * side + layer, t * TILE : t * TILE + TILE] = jnp.where(edge, 0.0, values)

    def load(part, z):
        if z < 0:
            return near_ref[part, z + 2]
        if z >= zs:
            return near_ref[part, z - zs + 2]
        return cross_ref[part, z]

    def behind(state, z):
        looked = [looked_ref[c, z if z < 2 else z - zs + 4] for c in range(4)]
        return shade(state, before_shade(load, z), looked)

    zero = jnp.zeros((xs, 128), jnp.float32)
    state = behind(behind((zero + 1.0, zero, zero, zero, zero), 0), 1)
    passed = state[0]
    state = (
        passed * inner_ref[0],
        state[1] + passed * inner_ref[1],
        state[2] + passed * inner_ref[2],
        state[3] + passed * inner_ref[3],
        state[4] + inner_ref[4],
    )
    state = behind(behind(state, zs - 2), zs - 1)
    for c in range(4):
        for t in range(tiles):
            image_ref[c, pl.ds(t, TILE, stride=tiles), :] = state[1 + c][t * TILE : t * TILE + TILE]
    if len(out_refs) == 1:
        out_refs[0][...] = image_ref[...]
    else:
        part = xs // len(out_refs)
        for k, ref in enumerate(out_refs):
            ref[...] = image_ref[:, pl.ds(pl.multiple_of((lax.axis_index("gz") ^ k) * part, part), part), :]


def blend_kernel(near_ref, *refs):
    images, out_ref = refs[:-1], refs[-1]
    count = len(images)
    depths = [image[3] for image in images]
    colours = [jnp.zeros_like(depths[0])] * 3
    for k in range(count):
        prior = jnp.zeros_like(depths[0])
        for other in range(count):
            if other != k:
                prior += near_ref[k * count + other] * depths[other]
        through = jnp.exp(-prior)
        colours = [colours[c] + through * images[k][c] for c in range(3)]
    total = functools.reduce(jnp.add, depths)
    out_ref[0], out_ref[1], out_ref[2] = colours
    small = total * polynomial(EXPM1, total)
    out_ref[3] = jnp.where(total < 0.5, small, 1.0 - jnp.exp(-total))


def call(kernel, out_shape, specs, scratch=(), cost=1.0, name=None, limit=VMEM_LIMIT):
    where = {"s": pltpu.SMEM, "v": pltpu.VMEM, "a": pl.ANY}
    return pl.pallas_call(
        kernel,
        out_shape=out_shape,
        in_specs=[pl.BlockSpec(memory_space=where[s]) for s in specs],
        out_specs=jax.tree.map(lambda _: pl.BlockSpec(memory_space=pltpu.VMEM), out_shape),
        scratch_shapes=list(scratch),
        compiler_params=pltpu.CompilerParams(vmem_limit_bytes=limit),
        cost_estimate=pl.CostEstimate(flops=0, bytes_accessed=int(cost * 3.0e6), transcendentals=0),
        name=name,
    )


def swap_pairs(first, second, axis, idle):
    count, others = lax.axis_size(axis), lax.axis_size(idle)
    even = [(i, i ^ 1) for i in range(count)]
    if count == 2:
        one = lax.ppermute(first, axis, even)
        return one, one
    pairs = []
    for i in range(count):
        for j in range(others):
            end = i in (0, count - 1)
            to = (i if end else i + 1 if i % 2 else i - 1, j ^ 1 if end else j)
            if axis < idle:
                pairs.append((i * others + j, to[0] * others + to[1]))
            else:
                pairs.append((j * count + i, to[1] * count + to[0]))
    two = lax.ppermute(second, tuple(sorted((axis, idle))), pairs)
    return lax.ppermute(first, axis, even), two


def swap_corners(values, x_kind, y_kind):
    counts = [lax.axis_size(a) for a in ("gx", "gy")]

    def partner(at, count, kind):
        to = at ^ 1 if kind == 0 else at + 1 if at % 2 else at - 1
        return to if 0 <= to < count else at

    pairs = []
    for i in range(counts[0]):
        for j in range(counts[1]):
            to = partner(i, counts[0], x_kind), partner(j, counts[1], y_kind)
            pairs.append((i * counts[1] + j, to[0] * counts[1] + to[1]))
    return lax.ppermute(values, ("gx", "gy"), pairs)


def on_device(fields, material, depth_order, table):
    _, zs, xs, ys = fields.shape
    nx, nz = lax.axis_size("gx"), lax.axis_size("gz")
    block = xs + TILE
    part = xs // nz
    swaps = nz in (2, 4)
    offsets = [0] + list(range(nz - 1, 0, -1)) if swaps else None
    groups = -(-zs // GROUP)
    f32 = lambda *shape: jax.ShapeDtypeStruct(shape, jnp.float32)

    def side(even_high):
        return call(functools.partial(rows_kernel, zs, xs, even_high), f32(FACE, zs, ys), "v", name="x_rows")(fields)

    x_a, x_b = swap_pairs(side(True), side(False) if nx > 2 else None, "gx", "gy")
    strip = jnp.asarray(strip_matrix(ys))
    strips, corners = f32(groups, xs, 128), f32(groups, TILE, 128)
    faces = f32(FACE * xs, ys)
    main, m_a, m_b, *c = call(
        functools.partial(pack_kernel, zs, xs),
        (strips, faces, faces) + (corners,) * (1 if nx == 2 else 2),
        "v",
        cost=0.7,
        name="pack",
    )(fields)
    y_a, y_b = swap_pairs(main, main, "gy", "gx")
    d = [swap_corners(values, x_kind, y_kind) for x_kind, values in enumerate(c) for y_kind in (0, 1)]
    rows, cell = call(
        functools.partial(cells_kernel, zs, xs),
        (f32(6, zs, xs, ys), jax.ShapeDtypeStruct((256, 3 * ys), jnp.bfloat16)),
        "v",
        cost=1.3,
        name="cells",
    )(fields)
    halo = call(functools.partial(x_halo_kernel, zs, xs), f32(4, zs, TILE, ys), "vvv", cost=0.2, name="x_halo")(
        fields, x_a, x_b
    )
    cross, nearer = call(
        functools.partial(cross_kernel, zs, xs, offsets),
        (f32(7, zs, xs, ys), f32(nz * nz, 1, 128)),
        "vvvv",
        [pltpu.VMEM((6, zs, TILE, ys), jnp.float32)],
        cost=1.0,
        name="cross",
    )(depth_order[None], rows, halo, cell)
    y_a, y_b, d, cross = lax.optimization_barrier((y_a, y_b, d, cross))

    faces = f32(FACE * xs + 3 * TILE, ys)
    merged, f_a, f_b = call(
        functools.partial(join_kernel, zs, xs),
        (f32(groups, block, 128), faces, faces),
        "v" * (6 + len(d)),
        name="join",
    )(m_a, m_b, halo, main, y_a, y_b, *d)
    z_a, z_b = swap_pairs(f_a, f_b, "gz", "gy")

    scale = 2.0 / (zs * nz)
    inner, full, looked = call(
        functools.partial(inner_kernel, zs, xs, scale),
        (f32(5, xs, ys), f32(7, zs, xs, ys), f32(4, 4, xs, ys)),
        "vvvvv",
        [
            pltpu.VMEM((3, groups, xs, 128), jnp.float32),
            pltpu.VMEM((10, 4, xs, ys), jnp.float32),
            pltpu.VMEM((4, 128), jnp.float32),
        ],
        cost=4.0,
        name="inner",
    )(cross, merged, table, material, strip)

    images = call(
        functools.partial(edge_kernel, zs, xs),
        [f32(4, part, ys)] * nz if swaps else [f32(4, xs, ys)],
        "vvvvv",
        [
            pltpu.VMEM((7, 4, xs, ys), jnp.float32),
            pltpu.VMEM((2, 2, 6, block, ys), jnp.float32),
            pltpu.VMEM((4, xs, ys), jnp.float32),
        ],
        name="edges",
    )(z_b, z_a, full, looked, inner)

    if swaps:
        mine = [images[0]]
        for k in offsets[1:]:
            mine.append(lax.ppermute(images[k], "gz", [(i, i ^ k) for i in range(nz)]))
    else:
        stacked = lax.all_to_all(images[0].reshape(4, nz, part, ys), "gz", split_axis=1, concat_axis=1)
        mine = [stacked[:, b] for b in range(nz)]
    return call(blend_kernel, f32(4, part, ys), "v" + "v" * nz, name="blend")(nearer, *mine)


def solution(mesh):
    return jax.shard_map(
        on_device,
        mesh=mesh,
        in_specs=(P(None, "gz", "gx", "gy"), P("gz", "gx", "gy"), P(), P()),
        out_specs=P(None, ("gx", "gz"), "gy"),
        check_vma=False,
    )
```
